32 devices in a mesh: row: 4 (over y, core), col: 8 (over z, x).
Axes of the slice: x: 2, y: 2, z: 4, core: 2. Of those that a mesh axis runs over, the one named last changes fastest.
Arguments:
- probes: bfloat16 [4, 8192, 256], P(None, ('row', 'col')), may hold values from -6 to 6
- points: bfloat16 [16, 4, 8192], P(None, None, ('row', 'col')), may hold values from -8 to 8
- leaf_skeleton: int32 [64, 64], P(('row', 'col')), may hold values from 0 to 127, as said below
- skeleton_one: int32 [32, 64], P(('row', 'col')), may hold values from 0 to 127, as said below
- skeleton_two: int32 [16, 64], P('row'), may hold values from 0 to 127, as said below
- skeleton_three: int32 [8, 64], P('row'), may hold values from 0 to 127, as said below
Outputs:
- leaf_interp: float32 [64, 128, 64], P(('row', 'col'))
- upper_interp: float32 [3, 32, 128, 64], P(None, ('row', 'col'))
- top_state: float32 [2, 32, 64, 256], P(None, ('row', 'col'))
The draws below stay inside these ranges and needn't reach their ends.
Inputs may be any that keep to these rules, and one draw needn't show every extreme that they name: `leaf_skeleton`: each row names 64 different rows of its leaf, in ascending order. `skeleton_one`: each row names 64 different rows of the node's stacked child skeletons, in ascending order. `skeleton_two`: each row names 64 different rows of the node's stacked child skeletons, in ascending order. `skeleton_three`: each row names 64 different rows of the node's stacked child skeletons, in ascending order.
All inputs are finite; a program needn't handle non-finite values.
Results may differ from the reference program's by a relative error of at most 0.0059.
Values may be sent and summed in bfloat16 or wider, within the bound.
No kernel may reach another device: no remote copies, remote signals or barrier semaphores. Data moves between devices by JAX's collectives and lax.ppermute only.
A program may use at most 64 MiB of HBM per device.

```python
import math
import jax
import jax.numpy as jnp
from jax import lax

LEAF = 128
RANK = 64
SAMPLES = 256
FEAT = 16
N = 8192


def choose_rows(key, count, pool):
    scores = jax.random.randint(key, (count, pool), 0, 1 << 20) * pool + jnp.arange(pool, dtype=jnp.int32)[None, :]
    order = jnp.argsort(scores, axis=1)[:, :RANK]
    return jnp.sort(order, axis=1).astype(jnp.int32)


def draw_points(key, part):
    first_key, second_key = jax.random.split(jax.random.fold_in(key, 7), 2)
    total_nodes = 4 * N
    stride = 4 * LEAF
    coarse = 0.8 * jax.random.normal(first_key, (FEAT, total_nodes // stride + 1), jnp.float32)
    offsets = jnp.arange(total_nodes, dtype=jnp.int32)
    lower_index = offsets // stride
    fraction = (offsets % stride).astype(jnp.float32) / stride
    smooth = coarse[:, lower_index] * (1.0 - fraction) + coarse[:, lower_index + 1] * fraction
    rough_part = 1.6 * jax.random.normal(second_key, (FEAT, total_nodes), jnp.float32)
    return jnp.clip(smooth + rough_part, -8.0, 8.0).reshape(FEAT, 4, N).astype(jnp.bfloat16)


def draw_leaf_skeleton(key, part):
    return choose_rows(jax.random.fold_in(key, 11), N // LEAF, LEAF)


def draw_skeleton_one(key, part):
    return choose_rows(jax.random.fold_in(key, 13), N // (2 * LEAF), 2 * RANK)


def draw_skeleton_two(key, part):
    return choose_rows(jax.random.fold_in(key, 17), N // (4 * LEAF), 2 * RANK)


def draw_skeleton_three(key, part):
    return choose_rows(jax.random.fold_in(key, 19), N // (8 * LEAF), 2 * RANK)


def level_of(stream_key, dims, cuts, low, largest):
    loudness, own = 1.0, jax.random.fold_in(stream_key, 6)
    for dim, blocks in cuts:
        heights = jnp.exp(jax.random.uniform(jax.random.fold_in(own, dim), (blocks,), jnp.float32, low / len(cuts), largest / len(cuts)))
        loudness = loudness * jnp.repeat(heights, dims[dim] // blocks).reshape([-1 if axis == dim else 1 for axis in range(len(dims))])
    return loudness


def noise(own_key, shape, scale, most, shards=(), kind=jnp.bfloat16):
    array = jax.random.normal(own_key, shape, jnp.float32) * scale
    if len(shards) > 0:
        array = level_of(own_key, shape, shards, -0.22, 0.18) * array
    return jnp.clip(array, min=-most, max=most).astype(kind)


def setup_inputs(seed: int = 0) -> dict:
    arg_keys = jax.random.split(jax.random.key(seed), 7)
    return {
        "probes": noise(arg_keys[0], (4, N, SAMPLES), 1.0, 6.0, ((1, 32),)),
        "points": draw_points(jax.random.fold_in(arg_keys[6], 71), 0),
        "leaf_skeleton": draw_leaf_skeleton(jax.random.fold_in(arg_keys[6], 71), 0),
        "skeleton_one": draw_skeleton_one(jax.random.fold_in(arg_keys[6], 71), 0),
        "skeleton_two": draw_skeleton_two(jax.random.fold_in(arg_keys[6], 71), 0),
        "skeleton_three": draw_skeleton_three(jax.random.fold_in(arg_keys[6], 71), 0),
    }


exact_mode = lax.Precision.HIGHEST

def couple(row_feats, col_feats, kernel_gain):
    cross = jnp.dot(row_feats.T, col_feats, precision=exact_mode)
    row_sq = lax.optimization_barrier(jnp.sum(row_feats * row_feats, axis=0))
    col_sq = lax.optimization_barrier(jnp.sum(col_feats * col_feats, axis=0))
    feat_count = row_feats.shape[0]
    return kernel_gain * jnp.exp((2.0 * cross - row_sq[:, None] - col_sq[None, :]) / (2.0 * feat_count))

def interpolate(stacked, chosen):
    skeleton = jnp.take(stacked, chosen, axis=0)
    gram_mat = jnp.dot(skeleton, skeleton.T, precision=exact_mode)
    damping = 0.05 * jnp.sum(skeleton * skeleton) / chosen.shape[0] + 1e-05
    factor = jnp.linalg.cholesky(gram_mat + damping * jnp.eye(chosen.shape[0], dtype=stacked.dtype))
    cross_mat = jnp.dot(stacked, skeleton.T, precision=exact_mode)
    solved = jax.scipy.linalg.cho_solve((factor, True), cross_mat.T)
    return (solved.T, skeleton)

def leaf_level(leaf_rows, leaf_probes, coords, chosen):
    interp, skeleton = interpolate(leaf_rows, chosen)
    reduced = jnp.dot(interp.T, leaf_probes.astype(interp.dtype), precision=exact_mode)
    picked = jnp.take(coords, chosen, axis=1).astype(jnp.float32)
    return (interp, (skeleton, reduced, picked))

def merge_pair(first_child, second_child, chosen, kernel_gain):
    first_samples, first_reduced, first_points = first_child
    second_samples, second_reduced, second_points = second_child
    upper_rows = first_samples - jnp.dot(couple(first_points, second_points, kernel_gain), second_reduced, precision=exact_mode)
    lower_rows = second_samples - jnp.dot(couple(second_points, first_points, kernel_gain), first_reduced, precision=exact_mode)
    stacked = jnp.concatenate([upper_rows, lower_rows], axis=0)
    interp, skeleton = interpolate(stacked, chosen)
    reduced = jnp.dot(interp.T, jnp.concatenate([first_reduced, second_reduced], axis=0), precision=exact_mode)
    joined = jnp.take(jnp.concatenate([first_points, second_points], axis=1), chosen, axis=1)
    return (interp, (skeleton, reduced, joined))

def take_evens(values):
    return values[0::2]

def take_odds(values):
    return values[1::2]

def reference(probes, points, leaf_skeleton, skeleton_one, skeleton_two, skeleton_three):
    feat_count = points.shape[0]
    extent = points.shape[2]
    total = 4 * extent
    kernel_gain = 16.0 / math.sqrt(total)
    all_points = points.reshape(feat_count, total).astype(jnp.float32)
    all_probes = probes.reshape(total, -1)
    indices = jnp.arange(total, dtype=jnp.int32)
    probes_wide = all_probes.astype(jnp.float32)
    height = min(512, extent)

    def sample_block(start_row):
        coords = lax.dynamic_slice_in_dim(all_points, start_row, height, 1)
        row_ids = start_row + jnp.arange(height, dtype=jnp.int32)
        kernel_tile = couple(coords, all_points, kernel_gain)
        kernel_tile = jnp.where((row_ids // LEAF)[:, None] == (indices // LEAF)[None, :], 0.0, kernel_tile)
        kernel_tile = lax.optimization_barrier(kernel_tile.astype(jnp.bfloat16)).astype(jnp.float32)
        return jnp.dot(kernel_tile, probes_wide, precision=exact_mode)
    starts = jnp.arange(extent // height, dtype=jnp.int32) * height
    samples = lax.map(sample_block, starts).reshape(extent, -1)
    leaf_count = extent // LEAF
    leaf_rows = samples.reshape(leaf_count, LEAF, -1)
    leaf_probes = probes[0].reshape(leaf_count, LEAF, -1)
    leaf_coords = points[:, 0].reshape(feat_count, leaf_count, LEAF).transpose(1, 0, 2)
    leaf_interp, carried = jax.vmap(leaf_level)(leaf_rows, leaf_probes, leaf_coords, leaf_skeleton)
    upper_list = []
    for level_num, chosen in enumerate((skeleton_one, skeleton_two, skeleton_three)):
        first_child = jax.tree.map(take_evens, carried)
        second_child = jax.tree.map(take_odds, carried)
        interp, carried = jax.vmap(merge_pair, in_axes=(0, 0, 0, None))(first_child, second_child, chosen, kernel_gain)
        upper_list.append(jnp.repeat(interp, 2 ** level_num, axis=0))
    upper_interp = jnp.stack(upper_list)
    top_state = jnp.stack([jnp.repeat(carried[0], 4, axis=0), jnp.repeat(carried[1], 4, axis=0)])
    return (leaf_interp, upper_interp, top_state)
```

```python
import math

import jax
import jax.numpy as jnp
import numpy as np
from jax import lax
from jax.experimental import pallas as pl
from jax.experimental.pallas import tpu as pltpu
from jax.sharding import PartitionSpec as P

LEAF = 128
FULL = lax.Precision.HIGHEST
F32 = jnp.float32
BF16 = jnp.bfloat16
DOUBLINGS = 9


def chebyshev_constants():
    taus = [1282.0 / 1280.0]
    for _ in range(DOUBLINGS):
        taus.append(2.0 * taus[-1] * taus[-1] - 1.0)
    front = 2.0**DOUBLINGS * math.prod(taus[:-1]) / taus[-1] / 640.0
    return taus[:-1], front


TAUS, FRONT = chebyshev_constants()


def split(value):
    high = value.astype(BF16).astype(F32)
    rest = value - high
    middle = rest.astype(BF16).astype(F32)
    return high, middle, rest - middle


def row_features(feats, gain):
    feats = feats.astype(F32)
    depth, width = feats.shape
    unit = math.log2(math.e) / (2.0 * depth)
    norm = jnp.sum(feats * feats, axis=0, keepdims=True) * -unit + math.log2(gain)
    parts = split(norm)
    place = lax.broadcasted_iota(jnp.int32, (16, width), 0)
    extra = jnp.where(place < 6, 1.0, 0.0)
    for pos in range(3):
        extra = jnp.where(place == pos, parts[pos], extra)
    return jnp.concatenate([*split(feats * (2.0 * unit)), extra], axis=0)


def col_features(feats):
    wide = feats.astype(F32)
    depth, width = wide.shape
    unit = math.log2(math.e) / (2.0 * depth)
    parts = split(jnp.sum(wide * wide, axis=0, keepdims=True) * -unit)
    place = lax.broadcasted_iota(jnp.int32, (16, width), 0)
    extra = jnp.where(place < 3, 1.0, 0.0)
    for pos in range(3):
        extra = jnp.where(place == pos + 3, parts[pos], extra)
    return jnp.concatenate([wide, wide, wide, extra], axis=0).astype(BF16)


def over(first, second, first_dim, second_dim, precision=None):
    return lax.dot_general(
        first,
        second,
        (((first_dim,), (second_dim,)), ((), ())),
        precision=precision,
        preferred_element_type=F32,
    )


def product_body(gain, span, first, last, chunk_count, source_count, *refs):
    refs = list(refs)
    sources = [refs.pop(0) for _ in range(source_count)]
    if first:
        row_points = [refs.pop(0) for _ in range(chunk_count)]
        rows_ref, acc_ref = refs
        for chunk in range(chunk_count):
            feats = row_points[chunk][...]
            rows_ref[pl.ds(chunk * span, span), :] = row_features(feats, gain).T.astype(BF16)
        acc_ref[...] = jnp.zeros_like(acc_ref)
    else:
        rows_ref, old_ref = refs[:2]
        if last:
            own_ref, *sent_refs, acc_ref = refs[2:]
        else:
            acc_ref = refs[2]
        acc_ref[...] = old_ref[...]

    def tile(source, quarter, diagonal):
        columns = col_features(source[quarter, pl.ds(span, 16), :])
        randoms = source[quarter, pl.ds(0, span), :]
        for chunk in range(chunk_count):
            rows = pl.ds(chunk * span, span)
            exponent = over(rows_ref[rows, :], columns, 1, 0)
            entries = jnp.exp2(exponent)
            if diagonal and chunk == 0:
                shape = (span, span)
                row_leaf = lax.broadcasted_iota(jnp.int32, shape, 0) // LEAF
                col_leaf = lax.broadcasted_iota(jnp.int32, shape, 1) // LEAF
                entries = jnp.where(row_leaf == col_leaf, 0.0, entries)
            acc_ref[rows, :] += over(entries.astype(BF16), randoms, 1, 0)

    for number, source in enumerate(sources):
        start = 0
        if first and number == 0:
            tile(source, 0, True)
            start = 1

        @pl.loop(start, source.shape[0])
        def _(quarter):
            tile(source, quarter, False)

    if last:
        own_ref[...] = acc_ref[pl.ds(0, span), :]
        for number, sent_ref in enumerate(sent_refs):
            sent_ref[...] = acc_ref[pl.ds((number + 1) * span, span), :].astype(BF16)


def product_cost(sources, rows, samples):
    columns = sum(s.shape[0] for s in sources) * (sources[0].shape[1] - 16)
    return pl.CostEstimate(
        flops=2 * rows * columns * (samples + 64),
        bytes_accessed=sum(2 * s.size for s in sources) + 8 * rows * samples,
        transcendentals=rows * columns,
    )


def product_start(sources, row_points, gain):
    span = sources[0].shape[1] - 16
    samples = sources[0].shape[2]
    chunks = len(row_points)
    rows = chunks * span
    return pl.pallas_call(
        lambda *refs: product_body(gain, span, True, False, chunks, len(sources), *refs),
        out_shape=(
            jax.ShapeDtypeStruct((rows, 64), BF16),
            jax.ShapeDtypeStruct((rows, samples), F32),
        ),
        cost_estimate=product_cost(sources, rows, samples),
        compiler_params=pltpu.CompilerParams(vmem_limit_bytes=48 << 20),
        name="product_start",
    )(*sources, *row_points)


def product_next(sources, row_feats, total, last):
    span = sources[0].shape[1] - 16
    rows, samples = total.shape
    chunks = rows // span
    if last:
        out_shape = [jax.ShapeDtypeStruct((span, samples), F32)]
        out_shape += [jax.ShapeDtypeStruct((span, samples), BF16)] * (chunks - 1)
        scratch = [pltpu.VMEM((rows, samples), F32)]
    else:
        out_shape = jax.ShapeDtypeStruct((rows, samples), F32)
        scratch = []
    return pl.pallas_call(
        lambda *refs: product_body(0.0, span, False, last, chunks, len(sources), *refs),
        out_shape=out_shape,
        scratch_shapes=scratch,
        cost_estimate=product_cost(sources, rows, samples),
        compiler_params=pltpu.CompilerParams(vmem_limit_bytes=48 << 20),
        name="product_last" if last else "product_next",
    )(*sources, row_feats, total)


def one_hot(chosen, pool):
    place = lax.broadcasted_iota(jnp.int32, (pool, chosen.shape[1]), 0)
    return jnp.where(place == chosen, 1.0, 0.0).astype(F32)


def interpolate(stacked, picks):
    rank = picks.shape[1]
    skeleton = over(picks, stacked, 0, 0, FULL)
    cross = over(skeleton, stacked, 1, 1, FULL)
    gram = over(skeleton, skeleton, 1, 1, FULL)
    ridge = 0.05 * jnp.sum(skeleton * skeleton, keepdims=True) / rank + 1e-05
    eye = jnp.where(
        lax.broadcasted_iota(jnp.int32, (rank, rank), 0)
        == lax.broadcasted_iota(jnp.int32, (rank, rank), 1),
        1.0,
        0.0,
    )
    inverse = 1.0 / (640.0 * ridge)
    power = eye - gram * inverse
    solved = cross
    pool = cross.shape[1]
    for number, tau in enumerate(TAUS):
        if number < DOUBLINGS - 1:
            both = over(power, jnp.concatenate([solved, power], axis=1), 1, 0, FULL)
            solved = solved + both[:, :pool] * (1.0 / tau)
            power = 2.0 * both[:, pool:] - eye
        else:
            solved = solved + over(power, solved, 1, 0, FULL) * (1.0 / tau)
    return solved * (inverse * (FRONT * 640.0)), skeleton


def merge(first, second, picks, gain):
    first_samples, first_reduced, first_points = first
    second_samples, second_reduced, second_points = second
    rank = first_samples.shape[0]
    upper = jnp.exp2(
        over(row_features(first_points, gain).astype(BF16), col_features(second_points), 0, 0)
    )
    lower = jnp.exp2(
        over(row_features(second_points, gain).astype(BF16), col_features(first_points), 0, 0)
    )
    stacked = jnp.concatenate(
        [
            first_samples - over(upper, second_reduced, 1, 0, FULL),
            second_samples - over(lower, first_reduced, 1, 0, FULL),
        ],
        axis=0,
    )
    interp, skeleton = interpolate(stacked, picks)
    reduced = over(interp, jnp.concatenate([first_reduced, second_reduced], axis=0), 1, 0, FULL)
    points = over(first_points, picks[:rank], 1, 0) + over(second_points, picks[rank:], 1, 0)
    return interp, (skeleton, reduced, points)


def store_state(state_ref, state):
    samples, reduced, points = state
    rank = samples.shape[0]
    state_ref[pl.ds(0, rank), :] = samples
    state_ref[pl.ds(rank, rank), :] = reduced
    state_ref[pl.ds(2 * rank, points.shape[0]), :] = jnp.concatenate(
        [points] * (state_ref.shape[1] // rank), axis=1
    )


def load_state(state, rank):
    return (state[:rank], state[rank : 2 * rank], state[2 * rank :, :rank])


def leaves_body(gain, received, *refs):
    own_ref, *others = refs[: received + 1]
    source_ref, leaf_skeleton_ref, skeleton_ref, leaf_ref, upper_ref, state_ref = refs[received + 1 :]
    span = own_ref.shape[0]
    total = own_ref[...]
    for other in others:
        total = total + other[...].astype(F32)
    children = []
    for leaf in range(span // LEAF):
        rows = slice(leaf * LEAF, (leaf + 1) * LEAF)
        picks = one_hot(leaf_skeleton_ref[leaf : leaf + 1, :], LEAF)
        interp, skeleton = interpolate(total[rows], picks)
        leaf_ref[leaf] = interp.T
        randoms = source_ref[0, pl.ds(leaf * LEAF, LEAF), :].astype(F32)
        feats = source_ref[0, pl.ds(span, 16), pl.ds(leaf * LEAF, LEAF)].astype(F32)
        children.append(
            (skeleton, over(interp, randoms, 1, 0, FULL), over(feats, picks, 1, 0))
        )
    interp, state = merge(*children, one_hot(skeleton_ref[...], LEAF), gain)
    upper_ref[...] = interp.T
    store_state(state_ref, state)


def leaves(own, others, source, leaf_skeleton, skeleton, gain):
    span, samples = own.shape
    leaf_count, rank = leaf_skeleton.shape
    return pl.pallas_call(
        lambda *refs: leaves_body(gain, len(others), *refs),
        out_shape=(
            jax.ShapeDtypeStruct((leaf_count, LEAF, rank), F32),
            jax.ShapeDtypeStruct((2 * rank, rank), F32),
            jax.ShapeDtypeStruct((2 * rank + 16, samples), F32),
        ),
        cost_estimate=pl.CostEstimate(flops=10**9, bytes_accessed=10**6, transcendentals=10**4),
        compiler_params=pltpu.CompilerParams(vmem_limit_bytes=48 << 20),
        name="leaves",
    )(own, *others, source, leaf_skeleton, skeleton)


def level_body(gain, place_ref, mine_ref, theirs_ref, table_ref, *refs):
    rank = table_ref.shape[1]
    mine_first = place_ref[0] == 0
    mine, theirs = mine_ref[...], theirs_ref[...]
    first = load_state(jnp.where(mine_first, mine, theirs), rank)
    second = load_state(jnp.where(mine_first, theirs, mine), rank)
    picks = one_hot(table_ref[pl.ds(place_ref[1], 1), :], 2 * rank)
    interp, state = merge(first, second, picks, gain)
    if len(refs) == 2:
        upper_ref, state_ref = refs
        upper_ref[...] = interp.T
        store_state(state_ref, state)
    else:
        one_ref, two_ref, upper_ref, top_ref = refs
        upper_ref[0, 0] = one_ref[...]
        upper_ref[1, 0] = two_ref[...]
        upper_ref[2, 0] = interp.T
        top_ref[0, 0] = state[0]
        top_ref[1, 0] = state[1]


def level(place, mine, theirs, table, gain, below=()):
    rank = table.shape[1]
    if below:
        out_shape = (
            jax.ShapeDtypeStruct((3, 1, 2 * rank, rank), F32),
            jax.ShapeDtypeStruct((2, 1, rank, mine.shape[1]), F32),
        )
    else:
        out_shape = (
            jax.ShapeDtypeStruct((2 * rank, rank), F32),
            jax.ShapeDtypeStruct(mine.shape, F32),
        )
    vmem = pl.BlockSpec(memory_space=pltpu.VMEM)
    return pl.pallas_call(
        lambda *refs: level_body(gain, *refs),
        out_shape=out_shape,
        in_specs=[pl.BlockSpec(memory_space=pltpu.SMEM)] + [vmem] * (3 + len(below)),
        cost_estimate=pl.CostEstimate(flops=10**9, bytes_accessed=10**6, transcendentals=10**4),
        compiler_params=pltpu.CompilerParams(vmem_limit_bytes=48 << 20),
        name="level",
    )(place, mine, theirs, table, *below)


def local(probes, points, leaf_skeleton, skeleton_one, skeleton_two, skeleton_three):
    own_rows = probes.shape[1]
    row_count = lax.axis_size("row")
    col_count = lax.axis_size("col")
    col_pos = lax.axis_index("col")
    gain = 16.0 / math.sqrt(4 * own_rows * row_count * col_count)

    def swap(value, row_bits, col_bits):
        pairs = [
            (r * col_count + c, (r ^ row_bits) * col_count + (c ^ col_bits))
            for r in range(row_count)
            for c in range(col_count)
        ]
        return lax.ppermute(value, ("row", "col"), pairs)

    own = jnp.concatenate([probes, points.transpose(1, 0, 2)], axis=1)
    half = own.shape[0] // 2
    own_points = points[:, 0]
    row_points = [own_points]
    for offset in range(1, col_count // 2):
        row_points.append(swap(own_points, 0, 2 * offset))
    sibling = swap(own, 1, 0)
    beside = swap(own, 0, 1)
    across = swap(own, 2, 0)
    beside_sibling = swap(beside, 1, 0)
    across_sibling = swap(across, 1, 0)
    diagonal = [swap(beside[:half], 2, 0), swap(across[half:], 0, 1)]
    diagonal_sibling = [swap(value, 1, 0) for value in diagonal]
    groups = [[beside, across], [beside_sibling, across_sibling], diagonal, diagonal_sibling]
    for bit in range(2, row_count.bit_length() - 1):
        everything = [own, sibling] + [value for group in groups for value in group]
        groups.append([swap(value, 1 << bit, 0) for value in everything])
    row_feats, total = product_start([own, sibling], row_points, gain)
    for number, group in enumerate(groups):
        total = product_next(group, row_feats, total, number == len(groups) - 1)
    kept, *sent = total
    received = [swap(value, 0, 2 * (number + 1)) for number, value in enumerate(sent)]

    leaf_interp, interp_one, state = leaves(
        kept, received, own, leaf_skeleton, skeleton_one, gain
    )
    place = jnp.stack([col_pos & 1, col_pos >> 1]).astype(jnp.int32)
    interp_two, state_two = level(place, state, swap(state, 0, 1), skeleton_two, gain)
    place = jnp.stack([col_pos >> 1 & 1, col_pos >> 2]).astype(jnp.int32)
    upper_interp, top_state = level(
        place,
        state_two,
        swap(state_two, 0, 2),
        skeleton_three,
        gain,
        (interp_one, interp_two),
    )
    return leaf_interp, upper_interp, top_state


def solution(mesh):
    placed = (
        P(None, ("row", "col"), None),
        P(None, None, ("row", "col")),
        P(("row", "col"), None),
        P(("row", "col"), None),
        P("row", None),
        P("row", None),
    )
    return jax.shard_map(
        local,
        mesh=mesh,
        in_specs=placed,
        out_specs=(
            P(("row", "col"), None, None),
            P(None, ("row", "col"), None, None),
            P(None, ("row", "col"), None, None),
        ),
        check_vma=False,
    )
```

```python
import math

import jax
import jax.numpy as jnp
from jax import lax
from jax.experimental import pallas as pl
from jax.experimental.pallas import tpu as pltpu
from jax.sharding import PartitionSpec as P

LEAF = 128
F32 = jnp.float32
BF16 = jnp.bfloat16
DOUBLINGS = 9
VMEM = pl.BlockSpec(memory_space=pltpu.VMEM)
SMEM = pl.BlockSpec(memory_space=pltpu.SMEM)
PARAMS = pltpu.CompilerParams(vmem_limit_bytes=40 << 20)


def chebyshev_constants():
    taus = [1282.0 / 1280.0]
    for _ in range(DOUBLINGS):
        taus.append(2.0 * taus[-1] * taus[-1] - 1.0)
    front = 2.0**DOUBLINGS * math.prod(taus[:-1]) / taus[-1]
    return taus[:-1], front


TAUS, FRONT = chebyshev_constants()


def over(first, second, first_dim, second_dim):
    return lax.dot_general(
        first,
        second,
        (((first_dim,), (second_dim,)), ((), ())),
        preferred_element_type=F32,
    )


def split(value):
    high = value.astype(BF16)
    rest = value - high.astype(F32)
    middle = rest.astype(BF16)
    return high, middle, (rest - middle.astype(F32)).astype(BF16)


def norm_rows(norm, first, width):
    parts = [part.astype(F32) for part in split(norm)]
    place = lax.broadcasted_iota(jnp.int32, (16, width), 0)
    extra = jnp.where(place < 6, 1.0, 0.0)
    for pos in range(3):
        extra = jnp.where(place == pos + first, parts[pos], extra)
    return extra


def row_features(feats, gain):
    feats = feats.astype(F32)
    depth, width = feats.shape
    unit = math.log2(math.e) / (2.0 * depth)
    norm = jnp.sum(feats * feats, axis=0, keepdims=True) * -unit + math.log2(gain)
    parts = [part.astype(F32) for part in split(feats * (2.0 * unit))]
    return jnp.concatenate([*parts, norm_rows(norm, 0, width)], axis=0)


def col_features(feats):
    feats = feats.astype(F32)
    depth, width = feats.shape
    unit = math.log2(math.e) / (2.0 * depth)
    norm = jnp.sum(feats * feats, axis=0, keepdims=True) * -unit
    return jnp.concatenate([feats, feats, feats, norm_rows(norm, 3, width)], axis=0).astype(BF16)


def pack_body(probes_ref, points_ref, packed_ref, own_ref, sem):
    quarters, span, _ = probes_ref.shape
    copies = [
        pltpu.make_async_copy(
            probes_ref.at[quarter], packed_ref.at[pl.ds(quarter * span, span)], sem.at[quarter]
        )
        for quarter in range(quarters)
    ]
    for copy in copies:
        copy.start()
    points = points_ref[...].astype(F32)
    for quarter in range(quarters):
        feats = points[:, quarter, :].astype(BF16)
        packed_ref[pl.ds(quarters * span + 16 * quarter, 16), :] = feats
        if quarter == 0:
            own_ref[...] = feats
    for copy in copies:
        copy.wait()


def pack(probes, points):
    quarters, span, samples = probes.shape
    return pl.pallas_call(
        pack_body,
        out_shape=(
            jax.ShapeDtypeStruct((quarters * (span + 16), samples), BF16),
            jax.ShapeDtypeStruct((16, span), BF16),
        ),
        in_specs=[pl.BlockSpec(memory_space=pl.ANY), VMEM],
        scratch_shapes=[pltpu.SemaphoreType.DMA((quarters,))],
        compiler_params=PARAMS,
        name="pack",
    )(probes, points)


def masked(entries):
    shape = entries.shape
    row_leaf = lax.broadcasted_iota(jnp.int32, shape, 0) // LEAF
    col_leaf = lax.broadcasted_iota(jnp.int32, shape, 1) // LEAF
    return jnp.where(row_leaf == col_leaf, 0.0, entries)


def add_source(source_ref, feats_ref, rows_ref, cols_ref, keep_ref, put, span, own, form):
    quarters = source_ref.shape[0] // (span + 16)
    columns = quarters * span
    rows = rows_ref.shape[0]
    for quarter in range(quarters):
        feats = source_ref[pl.ds(columns + 16 * quarter, 16), :]
        cols_ref[:, pl.ds(quarter * span, span)] = col_features(feats)

    def entries_of(start, size):
        return jnp.exp2(over(rows_ref[pl.ds(start, size), :], cols_ref[:, :columns], 1, 0))

    def randoms():
        return source_ref[pl.ds(0, columns), :]

    first = 0
    if own:
        entries = entries_of(0, span)
        entries = jnp.concatenate([masked(entries[:, :span]), entries[:, span:]], axis=1)
        put(0, span, over(entries.astype(BF16), randoms(), 1, 0))
        first = 1
    blocks = rows // span
    if form == "whole":

        @pl.loop(first, blocks)
        def _(block):
            start = pl.multiple_of(block * span, span)
            put(start, span, over(entries_of(start, span).astype(BF16), randoms(), 1, 0))

    elif form == "ahead":
        keep_ref[0, :, :columns] = entries_of(first * span, span).astype(BF16)

        @pl.loop(first, blocks)
        def _(block):
            start = pl.multiple_of(block * span, span)
            later = pl.multiple_of(jnp.minimum(block + 1, blocks - 1) * span, span)
            now = (block - first) % 2
            product = over(keep_ref[now, :, :columns], randoms(), 1, 0)
            keep_ref[1 - now, :, :columns] = entries_of(later, span).astype(BF16)
            put(start, span, product)

    else:
        for block in range(first, blocks):
            start = block * span
            put(start, span, over(entries_of(start, span).astype(BF16), randoms(), 1, 0))


def product_body(gain, span, form, first, source_count, *refs):
    refs = list(refs)
    sources = [refs.pop(0) for _ in range(source_count)]
    if first:
        points_ref, rows_ref, total_ref, cols_ref, keep_ref = refs
        width = points_ref.shape[1]
        for start in range(0, width, span):
            feats = points_ref[:, pl.ds(start, span)]
            rows_ref[pl.ds(start, span), :] = row_features(feats, gain).T.astype(BF16)
    else:
        rows_ref, old_ref, total_ref, cols_ref, keep_ref = refs
    for number, source in enumerate(sources):

        def put(start, size, value):
            place = pl.ds(start, size)
            if number > 0:
                total_ref[place, :] += value
            elif first:
                total_ref[place, :] = value
            else:
                total_ref[place, :] = old_ref[place, :] + value

        own = first and number == 0
        add_source(source, None, rows_ref, cols_ref, keep_ref, put, span, own, form)


def product(sources, rows, span, form, total=None, gain=None):
    samples = sources[0].shape[1]
    first = total is None
    row_count = rows.shape[1] if first else rows.shape[0]
    columns = [s.shape[0] // (span + 16) * span for s in sources]
    out = jax.ShapeDtypeStruct((row_count, samples), F32)
    if first:
        out = (jax.ShapeDtypeStruct((row_count, 64), BF16), out)
    return pl.pallas_call(
        lambda *refs: product_body(gain, span, form, first, len(sources), *refs),
        out_shape=out,
        scratch_shapes=[
            pltpu.VMEM((64, max(columns)), BF16),
            pltpu.VMEM((2, span, max(columns)), BF16),
        ],
        cost_estimate=pl.CostEstimate(
            flops=2 * row_count * sum(columns) * 512,
            bytes_accessed=2 * sum(s.size for s in sources) + 8 * row_count * samples,
            transcendentals=row_count * sum(columns),
        ),
        compiler_params=PARAMS,
        name="product_" + form,
    )(*sources, rows, *([] if first else [total]))


def halves_body(total_ref, *out_refs):
    size = total_ref.shape[0] // 2
    for number, out_ref in enumerate(out_refs):
        out_ref[...] = total_ref[pl.ds(number * size, size), :]


def combine_body(span, mine_ref, theirs_ref, own_ref, *sent_refs):
    own_ref[...] = mine_ref[pl.ds(0, span), :] + theirs_ref[pl.ds(0, span), :]
    for number, sent_ref in enumerate(sent_refs):
        place = pl.ds((number + 1) * span, span)
        sent_ref[...] = (mine_ref[place, :] + theirs_ref[place, :]).astype(BF16)


def combine(mine, theirs, span):
    rows, samples = mine.shape
    return pl.pallas_call(
        lambda *refs: combine_body(span, *refs),
        out_shape=[jax.ShapeDtypeStruct((span, samples), F32)]
        + [jax.ShapeDtypeStruct((span, samples), BF16)] * (rows // span - 1),
        compiler_params=PARAMS,
        name="combine",
    )(mine, theirs)


def wide_product(first, second, second_dim):
    high, middle, low = split(first)
    other_high, other_middle, other_low = split(second)
    return over(
        jnp.concatenate([high, high, middle, middle, low, high], axis=1),
        jnp.concatenate(
            [other_high, other_middle, other_high, other_middle, other_high, other_low],
            axis=second_dim,
        ),
        1,
        second_dim,
    )


def exact_product(first, second):
    second = second.astype(BF16)
    return over(
        jnp.concatenate(split(first), axis=1), jnp.concatenate([second] * 3, axis=0), 1, 0
    )


def twice_product(twice_parts, parts):
    high, middle, low = twice_parts
    other_high, other_middle, other_low = parts
    left = lax.broadcasted_iota(jnp.int32, high.shape, 1) < high.shape[1] // 2
    last = jnp.where(left, low.astype(F32), high.astype(F32)).astype(BF16)
    return over(
        jnp.concatenate([high, middle, last], axis=1),
        jnp.concatenate(
            [other_high, other_middle, other_high, other_middle, other_high, other_low], axis=0
        ),
        1,
        0,
    )


def select_rows(picks, value):
    return over(
        jnp.concatenate([picks] * 3, axis=1), jnp.concatenate(split(value), axis=0), 1, 0
    )


def interpolate(stacks, picks_list):
    rank, pool = picks_list[0].shape
    place = lax.broadcasted_iota(jnp.int32, (rank, 2 * rank), 0)
    other = lax.broadcasted_iota(jnp.int32, (rank, 2 * rank), 1)
    eyes = jnp.where((other == place) | (other == place + rank), 1.0, 0.0)
    skeletons = [select_rows(picks, stack) for picks, stack in zip(picks_list, stacks)]
    states = []
    for skeleton, stack in zip(skeletons, stacks):
        products = wide_product(skeleton, jnp.concatenate([stack, skeleton, skeleton], axis=0), 1)
        ridge = 0.05 * jnp.sum(skeleton * skeleton, keepdims=True) / rank + 1e-05
        inverse = 1.0 / (640.0 * ridge)
        states.append((products[:, :pool], eyes - products[:, pool:] * inverse, inverse))
    for number, tau in enumerate(TAUS):
        last = number == DOUBLINGS - 1
        later = []
        for solved, power, inverse in states:
            power_parts = split(power)
            parts = split(solved)
            if not last:
                parts = [jnp.concatenate(pair, axis=1) for pair in zip(parts, power_parts)]
            both = twice_product(power_parts, parts)
            solved = solved + both[:, :pool] * (1.0 / tau)
            later.append((solved, None if last else 2.0 * both[:, pool:] - eyes, inverse))
        states = later
    return [
        (solved * (inverse * FRONT), skeleton)
        for (solved, _, inverse), skeleton in zip(states, skeletons)
    ]


def merge(first, second, couplings_ref, picks):
    first_samples, first_reduced = first
    second_samples, second_reduced = second
    first_parts, second_parts = split(first_reduced), split(second_reduced)
    stacked = jnp.concatenate(
        [
            first_samples - twice_product(split(couplings_ref[0]), second_parts),
            second_samples - twice_product(split(couplings_ref[1]), first_parts),
        ],
        axis=0,
    )
    ((interp, skeleton),) = interpolate([stacked], [picks])
    reduced = wide_product(interp, jnp.concatenate([first_reduced, second_reduced], axis=0), 0)
    return interp, skeleton, reduced


def leaves_body(received, *refs):
    own_ref, *others = refs[: received + 1]
    source_ref, picks_ref, couplings_ref, leaf_ref, upper_ref, state_ref = refs[received + 1 :]
    rank = picks_ref.shape[1]
    total = own_ref[...]
    for other in others:
        total = total + other[...].astype(F32)
    count = total.shape[0] // LEAF
    stacks = [total[leaf * LEAF : (leaf + 1) * LEAF] for leaf in range(count)]
    children = []
    for leaf, (interp, skeleton) in enumerate(
        interpolate(stacks, [picks_ref[leaf] for leaf in range(count)])
    ):
        leaf_ref[leaf] = interp
        randoms = source_ref[pl.ds(leaf * LEAF, LEAF), :]
        children.append((skeleton, exact_product(interp, randoms)))
    interp, skeleton, reduced = merge(*children, couplings_ref, picks_ref[count])
    upper_ref[...] = interp
    state_ref[pl.ds(0, rank), :] = skeleton
    state_ref[pl.ds(rank, rank), :] = reduced


def leaves(own, others, source, picks, couplings, leaf_count):
    samples = own.shape[1]
    rank, pool = picks.shape[1:]
    return pl.pallas_call(
        lambda *refs: leaves_body(len(others), *refs),
        out_shape=(
            jax.ShapeDtypeStruct((leaf_count, rank, LEAF), F32),
            jax.ShapeDtypeStruct((rank, pool), F32),
            jax.ShapeDtypeStruct((2 * rank, samples), F32),
        ),
        cost_estimate=pl.CostEstimate(flops=10**9, bytes_accessed=10**6, transcendentals=10**4),
        compiler_params=PARAMS,
        name="leaves",
    )(own, *others, source, picks, couplings)


def level_body(number, place_ref, mine_ref, theirs_ref, picks_ref, couplings_ref, *refs):
    rank = picks_ref.shape[1]
    mine_first = place_ref[number - 2] == 0
    mine, theirs = mine_ref[...], theirs_ref[...]
    first = jnp.where(mine_first, mine, theirs)
    second = jnp.where(mine_first, theirs, mine)
    interp, skeleton, reduced = merge(
        (first[:rank], first[rank:]),
        (second[:rank], second[rank:]),
        couplings_ref,
        picks_ref[picks_ref.shape[0] + number - 4],
    )
    if number == 2:
        upper_ref, state_ref = refs
        upper_ref[...] = interp
        state_ref[pl.ds(0, rank), :] = skeleton
        state_ref[pl.ds(rank, rank), :] = reduced
    else:
        one_ref, two_ref, upper_ref, top_ref = refs
        upper_ref[0, 0] = one_ref[...]
        upper_ref[1, 0] = two_ref[...]
        upper_ref[2, 0] = interp
        top_ref[0, 0] = skeleton
        top_ref[1, 0] = reduced


def level(number, place, mine, theirs, picks, couplings, below=()):
    rank, pool = picks.shape[1:]
    samples = mine.shape[1]
    if below:
        out_shape = (
            jax.ShapeDtypeStruct((3, 1, rank, pool), F32),
            jax.ShapeDtypeStruct((2, 1, rank, samples), F32),
        )
    else:
        out_shape = (
            jax.ShapeDtypeStruct((rank, pool), F32),
            jax.ShapeDtypeStruct(mine.shape, F32),
        )
    return pl.pallas_call(
        lambda *refs: level_body(number, *refs),
        out_shape=out_shape,
        in_specs=[SMEM] + [VMEM] * (4 + len(below)),
        cost_estimate=pl.CostEstimate(flops=10**9, bytes_accessed=10**6, transcendentals=10**4),
        compiler_params=PARAMS,
        name="level",
    )(place, mine, theirs, picks, couplings, *below)


def one_hot(chosen, pool):
    place = lax.broadcasted_iota(jnp.int32, (pool, chosen.shape[1]), 0)
    return jnp.where(place == chosen, 1.0, 0.0).astype(F32)


def couple(first, second, picks, gain, couplings_ref, points_ref):
    for number, (left, right) in enumerate(((first, second), (second, first))):
        twice = jnp.concatenate([right, right], axis=1)
        rows = row_features(left, gain).astype(BF16)
        couplings_ref[number] = jnp.exp2(over(rows, col_features(twice), 0, 0))
    if points_ref is not None:
        rank = first.shape[1]
        points = over(first, picks[:rank], 1, 0) + over(second, picks[rank:], 1, 0)
        points_ref[...] = points.astype(BF16)


def skeletons_body(gain, place_ref, own_ref, leaf_ref, one_ref, two_ref, three_ref, *refs):
    picks_ref, couplings_ref, points_ref = refs
    count, rank = leaf_ref.shape
    rows = [leaf_ref[leaf : leaf + 1, :] for leaf in range(count)]
    rows.append(one_ref[...])
    rows.append(two_ref[pl.ds(place_ref[2], 1), :])
    rows.append(three_ref[pl.ds(place_ref[3], 1), :])
    hots = [one_hot(row, picks_ref.shape[2]) for row in rows]
    for number, hot in enumerate(hots):
        picks_ref[number] = hot.T.astype(BF16)
    children = [
        over(own_ref[:, pl.ds(leaf * LEAF, LEAF)], hots[leaf].astype(BF16), 1, 0)
        for leaf in range(count)
    ]
    couple(*children, hots[count], gain, couplings_ref, points_ref)


def skeletons(place, own_points, tables, gain):
    leaf_count, rank = tables[0].shape
    return pl.pallas_call(
        lambda *refs: skeletons_body(gain, *refs),
        out_shape=(
            jax.ShapeDtypeStruct((leaf_count + 3, rank, LEAF), BF16),
            jax.ShapeDtypeStruct((2, rank, 2 * rank), F32),
            jax.ShapeDtypeStruct((16, rank), BF16),
        ),
        in_specs=[SMEM] + [VMEM] * 5,
        compiler_params=PARAMS,
        name="skeletons",
    )(place, own_points, *tables)


def couplings_body(gain, number, place_ref, mine_ref, theirs_ref, picks_ref, couplings_ref, *refs):
    mine_first = place_ref[number - 2] == 0
    mine, theirs = mine_ref[...].astype(F32), theirs_ref[...].astype(F32)
    first = jnp.where(mine_first, mine, theirs)
    second = jnp.where(mine_first, theirs, mine)
    picks = picks_ref[picks_ref.shape[0] + number - 4].astype(F32).T
    couple(first, second, picks, gain, couplings_ref, refs[0] if refs else None)


def couplings(number, place, mine, theirs, picks, gain):
    rank = picks.shape[1]
    out_shape = [jax.ShapeDtypeStruct((2, rank, 2 * rank), F32)]
    if number == 2:
        out_shape.append(jax.ShapeDtypeStruct(mine.shape, BF16))
    return pl.pallas_call(
        lambda *refs: couplings_body(gain, number, *refs),
        out_shape=out_shape,
        in_specs=[SMEM] + [VMEM] * 3,
        compiler_params=PARAMS,
        name="couplings",
    )(place, mine, theirs, picks)


def local(probes, points, leaf_skeleton, skeleton_one, skeleton_two, skeleton_three):
    span = probes.shape[1]
    row_count = lax.axis_size("row")
    col_count = lax.axis_size("col")
    col_pos = lax.axis_index("col")
    gain = 16.0 / math.sqrt(4 * span * row_count * col_count)
    place = jnp.stack([col_pos & 1, col_pos >> 1 & 1, col_pos >> 1, col_pos >> 2])

    def swap(value, row_bits, col_bits):
        pairs = [
            (r * col_count + c, (r ^ row_bits) * col_count + (c ^ col_bits))
            for r in range(row_count)
            for c in range(col_count)
        ]
        return lax.ppermute(value, ("row", "col"), pairs)

    packed, own_points = pack(probes, points)
    beside = swap(packed, 0, 1)
    across = swap(packed, 2, 0)
    row_points = own_points
    for bit in range(1, col_count.bit_length() - 1):
        row_points = jnp.concatenate([row_points, swap(row_points, 0, 1 << bit)], axis=1)
    row_points = jnp.concatenate([row_points, swap(row_points, 1, 0)], axis=1)

    row_feats, total = product([packed], row_points, span, "whole", gain=gain)
    beside, across, total = lax.optimization_barrier((beside, across, total))
    pieces = [packed, beside, across]
    random_rows, half = 4 * span, 2 * span

    def part(value, number):
        return jnp.concatenate(
            [
                value[number * half : (number + 1) * half],
                value[random_rows + 32 * number : random_rows + 32 * (number + 1)],
            ],
            axis=0,
        )

    diagonal = [swap(part(beside, 0), 2, 0), swap(part(across, 1), 0, 1)]
    total = product([beside], row_feats, span, "ahead", total)
    total = product([across], row_feats, span, "straight", total)
    pieces += diagonal
    for bit in range(2, row_count.bit_length() - 1):
        more = [swap(value, 1 << bit, 0) for value in pieces]
        total = product(more, row_feats, span, "ahead", total)
        pieces += more
    rows = total.shape[0] // 2
    theirs = product(diagonal, row_feats[rows:], span, "straight", total[rows:])
    from_sibling = swap(theirs, 1, 0)
    mine = product(diagonal, row_feats[:rows], span, "straight", total[:rows])
    kept, *sent = combine(mine, from_sibling, span)
    received = [swap(value, 0, 2 * (number + 1)) for number, value in enumerate(sent)]

    own_points, kept = lax.optimization_barrier((own_points, kept))
    tables = (leaf_skeleton, skeleton_one, skeleton_two, skeleton_three)
    picks, couplings_one, points_one = skeletons(place, own_points, tables, gain)
    couplings_two, points_two = couplings(
        2, place, points_one, swap(points_one, 0, 1), picks, gain
    )
    (couplings_three,) = couplings(3, place, points_two, swap(points_two, 0, 2), picks, gain)

    leaf_count = leaf_skeleton.shape[0]
    leaf_interp, interp_one, state = leaves(
        kept, received, packed, picks, couplings_one, leaf_count
    )
    interp_two, state_two = level(2, place, state, swap(state, 0, 1), picks, couplings_two)
    upper_interp, top_state = level(
        3,
        place,
        state_two,
        swap(state_two, 0, 2),
        picks,
        couplings_three,
        (interp_one, interp_two),
    )
    return jnp.swapaxes(leaf_interp, 1, 2), jnp.swapaxes(upper_interp, 2, 3), top_state


def solution(mesh):
    placed = (
        P(None, ("row", "col"), None),
        P(None, None, ("row", "col")),
        P(("row", "col"), None),
        P(("row", "col"), None),
        P("row", None),
        P("row", None),
    )
    return jax.shard_map(
        local,
        mesh=mesh,
        in_specs=placed,
        out_specs=(
            P(("row", "col"), None, None),
            P(None, ("row", "col"), None, None),
            P(None, ("row", "col"), None, None),
        ),
        check_vma=False,
    )
```

```python
import math

import jax
import jax.numpy as jnp
from jax import lax
from jax.experimental import pallas as pl
from jax.experimental.pallas import tpu as pltpu
from jax.sharding import PartitionSpec as P

LEAF = 128
F32 = jnp.float32
BF16 = jnp.bfloat16
DOUBLINGS = 9
VMEM = pl.BlockSpec(memory_space=pltpu.VMEM)
SMEM = pl.BlockSpec(memory_space=pltpu.SMEM)
COST = pl.CostEstimate(flops=0, bytes_accessed=0, transcendentals=0)
PARAMS = pltpu.CompilerParams(vmem_limit_bytes=40 << 20)


def chebyshev_constants():
    taus = [1282.0 / 1280.0]
    for _ in range(DOUBLINGS):
        taus.append(2.0 * taus[-1] * taus[-1] - 1.0)
    front = 2.0**DOUBLINGS * math.prod(taus[:-1]) / taus[-1]
    return taus[:-1], front


TAUS, FRONT = chebyshev_constants()


def over(first, second, first_dim, second_dim):
    return lax.dot_general(
        first,
        second,
        (((first_dim,), (second_dim,)), ((), ())),
        preferred_element_type=F32,
    )


def split(value):
    high = value.astype(BF16)
    rest = value - high.astype(F32)
    middle = rest.astype(BF16)
    return high, middle, (rest - middle.astype(F32)).astype(BF16)


def norm_rows(norm, first, width):
    parts = [part.astype(F32) for part in split(norm)]
    place = lax.broadcasted_iota(jnp.int32, (16, width), 0)
    extra = jnp.where(place < 6, 1.0, 0.0)
    for pos in range(3):
        extra = jnp.where(place == pos + first, parts[pos], extra)
    return extra


def row_features(feats, gain):
    feats = feats.astype(F32)
    depth, width = feats.shape
    unit = math.log2(math.e) / (2.0 * depth)
    norm = jnp.sum(feats * feats, axis=0, keepdims=True) * -unit + math.log2(gain)
    parts = [part.astype(F32) for part in split(feats * (2.0 * unit))]
    return jnp.concatenate([*parts, norm_rows(norm, 0, width)], axis=0)


def col_features(feats):
    feats = feats.astype(F32)
    depth, width = feats.shape
    unit = math.log2(math.e) / (2.0 * depth)
    norm = jnp.sum(feats * feats, axis=0, keepdims=True) * -unit
    return jnp.concatenate([feats, feats, feats, norm_rows(norm, 3, width)], axis=0).astype(BF16)


def pack_body(probes_ref, points_ref, packed_ref, own_ref, held_ref, sem):
    quarters, span, _ = probes_ref.shape
    copies = [pltpu.make_async_copy(points_ref, held_ref, sem.at[quarters])]
    copies += [
        pltpu.make_async_copy(
            probes_ref.at[quarter], packed_ref.at[pl.ds(quarter * span, span)], sem.at[quarter]
        )
        for quarter in range(quarters)
    ]
    for copy in copies:
        copy.start()
    copies[0].wait()
    points = held_ref[...].astype(F32)
    for quarter in range(quarters):
        feats = points[:, quarter, :].astype(BF16)
        packed_ref[pl.ds(quarters * span + 16 * quarter, 16), :] = feats
        if quarter == 0:
            own_ref[...] = feats
    for copy in copies[1:]:
        copy.wait()


def pack(probes, points):
    quarters, span, samples = probes.shape
    return pl.pallas_call(
        pack_body,
        out_shape=(
            jax.ShapeDtypeStruct((quarters * (span + 16), samples), BF16),
            jax.ShapeDtypeStruct((16, span), BF16),
        ),
        in_specs=[pl.BlockSpec(memory_space=pl.ANY)] * 2,
        scratch_shapes=[
            pltpu.VMEM(points.shape, BF16),
            pltpu.SemaphoreType.DMA((quarters + 1,)),
        ],
        compiler_params=pltpu.CompilerParams(vmem_limit_bytes=60 << 20),
        name="pack",
    )(probes, points)


def masked(entries):
    shape = entries.shape
    row_leaf = lax.broadcasted_iota(jnp.int32, shape, 0) // LEAF
    col_leaf = lax.broadcasted_iota(jnp.int32, shape, 1) // LEAF
    return jnp.where(row_leaf == col_leaf, 0.0, entries)


def add_source(source_ref, row_refs, cols_ref, put, span, own):
    quarters = source_ref.shape[0] // (span + 16)
    columns = quarters * span
    for quarter in range(quarters):
        feats = source_ref[pl.ds(columns + 16 * quarter, 16), :]
        cols_ref[:, pl.ds(quarter * span, span)] = col_features(feats)
    for half, rows_ref in enumerate(row_refs):
        for start in range(0, rows_ref.shape[0], span):
            feats = rows_ref[pl.ds(start, span), :]
            entries = jnp.exp2(over(feats, cols_ref[:, :columns], 1, 0))
            if own and half == 0 and start == 0:
                entries = jnp.concatenate([masked(entries[:, :span]), entries[:, span:]], axis=1)
            randoms = source_ref[pl.ds(0, columns), :]
            put(half, start, over(entries.astype(BF16), randoms, 1, 0))


def product_body(gain, span, first, source_count, half_count, *refs):
    refs = list(refs)
    cols_ref = refs.pop()
    take = lambda count: [refs.pop(0) for _ in range(count)]
    sources = take(source_count)
    if first:
        point_refs, row_refs = take(half_count), take(half_count)
        for points_ref, rows_ref in zip(point_refs, row_refs):
            for start in range(0, points_ref.shape[1], span):
                feats = points_ref[:, pl.ds(start, span)]
                rows_ref[pl.ds(start, span), :] = row_features(feats, gain).T.astype(BF16)
    else:
        row_refs, old_refs = take(half_count), take(half_count)
    total_refs = take(half_count)
    for number, source in enumerate(sources):

        def put(half, start, value):
            place = pl.ds(start, span)
            if number > 0:
                total_refs[half][place, :] += value
            elif first:
                total_refs[half][place, :] = value
            else:
                total_refs[half][place, :] = old_refs[half][place, :] + value

        add_source(source, row_refs, cols_ref, put, span, first and number == 0)


def product(sources, rows, span, totals=None, gain=None):
    samples = sources[0].shape[1]
    first = totals is None
    halves = len(rows)
    counts = [half.shape[1] if first else half.shape[0] for half in rows]
    columns = max(s.shape[0] // (span + 16) * span for s in sources)
    out = [jax.ShapeDtypeStruct((count, samples), F32) for count in counts]
    if first:
        out = [jax.ShapeDtypeStruct((count, 64), BF16) for count in counts] + out
    out = pl.pallas_call(
        lambda *refs: product_body(gain, span, first, len(sources), halves, *refs),
        out_shape=out,
        scratch_shapes=[pltpu.VMEM((64, columns), BF16)],
        cost_estimate=COST,
        compiler_params=PARAMS,
        name="product",
    )(*sources, *rows, *([] if first else totals))
    return (out[:halves], out[halves:]) if first else out


def combine_body(span, mine_ref, theirs_ref, own_ref, *sent_refs):
    own_ref[...] = mine_ref[pl.ds(0, span), :] + theirs_ref[pl.ds(0, span), :]
    for number, sent_ref in enumerate(sent_refs):
        place = pl.ds((number + 1) * span, span)
        sent_ref[...] = (mine_ref[place, :] + theirs_ref[place, :]).astype(BF16)


def combine(mine, theirs, span):
    rows, samples = mine.shape
    return pl.pallas_call(
        lambda *refs: combine_body(span, *refs),
        out_shape=[jax.ShapeDtypeStruct((span, samples), F32)]
        + [jax.ShapeDtypeStruct((span, samples), BF16)] * (rows // span - 1),
        compiler_params=PARAMS,
        name="combine",
    )(mine, theirs)


def wide_product(first, second, second_dim):
    high, middle, low = split(first)
    other_high, other_middle, other_low = split(second)
    return over(
        jnp.concatenate([high, high, middle, middle, low, high], axis=1),
        jnp.concatenate(
            [other_high, other_middle, other_high, other_middle, other_high, other_low],
            axis=second_dim,
        ),
        1,
        second_dim,
    )


def exact_product(first, second):
    second = second.astype(BF16)
    return over(
        jnp.concatenate(split(first), axis=1), jnp.concatenate([second] * 3, axis=0), 1, 0
    )


def twice_product(twice_parts, parts):
    high, middle, low = twice_parts
    other_high, other_middle, other_low = parts
    left = lax.broadcasted_iota(jnp.int32, high.shape, 1) < high.shape[1] // 2
    last = jnp.where(left, low.astype(F32), high.astype(F32)).astype(BF16)
    return over(
        jnp.concatenate([high, middle, last], axis=1),
        jnp.concatenate(
            [other_high, other_middle, other_high, other_middle, other_high, other_low], axis=0
        ),
        1,
        0,
    )


def select_rows(picks, value):
    return over(
        jnp.concatenate([picks] * 3, axis=1), jnp.concatenate(split(value), axis=0), 1, 0
    )


def interpolate(stacks, picks_list, early=None):
    rank, pool = picks_list[0].shape
    place = lax.broadcasted_iota(jnp.int32, (rank, 2 * rank), 0)
    other = lax.broadcasted_iota(jnp.int32, (rank, 2 * rank), 1)
    eyes = jnp.where((other == place) | (other == place + rank), 1.0, 0.0)
    skeletons = [select_rows(picks, stack) for picks, stack in zip(picks_list, stacks)]
    if early is not None:
        early(*skeletons)
    states = []
    for skeleton, stack in zip(skeletons, stacks):
        products = wide_product(skeleton, jnp.concatenate([stack, skeleton, skeleton], axis=0), 1)
        ridge = 0.05 * jnp.sum(skeleton * skeleton, keepdims=True) / rank + 1e-05
        inverse = 1.0 / (640.0 * ridge)
        states.append((products[:, :pool], eyes - products[:, pool:] * inverse, inverse))
    for number, tau in enumerate(TAUS):
        last = number == DOUBLINGS - 1
        later = []
        for solved, power, inverse in states:
            power_parts = split(power)
            parts = split(solved)
            if not last:
                parts = [jnp.concatenate(pair, axis=1) for pair in zip(parts, power_parts)]
            both = twice_product(power_parts, parts)
            solved = solved + both[:, :pool] * (1.0 / tau)
            later.append((solved, None if last else 2.0 * both[:, pool:] - eyes, inverse))
        states = later
    return [
        (solved * (inverse * FRONT), skeleton)
        for (solved, _, inverse), skeleton in zip(states, skeletons)
    ]


def merge(first, second, couplings_ref, picks, early=None):
    first_samples, first_reduced = first
    second_samples, second_reduced = second
    first_parts, second_parts = split(first_reduced), split(second_reduced)
    stacked = jnp.concatenate(
        [
            first_samples - twice_product(split(couplings_ref[0]), second_parts),
            second_samples - twice_product(split(couplings_ref[1]), first_parts),
        ],
        axis=0,
    )
    ((interp, skeleton),) = interpolate([stacked], [picks], early)
    reduced = wide_product(interp, jnp.concatenate([first_reduced, second_reduced], axis=0), 0)
    return interp, skeleton, reduced


def leaves_body(received, *refs):
    own_ref, *others = refs[: received + 1]
    source_ref, picks_ref, couplings_ref = refs[received + 1 : received + 4]
    leaf_ref, upper_ref, state_ref, held_ref, sem = refs[-5:]
    rank = picks_ref.shape[1]
    total = own_ref[...]
    for other in others:
        total = total + other[...].astype(F32)
    count = total.shape[0] // LEAF
    stacks = [total[leaf * LEAF : (leaf + 1) * LEAF] for leaf in range(count)]
    children = []
    for leaf, (interp, skeleton) in enumerate(
        interpolate(stacks, [picks_ref[leaf] for leaf in range(count)])
    ):
        held_ref[leaf] = interp
        randoms = source_ref[pl.ds(leaf * LEAF, LEAF), :]
        children.append((skeleton, exact_product(interp, randoms)))
    copy = pltpu.make_async_copy(held_ref, leaf_ref, sem)
    copy.start()
    interp, skeleton, reduced = merge(*children, couplings_ref, picks_ref[count])
    upper_ref[...] = interp
    state_ref[pl.ds(0, rank), :] = skeleton
    state_ref[pl.ds(rank, rank), :] = reduced
    copy.wait()


def leaves(own, others, source, picks, couplings, upper_couplings, leaf_count):
    samples = own.shape[1]
    rank, pool = picks.shape[1:]
    return pl.pallas_call(
        lambda *refs: leaves_body(len(others), *refs),
        out_shape=(
            jax.ShapeDtypeStruct((leaf_count, rank, LEAF), F32),
            jax.ShapeDtypeStruct((rank, pool), F32),
            jax.ShapeDtypeStruct((2 * rank, samples), F32),
        ),
        out_specs=(pl.BlockSpec(memory_space=pl.ANY), VMEM, VMEM),
        scratch_shapes=[pltpu.VMEM((leaf_count, rank, LEAF), F32), pltpu.SemaphoreType.DMA],
        cost_estimate=COST,
        compiler_params=PARAMS,
        name="leaves",
    )(own, *others, source, picks, couplings, *upper_couplings)


def level_body(number, place_ref, mine_ref, theirs_ref, picks_ref, couplings_ref, *refs):
    rank = picks_ref.shape[1]
    if number == 2:
        upper_ref, state_ref = refs
    else:
        one_ref, two_ref, upper_out, top_out, upper_ref, state_ref, sem = refs
        places = [
            (one_ref, upper_out.at[0, 0]),
            (two_ref, upper_out.at[1, 0]),
            (state_ref.at[pl.ds(0, rank)], top_out.at[0, 0]),
            (state_ref.at[pl.ds(rank, rank)], top_out.at[1, 0]),
            (upper_ref, upper_out.at[2, 0]),
        ]
        copies = [
            pltpu.make_async_copy(source, target, sem.at[pos])
            for pos, (source, target) in enumerate(places)
        ]
        copies[0].start()
        copies[1].start()

    def early(skeleton):
        state_ref[pl.ds(0, rank), :] = skeleton
        if number > 2:
            copies[2].start()

    mine_first = place_ref[number - 2] == 0
    mine, theirs = mine_ref[...], theirs_ref[...]
    first = jnp.where(mine_first, mine, theirs)
    second = jnp.where(mine_first, theirs, mine)
    interp, _, reduced = merge(
        (first[:rank], first[rank:]),
        (second[:rank], second[rank:]),
        couplings_ref,
        picks_ref[picks_ref.shape[0] + number - 4],
        early,
    )
    upper_ref[...] = interp
    state_ref[pl.ds(rank, rank), :] = reduced
    if number > 2:
        copies[3].start()
        copies[4].start()
        for copy in copies:
            copy.wait()


def level(number, place, mine, theirs, picks, couplings, below=()):
    rank, pool = picks.shape[1:]
    samples = mine.shape[1]
    out_shape = (
        jax.ShapeDtypeStruct((rank, pool), F32),
        jax.ShapeDtypeStruct(mine.shape, F32),
    )
    out_specs = (VMEM, VMEM)
    scratch = []
    if below:
        scratch = [pltpu.VMEM(out.shape, F32) for out in out_shape]
        scratch.append(pltpu.SemaphoreType.DMA((5,)))
        out_shape = (
            jax.ShapeDtypeStruct((3, 1, rank, pool), F32),
            jax.ShapeDtypeStruct((2, 1, rank, samples), F32),
        )
        out_specs = (pl.BlockSpec(memory_space=pl.ANY),) * 2
    return pl.pallas_call(
        lambda *refs: level_body(number, *refs),
        out_shape=out_shape,
        in_specs=[SMEM] + [VMEM] * (4 + len(below)),
        out_specs=out_specs,
        scratch_shapes=scratch,
        cost_estimate=COST,
        compiler_params=PARAMS,
        name="level",
    )(place, mine, theirs, picks, couplings, *below)


def one_hot(chosen, pool):
    place = lax.broadcasted_iota(jnp.int32, (pool, chosen.shape[1]), 0)
    return jnp.where(place == chosen, 1.0, 0.0).astype(F32)


def couple(first, second, picks, gain, couplings_ref, points_ref):
    for number, (left, right) in enumerate(((first, second), (second, first))):
        twice = jnp.concatenate([right, right], axis=1)
        rows = row_features(left, gain).astype(BF16)
        couplings_ref[number] = jnp.exp2(over(rows, col_features(twice), 0, 0))
    if points_ref is not None:
        rank = first.shape[1]
        points = over(first, picks[:rank], 1, 0) + over(second, picks[rank:], 1, 0)
        points_ref[...] = points.astype(BF16)


def skeletons_body(gain, place_ref, own_ref, leaf_ref, one_ref, two_ref, three_ref, *refs):
    picks_ref, couplings_ref, points_ref = refs
    count, rank = leaf_ref.shape
    rows = [leaf_ref[leaf : leaf + 1, :] for leaf in range(count)]
    rows.append(one_ref[...])
    rows.append(two_ref[pl.ds(place_ref[2], 1), :])
    rows.append(three_ref[pl.ds(place_ref[3], 1), :])
    hots = [one_hot(row, picks_ref.shape[2]) for row in rows]
    for number, hot in enumerate(hots):
        picks_ref[number] = hot.T.astype(BF16)
    children = [
        over(own_ref[:, pl.ds(leaf * LEAF, LEAF)], hots[leaf].astype(BF16), 1, 0)
        for leaf in range(count)
    ]
    couple(*children, hots[count], gain, couplings_ref, points_ref)


def skeletons(place, own_points, tables, gain):
    leaf_count, rank = tables[0].shape
    return pl.pallas_call(
        lambda *refs: skeletons_body(gain, *refs),
        out_shape=(
            jax.ShapeDtypeStruct((leaf_count + 3, rank, LEAF), BF16),
            jax.ShapeDtypeStruct((2, rank, 2 * rank), F32),
            jax.ShapeDtypeStruct((16, rank), BF16),
        ),
        in_specs=[SMEM] + [VMEM] * 5,
        compiler_params=PARAMS,
        name="skeletons",
    )(place, own_points, *tables)


def couplings_body(gain, number, place_ref, mine_ref, theirs_ref, picks_ref, couplings_ref, *refs):
    mine_first = place_ref[number - 2] == 0
    mine, theirs = mine_ref[...].astype(F32), theirs_ref[...].astype(F32)
    first = jnp.where(mine_first, mine, theirs)
    second = jnp.where(mine_first, theirs, mine)
    picks = picks_ref[picks_ref.shape[0] + number - 4].astype(F32).T
    couple(first, second, picks, gain, couplings_ref, refs[0] if refs else None)


def couplings(number, place, mine, theirs, picks, gain):
    rank = picks.shape[1]
    out_shape = [jax.ShapeDtypeStruct((2, rank, 2 * rank), F32)]
    if number == 2:
        out_shape.append(jax.ShapeDtypeStruct(mine.shape, BF16))
    return pl.pallas_call(
        lambda *refs: couplings_body(gain, number, *refs),
        out_shape=out_shape,
        in_specs=[SMEM] + [VMEM] * 3,
        compiler_params=PARAMS,
        name="couplings",
    )(place, mine, theirs, picks)


def local(probes, points, leaf_skeleton, skeleton_one, skeleton_two, skeleton_three):
    span = probes.shape[1]
    row_count = lax.axis_size("row")
    col_count = lax.axis_size("col")
    col_pos = lax.axis_index("col")
    gain = 16.0 / math.sqrt(4 * span * row_count * col_count)
    place = jnp.stack([col_pos & 1, col_pos >> 1 & 1, col_pos >> 1, col_pos >> 2])

    def swap(value, row_bits, col_bits):
        pairs = [
            (r * col_count + c, (r ^ row_bits) * col_count + (c ^ col_bits))
            for r in range(row_count)
            for c in range(col_count)
        ]
        return lax.ppermute(value, ("row", "col"), pairs)

    packed, own_points = pack(probes, points)
    beside = swap(packed, 0, 1)
    across = swap(packed, 2, 0)
    line_points = [own_points]
    for offset in range(1, col_count // 2):
        line_points.append(swap(own_points, 0, 2 * offset))
    line_points = jnp.concatenate(line_points, axis=1)
    row_points = [line_points, swap(line_points, 1, 0)]

    row_feats, totals = product([packed], row_points, span, gain=gain)
    beside, across, *totals = lax.optimization_barrier((beside, across, *totals))
    pieces = [packed, beside, across]
    random_rows, half = 4 * span, 2 * span

    def part(value, number):
        return jnp.concatenate(
            [
                value[number * half : (number + 1) * half],
                value[random_rows + 32 * number : random_rows + 32 * (number + 1)],
            ],
            axis=0,
        )

    diagonal = [swap(part(beside, 0), 2, 0), swap(part(across, 1), 0, 1)]
    totals = product([beside], row_feats, span, totals)
    totals = product([across], row_feats, span, totals)
    pieces += diagonal
    for bit in range(2, row_count.bit_length() - 1):
        more = [swap(value, 1 << bit, 0) for value in pieces]
        totals = product(more, row_feats, span, totals)
        pieces += more
    (theirs,) = product(diagonal, row_feats[1:], span, totals[1:])
    from_sibling = swap(theirs, 1, 0)
    (mine,) = product(diagonal, row_feats[:1], span, totals[:1])
    kept, *sent = combine(mine, from_sibling, span)
    received = [swap(value, 0, 2 * (number + 1)) for number, value in enumerate(sent)]

    own_points, kept = lax.optimization_barrier((own_points, kept))
    tables = (leaf_skeleton, skeleton_one, skeleton_two, skeleton_three)
    picks, couplings_one, points_one = skeletons(place, own_points, tables, gain)
    couplings_two, points_two = couplings(
        2, place, points_one, swap(points_one, 0, 1), picks, gain
    )
    (couplings_three,) = couplings(3, place, points_two, swap(points_two, 0, 2), picks, gain)

    leaf_count = leaf_skeleton.shape[0]
    leaf_interp, interp_one, state = leaves(
        kept, received, packed, picks, couplings_one, (couplings_two, couplings_three), leaf_count
    )
    interp_two, state_two = level(2, place, state, swap(state, 0, 1), picks, couplings_two)
    upper_interp, top_state = level(
        3,
        place,
        state_two,
        swap(state_two, 0, 2),
        picks,
        couplings_three,
        (interp_one, interp_two),
    )
    return jnp.swapaxes(leaf_interp, 1, 2), jnp.swapaxes(upper_interp, 2, 3), top_state


def solution(mesh):
    placed = (
        P(None, ("row", "col"), None),
        P(None, None, ("row", "col")),
        P(("row", "col"), None),
        P(("row", "col"), None),
        P("row", None),
        P("row", None),
    )
    return jax.shard_map(
        local,
        mesh=mesh,
        in_specs=placed,
        out_specs=(
            P(("row", "col"), None, None),
            P(None, ("row", "col"), None, None),
            P(None, ("row", "col"), None, None),
        ),
        check_vma=False,
    )
```

```python
import math

import jax
import jax.numpy as jnp
from jax import lax
from jax.experimental import pallas as pl
from jax.experimental.pallas import tpu as pltpu
from jax.sharding import PartitionSpec as P

LEAF = 128
F32 = jnp.float32
BF16 = jnp.bfloat16
DOUBLINGS = 9
VMEM = pl.BlockSpec(memory_space=pltpu.VMEM)
SMEM = pl.BlockSpec(memory_space=pltpu.SMEM)
COST = pl.CostEstimate(flops=0, bytes_accessed=0, transcendentals=0)
PARAMS = pltpu.CompilerParams(vmem_limit_bytes=16 << 20)


def chebyshev_constants():
    taus = [1282.0 / 1280.0]
    for _ in range(DOUBLINGS):
        taus.append(2.0 * taus[-1] * taus[-1] - 1.0)
    front = 2.0**DOUBLINGS * math.prod(taus[:-1]) / taus[-1]
    return taus[:-1], front


TAUS, FRONT = chebyshev_constants()


def over(first, second, first_dim, second_dim):
    return lax.dot_general(
        first,
        second,
        (((first_dim,), (second_dim,)), ((), ())),
        preferred_element_type=F32,
    )


def split(value):
    high = value.astype(BF16)
    rest = value - high.astype(F32)
    middle = rest.astype(BF16)
    return high, middle, (rest - middle.astype(F32)).astype(BF16)


def norm_rows(norm, first, width):
    parts = [part.astype(F32) for part in split(norm)]
    place = lax.broadcasted_iota(jnp.int32, (16, width), 0)
    extra = jnp.where(place < 6, 1.0, 0.0)
    for pos in range(3):
        extra = jnp.where(place == pos + first, parts[pos], extra)
    return extra


def row_features(feats, gain):
    feats = feats.astype(F32)
    depth, width = feats.shape
    unit = math.log2(math.e) / (2.0 * depth)
    norm = jnp.sum(feats * feats, axis=0, keepdims=True) * -unit + math.log2(gain)
    parts = [part.astype(F32) for part in split(feats * (2.0 * unit))]
    return jnp.concatenate([*parts, norm_rows(norm, 0, width)], axis=0)


def col_features(feats):
    feats = feats.astype(F32)
    depth, width = feats.shape
    unit = math.log2(math.e) / (2.0 * depth)
    norm = jnp.sum(feats * feats, axis=0, keepdims=True) * -unit
    return jnp.concatenate([feats, feats, feats, norm_rows(norm, 3, width)], axis=0).astype(BF16)


def pack_body(probes_ref, points_ref, packed_ref, own_ref, held_ref, sem):
    quarters, span, _ = probes_ref.shape
    copies = [pltpu.make_async_copy(points_ref, held_ref, sem.at[quarters])]
    copies += [
        pltpu.make_async_copy(
            probes_ref.at[quarter], packed_ref.at[pl.ds(quarter * span, span)], sem.at[quarter]
        )
        for quarter in range(quarters)
    ]
    for copy in copies:
        copy.start()
    copies[0].wait()
    points = held_ref[...].astype(F32)
    for quarter in range(quarters):
        feats = points[:, quarter, :].astype(BF16)
        packed_ref[pl.ds(quarters * span + 16 * quarter, 16), :] = feats
        if quarter == 0:
            own_ref[...] = feats
    for copy in copies[1:]:
        copy.wait()


def pack(probes, points):
    quarters, span, samples = probes.shape
    return pl.pallas_call(
        pack_body,
        out_shape=(
            jax.ShapeDtypeStruct((quarters * (span + 16), samples), BF16),
            jax.ShapeDtypeStruct((16, span), BF16),
        ),
        in_specs=[pl.BlockSpec(memory_space=pltpu.HBM)] * 2,
        scratch_shapes=[
            pltpu.VMEM(points.shape, BF16),
            pltpu.SemaphoreType.DMA((quarters + 1,)),
        ],
        cost_estimate=COST,
        compiler_params=pltpu.CompilerParams(vmem_limit_bytes=64512 << 10),
        name="pack",
    )(probes, points)


def masked(entries):
    shape = entries.shape
    row_leaf = lax.broadcasted_iota(jnp.int32, shape, 0) // LEAF
    col_leaf = lax.broadcasted_iota(jnp.int32, shape, 1) // LEAF
    return jnp.where(row_leaf == col_leaf, 0.0, entries)


def add_source(source_ref, row_refs, cols_ref, put, span, own):
    quarters = source_ref.shape[0] // (span + 16)
    columns = quarters * span
    for quarter in range(quarters):
        feats = source_ref[pl.ds(columns + 16 * quarter, 16), :]
        cols_ref[:, pl.ds(quarter * span, span)] = col_features(feats)
    for half, rows_ref in enumerate(row_refs):
        for start in range(0, rows_ref.shape[0], span):
            feats = rows_ref[pl.ds(start, span), :]
            entries = jnp.exp2(over(feats, cols_ref[:, :columns], 1, 0))
            if own and half == 0 and start == 0:
                entries = jnp.concatenate([masked(entries[:, :span]), entries[:, span:]], axis=1)
            randoms = source_ref[pl.ds(0, columns), :]
            put(half, start, over(entries.astype(BF16), randoms, 1, 0))


def product_body(gain, span, first, own, source_count, half_count, *refs):
    refs = list(refs)
    cols_ref = refs.pop()
    take = lambda count: [refs.pop(0) for _ in range(count)]
    sources = take(source_count)
    if first:
        point_refs, row_refs = take(half_count), take(half_count)
        for points_ref, rows_ref in zip(point_refs, row_refs):
            for start in range(0, points_ref.shape[1], span):
                feats = points_ref[:, pl.ds(start, span)]
                rows_ref[pl.ds(start, span), :] = row_features(feats, gain).T.astype(BF16)
    else:
        row_refs, old_refs = take(half_count), take(half_count)
    total_refs = take(half_count)
    for number, source in enumerate(sources):

        def put(half, start, value):
            place = pl.ds(start, span)
            if number > 0:
                total_refs[half][place, :] += value
            elif first:
                total_refs[half][place, :] = value
            else:
                total_refs[half][place, :] = old_refs[half][place, :] + value

        add_source(source, row_refs, cols_ref, put, span, first and own and number == 0)


def product(sources, rows, span, totals=None, gain=None, own=True):
    samples = sources[0].shape[1]
    first = totals is None
    count = len(rows)
    counts = [half.shape[1] if first else half.shape[0] for half in rows]
    columns = max(s.shape[0] // (span + 16) * span for s in sources)
    out = [jax.ShapeDtypeStruct((count, samples), F32) for count in counts]
    if first:
        out = [jax.ShapeDtypeStruct((count, 64), BF16) for count in counts] + out
    out = pl.pallas_call(
        lambda *refs: product_body(gain, span, first, own, len(sources), count, *refs),
        out_shape=out,
        scratch_shapes=[pltpu.VMEM((64, columns), BF16)],
        cost_estimate=COST,
        compiler_params=PARAMS,
        name="product",
    )(*sources, *rows, *([] if first else totals))
    return (out[:count], out[count:]) if first else out


def halves_body(quarters, span, *refs):
    size = quarters * span // 2
    for number, (source_ref, half_ref) in enumerate(zip(refs[:2], refs[2:])):
        feats = quarters * span + 8 * quarters * number
        half_ref[pl.ds(0, size), :] = source_ref[pl.ds(size * number, size), :]
        half_ref[pl.ds(size, 8 * quarters), :] = source_ref[pl.ds(feats, 8 * quarters), :]


def halves(first, second, span):
    rows, samples = first.shape
    return pl.pallas_call(
        lambda *refs: halves_body(rows // (span + 16), span, *refs),
        out_shape=[jax.ShapeDtypeStruct((rows // 2, samples), BF16)] * 2,
        cost_estimate=COST,
        compiler_params=PARAMS,
        name="halves",
    )(first, second)


def combine_body(span, mine_ref, theirs_ref, own_ref, *sent_refs):
    own_ref[...] = mine_ref[pl.ds(0, span), :] + theirs_ref[pl.ds(0, span), :]
    for number, sent_ref in enumerate(sent_refs):
        place = pl.ds((number + 1) * span, span)
        sent_ref[...] = (mine_ref[place, :] + theirs_ref[place, :]).astype(BF16)


def combine(mine, theirs, span):
    rows, samples = mine.shape
    return pl.pallas_call(
        lambda *refs: combine_body(span, *refs),
        out_shape=[jax.ShapeDtypeStruct((span, samples), F32)]
        + [jax.ShapeDtypeStruct((span, samples), BF16)] * (rows // span - 1),
        cost_estimate=COST,
        compiler_params=PARAMS,
        name="combine",
    )(mine, theirs)


def wide_product(first, second, second_dim):
    high, middle, low = split(first)
    other_high, other_middle, other_low = split(second)
    return over(
        jnp.concatenate([high, high, middle, middle, low, high], axis=1),
        jnp.concatenate(
            [other_high, other_middle, other_high, other_middle, other_high, other_low],
            axis=second_dim,
        ),
        1,
        second_dim,
    )


def exact_product(first, second):
    second = second.astype(BF16)
    return over(
        jnp.concatenate(split(first), axis=1), jnp.concatenate([second] * 3, axis=0), 1, 0
    )


def twice_product(twice_parts, parts):
    high, middle, low = twice_parts
    other_high, other_middle, other_low = parts
    left = lax.broadcasted_iota(jnp.int32, high.shape, 1) < high.shape[1] // 2
    last = jnp.where(left, low.astype(F32), high.astype(F32)).astype(BF16)
    return over(
        jnp.concatenate([high, middle, last], axis=1),
        jnp.concatenate(
            [other_high, other_middle, other_high, other_middle, other_high, other_low], axis=0
        ),
        1,
        0,
    )


def select_rows(picks, value):
    return over(
        jnp.concatenate([picks] * 3, axis=1), jnp.concatenate(split(value), axis=0), 1, 0
    )


def interpolate(stacks, skeletons):
    rank, pool = skeletons[0].shape[0], stacks[0].shape[0]
    place = lax.broadcasted_iota(jnp.int32, (rank, 2 * rank), 0)
    other = lax.broadcasted_iota(jnp.int32, (rank, 2 * rank), 1)
    eyes = jnp.where((other == place) | (other == place + rank), 1.0, 0.0)
    states = []
    for skeleton, stack in zip(skeletons, stacks):
        products = wide_product(skeleton, jnp.concatenate([stack, skeleton, skeleton], axis=0), 1)
        ridge = 0.05 * jnp.sum(skeleton * skeleton, keepdims=True) / rank + 1e-05
        inverse = 1.0 / (640.0 * ridge)
        states.append((products[:, :pool], eyes - products[:, pool:] * inverse, inverse))
    for number, tau in enumerate(TAUS):
        last = number == DOUBLINGS - 1
        later = []
        for solved, power, inverse in states:
            power_parts = split(power)
            parts = split(solved)
            if not last:
                parts = [jnp.concatenate(pair, axis=1) for pair in zip(parts, power_parts)]
            both = twice_product(power_parts, parts)
            solved = solved + both[:, :pool] * (1.0 / tau)
            later.append((solved, None if last else 2.0 * both[:, pool:] - eyes, inverse))
        states = later
    return [solved * (inverse * FRONT) for solved, _, inverse in states]


def merge(samples, reduced, coupling, picks, early=None):
    pool = samples.shape[0]
    high, middle, low = split(reduced)
    coupled = over(
        coupling, jnp.concatenate([high, middle, high, middle, high, low], axis=0), 1, 0
    )
    stacked = samples - coupled[:pool]
    skeleton = select_rows(picks, samples) - coupled[pool:]
    if early is not None:
        early(skeleton)
    (interp,) = interpolate([stacked], [skeleton])
    return interp, skeleton, wide_product(interp, reduced, 0)


def leaves_body(received, *refs):
    own_ref, *others = refs[: received + 1]
    source_ref, picks_ref, couplings_ref = refs[received + 1 : received + 4]
    leaf_ref, upper_ref, state_ref, held_ref, sem = refs[-5:]
    rank = picks_ref.shape[1]
    total = own_ref[...]
    for other in others:
        total = total + other[...].astype(F32)
    count = total.shape[0] // LEAF
    stacks = [total[leaf * LEAF : (leaf + 1) * LEAF] for leaf in range(count)]
    skeletons = [select_rows(picks_ref[leaf], stack) for leaf, stack in enumerate(stacks)]
    reduced = []
    for leaf, interp in enumerate(interpolate(stacks, skeletons)):
        held_ref[leaf] = interp
        reduced.append(exact_product(interp, source_ref[pl.ds(leaf * LEAF, LEAF), :]))
    copy = pltpu.make_async_copy(held_ref, leaf_ref, sem)
    copy.start()
    interp, skeleton, reduced = merge(
        jnp.concatenate(skeletons, axis=0),
        jnp.concatenate(reduced, axis=0),
        couplings_ref[...],
        picks_ref[count],
    )
    upper_ref[...] = interp
    state_ref[pl.ds(0, rank), :] = skeleton
    state_ref[pl.ds(rank, rank), :] = reduced
    copy.wait()


def leaves(own, others, source, picks, couplings, upper_couplings, leaf_count):
    samples = own.shape[1]
    rank, pool = picks.shape[1:]
    return pl.pallas_call(
        lambda *refs: leaves_body(len(others), *refs),
        out_shape=(
            jax.ShapeDtypeStruct((leaf_count, rank, LEAF), F32),
            jax.ShapeDtypeStruct((rank, pool), F32),
            jax.ShapeDtypeStruct((2 * rank, samples), F32),
        ),
        out_specs=(pl.BlockSpec(memory_space=pl.ANY), VMEM, VMEM),
        scratch_shapes=[pltpu.VMEM((leaf_count, rank, LEAF), F32), pltpu.SemaphoreType.DMA],
        cost_estimate=COST,
        compiler_params=PARAMS,
        name="leaves",
    )(own, *others, source, picks, couplings, *upper_couplings)


def level_body(number, place_ref, mine_ref, theirs_ref, picks_ref, couplings_ref, *refs):
    rank = picks_ref.shape[1]
    if number == 2:
        upper_ref, state_ref = refs
    else:
        one_ref, two_ref, upper_out, top_out, upper_ref, state_ref, sem = refs
        places = [
            (one_ref, upper_out.at[0, 0]),
            (two_ref, upper_out.at[1, 0]),
            (state_ref.at[pl.ds(0, rank)], top_out.at[0, 0]),
            (state_ref.at[pl.ds(rank, rank)], top_out.at[1, 0]),
            (upper_ref, upper_out.at[2, 0]),
        ]
        copies = [
            pltpu.make_async_copy(source, target, sem.at[pos])
            for pos, (source, target) in enumerate(places)
        ]
        copies[0].start()
        copies[1].start()

    def early(skeleton):
        state_ref[pl.ds(0, rank), :] = skeleton
        if number > 2:
            copies[2].start()

    mine_first = place_ref[number - 2] == 0
    mine, theirs = mine_ref[...], theirs_ref[...]
    first = jnp.where(mine_first, mine, theirs)
    second = jnp.where(mine_first, theirs, mine)
    interp, _, reduced = merge(
        jnp.concatenate([first[:rank], second[:rank]], axis=0),
        jnp.concatenate([first[rank:], second[rank:]], axis=0),
        couplings_ref[...],
        picks_ref[picks_ref.shape[0] + number - 4],
        early,
    )
    upper_ref[...] = interp
    state_ref[pl.ds(rank, rank), :] = reduced
    if number > 2:
        copies[3].start()
        copies[4].start()
        for copy in copies:
            copy.wait()


def level(number, place, mine, theirs, picks, couplings, below=()):
    rank, pool = picks.shape[1:]
    samples = mine.shape[1]
    out_shape = (
        jax.ShapeDtypeStruct((rank, pool), F32),
        jax.ShapeDtypeStruct(mine.shape, F32),
    )
    out_specs = (VMEM, VMEM)
    scratch = []
    if below:
        scratch = [pltpu.VMEM(out.shape, F32) for out in out_shape]
        scratch.append(pltpu.SemaphoreType.DMA((5,)))
        out_shape = (
            jax.ShapeDtypeStruct((3, 1, rank, pool), F32),
            jax.ShapeDtypeStruct((2, 1, rank, samples), F32),
        )
        out_specs = (pl.BlockSpec(memory_space=pl.ANY),) * 2
    return pl.pallas_call(
        lambda *refs: level_body(number, *refs),
        out_shape=out_shape,
        in_specs=[SMEM] + [VMEM] * (4 + len(below)),
        out_specs=out_specs,
        scratch_shapes=scratch,
        cost_estimate=COST,
        compiler_params=PARAMS,
        name="level",
    )(place, mine, theirs, picks, couplings, *below)


def one_hot(chosen, pool):
    place = lax.broadcasted_iota(jnp.int32, (pool, chosen.shape[1]), 0)
    return jnp.where(place == chosen, 1.0, 0.0).astype(F32)


def couple(first, second, picks, gain, couplings_ref, points_ref):
    rank = first.shape[1]
    points = jnp.concatenate([first, second], axis=1)
    entries = jnp.exp2(over(row_features(points, gain).astype(BF16), col_features(points), 0, 0))
    left = lax.broadcasted_iota(jnp.int32, entries.shape, 1) < rank
    upper = lax.broadcasted_iota(jnp.int32, entries.shape, 0) < rank
    entries = jnp.where(left == upper, 0.0, entries)
    chosen = select_rows(picks.T.astype(BF16), entries)
    high, middle, low = split(jnp.concatenate([entries, chosen], axis=0))
    couplings_ref[...] = jnp.concatenate([high, high, middle, middle, low, high], axis=1)
    if points_ref is not None:
        points_ref[...] = over(points, picks, 1, 0).astype(BF16)


def coupling_shape(rank):
    return jax.ShapeDtypeStruct((3 * rank, 12 * rank), BF16)


def skeletons_body(gain, place_ref, own_ref, leaf_ref, one_ref, two_ref, three_ref, *refs):
    picks_ref, couplings_ref, points_ref = refs
    count, rank = leaf_ref.shape
    rows = [leaf_ref[leaf : leaf + 1, :] for leaf in range(count)]
    rows.append(one_ref[...])
    rows.append(two_ref[pl.ds(place_ref[2], 1), :])
    rows.append(three_ref[pl.ds(place_ref[3], 1), :])
    hots = [one_hot(row, picks_ref.shape[2]) for row in rows]
    for number, hot in enumerate(hots):
        picks_ref[number] = hot.T.astype(BF16)
    children = [
        over(own_ref[:, pl.ds(leaf * LEAF, LEAF)], hots[leaf].astype(BF16), 1, 0)
        for leaf in range(count)
    ]
    couple(*children, hots[count], gain, couplings_ref, points_ref)


def skeletons(place, own_points, tables, gain):
    leaf_count, rank = tables[0].shape
    return pl.pallas_call(
        lambda *refs: skeletons_body(gain, *refs),
        out_shape=(
            jax.ShapeDtypeStruct((leaf_count + 3, rank, LEAF), BF16),
            coupling_shape(rank),
            jax.ShapeDtypeStruct((16, rank), BF16),
        ),
        in_specs=[SMEM] + [VMEM] * 5,
        cost_estimate=COST,
        compiler_params=PARAMS,
        name="skeletons",
    )(place, own_points, *tables)


def couplings_body(gain, number, place_ref, mine_ref, theirs_ref, picks_ref, couplings_ref, *refs):
    mine_first = place_ref[number - 2] == 0
    mine, theirs = mine_ref[...].astype(F32), theirs_ref[...].astype(F32)
    first = jnp.where(mine_first, mine, theirs)
    second = jnp.where(mine_first, theirs, mine)
    picks = picks_ref[picks_ref.shape[0] + number - 4].astype(F32).T
    couple(first, second, picks, gain, couplings_ref, refs[0] if refs else None)


def couplings(number, place, mine, theirs, picks, gain):
    rank = picks.shape[1]
    out_shape = [coupling_shape(rank)]
    if number == 2:
        out_shape.append(jax.ShapeDtypeStruct(mine.shape, BF16))
    return pl.pallas_call(
        lambda *refs: couplings_body(gain, number, *refs),
        out_shape=out_shape,
        in_specs=[SMEM] + [VMEM] * 3,
        cost_estimate=COST,
        compiler_params=PARAMS,
        name="couplings",
    )(place, mine, theirs, picks)


def local(probes, points, leaf_skeleton, skeleton_one, skeleton_two, skeleton_three):
    span = probes.shape[1]
    row_count = lax.axis_size("row")
    col_count = lax.axis_size("col")
    col_pos = lax.axis_index("col")
    gain = 16.0 / math.sqrt(4 * span * row_count * col_count)
    place = jnp.stack([col_pos & 1, col_pos >> 1 & 1, col_pos >> 1, col_pos >> 2])

    def swap(value, row_bits, col_bits):
        pairs = [
            (r * col_count + c, (r ^ row_bits) * col_count + (c ^ col_bits))
            for r in range(row_count)
            for c in range(col_count)
        ]
        return lax.ppermute(value, ("row", "col"), pairs)

    packed, own_points = pack(probes, points)
    beside = swap(packed, 0, 1)
    across = swap(packed, 2, 0)
    line_points = [own_points]
    for offset in range(1, col_count // 2):
        line_points.append(swap(own_points, 0, 2 * offset))
    line_points = jnp.concatenate(line_points, axis=1)
    row_points = [line_points, swap(line_points, 1, 0)]

    row_feats, totals = product([packed], row_points[:1], span, gain=gain)
    more_feats, more_totals = product([packed], row_points[1:], span, gain=gain, own=False)
    row_feats, totals = row_feats + more_feats, totals + more_totals
    beside, across, *totals = lax.optimization_barrier((beside, across, *totals))
    pieces = [packed, beside, across]
    relayed = halves(beside, across, span)
    diagonal = [swap(relayed[0], 2, 0), swap(relayed[1], 0, 1)]
    totals = product([beside], row_feats, span, totals)
    totals = product([across], row_feats, span, totals)
    tables = (leaf_skeleton, skeleton_one, skeleton_two, skeleton_three)
    picks, couplings_one, points_one = skeletons(place, own_points, tables, gain)
    points_one, *totals = lax.optimization_barrier((points_one, *totals))
    pieces += diagonal
    for bit in range(2, row_count.bit_length() - 1):
        more = [swap(value, 1 << bit, 0) for value in pieces]
        totals = product(more, row_feats, span, totals)
        pieces += more
    (theirs,) = product(diagonal, row_feats[1:], span, totals[1:])
    from_sibling = swap(theirs, 1, 0)
    (mine,) = product(diagonal, row_feats[:1], span, totals[:1])
    kept, *sent = combine(mine, from_sibling, span)
    received = [swap(value, 0, 2 * (number + 1)) for number, value in enumerate(sent)]

    points_one, kept = lax.optimization_barrier((points_one, kept))
    couplings_two, points_two = couplings(
        2, place, points_one, swap(points_one, 0, 1), picks, gain
    )
    (couplings_three,) = couplings(3, place, points_two, swap(points_two, 0, 2), picks, gain)

    leaf_count = leaf_skeleton.shape[0]
    leaf_interp, interp_one, state = leaves(
        kept, received, packed, picks, couplings_one, (couplings_two, couplings_three), leaf_count
    )
    interp_two, state_two = level(2, place, state, swap(state, 0, 1), picks, couplings_two)
    upper_interp, top_state = level(
        3,
        place,
        state_two,
        swap(state_two, 0, 2),
        picks,
        couplings_three,
        (interp_one, interp_two),
    )
    return jnp.swapaxes(leaf_interp, 1, 2), jnp.swapaxes(upper_interp, 2, 3), top_state


def solution(mesh):
    placed = (
        P(None, ("row", "col"), None),
        P(None, None, ("row", "col")),
        P(("row", "col"), None),
        P(("row", "col"), None),
        P("row", None),
        P("row", None),
    )
    return jax.shard_map(
        local,
        mesh=mesh,
        in_specs=placed,
        out_specs=(
            P(("row", "col"), None, None),
            P(None, ("row", "col"), None, None),
            P(None, ("row", "col"), None, None),
        ),
        check_vma=False,
    )
```

```python
import math

import jax
import jax.numpy as jnp
from jax import lax
from jax.experimental import pallas as pl
from jax.experimental.pallas import tpu as pltpu
from jax.sharding import PartitionSpec as P

LEAF = 128
F32 = jnp.float32
BF16 = jnp.bfloat16
DOUBLINGS = 9
VMEM = pl.BlockSpec(memory_space=pltpu.VMEM)
SMEM = pl.BlockSpec(memory_space=pltpu.SMEM)


def vmem(shape, kind=F32):
    return pltpu.VMEM(tuple(shape), kind)


COST = pl.CostEstimate(flops=0, bytes_accessed=0, transcendentals=0)
PARAMS = pltpu.CompilerParams(vmem_limit_bytes=16 << 20)


def chebyshev_constants():
    taus = [1282.0 / 1280.0]
    for _ in range(DOUBLINGS):
        taus.append(2.0 * taus[-1] * taus[-1] - 1.0)
    front = 2.0**DOUBLINGS * math.prod(taus[:-1]) / taus[-1]
    return taus[:-1], front


TAUS, FRONT = chebyshev_constants()


def over(first, second, first_dim, second_dim):
    return lax.dot_general(
        first,
        second,
        (((first_dim,), (second_dim,)), ((), ())),
        preferred_element_type=F32,
    )


def split(value):
    high = value.astype(BF16)
    rest = value - high.astype(F32)
    middle = rest.astype(BF16)
    return high, middle, (rest - middle.astype(F32)).astype(BF16)


def norm_rows(norm, first, width):
    parts = [part.astype(F32) for part in split(norm)]
    place = lax.broadcasted_iota(jnp.int32, (16, width), 0)
    extra = jnp.where(place < 6, 1.0, 0.0)
    for pos in range(3):
        extra = jnp.where(place == pos + first, parts[pos], extra)
    return extra


def row_features(feats, gain):
    feats = feats.astype(F32)
    depth, width = feats.shape
    unit = math.log2(math.e) / (2.0 * depth)
    norm = jnp.sum(feats * feats, axis=0, keepdims=True) * -unit + math.log2(gain)
    parts = [part.astype(F32) for part in split(feats * (2.0 * unit))]
    return jnp.concatenate([*parts, norm_rows(norm, 0, width)], axis=0)


def col_features(feats):
    feats = feats.astype(F32)
    depth, width = feats.shape
    unit = math.log2(math.e) / (2.0 * depth)
    norm = jnp.sum(feats * feats, axis=0, keepdims=True) * -unit
    return jnp.concatenate([feats, feats, feats, norm_rows(norm, 3, width)], axis=0).astype(BF16)


def pack_body(probes_ref, points_ref, packed_ref, own_ref, held_ref, sem):
    quarters, span, _ = probes_ref.shape
    half = quarters // 2
    rows = half * (span + 16)
    copies = [pltpu.make_async_copy(points_ref, held_ref, sem.at[quarters])]
    for quarter in range(quarters):
        start = quarter // half * rows + quarter % half * span
        target = packed_ref.at[pl.ds(start, span)]
        copies.append(pltpu.make_async_copy(probes_ref.at[quarter], target, sem.at[quarter]))
    for copy in copies:
        copy.start()
    copies[0].wait()
    points = held_ref[...].astype(F32)
    for quarter in range(quarters):
        feats = points[:, quarter, :].astype(BF16)
        start = quarter // half * rows + half * span + quarter % half * 16
        packed_ref[pl.ds(start, 16), :] = feats
        if quarter == 0:
            own_ref[...] = feats
    for copy in copies[1:]:
        copy.wait()


def pack(probes, points):
    quarters, span, samples = probes.shape
    return pl.pallas_call(
        pack_body,
        out_shape=(
            vmem((quarters * (span + 16), samples), BF16),
            vmem((16, span), BF16),
        ),
        in_specs=[pl.BlockSpec(memory_space=pltpu.HBM)] * 2,
        scratch_shapes=[
            pltpu.VMEM(points.shape, BF16),
            pltpu.SemaphoreType.DMA((quarters + 1,)),
        ],
        cost_estimate=COST,
        compiler_params=PARAMS,
        name="pack",
    )(*(pltpu.with_memory_space_constraint(value, pltpu.HBM) for value in (probes, points)))


def masked(entries):
    shape = entries.shape
    row_leaf = lax.broadcasted_iota(jnp.int32, shape, 0) // LEAF
    col_leaf = lax.broadcasted_iota(jnp.int32, shape, 1) // LEAF
    return jnp.where(row_leaf == col_leaf, 0.0, entries)


def add_source(source_ref, row_refs, cols_ref, put, span, own):
    size = 2 * (span + 16)
    parts = range(0, source_ref.shape[0], size)
    for number, part in enumerate(parts):
        for quarter in range(2):
            feats = source_ref[pl.ds(part + 2 * span + 16 * quarter, 16), :]
            cols_ref[:, pl.ds((2 * number + quarter) * span, span)] = col_features(feats)
    columns = 2 * span * len(parts)
    for half, rows_ref in enumerate(row_refs):
        for start in range(0, rows_ref.shape[0], span):
            feats = rows_ref[pl.ds(start, span), :]
            entries = jnp.exp2(over(feats, cols_ref[:, :columns], 1, 0))
            if own and half == 0 and start == 0:
                entries = jnp.concatenate([masked(entries[:, :span]), entries[:, span:]], axis=1)
            randoms = [source_ref[pl.ds(part, 2 * span), :] for part in parts]
            put(half, start, over(entries.astype(BF16), jnp.concatenate(randoms, axis=0), 1, 0))


def product_body(gain, span, first, own, source_count, half_count, *refs):
    refs = list(refs)
    cols_ref = refs.pop()
    take = lambda count: [refs.pop(0) for _ in range(count)]
    sources = take(source_count)
    if first:
        point_refs, row_refs = take(half_count), take(half_count)
        for points_ref, rows_ref in zip(point_refs, row_refs):
            for start in range(0, points_ref.shape[1], span):
                feats = points_ref[:, pl.ds(start, span)]
                rows_ref[pl.ds(start, span), :] = row_features(feats, gain).T.astype(BF16)
    else:
        row_refs, old_refs = take(half_count), take(half_count)
    total_refs = take(half_count)
    for number, source in enumerate(sources):

        def put(half, start, value):
            place = pl.ds(start, span)
            if number > 0:
                total_refs[half][place, :] += value
            elif first:
                total_refs[half][place, :] = value
            else:
                total_refs[half][place, :] = old_refs[half][place, :] + value

        add_source(source, row_refs, cols_ref, put, span, first and own and number == 0)


def product(sources, rows, span, totals=None, gain=None, own=True):
    samples = sources[0].shape[1]
    first = totals is None
    count = len(rows)
    counts = [half.shape[1] if first else half.shape[0] for half in rows]
    columns = max(s.shape[0] // (span + 16) * span for s in sources)
    out = [vmem((count, samples), F32) for count in counts]
    if first:
        out = [vmem((count, 64), BF16) for count in counts] + out
    out = pl.pallas_call(
        lambda *refs: product_body(gain, span, first, own, len(sources), count, *refs),
        out_shape=out,
        scratch_shapes=[pltpu.VMEM((64, columns), BF16)],
        cost_estimate=COST,
        compiler_params=PARAMS,
        name="product",
    )(*sources, *rows, *([] if first else totals))
    return (out[:count], out[count:]) if first else out


def combine_body(span, mine_ref, theirs_ref, own_ref, *sent_refs):
    own_ref[...] = mine_ref[pl.ds(0, span), :] + theirs_ref[pl.ds(0, span), :]
    for number, sent_ref in enumerate(sent_refs):
        place = pl.ds((number + 1) * span, span)
        sent_ref[...] = (mine_ref[place, :] + theirs_ref[place, :]).astype(BF16)


def combine(mine, theirs, span):
    rows, samples = mine.shape
    return pl.pallas_call(
        lambda *refs: combine_body(span, *refs),
        out_shape=[vmem((span, samples), F32)]
        + [vmem((span, samples), BF16)] * (rows // span - 1),
        cost_estimate=COST,
        compiler_params=PARAMS,
        name="combine",
    )(mine, theirs)


def wide_product(first, second, second_dim):
    high, middle, low = split(first)
    other_high, other_middle, other_low = split(second)
    return over(
        jnp.concatenate([high, high, middle, middle, low, high], axis=1),
        jnp.concatenate(
            [other_high, other_middle, other_high, other_middle, other_high, other_low],
            axis=second_dim,
        ),
        1,
        second_dim,
    )


def exact_product(first, second):
    second = second.astype(BF16)
    return over(
        jnp.concatenate(split(first), axis=1), jnp.concatenate([second] * 3, axis=0), 1, 0
    )


def twice_product(twice_parts, parts):
    high, middle, low = twice_parts
    other_high, other_middle, other_low = parts
    left = lax.broadcasted_iota(jnp.int32, high.shape, 1) < high.shape[1] // 2
    last = jnp.where(left, low.astype(F32), high.astype(F32)).astype(BF16)
    return over(
        jnp.concatenate([high, middle, last], axis=1),
        jnp.concatenate(
            [other_high, other_middle, other_high, other_middle, other_high, other_low], axis=0
        ),
        1,
        0,
    )


def select_rows(picks, value):
    return over(
        jnp.concatenate([picks] * 3, axis=1), jnp.concatenate(split(value), axis=0), 1, 0
    )


def interpolate(stacks, skeletons):
    rank, pool = skeletons[0].shape[0], stacks[0].shape[0]
    place = lax.broadcasted_iota(jnp.int32, (rank, 2 * rank), 0)
    other = lax.broadcasted_iota(jnp.int32, (rank, 2 * rank), 1)
    eyes = jnp.where((other == place) | (other == place + rank), 1.0, 0.0)
    states = []
    for skeleton, stack in zip(skeletons, stacks):
        products = wide_product(skeleton, jnp.concatenate([stack, skeleton, skeleton], axis=0), 1)
        ridge = 0.05 * jnp.sum(skeleton * skeleton, keepdims=True) / rank + 1e-05
        inverse = 1.0 / (640.0 * ridge)
        states.append((products[:, :pool], eyes - products[:, pool:] * inverse, inverse))
    for number, tau in enumerate(TAUS):
        last = number == DOUBLINGS - 1
        later = []
        for solved, power, inverse in states:
            power_parts = split(power)
            parts = split(solved)
            if not last:
                parts = [jnp.concatenate(pair, axis=1) for pair in zip(parts, power_parts)]
            both = twice_product(power_parts, parts)
            solved = solved + both[:, :pool] * (1.0 / tau)
            later.append((solved, None if last else 2.0 * both[:, pool:] - eyes, inverse))
        states = later
    return [solved * (inverse * FRONT) for solved, _, inverse in states]


def merge(samples, reduced, coupling, picks, early=None):
    pool = samples.shape[0]
    high, middle, low = split(reduced)
    coupled = over(
        coupling, jnp.concatenate([high, middle, high, middle, high, low], axis=0), 1, 0
    )
    stacked = samples - coupled[:pool]
    skeleton = select_rows(picks, samples) - coupled[pool:]
    if early is not None:
        early(skeleton)
    (interp,) = interpolate([stacked], [skeleton])
    return interp, skeleton, wide_product(interp, reduced, 0)


def leaves_body(received, *refs):
    own_ref, *others = refs[: received + 1]
    source_ref, picks_ref, couplings_ref = refs[received + 1 : received + 4]
    leaf_ref, upper_ref, state_ref, held_ref, sem = refs[-5:]
    rank = picks_ref.shape[1]
    total = own_ref[...]
    for other in others:
        total = total + other[...].astype(F32)
    count = total.shape[0] // LEAF
    stacks = [total[leaf * LEAF : (leaf + 1) * LEAF] for leaf in range(count)]
    skeletons = [select_rows(picks_ref[leaf], stack) for leaf, stack in enumerate(stacks)]
    reduced = []
    for leaf, interp in enumerate(interpolate(stacks, skeletons)):
        held_ref[leaf] = interp
        reduced.append(exact_product(interp, source_ref[pl.ds(leaf * LEAF, LEAF), :]))
    copy = pltpu.make_async_copy(held_ref, leaf_ref, sem)
    copy.start()
    interp, skeleton, reduced = merge(
        jnp.concatenate(skeletons, axis=0),
        jnp.concatenate(reduced, axis=0),
        couplings_ref[...],
        picks_ref[count],
    )
    upper_ref[...] = interp
    state_ref[pl.ds(0, rank), :] = skeleton
    state_ref[pl.ds(rank, rank), :] = reduced
    copy.wait()


def leaves(own, others, source, picks, couplings, upper_couplings, leaf_count):
    samples = own.shape[1]
    rank, pool = picks.shape[1:]
    return pl.pallas_call(
        lambda *refs: leaves_body(len(others), *refs),
        out_shape=(
            jax.ShapeDtypeStruct((leaf_count, rank, LEAF), F32),
            vmem((rank, pool), F32),
            vmem((2 * rank, samples), F32),
        ),
        out_specs=(pl.BlockSpec(memory_space=pl.ANY), VMEM, VMEM),
        scratch_shapes=[pltpu.VMEM((leaf_count, rank, LEAF), F32), pltpu.SemaphoreType.DMA],
        cost_estimate=COST,
        compiler_params=PARAMS,
        name="leaves",
    )(own, *others, source, picks, couplings, *upper_couplings)


def level_body(number, place_ref, mine_ref, theirs_ref, picks_ref, couplings_ref, *refs):
    rank = picks_ref.shape[1]
    if number == 2:
        upper_ref, state_ref = refs
    else:
        one_ref, two_ref, upper_out, top_out, upper_ref, state_ref, sem = refs
        places = [
            (one_ref, upper_out.at[0, 0]),
            (two_ref, upper_out.at[1, 0]),
            (state_ref.at[pl.ds(0, rank)], top_out.at[0, 0]),
            (state_ref.at[pl.ds(rank, rank)], top_out.at[1, 0]),
            (upper_ref, upper_out.at[2, 0]),
        ]
        copies = [
            pltpu.make_async_copy(source, target, sem.at[pos])
            for pos, (source, target) in enumerate(places)
        ]
        copies[0].start()
        copies[1].start()

    def early(skeleton):
        state_ref[pl.ds(0, rank), :] = skeleton
        if number > 2:
            copies[2].start()

    mine_first = place_ref[number - 2] == 0
    mine, theirs = mine_ref[...], theirs_ref[...]
    first = jnp.where(mine_first, mine, theirs)
    second = jnp.where(mine_first, theirs, mine)
    interp, _, reduced = merge(
        jnp.concatenate([first[:rank], second[:rank]], axis=0),
        jnp.concatenate([first[rank:], second[rank:]], axis=0),
        couplings_ref[...],
        picks_ref[picks_ref.shape[0] + number - 4],
        early,
    )
    upper_ref[...] = interp
    state_ref[pl.ds(rank, rank), :] = reduced
    if number > 2:
        copies[3].start()
        copies[4].start()
        for copy in copies:
            copy.wait()


def level(number, place, mine, theirs, picks, couplings, below=()):
    rank, pool = picks.shape[1:]
    samples = mine.shape[1]
    out_shape = (
        vmem((rank, pool), F32),
        vmem(mine.shape, F32),
    )
    out_specs = (VMEM, VMEM)
    scratch = []
    if below:
        scratch = [pltpu.VMEM(out.shape, F32) for out in out_shape]
        scratch.append(pltpu.SemaphoreType.DMA((5,)))
        out_shape = (
            jax.ShapeDtypeStruct((3, 1, rank, pool), F32),
            jax.ShapeDtypeStruct((2, 1, rank, samples), F32),
        )
        out_specs = (pl.BlockSpec(memory_space=pl.ANY),) * 2
    return pl.pallas_call(
        lambda *refs: level_body(number, *refs),
        out_shape=out_shape,
        in_specs=[SMEM] + [VMEM] * (4 + len(below)),
        out_specs=out_specs,
        scratch_shapes=scratch,
        cost_estimate=COST,
        compiler_params=PARAMS,
        name="level",
    )(place, mine, theirs, picks, couplings, *below)


def one_hot(chosen, pool):
    place = lax.broadcasted_iota(jnp.int32, (pool, chosen.shape[1]), 0)
    return jnp.where(place == chosen, 1.0, 0.0).astype(F32)


def couple(first, second, picks, gain, couplings_ref, points_ref):
    rank = first.shape[1]
    points = jnp.concatenate([first, second], axis=1)
    entries = jnp.exp2(over(row_features(points, gain).astype(BF16), col_features(points), 0, 0))
    left = lax.broadcasted_iota(jnp.int32, entries.shape, 1) < rank
    upper = lax.broadcasted_iota(jnp.int32, entries.shape, 0) < rank
    entries = jnp.where(left == upper, 0.0, entries)
    chosen = select_rows(picks.T.astype(BF16), entries)
    high, middle, low = split(jnp.concatenate([entries, chosen], axis=0))
    couplings_ref[...] = jnp.concatenate([high, high, middle, middle, low, high], axis=1)
    if points_ref is not None:
        points_ref[...] = over(points, picks, 1, 0).astype(BF16)


def coupling_shape(rank):
    return vmem((3 * rank, 12 * rank), BF16)


def skeletons_body(gain, place_ref, own_ref, leaf_ref, one_ref, two_ref, three_ref, *refs):
    picks_ref, couplings_ref, points_ref = refs
    count, rank = leaf_ref.shape
    rows = [leaf_ref[leaf : leaf + 1, :] for leaf in range(count)]
    rows.append(one_ref[...])
    rows.append(two_ref[pl.ds(place_ref[2], 1), :])
    rows.append(three_ref[pl.ds(place_ref[3], 1), :])
    hots = [one_hot(row, picks_ref.shape[2]) for row in rows]
    for number, hot in enumerate(hots):
        picks_ref[number] = hot.T.astype(BF16)
    children = [
        over(own_ref[:, pl.ds(leaf * LEAF, LEAF)], hots[leaf].astype(BF16), 1, 0)
        for leaf in range(count)
    ]
    couple(*children, hots[count], gain, couplings_ref, points_ref)


def skeletons(place, own_points, tables, gain):
    leaf_count, rank = tables[0].shape
    return pl.pallas_call(
        lambda *refs: skeletons_body(gain, *refs),
        out_shape=(
            vmem((leaf_count + 3, rank, LEAF), BF16),
            coupling_shape(rank),
            vmem((16, rank), BF16),
        ),
        in_specs=[SMEM] + [VMEM] * 5,
        cost_estimate=COST,
        compiler_params=PARAMS,
        name="skeletons",
    )(place, own_points, *tables)


def couplings_body(gain, number, place_ref, mine_ref, theirs_ref, picks_ref, couplings_ref, *refs):
    mine_first = place_ref[number - 2] == 0
    mine, theirs = mine_ref[...].astype(F32), theirs_ref[...].astype(F32)
    first = jnp.where(mine_first, mine, theirs)
    second = jnp.where(mine_first, theirs, mine)
    picks = picks_ref[picks_ref.shape[0] + number - 4].astype(F32).T
    couple(first, second, picks, gain, couplings_ref, refs[0] if refs else None)


def couplings(number, place, mine, theirs, picks, gain):
    rank = picks.shape[1]
    out_shape = [coupling_shape(rank)]
    if number == 2:
        out_shape.append(vmem(mine.shape, BF16))
    return pl.pallas_call(
        lambda *refs: couplings_body(gain, number, *refs),
        out_shape=out_shape,
        in_specs=[SMEM] + [VMEM] * 3,
        cost_estimate=COST,
        compiler_params=PARAMS,
        name="couplings",
    )(place, mine, theirs, picks)


def local(probes, points, leaf_skeleton, skeleton_one, skeleton_two, skeleton_three):
    span = probes.shape[1]
    row_count = lax.axis_size("row")
    col_count = lax.axis_size("col")
    col_pos = lax.axis_index("col")
    gain = 16.0 / math.sqrt(4 * span * row_count * col_count)
    place = jnp.stack([col_pos & 1, col_pos >> 1 & 1, col_pos >> 1, col_pos >> 2])

    def swap(value, row_bits, col_bits):
        pairs = [
            (r * col_count + c, (r ^ row_bits) * col_count + (c ^ col_bits))
            for r in range(row_count)
            for c in range(col_count)
        ]
        return lax.ppermute(value, ("row", "col"), pairs)

    packed, own_points = pack(probes, points)
    beside = swap(packed, 0, 1)
    across = swap(packed, 2, 0)
    line_points = [own_points]
    for offset in range(1, col_count // 2):
        line_points.append(swap(own_points, 0, 2 * offset))
    line_points = jnp.concatenate(line_points, axis=1)
    row_points = [line_points, swap(line_points, 1, 0)]

    row_feats, totals = product([packed], row_points[:1], span, gain=gain)
    more_feats, more_totals = product([packed], row_points[1:], span, gain=gain, own=False)
    row_feats, totals = row_feats + more_feats, totals + more_totals
    beside, across, *totals = lax.optimization_barrier((beside, across, *totals))
    pieces = [packed, beside, across]
    half = packed.shape[0] // 2
    diagonal = [swap(beside[:half], 2, 0), swap(across[half:], 0, 1)]
    totals = product([beside], row_feats, span, totals)
    totals = product([across], row_feats, span, totals)
    tables = (leaf_skeleton, skeleton_one, skeleton_two, skeleton_three)
    picks, couplings_one, points_one = skeletons(place, own_points, tables, gain)
    points_one, *totals = lax.optimization_barrier((points_one, *totals))
    pieces += diagonal
    for bit in range(2, row_count.bit_length() - 1):
        more = [swap(value, 1 << bit, 0) for value in pieces]
        totals = product(more, row_feats, span, totals)
        pieces += more
    (theirs,) = product(diagonal, row_feats[1:], span, totals[1:])
    from_sibling = swap(theirs, 1, 0)
    (mine,) = product(diagonal, row_feats[:1], span, totals[:1])
    kept, *sent = combine(mine, from_sibling, span)
    received = [swap(value, 0, 2 * (number + 1)) for number, value in enumerate(sent)]

    points_one, kept = lax.optimization_barrier((points_one, kept))
    couplings_two, points_two = couplings(
        2, place, points_one, swap(points_one, 0, 1), picks, gain
    )
    (couplings_three,) = couplings(3, place, points_two, swap(points_two, 0, 2), picks, gain)

    leaf_count = leaf_skeleton.shape[0]
    leaf_interp, interp_one, state = leaves(
        kept, received, packed, picks, couplings_one, (couplings_two, couplings_three), leaf_count
    )
    interp_two, state_two = level(2, place, state, swap(state, 0, 1), picks, couplings_two)
    upper_interp, top_state = level(
        3,
        place,
        state_two,
        swap(state_two, 0, 2),
        picks,
        couplings_three,
        (interp_one, interp_two),
    )
    return jnp.swapaxes(leaf_interp, 1, 2), jnp.swapaxes(upper_interp, 2, 3), top_state


def solution(mesh):
    placed = (
        P(None, ("row", "col"), None),
        P(None, None, ("row", "col")),
        P(("row", "col"), None),
        P(("row", "col"), None),
        P("row", None),
        P("row", None),
    )
    return jax.shard_map(
        local,
        mesh=mesh,
        in_specs=placed,
        out_specs=(
            P(("row", "col"), None, None),
            P(None, ("row", "col"), None, None),
            P(None, ("row", "col"), None, None),
        ),
        check_vma=False,
    )
```

```python
import math

import jax
import jax.numpy as jnp
from jax import lax
from jax.experimental import pallas as pl
from jax.experimental.pallas import tpu as pltpu
from jax.sharding import PartitionSpec as P

LEAF = 128
F32 = jnp.float32
BF16 = jnp.bfloat16
DOUBLINGS = 9
VMEM = pl.BlockSpec(memory_space=pltpu.VMEM)


def vmem(shape, kind=F32):
    return pltpu.VMEM(tuple(shape), kind)


COST = pl.CostEstimate(flops=0, bytes_accessed=0, transcendentals=0)
LONG = pl.CostEstimate(flops=10**10, bytes_accessed=0, transcendentals=0)
PARAMS = pltpu.CompilerParams(vmem_limit_bytes=16 << 20)


def chebyshev_constants():
    taus = [1282.0 / 1280.0]
    for _ in range(DOUBLINGS):
        taus.append(2.0 * taus[-1] * taus[-1] - 1.0)
    front = 2.0**DOUBLINGS * math.prod(taus[:-1]) / taus[-1]
    return taus[:-1], front


TAUS, FRONT = chebyshev_constants()


def over(first, second, first_dim, second_dim):
    return lax.dot_general(
        first,
        second,
        (((first_dim,), (second_dim,)), ((), ())),
        preferred_element_type=F32,
    )


def split(value):
    high = value.astype(BF16)
    rest = value - high.astype(F32)
    middle = rest.astype(BF16)
    return high, middle, (rest - middle.astype(F32)).astype(BF16)


def norm_rows(norm, first, width):
    parts = [part.astype(F32) for part in split(norm)]
    place = lax.broadcasted_iota(jnp.int32, (16, width), 0)
    extra = jnp.where(place < 6, 1.0, 0.0)
    for pos in range(3):
        extra = jnp.where(place == pos + first, parts[pos], extra)
    return extra


def row_features(feats, gain):
    feats = feats.astype(F32)
    depth, width = feats.shape
    unit = math.log2(math.e) / (2.0 * depth)
    norm = jnp.sum(feats * feats, axis=0, keepdims=True) * -unit + math.log2(gain)
    parts = [part.astype(F32) for part in split(feats * (2.0 * unit))]
    return jnp.concatenate([*parts, norm_rows(norm, 0, width)], axis=0)


def col_features(feats):
    feats = feats.astype(F32)
    depth, width = feats.shape
    unit = math.log2(math.e) / (2.0 * depth)
    norm = jnp.sum(feats * feats, axis=0, keepdims=True) * -unit
    return jnp.concatenate([feats, feats, feats, norm_rows(norm, 3, width)], axis=0).astype(BF16)


def pack_body(*refs):
    probes_ref, points_ref, *table_refs = refs[:6]
    packed_ref, own_ref, held_ref, rows_ref, *held_tables, sem = refs[6:]
    quarters, span, _ = probes_ref.shape
    half = quarters // 2
    rows = half * (span + 16)
    pairs = [(points_ref, held_ref), *zip(table_refs, held_tables)]
    small = len(pairs)
    for quarter in range(quarters):
        start = quarter // half * rows + quarter % half * span
        pairs.append((probes_ref.at[quarter], packed_ref.at[pl.ds(start, span)]))
    copies = [
        pltpu.make_async_copy(source, target, sem.at[pos])
        for pos, (source, target) in enumerate(pairs)
    ]
    for copy in copies:
        copy.start()
    rows_ref[...] = jnp.zeros_like(rows_ref)
    for copy in copies[:small]:
        copy.wait()
    points = held_ref[...].astype(F32)
    for quarter in range(quarters):
        feats = points[:, quarter, :].astype(BF16)
        start = quarter // half * rows + half * span + quarter % half * 16
        packed_ref[pl.ds(start, 16), :] = feats
        if quarter == 0:
            own_ref[...] = feats
    start = 0
    for table in held_tables:
        count, rank = table.shape
        rows_ref[pl.ds(start, count), pl.ds(0, rank)] = table[...].astype(F32)
        start += count
    packed_ref[pl.ds(2 * rows, rows_ref.shape[0]), :] = rows_ref[...].astype(BF16)
    for copy in copies[small:]:
        copy.wait()


def pack(probes, points, tables):
    quarters, span, samples = probes.shape
    table_rows = -(-sum(table.shape[0] for table in tables) // 16) * 16
    inputs = (probes, points, *tables)
    return pl.pallas_call(
        pack_body,
        out_shape=(
            vmem((quarters * (span + 16) + table_rows, samples), BF16),
            vmem((16, span), BF16),
        ),
        in_specs=[pl.BlockSpec(memory_space=pltpu.HBM)] * len(inputs),
        scratch_shapes=[
            pltpu.VMEM(points.shape, BF16),
            pltpu.VMEM((table_rows, samples), F32),
            *[pltpu.VMEM(table.shape, jnp.int32) for table in tables],
            pltpu.SemaphoreType.DMA((quarters + 1 + len(tables),)),
        ],
        cost_estimate=COST,
        compiler_params=PARAMS,
        name="pack",
    )(*(pltpu.with_memory_space_constraint(value, pltpu.HBM) for value in inputs))


def masked(entries):
    shape = entries.shape
    row_leaf = lax.broadcasted_iota(jnp.int32, shape, 0) // LEAF
    col_leaf = lax.broadcasted_iota(jnp.int32, shape, 1) // LEAF
    return jnp.where(row_leaf == col_leaf, 0.0, entries)


def add_source(source_ref, row_refs, cols_ref, put, span, own):
    size = 2 * (span + 16)
    parts = range(0, source_ref.shape[0] // size * size, size)
    for number, part in enumerate(parts):
        for quarter in range(2):
            feats = source_ref[pl.ds(part + 2 * span + 16 * quarter, 16), :]
            cols_ref[:, pl.ds((2 * number + quarter) * span, span)] = col_features(feats)
    columns = 2 * span * len(parts)
    for group, rows_ref in enumerate(row_refs):
        for start in range(0, rows_ref.shape[0], span):
            feats = rows_ref[pl.ds(start, span), :]
            entries = jnp.exp2(over(feats, cols_ref[:, :columns], 1, 0))
            if own and group == 0 and start == 0:
                entries = jnp.concatenate([masked(entries[:, :span]), entries[:, span:]], axis=1)
            randoms = [source_ref[pl.ds(part, 2 * span), :] for part in parts]
            put(group, start, over(entries.astype(BF16), jnp.concatenate(randoms, axis=0), 1, 0))


def first_product_body(gain, span, own, groups, point_count, *refs):
    source_ref, *point_refs = refs[: point_count + 1]
    row_refs = refs[point_count + 1 : point_count + 1 + len(groups)]
    total_refs, cols_ref = refs[point_count + 1 + len(groups) : -1], refs[-1]
    for rows_ref, places in zip(row_refs, groups):
        for pos, (array, start) in enumerate(places):
            feats = point_refs[array][:, pl.ds(start, span)]
            rows_ref[pl.ds(pos * span, span), :] = row_features(feats, gain).T.astype(BF16)

    def put(group, start, value):
        total_refs[group][pl.ds(start, span), :] = value

    add_source(source_ref, row_refs, cols_ref, put, span, own)


def first_product(source, points, groups, span, gain, own):
    samples = source.shape[1]
    rows = [len(places) * span for places in groups]
    out = pl.pallas_call(
        lambda *refs: first_product_body(gain, span, own, groups, len(points), *refs),
        out_shape=[vmem((count, 64), BF16) for count in rows]
        + [vmem((count, samples), F32) for count in rows],
        scratch_shapes=[pltpu.VMEM((64, 4 * span), BF16)],
        cost_estimate=COST,
        compiler_params=PARAMS,
        name="first_product",
    )(source, *points)
    return out[: len(groups)], out[len(groups) :]


def product_body(span, source_count, count, *refs):
    sources, refs = refs[:source_count], refs[source_count:]
    row_refs, old_refs, total_refs = refs[:count], refs[count : 2 * count], refs[2 * count : -1]
    cols_ref = refs[-1]
    for number, source in enumerate(sources):

        def put(group, start, value):
            place = pl.ds(start, span)
            base = old_refs if number == 0 else total_refs
            total_refs[group][place, :] = base[group][place, :] + value

        add_source(source, row_refs, cols_ref, put, span, False)


def product(sources, rows, totals, span):
    return pl.pallas_call(
        lambda *refs: product_body(span, len(sources), len(rows), *refs),
        out_shape=[vmem(total.shape, F32) for total in totals],
        scratch_shapes=[pltpu.VMEM((64, 4 * span), BF16)],
        cost_estimate=COST,
        compiler_params=PARAMS,
        name="product",
    )(*sources, *rows, *totals)


def halves_body(first_ref, second_ref, first_half, second_half):
    rows = first_half.shape[0]
    first_half[...] = first_ref[pl.ds(0, rows), :]
    second_half[...] = second_ref[pl.ds(rows, rows), :]


def halves(first, second, rows):
    return pl.pallas_call(
        halves_body,
        out_shape=[vmem((rows, first.shape[1]), BF16)] * 2,
        cost_estimate=COST,
        compiler_params=PARAMS,
        name="halves",
    )(first, second)


def add_up_body(span, kept, sent, mine_ref, theirs_ref, *refs):
    kept_ref, sent_ref = refs[-2:]
    for chunks, out_ref in ((kept, kept_ref), (sent, sent_ref)):
        for pos, chunk in enumerate(chunks):
            place = pl.ds(chunk * span, span)
            value = mine_ref[place, :] + theirs_ref[place, :].astype(F32)
            out_ref[pl.ds(pos * span, span), :] = value.astype(out_ref.dtype)


def add_up(mine, theirs, kept, sent, span, after=(), cost=COST):
    samples = mine.shape[1]
    return pl.pallas_call(
        lambda *refs: add_up_body(span, kept, sent, *refs),
        out_shape=(
            vmem((len(kept) * span, samples), F32),
            vmem((len(sent) * span, samples), BF16),
        ),
        cost_estimate=cost,
        compiler_params=PARAMS,
        name="add_up",
    )(mine, theirs, *after)


def wide_product(first, second, second_dim):
    high, middle, low = split(first)
    other_high, other_middle, other_low = split(second)
    return over(
        jnp.concatenate([high, high, middle, middle, low, high], axis=1),
        jnp.concatenate(
            [other_high, other_middle, other_high, other_middle, other_high, other_low],
            axis=second_dim,
        ),
        1,
        second_dim,
    )


def exact_product(first, second):
    second = second.astype(BF16)
    return over(
        jnp.concatenate(split(first), axis=1), jnp.concatenate([second] * 3, axis=0), 1, 0
    )


def twice_product(twice_parts, parts):
    high, middle, low = twice_parts
    other_high, other_middle, other_low = parts
    left = lax.broadcasted_iota(jnp.int32, high.shape, 1) < high.shape[1] // 2
    last = jnp.where(left, low.astype(F32), high.astype(F32)).astype(BF16)
    return over(
        jnp.concatenate([high, middle, last], axis=1),
        jnp.concatenate(
            [other_high, other_middle, other_high, other_middle, other_high, other_low], axis=0
        ),
        1,
        0,
    )


def select_rows(picks, value):
    return over(
        jnp.concatenate([picks] * 3, axis=1), jnp.concatenate(split(value), axis=0), 1, 0
    )


def interpolate(stacks, skeletons):
    rank, pool = skeletons[0].shape[0], stacks[0].shape[0]
    place = lax.broadcasted_iota(jnp.int32, (rank, 2 * rank), 0)
    other = lax.broadcasted_iota(jnp.int32, (rank, 2 * rank), 1)
    eyes = jnp.where((other == place) | (other == place + rank), 1.0, 0.0)
    states = []
    for skeleton, stack in zip(skeletons, stacks):
        products = wide_product(skeleton, jnp.concatenate([stack, skeleton, skeleton], axis=0), 1)
        ridge = 0.05 * jnp.sum(skeleton * skeleton, keepdims=True) / rank + 1e-05
        inverse = 1.0 / (640.0 * ridge)
        states.append((products[:, :pool], eyes - products[:, pool:] * inverse, inverse))
    for number, tau in enumerate(TAUS):
        last = number == DOUBLINGS - 1
        later = []
        for solved, power, inverse in states:
            power_parts = split(power)
            parts = split(solved)
            if not last:
                parts = [jnp.concatenate(pair, axis=1) for pair in zip(parts, power_parts)]
            both = twice_product(power_parts, parts)
            solved = solved + both[:, :pool] * (1.0 / tau)
            later.append((solved, None if last else 2.0 * both[:, pool:] - eyes, inverse))
        states = later
    return [solved * (inverse * FRONT) for solved, _, inverse in states]


def merge(samples, reduced, coupling, picks, early=None):
    pool = samples.shape[0]
    high, middle, low = split(reduced)
    coupled = over(
        coupling, jnp.concatenate([high, middle, high, middle, high, low], axis=0), 1, 0
    )
    stacked = samples - coupled[:pool]
    skeleton = select_rows(picks, samples) - coupled[pool:]
    if early is not None:
        early(skeleton)
    (interp,) = interpolate([stacked], [skeleton])
    return interp, skeleton, wide_product(interp, reduced, 0)


def leaves_body(received, *refs):
    own_ref, *others = refs[: received + 1]
    source_ref, picks_ref, couplings_ref = refs[received + 1 : received + 4]
    leaf_ref, upper_ref, state_ref, held_ref, sem = refs[-5:]
    rank = picks_ref.shape[1]
    total = own_ref[...]
    for other in others:
        total = total + other[...].astype(F32)
    count = total.shape[0] // LEAF
    stacks = [total[leaf * LEAF : (leaf + 1) * LEAF] for leaf in range(count)]
    skeletons = [select_rows(picks_ref[leaf], stack) for leaf, stack in enumerate(stacks)]
    reduced = []
    for leaf, interp in enumerate(interpolate(stacks, skeletons)):
        held_ref[leaf] = interp
        reduced.append(exact_product(interp, source_ref[pl.ds(leaf * LEAF, LEAF), :]))
    copy = pltpu.make_async_copy(held_ref, leaf_ref, sem)
    copy.start()
    interp, skeleton, reduced = merge(
        jnp.concatenate(skeletons, axis=0),
        jnp.concatenate(reduced, axis=0),
        couplings_ref[...],
        picks_ref[count],
    )
    upper_ref[...] = interp
    state_ref[pl.ds(0, rank), :] = skeleton
    state_ref[pl.ds(rank, rank), :] = reduced
    copy.wait()


def leaves(own, others, source, picks, couplings, later, leaf_count):
    samples = own.shape[1]
    rank, pool = picks.shape[1:]
    return pl.pallas_call(
        lambda *refs: leaves_body(len(others), *refs),
        out_shape=(
            jax.ShapeDtypeStruct((leaf_count, rank, LEAF), F32),
            vmem((rank, pool), F32),
            vmem((2 * rank, samples), F32),
        ),
        out_specs=(pl.BlockSpec(memory_space=pl.ANY), VMEM, VMEM),
        scratch_shapes=[pltpu.VMEM((leaf_count, rank, LEAF), F32), pltpu.SemaphoreType.DMA],
        cost_estimate=COST,
        compiler_params=PARAMS,
        name="leaves",
    )(own, *others, source, picks, couplings, later)


def first_of_pair(number):
    return (lax.axis_index("col") >> (number - 2)) % 2 == 0


def level_body(number, mine_ref, theirs_ref, picks_ref, couplings_ref, *refs):
    rank = picks_ref.shape[1]
    if number == 2:
        upper_ref, state_ref = refs
    else:
        one_ref, two_ref, upper_out, top_out, upper_ref, state_ref, sem = refs
        places = [
            (one_ref, upper_out.at[0, 0]),
            (two_ref, upper_out.at[1, 0]),
            (state_ref.at[pl.ds(0, rank)], top_out.at[0, 0]),
            (state_ref.at[pl.ds(rank, rank)], top_out.at[1, 0]),
            (upper_ref, upper_out.at[2, 0]),
        ]
        copies = [
            pltpu.make_async_copy(source, target, sem.at[pos])
            for pos, (source, target) in enumerate(places)
        ]
        copies[0].start()
        copies[1].start()

    def early(skeleton):
        state_ref[pl.ds(0, rank), :] = skeleton
        if number > 2:
            copies[2].start()

    mine_first = first_of_pair(number)
    mine, theirs = mine_ref[...], theirs_ref[...]
    first = jnp.where(mine_first, mine, theirs)
    second = jnp.where(mine_first, theirs, mine)
    interp, _, reduced = merge(
        jnp.concatenate([first[:rank], second[:rank]], axis=0),
        jnp.concatenate([first[rank:], second[rank:]], axis=0),
        couplings_ref[...],
        picks_ref[picks_ref.shape[0] + number - 4],
        early,
    )
    upper_ref[...] = interp
    state_ref[pl.ds(rank, rank), :] = reduced
    if number > 2:
        copies[3].start()
        copies[4].start()
        for copy in copies:
            copy.wait()


def level(number, mine, theirs, picks, couplings, below=()):
    rank, pool = picks.shape[1:]
    samples = mine.shape[1]
    out_shape = (
        vmem((rank, pool), F32),
        vmem(mine.shape, F32),
    )
    out_specs = (VMEM, VMEM)
    scratch = []
    if below:
        scratch = [pltpu.VMEM(out.shape, F32) for out in out_shape]
        scratch.append(pltpu.SemaphoreType.DMA((5,)))
        out_shape = (
            jax.ShapeDtypeStruct((3, 1, rank, pool), F32),
            jax.ShapeDtypeStruct((2, 1, rank, samples), F32),
        )
        out_specs = (pl.BlockSpec(memory_space=pl.ANY),) * 2
    return pl.pallas_call(
        lambda *refs: level_body(number, *refs),
        out_shape=out_shape,
        in_specs=[VMEM] * (4 + len(below)),
        out_specs=out_specs,
        scratch_shapes=scratch,
        cost_estimate=COST,
        compiler_params=PARAMS,
        name="level",
    )(mine, theirs, picks, couplings, *below)


def one_hot(chosen, pool):
    place = lax.broadcasted_iota(jnp.int32, (pool, chosen.shape[1]), 0)
    return jnp.where(place.astype(F32) == chosen, 1.0, 0.0).astype(F32)


def couple(first, second, picks, gain, couplings_ref):
    rank = first.shape[1]
    points = jnp.concatenate([first, second], axis=1)
    entries = jnp.exp2(over(row_features(points, gain).astype(BF16), col_features(points), 0, 0))
    left = lax.broadcasted_iota(jnp.int32, entries.shape, 1) < rank
    upper = lax.broadcasted_iota(jnp.int32, entries.shape, 0) < rank
    entries = jnp.where(left == upper, 0.0, entries)
    chosen = select_rows(picks.T.astype(BF16), entries)
    high, middle, low = split(jnp.concatenate([entries, chosen], axis=0))
    couplings_ref[...] = jnp.concatenate([high, high, middle, middle, low, high], axis=1)


def coupling_shape(rank):
    return vmem((3 * rank, 12 * rank), BF16)


def skeletons_body(gain, span, counts, mine_ref, beside_ref, *refs):
    picks_ref, one_ref, two_ref, points_ref = refs
    rank, pool = picks_ref.shape[1:]
    leaf_count = counts[0]
    tables = 4 * (span + 16)
    nodes = []
    for source_ref in (mine_ref, beside_ref):
        rows = source_ref[pl.ds(tables, source_ref.shape[0] - tables), :rank].astype(F32)
        hots = [one_hot(rows[pos : pos + 1], pool) for pos in range(leaf_count + 1)]
        children = []
        for leaf in range(leaf_count):
            feats = source_ref[pl.ds(2 * span, 16), pl.ds(leaf * LEAF, LEAF)]
            children.append(over(feats, hots[leaf].astype(BF16), 1, 0))
        points = jnp.concatenate(children, axis=1)
        nodes.append(over(points, hots[leaf_count], 1, 0))
        if source_ref is mine_ref:
            couple(*children, hots[leaf_count], gain, one_ref)
            table, start = rows, leaf_count + counts[1]
            for number, count in enumerate(counts[2:]):
                wanted = start + (lax.axis_index("col") >> (number + 1))
                place = lax.broadcasted_iota(jnp.int32, table.shape, 0)
                row = jnp.sum(jnp.where(place == wanted, table, 0.0), axis=0, keepdims=True)
                hots.append(one_hot(row, pool))
                start += count
            for number, hot in enumerate(hots):
                picks_ref[number] = hot.T.astype(BF16)
            upper = hots[leaf_count + 1]
    mine, theirs = nodes
    mine_first = first_of_pair(2)
    first = jnp.where(mine_first, mine, theirs)
    second = jnp.where(mine_first, theirs, mine)
    couple(first, second, upper, gain, two_ref)
    points_ref[...] = over(jnp.concatenate([first, second], axis=1), upper, 1, 0).astype(BF16)


def skeletons(packed, beside, tables, span, gain):
    leaf_count, rank = tables[0].shape
    counts = [table.shape[0] for table in tables]
    return pl.pallas_call(
        lambda *refs: skeletons_body(gain, span, counts, *refs),
        out_shape=(
            vmem((leaf_count + 3, rank, LEAF), BF16),
            coupling_shape(rank),
            coupling_shape(rank),
            vmem((16, rank), BF16),
        ),
        cost_estimate=COST,
        compiler_params=PARAMS,
        name="skeletons",
    )(packed, beside)


def top_couplings_body(gain, mine_ref, theirs_ref, picks_ref, couplings_ref):
    mine_first = first_of_pair(3)
    mine, theirs = mine_ref[...].astype(F32), theirs_ref[...].astype(F32)
    first = jnp.where(mine_first, mine, theirs)
    second = jnp.where(mine_first, theirs, mine)
    picks = picks_ref[picks_ref.shape[0] - 1].astype(F32).T
    couple(first, second, picks, gain, couplings_ref)


def top_couplings(mine, theirs, picks, gain):
    return pl.pallas_call(
        lambda *refs: top_couplings_body(gain, *refs),
        out_shape=coupling_shape(picks.shape[1]),
        cost_estimate=COST,
        compiler_params=PARAMS,
        name="top_couplings",
    )(mine, theirs, picks)


def local(probes, points, leaf_skeleton, skeleton_one, skeleton_two, skeleton_three):
    span = probes.shape[1]
    row_count = lax.axis_size("row")
    col_count = lax.axis_size("col")
    gain = 16.0 / math.sqrt(4 * span * row_count * col_count)

    def swap(value, row_bits, col_bits):
        pairs = [
            (r * col_count + c, (r ^ row_bits) * col_count + (c ^ col_bits))
            for r in range(row_count)
            for c in range(col_count)
        ]
        return lax.ppermute(value, ("row", "col"), pairs)

    tables = (leaf_skeleton, skeleton_one, skeleton_two, skeleton_three)
    packed, own_points = pack(probes, points, tables)
    beside = swap(packed, 0, 1)
    across = swap(packed, 2, 0)
    line = col_count // 2
    line_points = [own_points] + [swap(own_points, 0, 2 * chunk) for chunk in range(1, line)]
    sibling_points = swap(jnp.concatenate(line_points, axis=1), 1, 0)
    near, far = range(2), range(2, line)
    feats, totals = first_product(
        packed,
        line_points,
        [[(chunk, 0) for chunk in group] for group in (near, far)],
        span,
        gain,
        True,
    )
    more = first_product(
        packed,
        [sibling_points],
        [[(0, chunk * span) for chunk in group] for group in (near, far)],
        span,
        gain,
        False,
    )
    feats, totals = [*feats, *more[0]], [*totals, *more[1]]
    beside, across, *totals = lax.optimization_barrier((beside, across, *totals))
    pieces = [packed, beside, across]
    relayed = halves(beside, across, 2 * (span + 16))
    diagonal = [swap(relayed[0], 2, 0), swap(relayed[1], 0, 1)]
    picks, couplings_one, couplings_two, points_two = skeletons(packed, beside, tables, span, gain)
    totals = product([beside], feats, totals, span)
    totals = product([across], feats, totals, span)
    points_two, *totals = lax.optimization_barrier((points_two, *totals))
    pieces += diagonal
    for bit in range(2, row_count.bit_length() - 1):
        more = [swap(value, 1 << bit, 0) for value in pieces]
        totals = product(more, feats, totals, span)
        pieces += more
    (theirs,) = product(diagonal, feats[3:], totals[3:], span)
    from_sibling = swap(theirs, 1, 0)
    (mine,) = product(diagonal, feats[1:2], totals[1:2], span)
    kept, sent = add_up(mine, from_sibling, range(0, line - 2, 2), range(1, line - 2, 2), span)
    sent, total = lax.optimization_barrier((sent, totals[2]))
    arrived = swap(sent, 0, 2)
    (theirs,) = product(diagonal, feats[2:3], [total], span)
    from_sibling = swap(theirs, 1, 0)
    (mine,) = product(diagonal, feats[:1], totals[:1], span)
    received = []
    beside_two = swap(points_two, 0, 2)
    chunks = list(range(2, line, 2))
    bit = 2
    while chunks:
        sent_places = [pos for pos, chunk in enumerate(chunks) if chunk & bit]
        kept_places = [pos for pos, chunk in enumerate(chunks) if not chunk & bit]
        kept, sent = add_up(
            kept, arrived, kept_places or sent_places, sent_places, span, (beside_two,), LONG
        )
        arrived = swap(sent, 0, 2 * bit)
        received.append(arrived[:span] if len(sent_places) > 1 else arrived)
        arrived = arrived[span:]
        chunks = [chunks[pos] for pos in kept_places]
        bit *= 2
    own_sum, near_sent = add_up(mine, from_sibling, [0], [1], span, (sent,))
    received.append(swap(near_sent, 0, 2))

    couplings_three = top_couplings(points_two, beside_two, picks, gain)
    leaf_interp, interp_one, state = leaves(
        own_sum, received, packed, picks, couplings_one, couplings_three, leaf_skeleton.shape[0]
    )
    interp_two, state_two = level(2, state, swap(state, 0, 1), picks, couplings_two)
    upper_interp, top_state = level(
        3, state_two, swap(state_two, 0, 2), picks, couplings_three, (interp_one, interp_two)
    )
    return jnp.swapaxes(leaf_interp, 1, 2), jnp.swapaxes(upper_interp, 2, 3), top_state


def solution(mesh):
    placed = (
        P(None, ("row", "col"), None),
        P(None, None, ("row", "col")),
        P(("row", "col"), None),
        P(("row", "col"), None),
        P("row", None),
        P("row", None),
    )
    return jax.shard_map(
        local,
        mesh=mesh,
        in_specs=placed,
        out_specs=(
            P(("row", "col"), None, None),
            P(None, ("row", "col"), None, None),
            P(None, ("row", "col"), None, None),
        ),
        check_vma=False,
    )
```

```python
import math

import jax
import jax.numpy as jnp
from jax import lax
from jax.experimental import pallas as pl
from jax.experimental.pallas import tpu as pltpu
from jax.sharding import PartitionSpec as P

LEAF = 128
F32 = jnp.float32
BF16 = jnp.bfloat16
DOUBLINGS = 9
VMEM = pl.BlockSpec(memory_space=pltpu.VMEM)


def vmem(shape, kind=F32):
    return pltpu.VMEM(tuple(shape), kind)


COST = pl.CostEstimate(flops=0, bytes_accessed=0, transcendentals=0)
LONG = pl.CostEstimate(flops=10**10, bytes_accessed=0, transcendentals=0)
PARAMS = pltpu.CompilerParams(vmem_limit_bytes=16 << 20)


def chebyshev_constants():
    taus = [1282.0 / 1280.0]
    for _ in range(DOUBLINGS):
        taus.append(2.0 * taus[-1] * taus[-1] - 1.0)
    front = 2.0**DOUBLINGS * math.prod(taus[:-1]) / taus[-1]
    return taus[:-1], front


TAUS, FRONT = chebyshev_constants()


def over(first, second, first_dim, second_dim):
    return lax.dot_general(
        first,
        second,
        (((first_dim,), (second_dim,)), ((), ())),
        preferred_element_type=F32,
    )


def split(value):
    high = value.astype(BF16)
    rest = value - high.astype(F32)
    middle = rest.astype(BF16)
    return high, middle, (rest - middle.astype(F32)).astype(BF16)


def norm_rows(norm, first, width):
    parts = [part.astype(F32) for part in split(norm)]
    place = lax.broadcasted_iota(jnp.int32, (16, width), 0)
    extra = jnp.where(place < 6, 1.0, 0.0)
    for pos in range(3):
        extra = jnp.where(place == pos + first, parts[pos], extra)
    return extra


def row_features(feats, gain):
    feats = feats.astype(F32)
    depth, width = feats.shape
    unit = math.log2(math.e) / (2.0 * depth)
    norm = jnp.sum(feats * feats, axis=0, keepdims=True) * -unit + math.log2(gain)
    parts = [part.astype(F32) for part in split(feats * (2.0 * unit))]
    return jnp.concatenate([*parts, norm_rows(norm, 0, width)], axis=0)


def col_features(feats):
    feats = feats.astype(F32)
    depth, width = feats.shape
    unit = math.log2(math.e) / (2.0 * depth)
    norm = jnp.sum(feats * feats, axis=0, keepdims=True) * -unit
    return jnp.concatenate([feats, feats, feats, norm_rows(norm, 3, width)], axis=0).astype(BF16)


def pack_body(*refs):
    probes_ref, points_ref, *table_refs = refs[:6]
    packed_ref, own_ref, held_ref, feats_ref, rows_ref, *held_tables, sem = refs[6:]
    quarters, span, _ = probes_ref.shape
    half = quarters // 2
    rows = half * (span + 16)
    pairs = [(points_ref, held_ref), *zip(table_refs, held_tables)]
    small = len(pairs)
    for quarter in range(quarters):
        start = quarter // half * rows + quarter % half * span
        pairs.append((probes_ref.at[quarter], packed_ref.at[pl.ds(start, span)]))
    copies = [
        pltpu.make_async_copy(source, target, sem.at[pos])
        for pos, (source, target) in enumerate(pairs)
    ]
    for copy in copies:
        copy.start()
    rows_ref[...] = jnp.zeros_like(rows_ref)
    for copy in copies[:small]:
        copy.wait()
    points = held_ref[...].astype(F32)
    for quarter in range(quarters):
        feats = points[:, quarter, :].astype(BF16)
        start = quarter // half * rows + half * span + quarter % half * 16
        packed_ref[pl.ds(start, 16), :] = feats
        if quarter == 0:
            feats_ref[...] = feats
            copies.append(pltpu.make_async_copy(feats_ref, own_ref, sem.at[len(copies)]))
            copies[-1].start()
    start = 0
    for table in held_tables:
        count, rank = table.shape
        rows_ref[pl.ds(start, count), pl.ds(0, rank)] = table[...].astype(F32)
        start += count
    packed_ref[pl.ds(2 * rows, rows_ref.shape[0]), :] = rows_ref[...].astype(BF16)
    for copy in copies[small:]:
        copy.wait()


def pack(probes, points, tables):
    quarters, span, samples = probes.shape
    table_rows = -(-sum(table.shape[0] for table in tables) // 16) * 16
    inputs = (probes, points, *tables)
    return pl.pallas_call(
        pack_body,
        out_shape=(
            vmem((quarters * (span + 16) + table_rows, samples), BF16),
            pltpu.HBM((16, span), BF16),
        ),
        in_specs=[pl.BlockSpec(memory_space=pltpu.HBM)] * len(inputs),
        out_specs=(VMEM, pl.BlockSpec(memory_space=pltpu.HBM)),
        scratch_shapes=[
            pltpu.VMEM(points.shape, BF16),
            pltpu.VMEM((16, span), BF16),
            pltpu.VMEM((table_rows, samples), F32),
            *[pltpu.VMEM(table.shape, jnp.int32) for table in tables],
            pltpu.SemaphoreType.DMA((quarters + 2 + len(tables),)),
        ],
        cost_estimate=COST,
        compiler_params=PARAMS,
        name="pack",
    )(*(pltpu.with_memory_space_constraint(value, pltpu.HBM) for value in inputs))


def masked(entries):
    shape = entries.shape
    row_leaf = lax.broadcasted_iota(jnp.int32, shape, 0) // LEAF
    col_leaf = lax.broadcasted_iota(jnp.int32, shape, 1) // LEAF
    return jnp.where(row_leaf == col_leaf, 0.0, entries)


def add_source(source_ref, row_refs, cols_ref, put, span, own):
    size = 2 * (span + 16)
    parts = range(0, source_ref.shape[0] // size * size, size)
    for number, part in enumerate(parts):
        for quarter in range(2):
            feats = source_ref[pl.ds(part + 2 * span + 16 * quarter, 16), :]
            cols_ref[:, pl.ds((2 * number + quarter) * span, span)] = col_features(feats)
    columns = 2 * span * len(parts)
    for group, rows_ref in enumerate(row_refs):
        for start in range(0, rows_ref.shape[0], span):
            feats = rows_ref[pl.ds(start, span), :]
            entries = jnp.exp2(over(feats, cols_ref[:, :columns], 1, 0))
            if own and group == 0 and start == 0:
                entries = jnp.concatenate([masked(entries[:, :span]), entries[:, span:]], axis=1)
            randoms = [source_ref[pl.ds(part, 2 * span), :] for part in parts]
            put(group, start, over(entries.astype(BF16), jnp.concatenate(randoms, axis=0), 1, 0))


def flipped(value, bits):
    for bit in range(bits.bit_length()):
        if bits >> bit & 1:
            value = value + (1 << bit) * (1 - 2 * (value // (1 << bit) % 2))
    return value


def first_product_body(gain, span, groups, col_count, source_ref, points_ref, *refs):
    row_refs, total_refs = refs[: len(groups)], refs[len(groups) : 2 * len(groups)]
    cols_ref, held_ref, sem = refs[2 * len(groups) :]
    owners = [owner for group in groups for owner in group]
    copies = []
    for pos, (row_bits, col_bits) in enumerate(owners):
        owner = flipped(lax.axis_index("row"), row_bits) * col_count
        owner = owner + flipped(lax.axis_index("col"), col_bits)
        place = points_ref.at[pl.ds(pl.multiple_of(owner * 16, 16), 16)]
        copies.append(pltpu.make_async_copy(place, held_ref.at[pos], sem.at[pos]))
        copies[-1].start()
    for copy in copies:
        copy.wait()
    pos = 0
    for rows_ref, group in zip(row_refs, groups):
        for place in range(len(group)):
            feats = row_features(held_ref[pos], gain)
            rows_ref[pl.ds(place * span, span), :] = feats.T.astype(BF16)
            pos += 1

    def put(group, start, value):
        total_refs[group][pl.ds(start, span), :] = value

    add_source(source_ref, row_refs, cols_ref, put, span, True)


def first_product(source, points, groups, span, gain, col_count):
    samples = source.shape[1]
    rows = [len(group) * span for group in groups]
    count = sum(len(group) for group in groups)
    out = pl.pallas_call(
        lambda *refs: first_product_body(gain, span, groups, col_count, *refs),
        out_shape=[vmem((size, 64), BF16) for size in rows]
        + [vmem((size, samples), F32) for size in rows],
        in_specs=[VMEM, pl.BlockSpec(memory_space=pltpu.HBM)],
        scratch_shapes=[
            pltpu.VMEM((64, 4 * span), BF16),
            pltpu.VMEM((count, 16, span), BF16),
            pltpu.SemaphoreType.DMA((count,)),
        ],
        cost_estimate=COST,
        compiler_params=PARAMS,
        name="first_product",
    )(source, pltpu.with_memory_space_constraint(points, pltpu.HBM))
    return out[: len(groups)], out[len(groups) :]


def product_body(span, source_count, count, *refs):
    sources, refs = refs[:source_count], refs[source_count:]
    row_refs, old_refs, total_refs = refs[:count], refs[count : 2 * count], refs[2 * count : -1]
    cols_ref = refs[-1]
    for number, source in enumerate(sources):

        def put(group, start, value):
            place = pl.ds(start, span)
            base = old_refs if number == 0 else total_refs
            total_refs[group][place, :] = base[group][place, :] + value

        add_source(source, row_refs, cols_ref, put, span, False)


def product(sources, rows, totals, span):
    return pl.pallas_call(
        lambda *refs: product_body(span, len(sources), len(rows), *refs),
        out_shape=[vmem(total.shape, F32) for total in totals],
        scratch_shapes=[pltpu.VMEM((64, 4 * span), BF16)],
        cost_estimate=COST,
        compiler_params=PARAMS,
        name="product",
    )(*sources, *rows, *totals)


def halves_body(first_ref, second_ref, first_half, second_half):
    rows = first_half.shape[0]
    first_half[...] = first_ref[pl.ds(0, rows), :]
    second_half[...] = second_ref[pl.ds(rows, rows), :]


def halves(first, second, rows):
    return pl.pallas_call(
        halves_body,
        out_shape=[vmem((rows, first.shape[1]), BF16)] * 2,
        cost_estimate=COST,
        compiler_params=PARAMS,
        name="halves",
    )(first, second)


def add_up_body(span, kept, sent, mine_ref, theirs_ref, *refs):
    wanted = [chunks for chunks in (kept, sent) if chunks]
    for chunks, out_ref in zip(wanted, refs[-len(wanted) :]):
        for pos, chunk in enumerate(chunks):
            place = pl.ds(chunk * span, span)
            value = mine_ref[place, :] + theirs_ref[place, :].astype(F32)
            out_ref[pl.ds(pos * span, span), :] = value.astype(out_ref.dtype)


def add_up(mine, theirs, kept, sent, span, after=(), cost=COST):
    samples = mine.shape[1]
    out = pl.pallas_call(
        lambda *refs: add_up_body(span, kept, sent, *refs),
        out_shape=[
            vmem((len(chunks) * span, samples), kind)
            for chunks, kind in ((kept, F32), (sent, BF16))
            if chunks
        ],
        cost_estimate=cost,
        compiler_params=PARAMS,
        name="add_up",
    )(mine, theirs, *after)
    return out if kept else (None, *out)


def wide_product(first, second, second_dim):
    high, middle, low = split(first)
    other_high, other_middle, other_low = split(second)
    return over(
        jnp.concatenate([high, high, middle, middle, low, high], axis=1),
        jnp.concatenate(
            [other_high, other_middle, other_high, other_middle, other_high, other_low],
            axis=second_dim,
        ),
        1,
        second_dim,
    )


def exact_product(first, second):
    second = second.astype(BF16)
    return over(
        jnp.concatenate(split(first), axis=1), jnp.concatenate([second] * 3, axis=0), 1, 0
    )


def twice_product(twice_parts, parts):
    high, middle, low = twice_parts
    other_high, other_middle, other_low = parts
    left = lax.broadcasted_iota(jnp.int32, high.shape, 1) < high.shape[1] // 2
    last = jnp.where(left, low.astype(F32), high.astype(F32)).astype(BF16)
    return over(
        jnp.concatenate([high, middle, last], axis=1),
        jnp.concatenate(
            [other_high, other_middle, other_high, other_middle, other_high, other_low], axis=0
        ),
        1,
        0,
    )


def select_rows(picks, value):
    return over(
        jnp.concatenate([picks] * 3, axis=1), jnp.concatenate(split(value), axis=0), 1, 0
    )


def interpolate(stacks, skeletons):
    rank, pool = skeletons[0].shape[0], stacks[0].shape[0]
    place = lax.broadcasted_iota(jnp.int32, (rank, 2 * rank), 0)
    other = lax.broadcasted_iota(jnp.int32, (rank, 2 * rank), 1)
    eyes = jnp.where((other == place) | (other == place + rank), 1.0, 0.0)
    states = []
    for skeleton, stack in zip(skeletons, stacks):
        products = wide_product(skeleton, jnp.concatenate([stack, skeleton, skeleton], axis=0), 1)
        ridge = 0.05 * jnp.sum(skeleton * skeleton, keepdims=True) / rank + 1e-05
        inverse = 1.0 / (640.0 * ridge)
        states.append((products[:, :pool], eyes - products[:, pool:] * inverse, inverse))
    for number, tau in enumerate(TAUS):
        last = number == DOUBLINGS - 1
        later = []
        for solved, power, inverse in states:
            power_parts = split(power)
            parts = split(solved)
            if not last:
                parts = [jnp.concatenate(pair, axis=1) for pair in zip(parts, power_parts)]
            both = twice_product(power_parts, parts)
            solved = solved + both[:, :pool] * (1.0 / tau)
            later.append((solved, None if last else 2.0 * both[:, pool:] - eyes, inverse))
        states = later
    return [solved * (inverse * FRONT) for solved, _, inverse in states]


def merge(samples, reduced, coupling, picks, early=None):
    pool = samples.shape[0]
    high, middle, low = split(reduced)
    coupled = over(
        coupling, jnp.concatenate([high, middle, high, middle, high, low], axis=0), 1, 0
    )
    stacked = samples - coupled[:pool]
    skeleton = select_rows(picks, samples) - coupled[pool:]
    if early is not None:
        early(skeleton)
    (interp,) = interpolate([stacked], [skeleton])
    return interp, skeleton, wide_product(interp, reduced, 0)


def leaves_body(received, *refs):
    own_ref, *others = refs[: received + 1]
    source_ref, picks_ref, couplings_ref = refs[received + 1 : received + 4]
    leaf_ref, upper_ref, state_ref, held_ref, sem = refs[-5:]
    rank = picks_ref.shape[1]
    total = own_ref[...]
    for other in others:
        total = total + other[...].astype(F32)
    count = total.shape[0] // LEAF
    stacks = [total[leaf * LEAF : (leaf + 1) * LEAF] for leaf in range(count)]
    skeletons = [select_rows(picks_ref[leaf], stack) for leaf, stack in enumerate(stacks)]
    reduced = []
    for leaf, interp in enumerate(interpolate(stacks, skeletons)):
        held_ref[leaf] = interp
        reduced.append(exact_product(interp, source_ref[pl.ds(leaf * LEAF, LEAF), :]))
    copy = pltpu.make_async_copy(held_ref, leaf_ref, sem)
    copy.start()
    interp, skeleton, reduced = merge(
        jnp.concatenate(skeletons, axis=0),
        jnp.concatenate(reduced, axis=0),
        couplings_ref[...],
        picks_ref[count],
    )
    upper_ref[...] = interp
    state_ref[pl.ds(0, rank), :] = skeleton
    state_ref[pl.ds(rank, rank), :] = reduced
    copy.wait()


def leaves(own, others, source, picks, couplings, later, leaf_count):
    samples = own.shape[1]
    rank, pool = picks.shape[1:]
    return pl.pallas_call(
        lambda *refs: leaves_body(len(others), *refs),
        out_shape=(
            jax.ShapeDtypeStruct((leaf_count, rank, LEAF), F32),
            vmem((rank, pool), F32),
            vmem((2 * rank, samples), F32),
        ),
        out_specs=(pl.BlockSpec(memory_space=pl.ANY), VMEM, VMEM),
        scratch_shapes=[pltpu.VMEM((leaf_count, rank, LEAF), F32), pltpu.SemaphoreType.DMA],
        cost_estimate=COST,
        compiler_params=PARAMS,
        name="leaves",
    )(own, *others, source, picks, couplings, later)


def first_of_pair(number):
    return (lax.axis_index("col") >> (number - 2)) % 2 == 0


def level_body(number, mine_ref, theirs_ref, picks_ref, couplings_ref, *refs):
    rank = picks_ref.shape[1]
    if number == 2:
        upper_ref, state_ref = refs
    else:
        one_ref, two_ref, upper_out, top_out, upper_ref, state_ref, sem = refs
        places = [
            (one_ref, upper_out.at[0, 0]),
            (two_ref, upper_out.at[1, 0]),
            (state_ref.at[pl.ds(0, rank)], top_out.at[0, 0]),
            (state_ref.at[pl.ds(rank, rank)], top_out.at[1, 0]),
            (upper_ref, upper_out.at[2, 0]),
        ]
        copies = [
            pltpu.make_async_copy(source, target, sem.at[pos])
            for pos, (source, target) in enumerate(places)
        ]
        copies[0].start()
        copies[1].start()

    def early(skeleton):
        state_ref[pl.ds(0, rank), :] = skeleton
        if number > 2:
            copies[2].start()

    mine_first = first_of_pair(number)
    mine, theirs = mine_ref[...], theirs_ref[...]
    first = jnp.where(mine_first, mine, theirs)
    second = jnp.where(mine_first, theirs, mine)
    interp, _, reduced = merge(
        jnp.concatenate([first[:rank], second[:rank]], axis=0),
        jnp.concatenate([first[rank:], second[rank:]], axis=0),
        couplings_ref[...],
        picks_ref[picks_ref.shape[0] + number - 4],
        early,
    )
    upper_ref[...] = interp
    state_ref[pl.ds(rank, rank), :] = reduced
    if number > 2:
        copies[3].start()
        copies[4].start()
        for copy in copies:
            copy.wait()


def level(number, mine, theirs, picks, couplings, below=()):
    rank, pool = picks.shape[1:]
    samples = mine.shape[1]
    out_shape = (
        vmem((rank, pool), F32),
        vmem(mine.shape, F32),
    )
    out_specs = (VMEM, VMEM)
    scratch = []
    if below:
        scratch = [pltpu.VMEM(out.shape, F32) for out in out_shape]
        scratch.append(pltpu.SemaphoreType.DMA((5,)))
        out_shape = (
            jax.ShapeDtypeStruct((3, 1, rank, pool), F32),
            jax.ShapeDtypeStruct((2, 1, rank, samples), F32),
        )
        out_specs = (pl.BlockSpec(memory_space=pl.ANY),) * 2
    return pl.pallas_call(
        lambda *refs: level_body(number, *refs),
        out_shape=out_shape,
        in_specs=[VMEM] * (4 + len(below)),
        out_specs=out_specs,
        scratch_shapes=scratch,
        cost_estimate=COST,
        compiler_params=PARAMS,
        name="level",
    )(mine, theirs, picks, couplings, *below)


def one_hot(chosen, pool):
    place = lax.broadcasted_iota(jnp.int32, (pool, chosen.shape[1]), 0)
    return jnp.where(place.astype(F32) == chosen, 1.0, 0.0).astype(F32)


def couple(first, second, picks, gain, couplings_ref):
    rank = first.shape[1]
    points = jnp.concatenate([first, second], axis=1)
    entries = jnp.exp2(over(row_features(points, gain).astype(BF16), col_features(points), 0, 0))
    left = lax.broadcasted_iota(jnp.int32, entries.shape, 1) < rank
    upper = lax.broadcasted_iota(jnp.int32, entries.shape, 0) < rank
    entries = jnp.where(left == upper, 0.0, entries)
    chosen = select_rows(picks.T.astype(BF16), entries)
    high, middle, low = split(jnp.concatenate([entries, chosen], axis=0))
    couplings_ref[...] = jnp.concatenate([high, high, middle, middle, low, high], axis=1)


def coupling_shape(rank):
    return vmem((3 * rank, 12 * rank), BF16)


def skeletons_body(gain, span, counts, mine_ref, beside_ref, *refs):
    picks_ref, one_ref, two_ref, points_ref = refs
    rank, pool = picks_ref.shape[1:]
    leaf_count = counts[0]
    tables = 4 * (span + 16)
    nodes = []
    for source_ref in (mine_ref, beside_ref):
        rows = source_ref[pl.ds(tables, source_ref.shape[0] - tables), :rank].astype(F32)
        hots = [one_hot(rows[pos : pos + 1], pool) for pos in range(leaf_count + 1)]
        children = []
        for leaf in range(leaf_count):
            feats = source_ref[pl.ds(2 * span, 16), pl.ds(leaf * LEAF, LEAF)]
            children.append(over(feats, hots[leaf].astype(BF16), 1, 0))
        points = jnp.concatenate(children, axis=1)
        nodes.append(over(points, hots[leaf_count], 1, 0))
        if source_ref is mine_ref:
            couple(*children, hots[leaf_count], gain, one_ref)
            table, start = rows, leaf_count + counts[1]
            for number, count in enumerate(counts[2:]):
                wanted = start + (lax.axis_index("col") >> (number + 1))
                place = lax.broadcasted_iota(jnp.int32, table.shape, 0)
                row = jnp.sum(jnp.where(place == wanted, table, 0.0), axis=0, keepdims=True)
                hots.append(one_hot(row, pool))
                start += count
            for number, hot in enumerate(hots):
                picks_ref[number] = hot.T.astype(BF16)
            upper = hots[leaf_count + 1]
    mine, theirs = nodes
    mine_first = first_of_pair(2)
    first = jnp.where(mine_first, mine, theirs)
    second = jnp.where(mine_first, theirs, mine)
    couple(first, second, upper, gain, two_ref)
    points_ref[...] = over(jnp.concatenate([first, second], axis=1), upper, 1, 0).astype(BF16)


def skeletons(packed, beside, tables, span, gain):
    leaf_count, rank = tables[0].shape
    counts = [table.shape[0] for table in tables]
    return pl.pallas_call(
        lambda *refs: skeletons_body(gain, span, counts, *refs),
        out_shape=(
            vmem((leaf_count + 3, rank, LEAF), BF16),
            coupling_shape(rank),
            coupling_shape(rank),
            vmem((16, rank), BF16),
        ),
        cost_estimate=COST,
        compiler_params=PARAMS,
        name="skeletons",
    )(packed, beside)


def top_couplings_body(gain, mine_ref, theirs_ref, picks_ref, couplings_ref):
    mine_first = first_of_pair(3)
    mine, theirs = mine_ref[...].astype(F32), theirs_ref[...].astype(F32)
    first = jnp.where(mine_first, mine, theirs)
    second = jnp.where(mine_first, theirs, mine)
    picks = picks_ref[picks_ref.shape[0] - 1].astype(F32).T
    couple(first, second, picks, gain, couplings_ref)


def top_couplings(mine, theirs, picks, gain):
    return pl.pallas_call(
        lambda *refs: top_couplings_body(gain, *refs),
        out_shape=coupling_shape(picks.shape[1]),
        cost_estimate=COST,
        compiler_params=PARAMS,
        name="top_couplings",
    )(mine, theirs, picks)


def local(probes, points, leaf_skeleton, skeleton_one, skeleton_two, skeleton_three):
    span = probes.shape[1]
    row_count = lax.axis_size("row")
    col_count = lax.axis_size("col")
    gain = 16.0 / math.sqrt(4 * span * row_count * col_count)

    def swap(value, row_bits, col_bits):
        pairs = [
            (r * col_count + c, (r ^ row_bits) * col_count + (c ^ col_bits))
            for r in range(row_count)
            for c in range(col_count)
        ]
        return lax.ppermute(value, ("row", "col"), pairs)

    tables = (leaf_skeleton, skeleton_one, skeleton_two, skeleton_three)
    packed, own_points = pack(probes, points, tables)
    beside = swap(packed, 0, 1)
    across = swap(packed, 2, 0)
    all_points = lax.all_gather(own_points, ("row", "col"), axis=0, tiled=True)
    line = col_count // 2
    groups = [
        [(core, 2 * chunk) for chunk in chunks]
        for core in range(2)
        for chunks in (range(2), range(2, line))
    ]
    feats, totals = first_product(packed, all_points, groups, span, gain, col_count)
    beside, across, *totals = lax.optimization_barrier((beside, across, *totals))
    pieces = [packed, beside, across]
    relayed = halves(beside, across, 2 * (span + 16))
    diagonal = [swap(relayed[0], 2, 0), swap(relayed[1], 0, 1)]
    picks, couplings_one, couplings_two, points_two = skeletons(packed, beside, tables, span, gain)
    totals = product([beside], feats, totals, span)
    totals = product([across], feats, totals, span)
    points_two, *totals = lax.optimization_barrier((points_two, *totals))
    pieces += diagonal
    for bit in range(2, row_count.bit_length() - 1):
        more = [swap(value, 1 << bit, 0) for value in pieces]
        totals = product(more, feats, totals, span)
        pieces += more
    (theirs,) = product(diagonal, feats[3:], totals[3:], span)
    from_sibling = swap(theirs, 1, 0)
    (mine,) = product(diagonal, feats[1:2], totals[1:2], span)
    kept, sent = add_up(mine, from_sibling, range(0, line - 2, 2), range(1, line - 2, 2), span)
    sent, total = lax.optimization_barrier((sent, totals[2]))
    arrived = swap(sent, 0, 2)
    (theirs,) = product(diagonal, feats[2:3], [total], span)
    from_sibling = swap(theirs, 1, 0)
    (mine,) = product(diagonal, feats[:1], totals[:1], span)
    received = []
    beside_two = swap(points_two, 0, 2)
    chunks = list(range(2, line, 2))
    bit = 2
    while chunks:
        sent_places = [pos for pos, chunk in enumerate(chunks) if chunk & bit]
        kept_places = [pos for pos, chunk in enumerate(chunks) if not chunk & bit]
        kept, sent = add_up(
            kept, arrived, kept_places, sent_places, span, (beside_two,), LONG
        )
        arrived = swap(sent, 0, 2 * bit)
        received.append(arrived[:span] if len(sent_places) > 1 else arrived)
        arrived = arrived[span:]
        chunks = [chunks[pos] for pos in kept_places]
        bit *= 2
    own_sum, near_sent = add_up(mine, from_sibling, [0], [1], span, (sent,))
    received.append(swap(near_sent, 0, 2))

    couplings_three = top_couplings(points_two, beside_two, picks, gain)
    leaf_interp, interp_one, state = leaves(
        own_sum, received, packed, picks, couplings_one, couplings_three, leaf_skeleton.shape[0]
    )
    interp_two, state_two = level(2, state, swap(state, 0, 1), picks, couplings_two)
    upper_interp, top_state = level(
        3, state_two, swap(state_two, 0, 2), picks, couplings_three, (interp_one, interp_two)
    )
    return jnp.swapaxes(leaf_interp, 1, 2), jnp.swapaxes(upper_interp, 2, 3), top_state


def solution(mesh):
    placed = (
        P(None, ("row", "col"), None),
        P(None, None, ("row", "col")),
        P(("row", "col"), None),
        P(("row", "col"), None),
        P("row", None),
        P("row", None),
    )
    return jax.shard_map(
        local,
        mesh=mesh,
        in_specs=placed,
        out_specs=(
            P(("row", "col"), None, None),
            P(None, ("row", "col"), None, None),
            P(None, ("row", "col"), None, None),
        ),
        check_vma=False,
    )
```

```python
import math

import jax
import jax.numpy as jnp
from jax import lax
from jax.experimental import pallas as pl
from jax.experimental.pallas import tpu as pltpu
from jax.sharding import PartitionSpec as P

LEAF = 128
F32 = jnp.float32
BF16 = jnp.bfloat16
DOUBLINGS = 9
VMEM = pl.BlockSpec(memory_space=pltpu.VMEM)


def vmem(shape, kind=F32):
    return pltpu.VMEM(tuple(shape), kind)


COST = pl.CostEstimate(flops=0, bytes_accessed=0, transcendentals=0)
LONG = pl.CostEstimate(flops=10**10, bytes_accessed=0, transcendentals=0)
PARAMS = pltpu.CompilerParams(vmem_limit_bytes=16 << 20)


def chebyshev_constants():
    taus = [1282.0 / 1280.0]
    for _ in range(DOUBLINGS):
        taus.append(2.0 * taus[-1] * taus[-1] - 1.0)
    front = 2.0**DOUBLINGS * math.prod(taus[:-1]) / taus[-1]
    return taus[:-1], front


TAUS, FRONT = chebyshev_constants()


def over(first, second, first_dim, second_dim):
    return lax.dot_general(
        first,
        second,
        (((first_dim,), (second_dim,)), ((), ())),
        preferred_element_type=F32,
    )


def split(value):
    high = value.astype(BF16)
    rest = value - high.astype(F32)
    middle = rest.astype(BF16)
    return high, middle, (rest - middle.astype(F32)).astype(BF16)


def norm_rows(norm, first, width):
    parts = [part.astype(F32) for part in split(norm)]
    place = lax.broadcasted_iota(jnp.int32, (16, width), 0)
    extra = jnp.where(place < 6, 1.0, 0.0)
    for pos in range(3):
        extra = jnp.where(place == pos + first, parts[pos], extra)
    return extra


def row_features(feats, gain):
    feats = feats.astype(F32)
    depth, width = feats.shape
    unit = math.log2(math.e) / (2.0 * depth)
    norm = jnp.sum(feats * feats, axis=0, keepdims=True) * -unit + math.log2(gain)
    parts = [part.astype(F32) for part in split(feats * (2.0 * unit))]
    return jnp.concatenate([*parts, norm_rows(norm, 0, width)], axis=0)


def col_features(feats):
    feats = feats.astype(F32)
    depth, width = feats.shape
    unit = math.log2(math.e) / (2.0 * depth)
    norm = jnp.sum(feats * feats, axis=0, keepdims=True) * -unit
    return jnp.concatenate([feats, feats, feats, norm_rows(norm, 3, width)], axis=0).astype(BF16)


def pack_body(*refs):
    probes_ref, points_ref, *table_refs = refs[:6]
    packed_ref, own_ref, held_ref, rows_ref, *held_tables, sem = refs[6:]
    quarters, span, _ = probes_ref.shape
    half = quarters // 2
    rows = half * (span + 16)
    pairs = [(points_ref, held_ref), *zip(table_refs, held_tables)]
    small = len(pairs)
    for quarter in range(quarters):
        start = quarter // half * rows + quarter % half * span
        pairs.append((probes_ref.at[quarter], packed_ref.at[pl.ds(start, span)]))
    copies = [
        pltpu.make_async_copy(source, target, sem.at[pos])
        for pos, (source, target) in enumerate(pairs)
    ]
    for copy in copies:
        copy.start()
    rows_ref[...] = jnp.zeros_like(rows_ref)
    for copy in copies[:small]:
        copy.wait()
    points = held_ref[...].astype(F32)
    for quarter in range(quarters):
        feats = points[:, quarter, :].astype(BF16)
        start = quarter // half * rows + half * span + quarter % half * 16
        packed_ref[pl.ds(start, 16), :] = feats
        if quarter == 0:
            own_ref[...] = feats
    start = 0
    for table in held_tables:
        count, rank = table.shape
        rows_ref[pl.ds(start, count), pl.ds(0, rank)] = table[...].astype(F32)
        start += count
    packed_ref[pl.ds(2 * rows, rows_ref.shape[0]), :] = rows_ref[...].astype(BF16)
    for copy in copies[small:]:
        copy.wait()


def pack(probes, points, tables):
    quarters, span, samples = probes.shape
    table_rows = -(-sum(table.shape[0] for table in tables) // 16) * 16
    inputs = (probes, points, *tables)
    return pl.pallas_call(
        pack_body,
        out_shape=(
            vmem((quarters * (span + 16) + table_rows, samples), BF16),
            vmem((16, span), BF16),
        ),
        in_specs=[pl.BlockSpec(memory_space=pltpu.HBM)] * len(inputs),
        scratch_shapes=[
            pltpu.VMEM(points.shape, BF16),
            pltpu.VMEM((table_rows, samples), F32),
            *[pltpu.VMEM(table.shape, jnp.int32) for table in tables],
            pltpu.SemaphoreType.DMA((quarters + 1 + len(tables),)),
        ],
        cost_estimate=COST,
        compiler_params=PARAMS,
        name="pack",
    )(*(pltpu.with_memory_space_constraint(value, pltpu.HBM) for value in inputs))


def masked(entries):
    shape = entries.shape
    row_leaf = lax.broadcasted_iota(jnp.int32, shape, 0) // LEAF
    col_leaf = lax.broadcasted_iota(jnp.int32, shape, 1) // LEAF
    return jnp.where(row_leaf == col_leaf, 0.0, entries)


def add_source(source_ref, row_refs, cols_ref, put, span, own):
    size = 2 * (span + 16)
    parts = range(0, source_ref.shape[0] // size * size, size)
    for number, part in enumerate(parts):
        for quarter in range(2):
            feats = source_ref[pl.ds(part + 2 * span + 16 * quarter, 16), :]
            cols_ref[:, pl.ds((2 * number + quarter) * span, span)] = col_features(feats)
    columns = 2 * span * len(parts)
    for group, rows_ref in enumerate(row_refs):
        for start in range(0, rows_ref.shape[0], span):
            feats = rows_ref[pl.ds(start, span), :]
            entries = jnp.exp2(over(feats, cols_ref[:, :columns], 1, 0))
            if own and group == 0 and start == 0:
                entries = jnp.concatenate([masked(entries[:, :span]), entries[:, span:]], axis=1)
            randoms = [source_ref[pl.ds(part, 2 * span), :] for part in parts]
            put(group, start, over(entries.astype(BF16), jnp.concatenate(randoms, axis=0), 1, 0))


def first_product_body(gain, span, own, groups, point_count, *refs):
    source_ref, *point_refs = refs[: point_count + 1]
    row_refs = refs[point_count + 1 : point_count + 1 + len(groups)]
    total_refs, cols_ref = refs[point_count + 1 + len(groups) : -1], refs[-1]
    for rows_ref, places in zip(row_refs, groups):
        for pos, (array, start) in enumerate(places):
            feats = point_refs[array][:, pl.ds(start, span)]
            rows_ref[pl.ds(pos * span, span), :] = row_features(feats, gain).T.astype(BF16)

    def put(group, start, value):
        total_refs[group][pl.ds(start, span), :] = value

    add_source(source_ref, row_refs, cols_ref, put, span, own)


def first_product(source, points, groups, span, gain, own):
    samples = source.shape[1]
    rows = [len(places) * span for places in groups]
    out = pl.pallas_call(
        lambda *refs: first_product_body(gain, span, own, groups, len(points), *refs),
        out_shape=[vmem((count, 64), BF16) for count in rows]
        + [vmem((count, samples), F32) for count in rows],
        scratch_shapes=[pltpu.VMEM((64, 4 * span), BF16)],
        cost_estimate=COST,
        compiler_params=PARAMS,
        name="first_product",
    )(source, *points)
    return out[: len(groups)], out[len(groups) :]


def product_body(span, source_count, count, *refs):
    sources, refs = refs[:source_count], refs[source_count:]
    row_refs, old_refs, total_refs = refs[:count], refs[count : 2 * count], refs[2 * count : -1]
    cols_ref = refs[-1]
    for number, source in enumerate(sources):

        def put(group, start, value):
            place = pl.ds(start, span)
            base = old_refs if number == 0 else total_refs
            total_refs[group][place, :] = base[group][place, :] + value

        add_source(source, row_refs, cols_ref, put, span, False)


def product(sources, rows, totals, span):
    return pl.pallas_call(
        lambda *refs: product_body(span, len(sources), len(rows), *refs),
        out_shape=[vmem(total.shape, F32) for total in totals],
        scratch_shapes=[pltpu.VMEM((64, 4 * span), BF16)],
        cost_estimate=COST,
        compiler_params=PARAMS,
        name="product",
    )(*sources, *rows, *totals)


def halves_body(first_ref, second_ref, first_half, second_half):
    rows = first_half.shape[0]
    first_half[...] = first_ref[pl.ds(0, rows), :]
    second_half[...] = second_ref[pl.ds(rows, rows), :]


def halves(first, second, rows):
    return pl.pallas_call(
        halves_body,
        out_shape=[vmem((rows, first.shape[1]), BF16)] * 2,
        cost_estimate=COST,
        compiler_params=PARAMS,
        name="halves",
    )(first, second)


def add_up_body(span, outs, mine_ref, theirs_ref, *refs):
    for (chunks, _), out_ref in zip(outs, refs[-len(outs) :]):
        for pos, chunk in enumerate(chunks):
            place = pl.ds(chunk * span, span)
            value = mine_ref[place, :] + theirs_ref[place, :].astype(F32)
            out_ref[pl.ds(pos * span, span), :] = value.astype(out_ref.dtype)


def add_up(mine, theirs, outs, span, after=(), cost=COST):
    samples = mine.shape[1]
    return pl.pallas_call(
        lambda *refs: add_up_body(span, outs, *refs),
        out_shape=[vmem((len(chunks) * span, samples), kind) for chunks, kind in outs],
        cost_estimate=cost,
        compiler_params=PARAMS,
        name="add_up",
    )(mine, theirs, *after)


def wide_product(first, second, second_dim):
    high, middle, low = split(first)
    other_high, other_middle, other_low = split(second)
    return over(
        jnp.concatenate([high, high, middle, middle, low, high], axis=1),
        jnp.concatenate(
            [other_high, other_middle, other_high, other_middle, other_high, other_low],
            axis=second_dim,
        ),
        1,
        second_dim,
    )


def exact_product(first, second):
    second = second.astype(BF16)
    return over(
        jnp.concatenate(split(first), axis=1), jnp.concatenate([second] * 3, axis=0), 1, 0
    )


def twice_product(twice_parts, parts):
    high, middle, low = twice_parts
    other_high, other_middle, other_low = parts
    left = lax.broadcasted_iota(jnp.int32, high.shape, 1) < high.shape[1] // 2
    last = jnp.where(left, low.astype(F32), high.astype(F32)).astype(BF16)
    return over(
        jnp.concatenate([high, middle, last], axis=1),
        jnp.concatenate(
            [other_high, other_middle, other_high, other_middle, other_high, other_low], axis=0
        ),
        1,
        0,
    )


def select_rows(picks, value):
    return over(
        jnp.concatenate([picks] * 3, axis=1), jnp.concatenate(split(value), axis=0), 1, 0
    )


def interpolate(stacks, skeletons):
    rank, pool = skeletons[0].shape[0], stacks[0].shape[0]
    place = lax.broadcasted_iota(jnp.int32, (rank, 2 * rank), 0)
    other = lax.broadcasted_iota(jnp.int32, (rank, 2 * rank), 1)
    eyes = jnp.where((other == place) | (other == place + rank), 1.0, 0.0)
    states = []
    for skeleton, stack in zip(skeletons, stacks):
        products = wide_product(skeleton, jnp.concatenate([stack, skeleton, skeleton], axis=0), 1)
        ridge = 0.05 * jnp.sum(skeleton * skeleton, keepdims=True) / rank + 1e-05
        inverse = 1.0 / (640.0 * ridge)
        states.append((products[:, :pool], eyes - products[:, pool:] * inverse, inverse))
    for number, tau in enumerate(TAUS):
        last = number == DOUBLINGS - 1
        later = []
        for solved, power, inverse in states:
            power_parts = split(power)
            parts = split(solved)
            if not last:
                parts = [jnp.concatenate(pair, axis=1) for pair in zip(parts, power_parts)]
            both = twice_product(power_parts, parts)
            solved = solved + both[:, :pool] * (1.0 / tau)
            later.append((solved, None if last else 2.0 * both[:, pool:] - eyes, inverse))
        states = later
    return [solved * (inverse * FRONT) for solved, _, inverse in states]


def merge(nodes, early=None):
    stacks, skeletons = [], []
    for samples, reduced, coupling, picks in nodes:
        pool = samples.shape[0]
        high, middle, low = split(reduced)
        coupled = over(
            coupling, jnp.concatenate([high, middle, high, middle, high, low], axis=0), 1, 0
        )
        stacks.append(samples - coupled[:pool])
        skeletons.append(select_rows(picks, samples) - coupled[pool:])
    if early is not None:
        early(skeletons[0])
    interps = interpolate(stacks, skeletons)
    return [
        (interp, skeleton, wide_product(interp, node[1], 0))
        for interp, skeleton, node in zip(interps, skeletons, nodes)
    ]


def leaves_body(received, *refs):
    own_ref, *others = refs[: received + 1]
    source_ref, picks_ref, couplings_ref = refs[received + 1 : received + 4]
    leaf_ref, upper_ref, skeleton_ref, reduced_ref, sent_ref, held_ref, sem = refs[-7:]
    total = own_ref[...]
    for other in others:
        total = total + other[...].astype(F32)
    count = total.shape[0] // LEAF
    stacks = [total[leaf * LEAF : (leaf + 1) * LEAF] for leaf in range(count)]
    skeletons = [select_rows(picks_ref[leaf], stack) for leaf, stack in enumerate(stacks)]
    reduced = []
    for leaf, interp in enumerate(interpolate(stacks, skeletons)):
        held_ref[leaf] = interp
        reduced.append(exact_product(interp, source_ref[pl.ds(leaf * LEAF, LEAF), :]))
    copy = pltpu.make_async_copy(held_ref, leaf_ref, sem)
    copy.start()
    node = (
        jnp.concatenate(skeletons, axis=0),
        jnp.concatenate(reduced, axis=0),
        couplings_ref[...],
        picks_ref[count],
    )
    ((interp, skeleton, reduced),) = merge([node])
    upper_ref[...] = interp
    skeleton_ref[...] = skeleton
    reduced_ref[...] = reduced
    for pos, part in enumerate((*split(skeleton)[:2], reduced.astype(BF16))):
        sent_ref[pl.ds(pos * skeleton.shape[0], skeleton.shape[0]), :] = part
    copy.wait()


def leaves(own, others, source, picks, couplings, later, leaf_count):
    samples = own.shape[1]
    rank, pool = picks.shape[1:]
    return pl.pallas_call(
        lambda *refs: leaves_body(len(others), *refs),
        out_shape=(
            jax.ShapeDtypeStruct((leaf_count, rank, LEAF), F32),
            vmem((rank, pool), F32),
            vmem((rank, samples), F32),
            vmem((rank, samples), F32),
            vmem((3 * rank, samples), BF16),
        ),
        out_specs=(pl.BlockSpec(memory_space=pl.ANY), VMEM, VMEM, VMEM, VMEM),
        scratch_shapes=[pltpu.VMEM((leaf_count, rank, LEAF), F32), pltpu.SemaphoreType.DMA],
        cost_estimate=COST,
        compiler_params=PARAMS,
        name="leaves",
    )(own, *others, source, picks, couplings, *later)


def first_of_pair(number):
    return (lax.axis_index("col") >> (number - 2)) % 2 == 0


def pair(mine, theirs, mine_first):
    first = jnp.where(mine_first, mine, theirs)
    second = jnp.where(mine_first, theirs, mine)
    return jnp.concatenate([first, second], axis=0)


def upper_body(picks_count, *refs):
    states = [(refs[0][...], refs[1][...])]
    rank = refs[0].shape[0]
    for got_ref in refs[2:5]:
        high, middle, reduced = (got_ref[pl.ds(pos * rank, rank), :] for pos in range(3))
        states.append((high.astype(F32) + middle.astype(F32), reduced.astype(F32)))
    picks_ref, two_ref, other_ref, three_ref, one_ref, upper_out, top_out = refs[5:12]
    upper_ref, state_ref, sem = refs[12:]
    places = [
        (one_ref, upper_out.at[0, 0]),
        (upper_ref.at[0], upper_out.at[1, 0]),
        (upper_ref.at[1], upper_out.at[2, 0]),
        (state_ref.at[0], top_out.at[0, 0]),
        (state_ref.at[1], top_out.at[1, 0]),
    ]
    copies = [
        pltpu.make_async_copy(source, target, sem.at[pos])
        for pos, (source, target) in enumerate(places)
    ]
    copies[0].start()
    mine_first = first_of_pair(2)
    nodes = []
    for number, coupling_ref in enumerate((two_ref, other_ref)):
        mine, theirs = states[2 * number : 2 * number + 2]
        picks = picks_ref[picks_count - 3 + number]
        stacks = [pair(*parts, mine_first) for parts in zip(mine, theirs)]
        nodes.append((*stacks, coupling_ref[...], picks))
    mine, theirs = merge(nodes)
    upper_ref[0] = mine[0]
    copies[1].start()

    def early(skeleton):
        state_ref[0] = skeleton
        copies[3].start()

    mine_first = first_of_pair(3)
    stacks = [pair(*parts, mine_first) for parts in zip(mine[1:], theirs[1:])]
    ((interp, _, reduced),) = merge([(*stacks, three_ref[...], picks_ref[picks_count - 1])], early)
    upper_ref[1] = interp
    copies[2].start()
    state_ref[1] = reduced
    copies[4].start()
    for copy in copies:
        copy.wait()


def upper_levels(skeleton, reduced, got, picks, couplings, interp_one):
    rank, pool = picks.shape[1:]
    samples = skeleton.shape[1]
    return pl.pallas_call(
        lambda *refs: upper_body(picks.shape[0], *refs),
        out_shape=(
            jax.ShapeDtypeStruct((3, 1, rank, pool), F32),
            jax.ShapeDtypeStruct((2, 1, rank, samples), F32),
        ),
        out_specs=(pl.BlockSpec(memory_space=pl.ANY),) * 2,
        scratch_shapes=[
            pltpu.VMEM((2, rank, pool), F32),
            pltpu.VMEM((2, rank, samples), F32),
            pltpu.SemaphoreType.DMA((5,)),
        ],
        cost_estimate=COST,
        compiler_params=PARAMS,
        name="upper_levels",
    )(skeleton, reduced, *got, picks, *couplings, interp_one)


def one_hot(chosen, pool):
    place = lax.broadcasted_iota(jnp.int32, (pool, chosen.shape[1]), 0)
    return jnp.where(place.astype(F32) == chosen, 1.0, 0.0).astype(F32)


def couple(first, second, picks, gain, couplings_ref):
    rank = first.shape[1]
    points = jnp.concatenate([first, second], axis=1)
    entries = jnp.exp2(over(row_features(points, gain).astype(BF16), col_features(points), 0, 0))
    left = lax.broadcasted_iota(jnp.int32, entries.shape, 1) < rank
    upper = lax.broadcasted_iota(jnp.int32, entries.shape, 0) < rank
    entries = jnp.where(left == upper, 0.0, entries)
    chosen = select_rows(picks.T.astype(BF16), entries)
    high, middle, low = split(jnp.concatenate([entries, chosen], axis=0))
    couplings_ref[...] = jnp.concatenate([high, high, middle, middle, low, high], axis=1)


def coupling_shape(rank):
    return vmem((3 * rank, 12 * rank), BF16)


def skeletons_body(gain, span, counts, mine_ref, beside_ref, *refs):
    picks_ref, one_ref, two_ref, points_ref = refs
    rank, pool = picks_ref.shape[1:]
    leaf_count = counts[0]
    tables = 4 * (span + 16)
    nodes = []
    for source_ref in (mine_ref, beside_ref):
        rows = source_ref[pl.ds(tables, source_ref.shape[0] - tables), :rank].astype(F32)
        hots = [one_hot(rows[pos : pos + 1], pool) for pos in range(leaf_count + 1)]
        children = []
        for leaf in range(leaf_count):
            feats = source_ref[pl.ds(2 * span, 16), pl.ds(leaf * LEAF, LEAF)]
            children.append(over(feats, hots[leaf].astype(BF16), 1, 0))
        points = jnp.concatenate(children, axis=1)
        nodes.append(over(points, hots[leaf_count], 1, 0))
        if source_ref is mine_ref:
            couple(*children, hots[leaf_count], gain, one_ref)
            start = leaf_count + counts[1]
            level_two = lax.axis_index("col") // 2
            wanted = [level_two, level_two + 1 - 2 * (level_two % 2), counts[2] + level_two // 2]
            for row in wanted:
                place = lax.broadcasted_iota(jnp.int32, rows.shape, 0)
                named = jnp.where(place == start + row, rows, 0.0)
                hots.append(one_hot(jnp.sum(named, axis=0, keepdims=True), pool))
            for number, hot in enumerate(hots):
                picks_ref[number] = hot.T.astype(BF16)
            upper = hots[leaf_count + 1]
    mine, theirs = nodes
    mine_first = first_of_pair(2)
    first = jnp.where(mine_first, mine, theirs)
    second = jnp.where(mine_first, theirs, mine)
    couple(first, second, upper, gain, two_ref)
    points_ref[...] = jnp.concatenate([first, second], axis=1).astype(BF16)


def skeletons(packed, beside, tables, span, gain):
    leaf_count, rank = tables[0].shape
    counts = [table.shape[0] for table in tables]
    return pl.pallas_call(
        lambda *refs: skeletons_body(gain, span, counts, *refs),
        out_shape=(
            vmem((leaf_count + 4, rank, LEAF), BF16),
            coupling_shape(rank),
            coupling_shape(rank),
            vmem((16, 2 * rank), BF16),
        ),
        cost_estimate=COST,
        compiler_params=PARAMS,
        name="skeletons",
    )(packed, beside)


def top_couplings_body(gain, mine_ref, theirs_ref, picks_ref, other_ref, three_ref):
    count, rank, _ = picks_ref.shape
    picks = [picks_ref[count - pos].astype(F32).T for pos in (3, 2, 1)]
    mine, theirs = mine_ref[...].astype(F32), theirs_ref[...].astype(F32)
    couple(theirs[:, :rank], theirs[:, rank:], picks[1], gain, other_ref)
    mine, theirs = over(mine, picks[0], 1, 0), over(theirs, picks[1], 1, 0)
    mine_first = first_of_pair(3)
    first = jnp.where(mine_first, mine, theirs)
    second = jnp.where(mine_first, theirs, mine)
    couple(first, second, picks[2], gain, three_ref)


def top_couplings(mine, theirs, picks, gain):
    return pl.pallas_call(
        lambda *refs: top_couplings_body(gain, *refs),
        out_shape=[coupling_shape(picks.shape[1])] * 2,
        cost_estimate=COST,
        compiler_params=PARAMS,
        name="top_couplings",
    )(mine, theirs, picks)


def local(probes, points, leaf_skeleton, skeleton_one, skeleton_two, skeleton_three):
    span = probes.shape[1]
    row_count = lax.axis_size("row")
    col_count = lax.axis_size("col")
    gain = 16.0 / math.sqrt(4 * span * row_count * col_count)

    def swap(value, row_bits, col_bits):
        pairs = [
            (r * col_count + c, (r ^ row_bits) * col_count + (c ^ col_bits))
            for r in range(row_count)
            for c in range(col_count)
        ]
        return lax.ppermute(value, ("row", "col"), pairs)

    tables = (leaf_skeleton, skeleton_one, skeleton_two, skeleton_three)
    packed, own_points = pack(probes, points, tables)
    beside = swap(packed, 0, 1)
    across = swap(packed, 2, 0)
    line = col_count // 2
    line_points = [own_points] + [swap(own_points, 0, 2 * chunk) for chunk in range(1, line)]
    sibling_points = swap(jnp.concatenate(line_points, axis=1), 1, 0)
    near, far = range(2), range(2, line)
    feats, totals = first_product(
        packed,
        line_points,
        [[(chunk, 0) for chunk in group] for group in (near, far)],
        span,
        gain,
        True,
    )
    more = first_product(
        packed,
        [sibling_points],
        [[(0, chunk * span) for chunk in group] for group in (near, far)],
        span,
        gain,
        False,
    )
    feats, totals = [*feats, *more[0]], [*totals, *more[1]]
    beside, across, *totals = lax.optimization_barrier((beside, across, *totals))
    pieces = [packed, beside, across]
    relayed = halves(beside, across, 2 * (span + 16))
    diagonal = [swap(relayed[0], 2, 0), swap(relayed[1], 0, 1)]
    picks, couplings_one, couplings_two, points_two = skeletons(packed, beside, tables, span, gain)
    totals = product([beside], feats, totals, span)
    totals = product([across], feats, totals, span)
    points_two, *totals = lax.optimization_barrier((points_two, *totals))
    pieces += diagonal
    for bit in range(2, row_count.bit_length() - 1):
        more = [swap(value, 1 << bit, 0) for value in pieces]
        totals = product(more, feats, totals, span)
        pieces += more
    (theirs,) = product(diagonal, feats[3:], totals[3:], span)
    from_sibling = swap(theirs, 1, 0)
    (mine,) = product(diagonal, feats[1:2], totals[1:2], span)
    outs = [(range(0, line - 2, 2), F32), (range(1, line - 2, 2), BF16)]
    kept, sent = add_up(mine, from_sibling, outs, span)
    sent, total = lax.optimization_barrier((sent, totals[2]))
    arrived = swap(sent, 0, 2)
    (theirs,) = product(diagonal, feats[2:3], [total], span)
    from_sibling = swap(theirs, 1, 0)
    (mine,) = product(diagonal, feats[:1], totals[:1], span)
    other_points = swap(points_two, 0, 2)
    received = []
    chunks = list(range(2, line, 2))
    bit = 2
    while chunks:
        sent_places = [pos for pos, chunk in enumerate(chunks) if chunk & bit]
        kept_places = [pos for pos, chunk in enumerate(chunks) if not chunk & bit]
        outs = [(sent_places, BF16)] + [(kept_places, F32)] * (len(kept_places) > 0)
        sent, *kept = add_up(kept, arrived, outs, span, (other_points,), LONG)
        arrived = swap(sent, 0, 2 * bit)
        received.append(arrived[:span] if len(sent_places) > 1 else arrived)
        if kept:
            (kept,) = kept
            arrived = arrived[span:]
        chunks = [chunks[pos] for pos in kept_places]
        bit *= 2
    own_sum, near_sent = add_up(mine, from_sibling, [([0], F32), ([1], BF16)], span, (sent,))
    received.append(swap(near_sent, 0, 2))
    later = top_couplings(points_two, other_points, picks, gain)

    leaf_interp, interp_one, skeleton, reduced, sent = leaves(
        own_sum, received, packed, picks, couplings_one, later, leaf_skeleton.shape[0]
    )
    got = [swap(sent, 0, bits) for bits in (1, 2, 3)]
    upper_interp, top_state = upper_levels(
        skeleton, reduced, got, picks, (couplings_two, *later), interp_one
    )
    return jnp.swapaxes(leaf_interp, 1, 2), jnp.swapaxes(upper_interp, 2, 3), top_state


def solution(mesh):
    placed = (
        P(None, ("row", "col"), None),
        P(None, None, ("row", "col")),
        P(("row", "col"), None),
        P(("row", "col"), None),
        P("row", None),
        P("row", None),
    )
    return jax.shard_map(
        local,
        mesh=mesh,
        in_specs=placed,
        out_specs=(
            P(("row", "col"), None, None),
            P(None, ("row", "col"), None, None),
            P(None, ("row", "col"), None, None),
        ),
        check_vma=False,
    )
```

```python
import math

import jax
import jax.numpy as jnp
from jax import lax
from jax.experimental import pallas as pl
from jax.experimental.pallas import tpu as pltpu
from jax.sharding import PartitionSpec as P

LEAF = 128
F32 = jnp.float32
BF16 = jnp.bfloat16
DOUBLINGS = 9
VMEM = pl.BlockSpec(memory_space=pltpu.VMEM)


def vmem(shape, kind=F32):
    return pltpu.VMEM(tuple(shape), kind)


COST = pl.CostEstimate(flops=10**9, bytes_accessed=0, transcendentals=0)
LONG = pl.CostEstimate(flops=10**10, bytes_accessed=0, transcendentals=0)
PARAMS = pltpu.CompilerParams(vmem_limit_bytes=16 << 20)


def chebyshev_constants():
    taus = [1282.0 / 1280.0]
    for _ in range(DOUBLINGS):
        taus.append(2.0 * taus[-1] * taus[-1] - 1.0)
    front = 2.0**DOUBLINGS * math.prod(taus[:-1]) / taus[-1]
    return taus[:-1], front


TAUS, FRONT = chebyshev_constants()


def over(first, second, first_dim, second_dim):
    return lax.dot_general(
        first,
        second,
        (((first_dim,), (second_dim,)), ((), ())),
        preferred_element_type=F32,
    )


def split(value):
    high = value.astype(BF16)
    rest = value - high.astype(F32)
    middle = rest.astype(BF16)
    return high, middle, (rest - middle.astype(F32)).astype(BF16)


def norm_rows(norm, first, width):
    parts = [part.astype(F32) for part in split(norm)]
    place = lax.broadcasted_iota(jnp.int32, (16, width), 0)
    extra = jnp.where(place < 6, 1.0, 0.0)
    for pos in range(3):
        extra = jnp.where(place == pos + first, parts[pos], extra)
    return extra


def row_features(feats, gain):
    feats = feats.astype(F32)
    depth, width = feats.shape
    unit = math.log2(math.e) / (2.0 * depth)
    norm = jnp.sum(feats * feats, axis=0, keepdims=True) * -unit + math.log2(gain)
    parts = [part.astype(F32) for part in split(feats * (2.0 * unit))]
    return jnp.concatenate([*parts, norm_rows(norm, 0, width)], axis=0)


def col_features(feats):
    feats = feats.astype(F32)
    depth, width = feats.shape
    unit = math.log2(math.e) / (2.0 * depth)
    norm = jnp.sum(feats * feats, axis=0, keepdims=True) * -unit
    return jnp.concatenate([feats, feats, feats, norm_rows(norm, 3, width)], axis=0).astype(BF16)


def pack_body(*refs):
    probes_ref, points_ref, *table_refs = refs[:6]
    first_ref, second_ref, own_ref, held_ref, rows_ref, *held_tables, sem = refs[6:]
    span = probes_ref.shape[1]
    pairs = [(points_ref, held_ref), *zip(table_refs, held_tables)]
    small = len(pairs)
    for quarter in range(4):
        target = (first_ref, second_ref)[quarter // 2].at[pl.ds(quarter % 2 * span, span)]
        pairs.append((probes_ref.at[quarter], target))
    copies = [
        pltpu.make_async_copy(source, target, sem.at[pos])
        for pos, (source, target) in enumerate(pairs)
    ]
    for copy in copies:
        copy.start()
    rows_ref[...] = jnp.zeros_like(rows_ref)
    for copy in copies[:small]:
        copy.wait()
    points = held_ref[...].astype(F32)
    for quarter in range(4):
        feats = points[:, quarter, :].astype(BF16)
        half_ref = (first_ref, second_ref)[quarter // 2]
        half_ref[pl.ds(2 * span + quarter % 2 * 16, 16), :] = feats
        if quarter == 0:
            own_ref[...] = feats
    start = 0
    for table in held_tables:
        count, rank = table.shape
        rows_ref[pl.ds(start, count), pl.ds(0, rank)] = table[...].astype(F32)
        start += count
    first_ref[pl.ds(second_ref.shape[0], rows_ref.shape[0]), :] = rows_ref[...].astype(BF16)
    for copy in copies[small:]:
        copy.wait()


def pack(probes, points, tables):
    _, span, samples = probes.shape
    table_rows = -(-sum(table.shape[0] for table in tables) // 16) * 16
    inputs = (probes, points, *tables)
    return pl.pallas_call(
        pack_body,
        out_shape=(
            vmem((2 * (span + 16) + table_rows, samples), BF16),
            vmem((2 * (span + 16), samples), BF16),
            vmem((16, span), BF16),
        ),
        in_specs=[pl.BlockSpec(memory_space=pltpu.HBM)] * len(inputs),
        scratch_shapes=[
            pltpu.VMEM(points.shape, BF16),
            pltpu.VMEM((table_rows, samples), F32),
            *[pltpu.VMEM(table.shape, jnp.int32) for table in tables],
            pltpu.SemaphoreType.DMA((5 + len(tables),)),
        ],
        cost_estimate=COST,
        compiler_params=PARAMS,
        name="pack",
    )(*(pltpu.with_memory_space_constraint(value, pltpu.HBM) for value in inputs))


def masked(entries):
    shape = entries.shape
    row_leaf = lax.broadcasted_iota(jnp.int32, shape, 0) // LEAF
    col_leaf = lax.broadcasted_iota(jnp.int32, shape, 1) // LEAF
    return jnp.where(row_leaf == col_leaf, 0.0, entries)


def add_halves(half_refs, row_refs, cols_ref, put, span, own):
    for number, half_ref in enumerate(half_refs):
        for quarter in range(2):
            feats = half_ref[pl.ds(2 * span + 16 * quarter, 16), :]
            cols_ref[:, pl.ds((2 * number + quarter) * span, span)] = col_features(feats)
    columns = 2 * span * len(half_refs)
    for group, rows_ref in enumerate(row_refs):
        for start in range(0, rows_ref.shape[0], span):
            feats = rows_ref[pl.ds(start, span), :]
            entries = jnp.exp2(over(feats, cols_ref[:, :columns], 1, 0))
            if own and group == 0 and start == 0:
                entries = jnp.concatenate([masked(entries[:, :span]), entries[:, span:]], axis=1)
            randoms = [half_ref[pl.ds(0, 2 * span), :] for half_ref in half_refs]
            put(group, start, over(entries.astype(BF16), jnp.concatenate(randoms, axis=0), 1, 0))


def first_product_body(gain, span, groups, point_count, *refs):
    half_refs, point_refs = refs[:2], refs[2 : point_count + 2]
    row_refs = refs[point_count + 2 : point_count + 2 + len(groups)]
    total_refs, cols_ref = refs[point_count + 2 + len(groups) : -1], refs[-1]
    for rows_ref, places in zip(row_refs, groups):
        for pos, (array, start) in enumerate(places):
            feats = point_refs[array][:, pl.ds(start, span)]
            rows_ref[pl.ds(pos * span, span), :] = row_features(feats, gain).T.astype(BF16)

    def put(group, start, value):
        total_refs[group][pl.ds(start, span), :] = value

    add_halves(half_refs, row_refs, cols_ref, put, span, True)


def first_product(halves, points, groups, span, gain):
    samples = halves[0].shape[1]
    rows = [len(places) * span for places in groups]
    out = pl.pallas_call(
        lambda *refs: first_product_body(gain, span, groups, len(points), *refs),
        out_shape=[vmem((count, 64), BF16) for count in rows]
        + [vmem((count, samples), F32) for count in rows],
        scratch_shapes=[pltpu.VMEM((64, 4 * span), BF16)],
        cost_estimate=COST,
        compiler_params=PARAMS,
        name="first_product",
    )(*halves, *points)
    return out[: len(groups)], out[len(groups) :]


def product_body(span, half_count, count, *refs):
    half_refs, refs = refs[:half_count], refs[half_count:]
    row_refs, old_refs, total_refs = refs[:count], refs[count : 2 * count], refs[2 * count : -1]
    cols_ref = refs[-1]
    for number in range(0, half_count, 2):

        def put(group, start, value):
            place = pl.ds(start, span)
            base = old_refs if number == 0 else total_refs
            total_refs[group][place, :] = base[group][place, :] + value

        add_halves(half_refs[number : number + 2], row_refs, cols_ref, put, span, False)


def product(halves, rows, totals, span):
    return pl.pallas_call(
        lambda *refs: product_body(span, len(halves), len(rows), *refs),
        out_shape=[vmem(total.shape, F32) for total in totals],
        scratch_shapes=[pltpu.VMEM((64, 4 * span), BF16)],
        cost_estimate=COST,
        compiler_params=PARAMS,
        name="product",
    )(*halves, *rows, *totals)


def add_up_body(span, outs, mine_ref, theirs_ref, *refs):
    for (chunks, _), out_ref in zip(outs, refs[-len(outs) :]):
        for pos, chunk in enumerate(chunks):
            place = pl.ds(chunk * span, span)
            value = mine_ref[place, :] + theirs_ref[place, :].astype(F32)
            out_ref[pl.ds(pos * span, span), :] = value.astype(out_ref.dtype)


def add_up(mine, theirs, outs, span, after=(), cost=COST):
    samples = mine.shape[1]
    return pl.pallas_call(
        lambda *refs: add_up_body(span, outs, *refs),
        out_shape=[vmem((len(chunks) * span, samples), kind) for chunks, kind in outs],
        cost_estimate=cost,
        compiler_params=PARAMS,
        name="add_up",
    )(mine, theirs, *after)


def wide_product(first, second, second_dim):
    high, middle, low = split(first)
    other_high, other_middle, other_low = split(second)
    return over(
        jnp.concatenate([high, high, middle, middle, low, high], axis=1),
        jnp.concatenate(
            [other_high, other_middle, other_high, other_middle, other_high, other_low],
            axis=second_dim,
        ),
        1,
        second_dim,
    )


def exact_product(first, second):
    second = second.astype(BF16)
    return over(
        jnp.concatenate(split(first), axis=1), jnp.concatenate([second] * 3, axis=0), 1, 0
    )


def twice_product(twice_parts, parts):
    high, middle, low = twice_parts
    other_high, other_middle, other_low = parts
    left = lax.broadcasted_iota(jnp.int32, high.shape, 1) < high.shape[1] // 2
    last = jnp.where(left, low.astype(F32), high.astype(F32)).astype(BF16)
    return over(
        jnp.concatenate([high, middle, last], axis=1),
        jnp.concatenate(
            [other_high, other_middle, other_high, other_middle, other_high, other_low], axis=0
        ),
        1,
        0,
    )


def select_rows(picks, value):
    return over(
        jnp.concatenate([picks] * 3, axis=1), jnp.concatenate(split(value), axis=0), 1, 0
    )


def interpolate(stacks, skeletons):
    rank, pool = skeletons[0].shape[0], stacks[0].shape[0]
    place = lax.broadcasted_iota(jnp.int32, (rank, 2 * rank), 0)
    other = lax.broadcasted_iota(jnp.int32, (rank, 2 * rank), 1)
    eyes = jnp.where((other == place) | (other == place + rank), 1.0, 0.0)
    states = []
    for skeleton, stack in zip(skeletons, stacks):
        products = wide_product(skeleton, jnp.concatenate([stack, skeleton, skeleton], axis=0), 1)
        ridge = 0.05 * jnp.sum(skeleton * skeleton, keepdims=True) / rank + 1e-05
        inverse = 1.0 / (640.0 * ridge)
        states.append((products[:, :pool], eyes - products[:, pool:] * inverse, inverse))
    for number, tau in enumerate(TAUS):
        last = number == DOUBLINGS - 1
        later = []
        for solved, power, inverse in states:
            power_parts = split(power)
            parts = split(solved)
            if not last:
                parts = [jnp.concatenate(pair, axis=1) for pair in zip(parts, power_parts)]
            both = twice_product(power_parts, parts)
            solved = solved + both[:, :pool] * (1.0 / tau)
            later.append((solved, None if last else 2.0 * both[:, pool:] - eyes, inverse))
        states = later
    return [solved * (inverse * FRONT) for solved, _, inverse in states]


def merge(nodes, early=None):
    stacks, skeletons = [], []
    for samples, reduced, coupling, picks in nodes:
        pool = samples.shape[0]
        high, middle, low = split(reduced)
        coupled = over(
            coupling, jnp.concatenate([high, middle, high, middle, high, low], axis=0), 1, 0
        )
        stacks.append(samples - coupled[:pool])
        skeletons.append(select_rows(picks, samples) - coupled[pool:])
    if early is not None:
        early(skeletons[0])
    interps = interpolate(stacks, skeletons)
    return [
        (interp, skeleton, wide_product(interp, node[1], 0))
        for interp, skeleton, node in zip(interps, skeletons, nodes)
    ]


def leaves_body(received, *refs):
    own_ref, *others = refs[: received + 1]
    source_ref, picks_ref, couplings_ref = refs[received + 1 : received + 4]
    leaf_ref, upper_ref, skeleton_ref, reduced_ref, sent_ref, held_ref, sem = refs[-7:]
    total = own_ref[...]
    for other in others:
        total = total + other[...].astype(F32)
    count = total.shape[0] // LEAF
    stacks = [total[leaf * LEAF : (leaf + 1) * LEAF] for leaf in range(count)]
    skeletons = [select_rows(picks_ref[leaf], stack) for leaf, stack in enumerate(stacks)]
    reduced = []
    for leaf, interp in enumerate(interpolate(stacks, skeletons)):
        held_ref[leaf] = interp
        reduced.append(exact_product(interp, source_ref[pl.ds(leaf * LEAF, LEAF), :]))
    copy = pltpu.make_async_copy(held_ref, leaf_ref, sem)
    copy.start()
    node = (
        jnp.concatenate(skeletons, axis=0),
        jnp.concatenate(reduced, axis=0),
        couplings_ref[...],
        picks_ref[count],
    )
    ((interp, skeleton, reduced),) = merge([node])
    upper_ref[...] = interp
    skeleton_ref[...] = skeleton
    reduced_ref[...] = reduced
    for pos, part in enumerate((*split(skeleton)[:2], reduced.astype(BF16))):
        sent_ref[pl.ds(pos * skeleton.shape[0], skeleton.shape[0]), :] = part
    copy.wait()


def leaves(own, others, source, picks, couplings, later, leaf_count):
    samples = own.shape[1]
    rank, pool = picks.shape[1:]
    return pl.pallas_call(
        lambda *refs: leaves_body(len(others), *refs),
        out_shape=(
            jax.ShapeDtypeStruct((leaf_count, rank, LEAF), F32),
            vmem((rank, pool), F32),
            vmem((rank, samples), F32),
            vmem((rank, samples), F32),
            vmem((3 * rank, samples), BF16),
        ),
        out_specs=(pl.BlockSpec(memory_space=pl.ANY), VMEM, VMEM, VMEM, VMEM),
        scratch_shapes=[pltpu.VMEM((leaf_count, rank, LEAF), F32), pltpu.SemaphoreType.DMA],
        cost_estimate=COST,
        compiler_params=PARAMS,
        name="leaves",
    )(own, *others, source, picks, couplings, *later)


def first_of_pair(number):
    return (lax.axis_index("col") >> (number - 2)) % 2 == 0


def pair(mine, theirs, mine_first):
    first = jnp.where(mine_first, mine, theirs)
    second = jnp.where(mine_first, theirs, mine)
    return jnp.concatenate([first, second], axis=0)


def upper_body(picks_count, *refs):
    states = [(refs[0][...], refs[1][...])]
    rank = refs[0].shape[0]
    for got_ref in refs[2:5]:
        high, middle, reduced = (got_ref[pl.ds(pos * rank, rank), :] for pos in range(3))
        states.append((high.astype(F32) + middle.astype(F32), reduced.astype(F32)))
    picks_ref, two_ref, other_ref, three_ref, one_ref, upper_out, top_out = refs[5:12]
    upper_ref, state_ref, sem = refs[12:]
    places = [
        (one_ref, upper_out.at[0, 0]),
        (upper_ref.at[0], upper_out.at[1, 0]),
        (upper_ref.at[1], upper_out.at[2, 0]),
        (state_ref.at[0], top_out.at[0, 0]),
        (state_ref.at[1], top_out.at[1, 0]),
    ]
    copies = [
        pltpu.make_async_copy(source, target, sem.at[pos])
        for pos, (source, target) in enumerate(places)
    ]
    copies[0].start()
    mine_first = first_of_pair(2)
    nodes = []
    for number, coupling_ref in enumerate((two_ref, other_ref)):
        mine, theirs = states[2 * number : 2 * number + 2]
        picks = picks_ref[picks_count - 3 + number]
        stacks = [pair(*parts, mine_first) for parts in zip(mine, theirs)]
        nodes.append((*stacks, coupling_ref[...], picks))
    mine, theirs = merge(nodes)
    upper_ref[0] = mine[0]
    copies[1].start()

    def early(skeleton):
        state_ref[0] = skeleton
        copies[3].start()

    mine_first = first_of_pair(3)
    stacks = [pair(*parts, mine_first) for parts in zip(mine[1:], theirs[1:])]
    ((interp, _, reduced),) = merge([(*stacks, three_ref[...], picks_ref[picks_count - 1])], early)
    upper_ref[1] = interp
    copies[2].start()
    state_ref[1] = reduced
    copies[4].start()
    for copy in copies:
        copy.wait()


def upper_levels(skeleton, reduced, got, picks, couplings, interp_one):
    rank, pool = picks.shape[1:]
    samples = skeleton.shape[1]
    return pl.pallas_call(
        lambda *refs: upper_body(picks.shape[0], *refs),
        out_shape=(
            jax.ShapeDtypeStruct((3, 1, rank, pool), F32),
            jax.ShapeDtypeStruct((2, 1, rank, samples), F32),
        ),
        out_specs=(pl.BlockSpec(memory_space=pl.ANY),) * 2,
        scratch_shapes=[
            pltpu.VMEM((2, rank, pool), F32),
            pltpu.VMEM((2, rank, samples), F32),
            pltpu.SemaphoreType.DMA((5,)),
        ],
        cost_estimate=COST,
        compiler_params=PARAMS,
        name="upper_levels",
    )(skeleton, reduced, *got, picks, *couplings, interp_one)


def one_hot(chosen, pool):
    place = lax.broadcasted_iota(jnp.int32, (pool, chosen.shape[1]), 0)
    return jnp.where(place.astype(F32) == chosen, 1.0, 0.0).astype(F32)


def couple(first, second, picks, gain, couplings_ref):
    rank = first.shape[1]
    points = jnp.concatenate([first, second], axis=1)
    entries = jnp.exp2(over(row_features(points, gain).astype(BF16), col_features(points), 0, 0))
    left = lax.broadcasted_iota(jnp.int32, entries.shape, 1) < rank
    upper = lax.broadcasted_iota(jnp.int32, entries.shape, 0) < rank
    entries = jnp.where(left == upper, 0.0, entries)
    chosen = select_rows(picks.T.astype(BF16), entries)
    high, middle, low = split(jnp.concatenate([entries, chosen], axis=0))
    couplings_ref[...] = jnp.concatenate([high, high, middle, middle, low, high], axis=1)


def coupling_shape(rank):
    return vmem((3 * rank, 12 * rank), BF16)


def skeletons_body(gain, span, counts, mine_ref, beside_ref, *refs):
    picks_ref, one_ref, two_ref, points_ref = refs
    rank, pool = picks_ref.shape[1:]
    leaf_count = counts[0]
    tables = 2 * (span + 16)
    nodes = []
    for source_ref in (mine_ref, beside_ref):
        rows = source_ref[pl.ds(tables, source_ref.shape[0] - tables), :rank].astype(F32)
        hots = [one_hot(rows[pos : pos + 1], pool) for pos in range(leaf_count + 1)]
        children = []
        for leaf in range(leaf_count):
            feats = source_ref[pl.ds(2 * span, 16), pl.ds(leaf * LEAF, LEAF)]
            children.append(over(feats, hots[leaf].astype(BF16), 1, 0))
        points = jnp.concatenate(children, axis=1)
        nodes.append(over(points, hots[leaf_count], 1, 0))
        if source_ref is mine_ref:
            couple(*children, hots[leaf_count], gain, one_ref)
            start = leaf_count + counts[1]
            level_two = lax.axis_index("col") // 2
            wanted = [level_two, level_two + 1 - 2 * (level_two % 2), counts[2] + level_two // 2]
            for row in wanted:
                place = lax.broadcasted_iota(jnp.int32, rows.shape, 0)
                named = jnp.where(place == start + row, rows, 0.0)
                hots.append(one_hot(jnp.sum(named, axis=0, keepdims=True), pool))
            for number, hot in enumerate(hots):
                picks_ref[number] = hot.T.astype(BF16)
            upper = hots[leaf_count + 1]
    mine, theirs = nodes
    mine_first = first_of_pair(2)
    first = jnp.where(mine_first, mine, theirs)
    second = jnp.where(mine_first, theirs, mine)
    couple(first, second, upper, gain, two_ref)
    points_ref[...] = jnp.concatenate([first, second], axis=1).astype(BF16)


def skeletons(packed, beside, tables, span, gain):
    leaf_count, rank = tables[0].shape
    counts = [table.shape[0] for table in tables]
    return pl.pallas_call(
        lambda *refs: skeletons_body(gain, span, counts, *refs),
        out_shape=(
            vmem((leaf_count + 4, rank, LEAF), BF16),
            coupling_shape(rank),
            coupling_shape(rank),
            vmem((16, 2 * rank), BF16),
        ),
        cost_estimate=COST,
        compiler_params=PARAMS,
        name="skeletons",
    )(packed, beside)


def top_couplings_body(gain, mine_ref, theirs_ref, picks_ref, other_ref, three_ref):
    count, rank, _ = picks_ref.shape
    picks = [picks_ref[count - pos].astype(F32).T for pos in (3, 2, 1)]
    mine, theirs = mine_ref[...].astype(F32), theirs_ref[...].astype(F32)
    couple(theirs[:, :rank], theirs[:, rank:], picks[1], gain, other_ref)
    mine, theirs = over(mine, picks[0], 1, 0), over(theirs, picks[1], 1, 0)
    mine_first = first_of_pair(3)
    first = jnp.where(mine_first, mine, theirs)
    second = jnp.where(mine_first, theirs, mine)
    couple(first, second, picks[2], gain, three_ref)


def top_couplings(mine, theirs, picks, gain):
    return pl.pallas_call(
        lambda *refs: top_couplings_body(gain, *refs),
        out_shape=[coupling_shape(picks.shape[1])] * 2,
        cost_estimate=COST,
        compiler_params=PARAMS,
        name="top_couplings",
    )(mine, theirs, picks)


def local(probes, points, leaf_skeleton, skeleton_one, skeleton_two, skeleton_three):
    span = probes.shape[1]
    row_count = lax.axis_size("row")
    col_count = lax.axis_size("col")
    gain = 16.0 / math.sqrt(4 * span * row_count * col_count)

    def swap(value, row_bits, col_bits):
        pairs = [
            (r * col_count + c, (r ^ row_bits) * col_count + (c ^ col_bits))
            for r in range(row_count)
            for c in range(col_count)
        ]
        return lax.ppermute(value, ("row", "col"), pairs)

    tables = (leaf_skeleton, skeleton_one, skeleton_two, skeleton_three)
    first, second, own_points = pack(probes, points, tables)
    beside_first, across_second = swap(first, 0, 1), swap(second, 2, 0)
    line = col_count // 2
    line_points = own_points
    for bit in range(1, col_count.bit_length() - 1):
        line_points = jnp.concatenate([line_points, swap(line_points, 0, 1 << bit)], axis=1)
        if bit == 1:
            line_points, *late = lax.optimization_barrier((line_points, first, second))
    beside_second, across_first = swap(late[1], 0, 1), swap(late[0], 2, 0)
    line_points = [line_points, swap(line_points, 1, 0)]
    near, far = range(2), range(2, line)
    groups = [
        [(core, chunk * span) for chunk in group] for core in range(2) for group in (near, far)
    ]
    feats, totals = first_product((first, second), line_points, groups, span, gain)
    beside_first, across_second, *totals = lax.optimization_barrier(
        (beside_first, across_second, *totals)
    )
    diagonal = [swap(beside_first, 2, 0), swap(across_second, 0, 1)]
    picks, couplings_one, couplings_two, points_two = skeletons(
        first, beside_first, tables, span, gain
    )
    beside_second, across_first, points_two, *totals = lax.optimization_barrier(
        (beside_second, across_first, points_two, *totals)
    )
    totals = product([beside_first, beside_second], feats, totals, span)
    totals = product([across_first, across_second], feats, totals, span)
    pieces = [first, second, beside_first, beside_second, across_first, across_second, *diagonal]
    for bit in range(2, row_count.bit_length() - 1):
        more = [swap(value, 1 << bit, 0) for value in pieces]
        totals = product(more, feats, totals, span)
        pieces += more
    (theirs,) = product(diagonal, feats[3:], totals[3:], span)
    from_sibling = swap(theirs, 1, 0)
    (mine,) = product(diagonal, feats[1:2], totals[1:2], span)
    outs = [(range(0, line - 2, 2), F32), (range(1, line - 2, 2), BF16)]
    kept, sent = add_up(mine, from_sibling, outs, span)
    sent, total, points_two = lax.optimization_barrier((sent, totals[2], points_two))
    arrived = swap(sent, 0, 2)
    (theirs,) = product(diagonal, feats[2:3], [total], span)
    from_sibling = swap(theirs, 1, 0)
    (mine,) = product(diagonal, feats[:1], totals[:1], span)
    other_points = swap(points_two, 0, 2)
    received = []
    chunks = list(range(2, line, 2))
    bit = 2
    while chunks:
        sent_places = [pos for pos, chunk in enumerate(chunks) if chunk & bit]
        kept_places = [pos for pos, chunk in enumerate(chunks) if not chunk & bit]
        outs = [(sent_places, BF16)] + [(kept_places, F32)] * (len(kept_places) > 0)
        sent, *kept = add_up(kept, arrived, outs, span, (other_points,), LONG)
        arrived = swap(sent, 0, 2 * bit)
        received.append(arrived[:span] if len(sent_places) > 1 else arrived)
        if kept:
            (kept,) = kept
            arrived = arrived[span:]
        chunks = [chunks[pos] for pos in kept_places]
        bit *= 2
    own_sum, near_sent = add_up(mine, from_sibling, [([0], F32), ([1], BF16)], span, (sent,))
    received.append(swap(near_sent, 0, 2))
    later = top_couplings(points_two, other_points, picks, gain)

    leaf_interp, interp_one, skeleton, reduced, sent = leaves(
        own_sum, received, first, picks, couplings_one, later, leaf_skeleton.shape[0]
    )
    got = [swap(sent, 0, bits) for bits in (1, 2, 3)]
    upper_interp, top_state = upper_levels(
        skeleton, reduced, got, picks, (couplings_two, *later), interp_one
    )
    return jnp.swapaxes(leaf_interp, 1, 2), jnp.swapaxes(upper_interp, 2, 3), top_state


def solution(mesh):
    placed = (
        P(None, ("row", "col"), None),
        P(None, None, ("row", "col")),
        P(("row", "col"), None),
        P(("row", "col"), None),
        P("row", None),
        P("row", None),
    )
    return jax.shard_map(
        local,
        mesh=mesh,
        in_specs=placed,
        out_specs=(
            P(("row", "col"), None, None),
            P(None, ("row", "col"), None, None),
            P(None, ("row", "col"), None, None),
        ),
        check_vma=False,
    )
```

```python
import math

import jax
import jax.numpy as jnp
from jax import lax
from jax.experimental import pallas as pl
from jax.experimental.pallas import tpu as pltpu
from jax.sharding import PartitionSpec as P

LEAF = 128
F32 = jnp.float32
BF16 = jnp.bfloat16
DOUBLINGS = 9
VMEM = pl.BlockSpec(memory_space=pltpu.VMEM)


def vmem(shape, kind=F32):
    return pltpu.VMEM(tuple(shape), kind)


COST = pl.CostEstimate(flops=10**9, bytes_accessed=0, transcendentals=0)
LONG = pl.CostEstimate(flops=10**10, bytes_accessed=0, transcendentals=0)
PARAMS = pltpu.CompilerParams(vmem_limit_bytes=16 << 20)


def chebyshev_constants():
    taus = [1282.0 / 1280.0]
    for _ in range(DOUBLINGS):
        taus.append(2.0 * taus[-1] * taus[-1] - 1.0)
    front = 2.0**DOUBLINGS * math.prod(taus[:-1]) / taus[-1]
    return taus[:-1], front


TAUS, FRONT = chebyshev_constants()


def over(first, second, first_dim, second_dim):
    return lax.dot_general(
        first,
        second,
        (((first_dim,), (second_dim,)), ((), ())),
        preferred_element_type=F32,
    )


def split(value):
    high = value.astype(BF16)
    rest = value - high.astype(F32)
    middle = rest.astype(BF16)
    return high, middle, (rest - middle.astype(F32)).astype(BF16)


def norm_rows(norm, first, width):
    parts = [part.astype(F32) for part in split(norm)]
    place = lax.broadcasted_iota(jnp.int32, (16, width), 0)
    extra = jnp.where(place < 6, 1.0, 0.0)
    for pos in range(3):
        extra = jnp.where(place == pos + first, parts[pos], extra)
    return extra


def row_features(feats, gain):
    feats = feats.astype(F32)
    depth, width = feats.shape
    unit = math.log2(math.e) / (2.0 * depth)
    norm = jnp.sum(feats * feats, axis=0, keepdims=True) * -unit + math.log2(gain)
    parts = [part.astype(F32) for part in split(feats * (2.0 * unit))]
    return jnp.concatenate([*parts, norm_rows(norm, 0, width)], axis=0)


def col_features(feats):
    feats = feats.astype(F32)
    depth, width = feats.shape
    unit = math.log2(math.e) / (2.0 * depth)
    norm = jnp.sum(feats * feats, axis=0, keepdims=True) * -unit
    return jnp.concatenate([feats, feats, feats, norm_rows(norm, 3, width)], axis=0).astype(BF16)


def pack_body(*refs):
    probes_ref, points_ref, *table_refs = refs[:6]
    first_ref, second_ref, own_ref, held_ref, rows_ref, *held_tables, sem = refs[6:]
    span = probes_ref.shape[1]
    pairs = [(points_ref, held_ref), *zip(table_refs, held_tables)]
    small = len(pairs)
    for quarter in range(4):
        target = (first_ref, second_ref)[quarter // 2].at[pl.ds(quarter % 2 * span, span)]
        pairs.append((probes_ref.at[quarter], target))
    copies = [
        pltpu.make_async_copy(source, target, sem.at[pos])
        for pos, (source, target) in enumerate(pairs)
    ]
    for copy in copies:
        copy.start()
    rows_ref[...] = jnp.zeros_like(rows_ref)
    for copy in copies[:small]:
        copy.wait()
    points = held_ref[...].astype(F32)
    for quarter in range(4):
        feats = points[:, quarter, :].astype(BF16)
        half_ref = (first_ref, second_ref)[quarter // 2]
        half_ref[pl.ds(2 * span + quarter % 2 * 16, 16), :] = feats
        if quarter == 0:
            own_ref[...] = feats
    start = 0
    for table in held_tables:
        count, rank = table.shape
        rows_ref[pl.ds(start, count), pl.ds(0, rank)] = table[...].astype(F32)
        start += count
    first_ref[pl.ds(second_ref.shape[0], rows_ref.shape[0]), :] = rows_ref[...].astype(BF16)
    for copy in copies[small:]:
        copy.wait()


def pack(probes, points, tables):
    _, span, samples = probes.shape
    table_rows = -(-sum(table.shape[0] for table in tables) // 16) * 16
    inputs = (probes, points, *tables)
    return pl.pallas_call(
        pack_body,
        out_shape=(
            vmem((2 * (span + 16) + table_rows, samples), BF16),
            vmem((2 * (span + 16), samples), BF16),
            vmem((16, span), BF16),
        ),
        in_specs=[pl.BlockSpec(memory_space=pltpu.HBM)] * len(inputs),
        scratch_shapes=[
            pltpu.VMEM(points.shape, BF16),
            pltpu.VMEM((table_rows, samples), F32),
            *[pltpu.VMEM(table.shape, jnp.int32) for table in tables],
            pltpu.SemaphoreType.DMA((5 + len(tables),)),
        ],
        cost_estimate=COST,
        compiler_params=PARAMS,
        name="pack",
    )(*(pltpu.with_memory_space_constraint(value, pltpu.HBM) for value in inputs))


def masked(entries):
    shape = entries.shape
    row_leaf = lax.broadcasted_iota(jnp.int32, shape, 0) // LEAF
    col_leaf = lax.broadcasted_iota(jnp.int32, shape, 1) // LEAF
    return jnp.where(row_leaf == col_leaf, 0.0, entries)


def add_halves(half_refs, row_refs, cols_ref, put, span, own):
    for number, half_ref in enumerate(half_refs):
        for quarter in range(2):
            feats = half_ref[pl.ds(2 * span + 16 * quarter, 16), :]
            cols_ref[:, pl.ds((2 * number + quarter) * span, span)] = col_features(feats)
    columns = 2 * span * len(half_refs)
    for group, rows_ref in enumerate(row_refs):
        for start in range(0, rows_ref.shape[0], span):
            feats = rows_ref[pl.ds(start, span), :]
            entries = jnp.exp2(over(feats, cols_ref[:, :columns], 1, 0))
            if own and group == 0 and start == 0:
                entries = jnp.concatenate([masked(entries[:, :span]), entries[:, span:]], axis=1)
            randoms = [half_ref[pl.ds(0, 2 * span), :] for half_ref in half_refs]
            put(group, start, over(entries.astype(BF16), jnp.concatenate(randoms, axis=0), 1, 0))


def first_product_body(gain, span, groups, *refs):
    half_refs, points_ref = refs[:2], refs[2]
    row_refs, total_refs, cols_ref = refs[3 : 3 + len(groups)], refs[3 + len(groups) : -1], refs[-1]
    for rows_ref, places in zip(row_refs, groups):
        for pos, start in enumerate(places):
            feats = points_ref[:, pl.ds(start, span)]
            rows_ref[pl.ds(pos * span, span), :] = row_features(feats, gain).T.astype(BF16)

    def put(group, start, value):
        total_refs[group][pl.ds(start, span), :] = value

    add_halves(half_refs, row_refs, cols_ref, put, span, True)


def first_product(halves, points, groups, span, gain):
    samples = halves[0].shape[1]
    rows = [len(places) * span for places in groups]
    out = pl.pallas_call(
        lambda *refs: first_product_body(gain, span, groups, *refs),
        out_shape=[vmem((count, 64), BF16) for count in rows]
        + [vmem((count, samples), F32) for count in rows],
        scratch_shapes=[pltpu.VMEM((64, 4 * span), BF16)],
        cost_estimate=COST,
        compiler_params=PARAMS,
        name="first_product",
    )(*halves, points)
    return out[: len(groups)], out[len(groups) :]


def product_body(span, half_count, count, *refs):
    half_refs, refs = refs[:half_count], refs[half_count:]
    row_refs, old_refs, total_refs = refs[:count], refs[count : 2 * count], refs[2 * count : -1]
    cols_ref = refs[-1]
    for number in range(0, half_count, 2):

        def put(group, start, value):
            place = pl.ds(start, span)
            base = old_refs if number == 0 else total_refs
            total_refs[group][place, :] = base[group][place, :] + value

        add_halves(half_refs[number : number + 2], row_refs, cols_ref, put, span, False)


def product(halves, rows, totals, span):
    return pl.pallas_call(
        lambda *refs: product_body(span, len(halves), len(rows), *refs),
        out_shape=[vmem(total.shape, F32) for total in totals],
        scratch_shapes=[pltpu.VMEM((64, 4 * span), BF16)],
        cost_estimate=COST,
        compiler_params=PARAMS,
        name="product",
    )(*halves, *rows, *totals)


def add_up_body(span, outs, mine_ref, theirs_ref, *refs):
    for (chunks, _), out_ref in zip(outs, refs[-len(outs) :]):
        for pos, chunk in enumerate(chunks):
            place = pl.ds(chunk * span, span)
            value = mine_ref[place, :] + theirs_ref[place, :].astype(F32)
            out_ref[pl.ds(pos * span, span), :] = value.astype(out_ref.dtype)


def add_up(mine, theirs, outs, span, after=(), cost=COST):
    samples = mine.shape[1]
    return pl.pallas_call(
        lambda *refs: add_up_body(span, outs, *refs),
        out_shape=[vmem((len(chunks) * span, samples), kind) for chunks, kind in outs],
        cost_estimate=cost,
        compiler_params=PARAMS,
        name="add_up",
    )(mine, theirs, *after)


def wide_product(first, second, second_dim):
    high, middle, low = split(first)
    other_high, other_middle, other_low = split(second)
    return over(
        jnp.concatenate([high, high, middle, middle, low, high], axis=1),
        jnp.concatenate(
            [other_high, other_middle, other_high, other_middle, other_high, other_low],
            axis=second_dim,
        ),
        1,
        second_dim,
    )


def exact_product(first, second):
    second = second.astype(BF16)
    return over(
        jnp.concatenate(split(first), axis=1), jnp.concatenate([second] * 3, axis=0), 1, 0
    )


def twice_product(twice_parts, parts):
    high, middle, low = twice_parts
    other_high, other_middle, other_low = parts
    left = lax.broadcasted_iota(jnp.int32, high.shape, 1) < high.shape[1] // 2
    last = jnp.where(left, low.astype(F32), high.astype(F32)).astype(BF16)
    return over(
        jnp.concatenate([high, middle, last], axis=1),
        jnp.concatenate(
            [other_high, other_middle, other_high, other_middle, other_high, other_low], axis=0
        ),
        1,
        0,
    )


def select_rows(picks, value):
    return over(
        jnp.concatenate([picks] * 3, axis=1), jnp.concatenate(split(value), axis=0), 1, 0
    )


def interpolate(stacks, skeletons):
    rank, pool = skeletons[0].shape[0], stacks[0].shape[0]
    place = lax.broadcasted_iota(jnp.int32, (rank, 2 * rank), 0)
    other = lax.broadcasted_iota(jnp.int32, (rank, 2 * rank), 1)
    eyes = jnp.where((other == place) | (other == place + rank), 1.0, 0.0)
    states = []
    for skeleton, stack in zip(skeletons, stacks):
        products = wide_product(skeleton, jnp.concatenate([stack, skeleton, skeleton], axis=0), 1)
        ridge = 0.05 * jnp.sum(skeleton * skeleton, keepdims=True) / rank + 1e-05
        inverse = 1.0 / (640.0 * ridge)
        states.append((products[:, :pool], eyes - products[:, pool:] * inverse, inverse))
    for number, tau in enumerate(TAUS):
        last = number == DOUBLINGS - 1
        later = []
        for solved, power, inverse in states:
            power_parts = split(power)
            parts = split(solved)
            if not last:
                parts = [jnp.concatenate(pair, axis=1) for pair in zip(parts, power_parts)]
            both = twice_product(power_parts, parts)
            solved = solved + both[:, :pool] * (1.0 / tau)
            later.append((solved, None if last else 2.0 * both[:, pool:] - eyes, inverse))
        states = later
    return [solved * (inverse * FRONT) for solved, _, inverse in states]


def merge(nodes, early=None):
    stacks, skeletons = [], []
    for samples, reduced, coupling, picks in nodes:
        pool = samples.shape[0]
        high, middle, low = split(reduced)
        coupled = over(
            coupling, jnp.concatenate([high, middle, high, middle, high, low], axis=0), 1, 0
        )
        stacks.append(samples - coupled[:pool])
        skeletons.append(select_rows(picks, samples) - coupled[pool:])
    if early is not None:
        early(skeletons[0])
    interps = interpolate(stacks, skeletons)
    return [
        (interp, skeleton, wide_product(interp, node[1], 0))
        for interp, skeleton, node in zip(interps, skeletons, nodes)
    ]


def leaves_body(received, *refs):
    own_ref, *others = refs[: received + 1]
    source_ref, picks_ref, couplings_ref = refs[received + 1 : received + 4]
    leaf_ref, upper_ref, skeleton_ref, reduced_ref, sent_ref, held_ref, sem = refs[-7:]
    total = own_ref[...]
    for other in others:
        total = total + other[...].astype(F32)
    count = total.shape[0] // LEAF
    stacks = [total[leaf * LEAF : (leaf + 1) * LEAF] for leaf in range(count)]
    skeletons = [select_rows(picks_ref[leaf], stack) for leaf, stack in enumerate(stacks)]
    reduced = []
    for leaf, interp in enumerate(interpolate(stacks, skeletons)):
        held_ref[leaf] = interp
        reduced.append(exact_product(interp, source_ref[pl.ds(leaf * LEAF, LEAF), :]))
    copy = pltpu.make_async_copy(held_ref, leaf_ref, sem)
    copy.start()
    node = (
        jnp.concatenate(skeletons, axis=0),
        jnp.concatenate(reduced, axis=0),
        couplings_ref[...],
        picks_ref[count],
    )
    ((interp, skeleton, reduced),) = merge([node])
    upper_ref[...] = interp
    skeleton_ref[...] = skeleton
    reduced_ref[...] = reduced
    for pos, part in enumerate((*split(skeleton)[:2], reduced.astype(BF16))):
        sent_ref[pl.ds(pos * skeleton.shape[0], skeleton.shape[0]), :] = part
    copy.wait()


def leaves(own, others, source, picks, couplings, later, leaf_count):
    samples = own.shape[1]
    rank, pool = picks.shape[1:]
    return pl.pallas_call(
        lambda *refs: leaves_body(len(others), *refs),
        out_shape=(
            jax.ShapeDtypeStruct((leaf_count, rank, LEAF), F32),
            vmem((rank, pool), F32),
            vmem((rank, samples), F32),
            vmem((rank, samples), F32),
            vmem((3 * rank, samples), BF16),
        ),
        out_specs=(pl.BlockSpec(memory_space=pl.ANY), VMEM, VMEM, VMEM, VMEM),
        scratch_shapes=[pltpu.VMEM((leaf_count, rank, LEAF), F32), pltpu.SemaphoreType.DMA],
        cost_estimate=COST,
        compiler_params=PARAMS,
        name="leaves",
    )(own, *others, source, picks, couplings, *later)


def first_of_pair(number):
    return (lax.axis_index("col") >> (number - 2)) % 2 == 0


def pair(mine, theirs, mine_first):
    first = jnp.where(mine_first, mine, theirs)
    second = jnp.where(mine_first, theirs, mine)
    return jnp.concatenate([first, second], axis=0)


def upper_body(picks_count, *refs):
    states = [(refs[0][...], refs[1][...])]
    rank = refs[0].shape[0]
    for got_ref in refs[2:5]:
        high, middle, reduced = (got_ref[pl.ds(pos * rank, rank), :] for pos in range(3))
        states.append((high.astype(F32) + middle.astype(F32), reduced.astype(F32)))
    picks_ref, two_ref, other_ref, three_ref, one_ref, upper_out, top_out = refs[5:12]
    upper_ref, state_ref, sem = refs[12:]
    places = [
        (one_ref, upper_out.at[0, 0]),
        (upper_ref.at[0], upper_out.at[1, 0]),
        (upper_ref.at[1], upper_out.at[2, 0]),
        (state_ref.at[0], top_out.at[0, 0]),
        (state_ref.at[1], top_out.at[1, 0]),
    ]
    copies = [
        pltpu.make_async_copy(source, target, sem.at[pos])
        for pos, (source, target) in enumerate(places)
    ]
    copies[0].start()
    mine_first = first_of_pair(2)
    nodes = []
    for number, coupling_ref in enumerate((two_ref, other_ref)):
        mine, theirs = states[2 * number : 2 * number + 2]
        picks = picks_ref[picks_count - 3 + number]
        stacks = [pair(*parts, mine_first) for parts in zip(mine, theirs)]
        nodes.append((*stacks, coupling_ref[...], picks))
    mine, theirs = merge(nodes)
    upper_ref[0] = mine[0]
    copies[1].start()

    def early(skeleton):
        state_ref[0] = skeleton
        copies[3].start()

    mine_first = first_of_pair(3)
    stacks = [pair(*parts, mine_first) for parts in zip(mine[1:], theirs[1:])]
    ((interp, _, reduced),) = merge([(*stacks, three_ref[...], picks_ref[picks_count - 1])], early)
    upper_ref[1] = interp
    copies[2].start()
    state_ref[1] = reduced
    copies[4].start()
    for copy in copies:
        copy.wait()


def upper_levels(skeleton, reduced, got, picks, couplings, interp_one):
    rank, pool = picks.shape[1:]
    samples = skeleton.shape[1]
    return pl.pallas_call(
        lambda *refs: upper_body(picks.shape[0], *refs),
        out_shape=(
            jax.ShapeDtypeStruct((3, 1, rank, pool), F32),
            jax.ShapeDtypeStruct((2, 1, rank, samples), F32),
        ),
        out_specs=(pl.BlockSpec(memory_space=pl.ANY),) * 2,
        scratch_shapes=[
            pltpu.VMEM((2, rank, pool), F32),
            pltpu.VMEM((2, rank, samples), F32),
            pltpu.SemaphoreType.DMA((5,)),
        ],
        cost_estimate=COST,
        compiler_params=PARAMS,
        name="upper_levels",
    )(skeleton, reduced, *got, picks, *couplings, interp_one)


def one_hot(chosen, pool):
    place = lax.broadcasted_iota(jnp.int32, (pool, chosen.shape[1]), 0)
    return jnp.where(place.astype(F32) == chosen, 1.0, 0.0).astype(F32)


def couple(first, second, picks, gain, couplings_ref):
    rank = first.shape[1]
    points = jnp.concatenate([first, second], axis=1)
    entries = jnp.exp2(over(row_features(points, gain).astype(BF16), col_features(points), 0, 0))
    left = lax.broadcasted_iota(jnp.int32, entries.shape, 1) < rank
    upper = lax.broadcasted_iota(jnp.int32, entries.shape, 0) < rank
    entries = jnp.where(left == upper, 0.0, entries)
    chosen = select_rows(picks.T.astype(BF16), entries)
    high, middle, low = split(jnp.concatenate([entries, chosen], axis=0))
    couplings_ref[...] = jnp.concatenate([high, high, middle, middle, low, high], axis=1)


def coupling_shape(rank):
    return vmem((3 * rank, 12 * rank), BF16)


def skeletons_body(gain, span, counts, mine_ref, beside_ref, *refs):
    picks_ref, one_ref, two_ref, points_ref = refs
    rank, pool = picks_ref.shape[1:]
    leaf_count = counts[0]
    tables = 2 * (span + 16)
    nodes = []
    for source_ref in (mine_ref, beside_ref):
        rows = source_ref[pl.ds(tables, source_ref.shape[0] - tables), :rank].astype(F32)
        hots = [one_hot(rows[pos : pos + 1], pool) for pos in range(leaf_count + 1)]
        children = []
        for leaf in range(leaf_count):
            feats = source_ref[pl.ds(2 * span, 16), pl.ds(leaf * LEAF, LEAF)]
            children.append(over(feats, hots[leaf].astype(BF16), 1, 0))
        points = jnp.concatenate(children, axis=1)
        nodes.append(over(points, hots[leaf_count], 1, 0))
        if source_ref is mine_ref:
            couple(*children, hots[leaf_count], gain, one_ref)
            start = leaf_count + counts[1]
            level_two = lax.axis_index("col") // 2
            wanted = [level_two, level_two + 1 - 2 * (level_two % 2), counts[2] + level_two // 2]
            for row in wanted:
                place = lax.broadcasted_iota(jnp.int32, rows.shape, 0)
                named = jnp.where(place == start + row, rows, 0.0)
                hots.append(one_hot(jnp.sum(named, axis=0, keepdims=True), pool))
            for number, hot in enumerate(hots):
                picks_ref[number] = hot.T.astype(BF16)
            upper = hots[leaf_count + 1]
    mine, theirs = nodes
    mine_first = first_of_pair(2)
    first = jnp.where(mine_first, mine, theirs)
    second = jnp.where(mine_first, theirs, mine)
    couple(first, second, upper, gain, two_ref)
    points_ref[...] = jnp.concatenate([first, second], axis=1).astype(BF16)


def skeletons(packed, beside, tables, span, gain):
    leaf_count, rank = tables[0].shape
    counts = [table.shape[0] for table in tables]
    return pl.pallas_call(
        lambda *refs: skeletons_body(gain, span, counts, *refs),
        out_shape=(
            vmem((leaf_count + 4, rank, LEAF), BF16),
            coupling_shape(rank),
            coupling_shape(rank),
            vmem((16, 2 * rank), BF16),
        ),
        cost_estimate=COST,
        compiler_params=PARAMS,
        name="skeletons",
    )(packed, beside)


def top_couplings_body(gain, mine_ref, theirs_ref, picks_ref, other_ref, three_ref):
    count, rank, _ = picks_ref.shape
    picks = [picks_ref[count - pos].astype(F32).T for pos in (3, 2, 1)]
    mine, theirs = mine_ref[...].astype(F32), theirs_ref[...].astype(F32)
    couple(theirs[:, :rank], theirs[:, rank:], picks[1], gain, other_ref)
    mine, theirs = over(mine, picks[0], 1, 0), over(theirs, picks[1], 1, 0)
    mine_first = first_of_pair(3)
    first = jnp.where(mine_first, mine, theirs)
    second = jnp.where(mine_first, theirs, mine)
    couple(first, second, picks[2], gain, three_ref)


def top_couplings(mine, theirs, picks, gain):
    return pl.pallas_call(
        lambda *refs: top_couplings_body(gain, *refs),
        out_shape=[coupling_shape(picks.shape[1])] * 2,
        cost_estimate=COST,
        compiler_params=PARAMS,
        name="top_couplings",
    )(mine, theirs, picks)


def local(probes, points, leaf_skeleton, skeleton_one, skeleton_two, skeleton_three):
    span = probes.shape[1]
    row_count = lax.axis_size("row")
    col_count = lax.axis_size("col")
    gain = 16.0 / math.sqrt(4 * span * row_count * col_count)

    def swap(value, row_bits, col_bits):
        pairs = [
            (r * col_count + c, (r ^ row_bits) * col_count + (c ^ col_bits))
            for r in range(row_count)
            for c in range(col_count)
        ]
        return lax.ppermute(value, ("row", "col"), pairs)

    tables = (leaf_skeleton, skeleton_one, skeleton_two, skeleton_three)
    first, second, own_points = pack(probes, points, tables)
    beside_first, across_second = swap(first, 0, 1), swap(second, 2, 0)
    line = col_count // 2
    both_points = jnp.concatenate([own_points, swap(own_points, 1, 0)], axis=1)
    both_points, *late = lax.optimization_barrier((both_points, first, second))
    beside_second, across_first = swap(late[1], 0, 1), swap(late[0], 2, 0)
    for bit in range(1, col_count.bit_length() - 1):
        both_points = jnp.concatenate([both_points, swap(both_points, 0, 1 << bit)], axis=1)
    near, far = range(2), range(2, line)
    groups = [
        [(2 * chunk + core) * span for chunk in group] for core in range(2) for group in (near, far)
    ]
    feats, totals = first_product((first, second), both_points, groups, span, gain)
    beside_first, across_second, *totals = lax.optimization_barrier(
        (beside_first, across_second, *totals)
    )
    diagonal = [swap(beside_first, 2, 0), swap(across_second, 0, 1)]
    picks, couplings_one, couplings_two, points_two = skeletons(
        first, beside_first, tables, span, gain
    )
    beside_second, across_first, points_two, *totals = lax.optimization_barrier(
        (beside_second, across_first, points_two, *totals)
    )
    totals = product([beside_first, beside_second], feats, totals, span)
    totals = product([across_first, across_second], feats, totals, span)
    pieces = [first, second, beside_first, beside_second, across_first, across_second, *diagonal]
    for bit in range(2, row_count.bit_length() - 1):
        more = [swap(value, 1 << bit, 0) for value in pieces]
        totals = product(more, feats, totals, span)
        pieces += more
    other_points = swap(points_two, 0, 2)
    other_points, *totals = lax.optimization_barrier((other_points, *totals))
    (theirs,) = product(diagonal, feats[3:], totals[3:], span)
    from_sibling = swap(theirs, 1, 0)
    (mine,) = product(diagonal, feats[1:2], totals[1:2], span)
    outs = [(range(0, line - 2, 2), F32), (range(1, line - 2, 2), BF16)]
    kept, sent = add_up(mine, from_sibling, outs, span)
    sent, total = lax.optimization_barrier((sent, totals[2]))
    arrived = swap(sent, 0, 2)
    (theirs,) = product(diagonal, feats[2:3], [total], span)
    from_sibling = swap(theirs, 1, 0)
    (mine,) = product(diagonal, feats[:1], totals[:1], span)
    received = []
    chunks = list(range(2, line, 2))
    bit = 2
    while chunks:
        sent_places = [pos for pos, chunk in enumerate(chunks) if chunk & bit]
        kept_places = [pos for pos, chunk in enumerate(chunks) if not chunk & bit]
        outs = [(sent_places, BF16)] + [(kept_places, F32)] * (len(kept_places) > 0)
        sent, *kept = add_up(kept, arrived, outs, span, cost=LONG)
        arrived = swap(sent, 0, 2 * bit)
        received.append(arrived[:span] if len(sent_places) > 1 else arrived)
        if kept:
            (kept,) = kept
            arrived = arrived[span:]
        chunks = [chunks[pos] for pos in kept_places]
        bit *= 2
    own_sum, near_sent = add_up(mine, from_sibling, [([0], F32), ([1], BF16)], span, (sent,))
    received.append(swap(near_sent, 0, 2))
    later = top_couplings(points_two, other_points, picks, gain)

    leaf_interp, interp_one, skeleton, reduced, sent = leaves(
        own_sum, received, first, picks, couplings_one, later, leaf_skeleton.shape[0]
    )
    got = [swap(sent, 0, bits) for bits in (1, 2, 3)]
    upper_interp, top_state = upper_levels(
        skeleton, reduced, got, picks, (couplings_two, *later), interp_one
    )
    return jnp.swapaxes(leaf_interp, 1, 2), jnp.swapaxes(upper_interp, 2, 3), top_state


def solution(mesh):
    placed = (
        P(None, ("row", "col"), None),
        P(None, None, ("row", "col")),
        P(("row", "col"), None),
        P(("row", "col"), None),
        P("row", None),
        P("row", None),
    )
    return jax.shard_map(
        local,
        mesh=mesh,
        in_specs=placed,
        out_specs=(
            P(("row", "col"), None, None),
            P(None, ("row", "col"), None, None),
            P(None, ("row", "col"), None, None),
        ),
        check_vma=False,
    )
```

```python
import math

import jax
import jax.numpy as jnp
from jax import lax
from jax.experimental import pallas as pl
from jax.experimental.pallas import tpu as pltpu
from jax.sharding import PartitionSpec as P

LEAF = 128
F32 = jnp.float32
BF16 = jnp.bfloat16
DOUBLINGS = 9
VMEM = pl.BlockSpec(memory_space=pltpu.VMEM)


def vmem(shape, kind=F32):
    return pltpu.VMEM(tuple(shape), kind)


COST = pl.CostEstimate(flops=10**9, bytes_accessed=0, transcendentals=0)
LONG = pl.CostEstimate(flops=10**10, bytes_accessed=0, transcendentals=0)
PARAMS = pltpu.CompilerParams(vmem_limit_bytes=16 << 20)


def chebyshev_constants():
    taus = [1282.0 / 1280.0]
    for _ in range(DOUBLINGS):
        taus.append(2.0 * taus[-1] * taus[-1] - 1.0)
    front = 2.0**DOUBLINGS * math.prod(taus[:-1]) / taus[-1]
    return taus[:-1], front


TAUS, FRONT = chebyshev_constants()


def over(first, second, first_dim, second_dim):
    return lax.dot_general(
        first,
        second,
        (((first_dim,), (second_dim,)), ((), ())),
        preferred_element_type=F32,
    )


def split(value):
    high = value.astype(BF16)
    rest = value - high.astype(F32)
    middle = rest.astype(BF16)
    return high, middle, (rest - middle.astype(F32)).astype(BF16)


def norm_rows(norm, first, width):
    parts = [part.astype(F32) for part in split(norm)]
    place = lax.broadcasted_iota(jnp.int32, (16, width), 0)
    extra = jnp.where(place < 6, 1.0, 0.0)
    for pos in range(3):
        extra = jnp.where(place == pos + first, parts[pos], extra)
    return extra


def row_features(feats, gain):
    feats = feats.astype(F32)
    depth, width = feats.shape
    unit = math.log2(math.e) / (2.0 * depth)
    norm = jnp.sum(feats * feats, axis=0, keepdims=True) * -unit + math.log2(gain)
    parts = [part.astype(F32) for part in split(feats * (2.0 * unit))]
    return jnp.concatenate([*parts, norm_rows(norm, 0, width)], axis=0)


def col_features(feats):
    feats = feats.astype(F32)
    depth, width = feats.shape
    unit = math.log2(math.e) / (2.0 * depth)
    norm = jnp.sum(feats * feats, axis=0, keepdims=True) * -unit
    return jnp.concatenate([feats, feats, feats, norm_rows(norm, 3, width)], axis=0).astype(BF16)


def pack_body(*refs):
    probes_ref, points_ref, *table_refs = refs[:6]
    first_ref, second_ref, own_ref, held_ref, rows_ref, *held_tables, sem = refs[6:]
    span = probes_ref.shape[1]
    pairs = [(points_ref, held_ref), *zip(table_refs, held_tables)]
    small = len(pairs)
    for quarter in range(4):
        target = (first_ref, second_ref)[quarter // 2].at[pl.ds(quarter % 2 * span, span)]
        pairs.append((probes_ref.at[quarter], target))
    copies = [
        pltpu.make_async_copy(source, target, sem.at[pos])
        for pos, (source, target) in enumerate(pairs)
    ]
    for copy in copies:
        copy.start()
    rows_ref[...] = jnp.zeros_like(rows_ref)
    for copy in copies[:small]:
        copy.wait()
    points = held_ref[...].astype(F32)
    for quarter in range(4):
        feats = points[:, quarter, :].astype(BF16)
        half_ref = (first_ref, second_ref)[quarter // 2]
        half_ref[pl.ds(2 * span + quarter % 2 * 16, 16), :] = feats
        if quarter == 0:
            own_ref[...] = feats
    start = 0
    for table in held_tables:
        count, rank = table.shape
        rows_ref[pl.ds(start, count), pl.ds(0, rank)] = table[...].astype(F32)
        start += count
    first_ref[pl.ds(second_ref.shape[0], rows_ref.shape[0]), :] = rows_ref[...].astype(BF16)
    for copy in copies[small:]:
        copy.wait()


def pack(probes, points, tables):
    _, span, samples = probes.shape
    table_rows = -(-sum(table.shape[0] for table in tables) // 16) * 16
    inputs = (probes, points, *tables)
    return pl.pallas_call(
        pack_body,
        out_shape=(
            vmem((2 * (span + 16) + table_rows, samples), BF16),
            vmem((2 * (span + 16), samples), BF16),
            vmem((16, span), BF16),
        ),
        in_specs=[pl.BlockSpec(memory_space=pltpu.HBM)] * len(inputs),
        scratch_shapes=[
            pltpu.VMEM(points.shape, BF16),
            pltpu.VMEM((table_rows, samples), F32),
            *[pltpu.VMEM(table.shape, jnp.int32) for table in tables],
            pltpu.SemaphoreType.DMA((5 + len(tables),)),
        ],
        cost_estimate=COST,
        compiler_params=PARAMS,
        name="pack",
    )(*(pltpu.with_memory_space_constraint(value, pltpu.HBM) for value in inputs))


def masked(entries):
    shape = entries.shape
    row_leaf = lax.broadcasted_iota(jnp.int32, shape, 0) // LEAF
    col_leaf = lax.broadcasted_iota(jnp.int32, shape, 1) // LEAF
    return jnp.where(row_leaf == col_leaf, 0.0, entries)


def add_halves(half_refs, row_refs, cols_ref, put, span, own):
    for number, half_ref in enumerate(half_refs):
        for quarter in range(2):
            feats = half_ref[pl.ds(2 * span + 16 * quarter, 16), :]
            cols_ref[:, pl.ds((2 * number + quarter) * span, span)] = col_features(feats)
    columns = 2 * span * len(half_refs)
    for group, rows_ref in enumerate(row_refs):
        for start in range(0, rows_ref.shape[0], span):
            feats = rows_ref[pl.ds(start, span), :]
            entries = jnp.exp2(over(feats, cols_ref[:, :columns], 1, 0))
            if own and group == 0 and start == 0:
                entries = jnp.concatenate([masked(entries[:, :span]), entries[:, span:]], axis=1)
            randoms = [half_ref[pl.ds(0, 2 * span), :] for half_ref in half_refs]
            put(group, start, over(entries.astype(BF16), jnp.concatenate(randoms, axis=0), 1, 0))


def first_product_body(gain, span, groups, point_count, *refs):
    half_refs, point_refs = refs[:2], refs[2 : point_count + 2]
    row_refs = refs[point_count + 2 : point_count + 2 + len(groups)]
    total_refs, cols_ref = refs[point_count + 2 + len(groups) : -1], refs[-1]
    for rows_ref, places in zip(row_refs, groups):
        for pos, (array, start) in enumerate(places):
            feats = point_refs[array][:, pl.ds(start, span)]
            rows_ref[pl.ds(pos * span, span), :] = row_features(feats, gain).T.astype(BF16)

    def put(group, start, value):
        total_refs[group][pl.ds(start, span), :] = value

    add_halves(half_refs, row_refs, cols_ref, put, span, True)


def first_product(halves, points, groups, span, gain):
    samples = halves[0].shape[1]
    rows = [len(places) * span for places in groups]
    out = pl.pallas_call(
        lambda *refs: first_product_body(gain, span, groups, len(points), *refs),
        out_shape=[vmem((count, 64), BF16) for count in rows]
        + [vmem((count, samples), F32) for count in rows],
        scratch_shapes=[pltpu.VMEM((64, 4 * span), BF16)],
        cost_estimate=COST,
        compiler_params=PARAMS,
        name="first_product",
    )(*halves, *points)
    return out[: len(groups)], out[len(groups) :]


def product_body(span, half_count, count, *refs):
    half_refs, refs = refs[:half_count], refs[half_count:]
    row_refs, old_refs, total_refs = refs[:count], refs[count : 2 * count], refs[2 * count : -1]
    cols_ref = refs[-1]
    for number in range(0, half_count, 2):

        def put(group, start, value):
            place = pl.ds(start, span)
            base = old_refs if number == 0 else total_refs
            total_refs[group][place, :] = base[group][place, :] + value

        add_halves(half_refs[number : number + 2], row_refs, cols_ref, put, span, False)


def product(halves, rows, totals, span):
    return pl.pallas_call(
        lambda *refs: product_body(span, len(halves), len(rows), *refs),
        out_shape=[vmem(total.shape, F32) for total in totals],
        scratch_shapes=[pltpu.VMEM((64, 4 * span), BF16)],
        cost_estimate=COST,
        compiler_params=PARAMS,
        name="product",
    )(*halves, *rows, *totals)


def add_up_body(span, outs, mine_ref, theirs_ref, *refs):
    for (chunks, _), out_ref in zip(outs, refs[-len(outs) :]):
        for pos, chunk in enumerate(chunks):
            place = pl.ds(chunk * span, span)
            value = mine_ref[place, :] + theirs_ref[place, :].astype(F32)
            out_ref[pl.ds(pos * span, span), :] = value.astype(out_ref.dtype)


def add_up(mine, theirs, outs, span, after=(), cost=COST):
    samples = mine.shape[1]
    return pl.pallas_call(
        lambda *refs: add_up_body(span, outs, *refs),
        out_shape=[vmem((len(chunks) * span, samples), kind) for chunks, kind in outs],
        cost_estimate=cost,
        compiler_params=PARAMS,
        name="add_up",
    )(mine, theirs, *after)


def wide_product(first, second, second_dim):
    high, middle, low = split(first)
    other_high, other_middle, other_low = split(second)
    return over(
        jnp.concatenate([high, high, middle, middle, low, high], axis=1),
        jnp.concatenate(
            [other_high, other_middle, other_high, other_middle, other_high, other_low],
            axis=second_dim,
        ),
        1,
        second_dim,
    )


def exact_product(first, second):
    second = second.astype(BF16)
    return over(
        jnp.concatenate(split(first), axis=1), jnp.concatenate([second] * 3, axis=0), 1, 0
    )


def twice_product(twice_parts, parts):
    high, middle, low = twice_parts
    other_high, other_middle, other_low = parts
    left = lax.broadcasted_iota(jnp.int32, high.shape, 1) < high.shape[1] // 2
    last = jnp.where(left, low.astype(F32), high.astype(F32)).astype(BF16)
    return over(
        jnp.concatenate([high, middle, last], axis=1),
        jnp.concatenate(
            [other_high, other_middle, other_high, other_middle, other_high, other_low], axis=0
        ),
        1,
        0,
    )


def select_rows(picks, value):
    return over(
        jnp.concatenate([picks] * 3, axis=1), jnp.concatenate(split(value), axis=0), 1, 0
    )


def interpolate(stacks, skeletons):
    rank, pool = skeletons[0].shape[0], stacks[0].shape[0]
    place = lax.broadcasted_iota(jnp.int32, (rank, 2 * rank), 0)
    other = lax.broadcasted_iota(jnp.int32, (rank, 2 * rank), 1)
    eyes = jnp.where((other == place) | (other == place + rank), 1.0, 0.0)
    states = []
    for skeleton, stack in zip(skeletons, stacks):
        products = wide_product(skeleton, jnp.concatenate([stack, skeleton, skeleton], axis=0), 1)
        ridge = 0.05 * jnp.sum(skeleton * skeleton, keepdims=True) / rank + 1e-05
        inverse = 1.0 / (640.0 * ridge)
        states.append((products[:, :pool], eyes - products[:, pool:] * inverse, inverse))
    for number, tau in enumerate(TAUS):
        last = number == DOUBLINGS - 1
        later = []
        for solved, power, inverse in states:
            power_parts = split(power)
            parts = split(solved)
            if not last:
                parts = [jnp.concatenate(pair, axis=1) for pair in zip(parts, power_parts)]
            both = twice_product(power_parts, parts)
            solved = solved + both[:, :pool] * (1.0 / tau)
            later.append((solved, None if last else 2.0 * both[:, pool:] - eyes, inverse))
        states = later
    return [solved * (inverse * FRONT) for solved, _, inverse in states]


def merge(nodes, early=None):
    stacks, skeletons = [], []
    for samples, reduced, coupling, picks in nodes:
        pool = samples.shape[0]
        high, middle, low = split(reduced)
        coupled = over(
            coupling, jnp.concatenate([high, middle, high, middle, high, low], axis=0), 1, 0
        )
        stacks.append(samples - coupled[:pool])
        skeletons.append(select_rows(picks, samples) - coupled[pool:])
    if early is not None:
        early(skeletons[0])
    interps = interpolate(stacks, skeletons)
    return [
        (interp, skeleton, wide_product(interp, node[1], 0))
        for interp, skeleton, node in zip(interps, skeletons, nodes)
    ]


def leaves_body(received, *refs):
    own_ref, *others = refs[: received + 1]
    source_ref, picks_ref, couplings_ref = refs[received + 1 : received + 4]
    leaf_ref, upper_ref, skeleton_ref, reduced_ref, sent_ref, held_ref, sem = refs[-7:]
    total = own_ref[...]
    for other in others:
        total = total + other[...].astype(F32)
    count = total.shape[0] // LEAF
    stacks = [total[leaf * LEAF : (leaf + 1) * LEAF] for leaf in range(count)]
    skeletons = [select_rows(picks_ref[leaf], stack) for leaf, stack in enumerate(stacks)]
    reduced = []
    for leaf, interp in enumerate(interpolate(stacks, skeletons)):
        held_ref[leaf] = interp
        reduced.append(exact_product(interp, source_ref[pl.ds(leaf * LEAF, LEAF), :]))
    copy = pltpu.make_async_copy(held_ref, leaf_ref, sem)
    copy.start()
    node = (
        jnp.concatenate(skeletons, axis=0),
        jnp.concatenate(reduced, axis=0),
        couplings_ref[...],
        picks_ref[count],
    )
    ((interp, skeleton, reduced),) = merge([node])
    upper_ref[...] = interp
    skeleton_ref[...] = skeleton
    reduced_ref[...] = reduced
    for pos, part in enumerate((*split(skeleton)[:2], reduced.astype(BF16))):
        sent_ref[pl.ds(pos * skeleton.shape[0], skeleton.shape[0]), :] = part
    copy.wait()


def leaves(own, others, source, picks, couplings, later, leaf_count):
    samples = own.shape[1]
    rank, pool = picks.shape[1:]
    return pl.pallas_call(
        lambda *refs: leaves_body(len(others), *refs),
        out_shape=(
            jax.ShapeDtypeStruct((leaf_count, rank, LEAF), F32),
            vmem((rank, pool), F32),
            vmem((rank, samples), F32),
            vmem((rank, samples), F32),
            vmem((3 * rank, samples), BF16),
        ),
        out_specs=(pl.BlockSpec(memory_space=pl.ANY), VMEM, VMEM, VMEM, VMEM),
        scratch_shapes=[pltpu.VMEM((leaf_count, rank, LEAF), F32), pltpu.SemaphoreType.DMA],
        cost_estimate=COST,
        compiler_params=PARAMS,
        name="leaves",
    )(own, *others, source, picks, couplings, *later)


def first_of_pair(number):
    return (lax.axis_index("col") >> (number - 2)) % 2 == 0


def pair(mine, theirs, mine_first):
    first = jnp.where(mine_first, mine, theirs)
    second = jnp.where(mine_first, theirs, mine)
    return jnp.concatenate([first, second], axis=0)


def upper_body(picks_count, *refs):
    states = [(refs[0][...], refs[1][...])]
    rank = refs[0].shape[0]
    for got_ref in refs[2:5]:
        high, middle, reduced = (got_ref[pl.ds(pos * rank, rank), :] for pos in range(3))
        states.append((high.astype(F32) + middle.astype(F32), reduced.astype(F32)))
    picks_ref, two_ref, other_ref, three_ref, one_ref, upper_out, top_out = refs[5:12]
    upper_ref, state_ref, sem = refs[12:]
    places = [
        (one_ref, upper_out.at[0, 0]),
        (upper_ref.at[0], upper_out.at[1, 0]),
        (upper_ref.at[1], upper_out.at[2, 0]),
        (state_ref.at[0], top_out.at[0, 0]),
        (state_ref.at[1], top_out.at[1, 0]),
    ]
    copies = [
        pltpu.make_async_copy(source, target, sem.at[pos])
        for pos, (source, target) in enumerate(places)
    ]
    copies[0].start()
    mine_first = first_of_pair(2)
    nodes = []
    for number, coupling_ref in enumerate((two_ref, other_ref)):
        mine, theirs = states[2 * number : 2 * number + 2]
        picks = picks_ref[picks_count - 3 + number]
        stacks = [pair(*parts, mine_first) for parts in zip(mine, theirs)]
        nodes.append((*stacks, coupling_ref[...], picks))
    mine, theirs = merge(nodes)
    upper_ref[0] = mine[0]
    copies[1].start()

    def early(skeleton):
        state_ref[0] = skeleton
        copies[3].start()

    mine_first = first_of_pair(3)
    stacks = [pair(*parts, mine_first) for parts in zip(mine[1:], theirs[1:])]
    ((interp, _, reduced),) = merge([(*stacks, three_ref[...], picks_ref[picks_count - 1])], early)
    upper_ref[1] = interp
    copies[2].start()
    state_ref[1] = reduced
    copies[4].start()
    for copy in copies:
        copy.wait()


def upper_levels(skeleton, reduced, got, picks, couplings, interp_one):
    rank, pool = picks.shape[1:]
    samples = skeleton.shape[1]
    return pl.pallas_call(
        lambda *refs: upper_body(picks.shape[0], *refs),
        out_shape=(
            jax.ShapeDtypeStruct((3, 1, rank, pool), F32),
            jax.ShapeDtypeStruct((2, 1, rank, samples), F32),
        ),
        out_specs=(pl.BlockSpec(memory_space=pl.ANY),) * 2,
        scratch_shapes=[
            pltpu.VMEM((2, rank, pool), F32),
            pltpu.VMEM((2, rank, samples), F32),
            pltpu.SemaphoreType.DMA((5,)),
        ],
        cost_estimate=COST,
        compiler_params=PARAMS,
        name="upper_levels",
    )(skeleton, reduced, *got, picks, *couplings, interp_one)


def one_hot(chosen, pool):
    place = lax.broadcasted_iota(jnp.int32, (pool, chosen.shape[1]), 0)
    return jnp.where(place.astype(F32) == chosen, 1.0, 0.0).astype(F32)


def couple(first, second, picks, gain, couplings_ref):
    rank = first.shape[1]
    points = jnp.concatenate([first, second], axis=1)
    entries = jnp.exp2(over(row_features(points, gain).astype(BF16), col_features(points), 0, 0))
    left = lax.broadcasted_iota(jnp.int32, entries.shape, 1) < rank
    upper = lax.broadcasted_iota(jnp.int32, entries.shape, 0) < rank
    entries = jnp.where(left == upper, 0.0, entries)
    chosen = select_rows(picks.T.astype(BF16), entries)
    high, middle, low = split(jnp.concatenate([entries, chosen], axis=0))
    couplings_ref[...] = jnp.concatenate([high, high, middle, middle, low, high], axis=1)


def coupling_shape(rank):
    return vmem((3 * rank, 12 * rank), BF16)


def skeletons_body(gain, span, counts, mine_ref, beside_ref, *refs):
    picks_ref, one_ref, two_ref, points_ref = refs
    rank, pool = picks_ref.shape[1:]
    leaf_count = counts[0]
    tables = 2 * (span + 16)
    nodes = []
    for source_ref in (mine_ref, beside_ref):
        rows = source_ref[pl.ds(tables, source_ref.shape[0] - tables), :rank].astype(F32)
        hots = [one_hot(rows[pos : pos + 1], pool) for pos in range(leaf_count + 1)]
        children = []
        for leaf in range(leaf_count):
            feats = source_ref[pl.ds(2 * span, 16), pl.ds(leaf * LEAF, LEAF)]
            children.append(over(feats, hots[leaf].astype(BF16), 1, 0))
        points = jnp.concatenate(children, axis=1)
        nodes.append(over(points, hots[leaf_count], 1, 0))
        if source_ref is mine_ref:
            couple(*children, hots[leaf_count], gain, one_ref)
            start = leaf_count + counts[1]
            level_two = lax.axis_index("col") // 2
            wanted = [level_two, level_two + 1 - 2 * (level_two % 2), counts[2] + level_two // 2]
            for row in wanted:
                place = lax.broadcasted_iota(jnp.int32, rows.shape, 0)
                named = jnp.where(place == start + row, rows, 0.0)
                hots.append(one_hot(jnp.sum(named, axis=0, keepdims=True), pool))
            for number, hot in enumerate(hots):
                picks_ref[number] = hot.T.astype(BF16)
            upper = hots[leaf_count + 1]
    mine, theirs = nodes
    mine_first = first_of_pair(2)
    first = jnp.where(mine_first, mine, theirs)
    second = jnp.where(mine_first, theirs, mine)
    couple(first, second, upper, gain, two_ref)
    points_ref[...] = jnp.concatenate([first, second], axis=1).astype(BF16)


def skeletons(packed, beside, tables, span, gain):
    leaf_count, rank = tables[0].shape
    counts = [table.shape[0] for table in tables]
    return pl.pallas_call(
        lambda *refs: skeletons_body(gain, span, counts, *refs),
        out_shape=(
            vmem((leaf_count + 4, rank, LEAF), BF16),
            coupling_shape(rank),
            coupling_shape(rank),
            vmem((16, 2 * rank), BF16),
        ),
        cost_estimate=COST,
        compiler_params=PARAMS,
        name="skeletons",
    )(packed, beside)


def top_couplings_body(gain, mine_ref, theirs_ref, picks_ref, other_ref, three_ref):
    count, rank, _ = picks_ref.shape
    picks = [picks_ref[count - pos].astype(F32).T for pos in (3, 2, 1)]
    mine, theirs = mine_ref[...].astype(F32), theirs_ref[...].astype(F32)
    couple(theirs[:, :rank], theirs[:, rank:], picks[1], gain, other_ref)
    mine, theirs = over(mine, picks[0], 1, 0), over(theirs, picks[1], 1, 0)
    mine_first = first_of_pair(3)
    first = jnp.where(mine_first, mine, theirs)
    second = jnp.where(mine_first, theirs, mine)
    couple(first, second, picks[2], gain, three_ref)


def top_couplings(mine, theirs, picks, gain):
    return pl.pallas_call(
        lambda *refs: top_couplings_body(gain, *refs),
        out_shape=[coupling_shape(picks.shape[1])] * 2,
        cost_estimate=COST,
        compiler_params=PARAMS,
        name="top_couplings",
    )(mine, theirs, picks)


def local(probes, points, leaf_skeleton, skeleton_one, skeleton_two, skeleton_three):
    span = probes.shape[1]
    row_count = lax.axis_size("row")
    col_count = lax.axis_size("col")
    gain = 16.0 / math.sqrt(4 * span * row_count * col_count)

    def swap(value, row_bits, col_bits):
        pairs = [
            (r * col_count + c, (r ^ row_bits) * col_count + (c ^ col_bits))
            for r in range(row_count)
            for c in range(col_count)
        ]
        return lax.ppermute(value, ("row", "col"), pairs)

    tables = (leaf_skeleton, skeleton_one, skeleton_two, skeleton_three)
    first, second, own_points = pack(probes, points, tables)
    beside_first, across_second = swap(first, 0, 1), swap(second, 2, 0)
    line = col_count // 2
    line_points = own_points
    for bit in range(1, col_count.bit_length() - 1):
        line_points = jnp.concatenate([line_points, swap(line_points, 0, 1 << bit)], axis=1)
        if bit == 1:
            line_points, *late = lax.optimization_barrier((line_points, first, second))
    beside_second, across_first = swap(late[1], 0, 1), swap(late[0], 2, 0)
    line_points = [line_points, swap(line_points, 1, 0)]
    near, far = range(2), range(2, line)
    groups = [
        [(core, chunk * span) for chunk in group] for core in range(2) for group in (near, far)
    ]
    feats, totals = first_product((first, second), line_points, groups, span, gain)
    beside_first, across_second, *totals = lax.optimization_barrier(
        (beside_first, across_second, *totals)
    )
    diagonal = [swap(beside_first, 2, 0), swap(across_second, 0, 1)]
    picks, couplings_one, couplings_two, points_two = skeletons(
        first, beside_first, tables, span, gain
    )
    beside_second, across_first, points_two, *totals = lax.optimization_barrier(
        (beside_second, across_first, points_two, *totals)
    )
    totals = product([beside_first, beside_second], feats, totals, span)
    totals = product([across_first, across_second], feats, totals, span)
    pieces = [first, second, beside_first, beside_second, across_first, across_second, *diagonal]
    for bit in range(2, row_count.bit_length() - 1):
        more = [swap(value, 1 << bit, 0) for value in pieces]
        totals = product(more, feats, totals, span)
        pieces += more
    other_points = swap(points_two, 0, 2)
    other_points, *totals = lax.optimization_barrier((other_points, *totals))
    (theirs,) = product(diagonal, feats[3:], totals[3:], span)
    from_sibling = swap(theirs, 1, 0)
    (mine,) = product(diagonal, feats[1:2], totals[1:2], span)
    outs = [(range(0, line - 2, 2), F32), (range(1, line - 2, 2), BF16)]
    kept, sent = add_up(mine, from_sibling, outs, span)
    sent, total = lax.optimization_barrier((sent, totals[2]))
    arrived = swap(sent, 0, 2)
    (theirs,) = product(diagonal, feats[2:3], [total], span)
    from_sibling = swap(theirs, 1, 0)
    (mine,) = product(diagonal, feats[:1], totals[:1], span)
    received = []
    chunks = list(range(2, line, 2))
    bit = 2
    while chunks:
        sent_places = [pos for pos, chunk in enumerate(chunks) if chunk & bit]
        kept_places = [pos for pos, chunk in enumerate(chunks) if not chunk & bit]
        outs = [(sent_places, BF16)] + [(kept_places, F32)] * (len(kept_places) > 0)
        sent, *kept = add_up(kept, arrived, outs, span, cost=LONG)
        arrived = swap(sent, 0, 2 * bit)
        received.append(arrived[:span] if len(sent_places) > 1 else arrived)
        if kept:
            (kept,) = kept
            arrived = arrived[span:]
        chunks = [chunks[pos] for pos in kept_places]
        bit *= 2
    own_sum, near_sent = add_up(mine, from_sibling, [([0], F32), ([1], BF16)], span, (sent,))
    received.append(swap(near_sent, 0, 2))
    later = top_couplings(points_two, other_points, picks, gain)

    leaf_interp, interp_one, skeleton, reduced, sent = leaves(
        own_sum, received, first, picks, couplings_one, later, leaf_skeleton.shape[0]
    )
    got = [swap(sent, 0, bits) for bits in (1, 2, 3)]
    upper_interp, top_state = upper_levels(
        skeleton, reduced, got, picks, (couplings_two, *later), interp_one
    )
    return jnp.swapaxes(leaf_interp, 1, 2), jnp.swapaxes(upper_interp, 2, 3), top_state


def solution(mesh):
    placed = (
        P(None, ("row", "col"), None),
        P(None, None, ("row", "col")),
        P(("row", "col"), None),
        P(("row", "col"), None),
        P("row", None),
        P("row", None),
    )
    return jax.shard_map(
        local,
        mesh=mesh,
        in_specs=placed,
        out_specs=(
            P(("row", "col"), None, None),
            P(None, ("row", "col"), None, None),
            P(None, ("row", "col"), None, None),
        ),
        check_vma=False,
    )
```

```python
import math

import jax
import jax.numpy as jnp
from jax import lax
from jax.experimental import pallas as pl
from jax.experimental.pallas import tpu as pltpu
from jax.sharding import PartitionSpec as P

LEAF = 128
F32 = jnp.float32
BF16 = jnp.bfloat16
DOUBLINGS = 9
VMEM = pl.BlockSpec(memory_space=pltpu.VMEM)


def vmem(shape, kind=F32):
    return pltpu.VMEM(tuple(shape), kind)


COST = pl.CostEstimate(flops=10**9, bytes_accessed=0, transcendentals=0)
LONG = pl.CostEstimate(flops=10**10, bytes_accessed=0, transcendentals=0)
PARAMS = pltpu.CompilerParams(vmem_limit_bytes=16 << 20)


def chebyshev_constants():
    taus = [1282.0 / 1280.0]
    for _ in range(DOUBLINGS):
        taus.append(2.0 * taus[-1] * taus[-1] - 1.0)
    front = 2.0**DOUBLINGS * math.prod(taus[:-1]) / taus[-1]
    return taus[:-1], front


TAUS, FRONT = chebyshev_constants()


def over(first, second, first_dim, second_dim):
    return lax.dot_general(
        first,
        second,
        (((first_dim,), (second_dim,)), ((), ())),
        preferred_element_type=F32,
    )


def split(value):
    high = value.astype(BF16)
    rest = value - high.astype(F32)
    middle = rest.astype(BF16)
    return high, middle, (rest - middle.astype(F32)).astype(BF16)


def norm_rows(norm, first, width):
    parts = [part.astype(F32) for part in split(norm)]
    place = lax.broadcasted_iota(jnp.int32, (16, width), 0)
    extra = jnp.where(place < 6, 1.0, 0.0)
    for pos in range(3):
        extra = jnp.where(place == pos + first, parts[pos], extra)
    return extra


def row_features(feats, gain):
    feats = feats.astype(F32)
    depth, width = feats.shape
    unit = math.log2(math.e) / (2.0 * depth)
    norm = jnp.sum(feats * feats, axis=0, keepdims=True) * -unit + math.log2(gain)
    parts = [part.astype(F32) for part in split(feats * (2.0 * unit))]
    return jnp.concatenate([*parts, norm_rows(norm, 0, width)], axis=0)


def col_features(feats):
    feats = feats.astype(F32)
    depth, width = feats.shape
    unit = math.log2(math.e) / (2.0 * depth)
    norm = jnp.sum(feats * feats, axis=0, keepdims=True) * -unit
    return jnp.concatenate([feats, feats, feats, norm_rows(norm, 3, width)], axis=0).astype(BF16)


def pack_body(*refs):
    probes_ref, points_ref, *table_refs = refs[:6]
    first_ref, second_ref, own_ref, held_ref, rows_ref, *held_tables, sem = refs[6:]
    span = probes_ref.shape[1]
    pairs = [(points_ref, held_ref), *zip(table_refs, held_tables)]
    small = len(pairs)
    for quarter in range(4):
        target = (first_ref, second_ref)[quarter // 2].at[pl.ds(quarter % 2 * span, span)]
        pairs.append((probes_ref.at[quarter], target))
    copies = [
        pltpu.make_async_copy(source, target, sem.at[pos])
        for pos, (source, target) in enumerate(pairs)
    ]
    for copy in copies:
        copy.start()
    rows_ref[...] = jnp.zeros_like(rows_ref)
    for copy in copies[:small]:
        copy.wait()
    points = held_ref[...].astype(F32)
    for quarter in range(4):
        feats = points[:, quarter, :].astype(BF16)
        half_ref = (first_ref, second_ref)[quarter // 2]
        half_ref[pl.ds(2 * span + quarter % 2 * 16, 16), :] = feats
        if quarter == 0:
            own_ref[...] = feats
    start = 0
    for table in held_tables:
        count, rank = table.shape
        rows_ref[pl.ds(start, count), pl.ds(0, rank)] = table[...].astype(F32)
        start += count
    first_ref[pl.ds(second_ref.shape[0], rows_ref.shape[0]), :] = rows_ref[...].astype(BF16)
    for copy in copies[small:]:
        copy.wait()


def pack(probes, points, tables):
    _, span, samples = probes.shape
    table_rows = -(-sum(table.shape[0] for table in tables) // 16) * 16
    inputs = (probes, points, *tables)
    return pl.pallas_call(
        pack_body,
        out_shape=(
            vmem((2 * (span + 16) + table_rows, samples), BF16),
            vmem((2 * (span + 16), samples), BF16),
            vmem((16, span), BF16),
        ),
        in_specs=[pl.BlockSpec(memory_space=pltpu.HBM)] * len(inputs),
        scratch_shapes=[
            pltpu.VMEM(points.shape, BF16),
            pltpu.VMEM((table_rows, samples), F32),
            *[pltpu.VMEM(table.shape, jnp.int32) for table in tables],
            pltpu.SemaphoreType.DMA((5 + len(tables),)),
        ],
        cost_estimate=COST,
        compiler_params=PARAMS,
        name="pack",
    )(*(pltpu.with_memory_space_constraint(value, pltpu.HBM) for value in inputs))


def masked(entries):
    shape = entries.shape
    row_leaf = lax.broadcasted_iota(jnp.int32, shape, 0) // LEAF
    col_leaf = lax.broadcasted_iota(jnp.int32, shape, 1) // LEAF
    return jnp.where(row_leaf == col_leaf, 0.0, entries)


def add_halves(half_refs, row_refs, cols_ref, put, span, own):
    for number, half_ref in enumerate(half_refs):
        for quarter in range(2):
            feats = half_ref[pl.ds(2 * span + 16 * quarter, 16), :]
            cols_ref[:, pl.ds((2 * number + quarter) * span, span)] = col_features(feats)
    columns = 2 * span * len(half_refs)
    for group, rows_ref in enumerate(row_refs):
        for start in range(0, rows_ref.shape[0], span):
            feats = rows_ref[pl.ds(start, span), :]
            entries = jnp.exp2(over(feats, cols_ref[:, :columns], 1, 0))
            if own and group == 0 and start == 0:
                entries = jnp.concatenate([masked(entries[:, :span]), entries[:, span:]], axis=1)
            randoms = [half_ref[pl.ds(0, 2 * span), :] for half_ref in half_refs]
            put(group, start, over(entries.astype(BF16), jnp.concatenate(randoms, axis=0), 1, 0))


def first_product_body(gain, span, groups, point_count, *refs):
    half_refs, point_refs = refs[:2], refs[2 : point_count + 2]
    row_refs = refs[point_count + 2 : point_count + 2 + len(groups)]
    total_refs, cols_ref = refs[point_count + 2 + len(groups) : -1], refs[-1]
    for rows_ref, places in zip(row_refs, groups):
        for pos, (array, start) in enumerate(places):
            feats = point_refs[array][:, pl.ds(start, span)]
            rows_ref[pl.ds(pos * span, span), :] = row_features(feats, gain).T.astype(BF16)

    def put(group, start, value):
        total_refs[group][pl.ds(start, span), :] = value

    add_halves(half_refs, row_refs, cols_ref, put, span, True)


def first_product(halves, points, groups, span, gain):
    samples = halves[0].shape[1]
    rows = [len(places) * span for places in groups]
    out = pl.pallas_call(
        lambda *refs: first_product_body(gain, span, groups, len(points), *refs),
        out_shape=[vmem((count, 64), BF16) for count in rows]
        + [vmem((count, samples), F32) for count in rows],
        scratch_shapes=[pltpu.VMEM((64, 4 * span), BF16)],
        cost_estimate=COST,
        compiler_params=PARAMS,
        name="first_product",
    )(*halves, *points)
    return out[: len(groups)], out[len(groups) :]


def product_body(span, half_count, count, *refs):
    half_refs, refs = refs[:half_count], refs[half_count:]
    row_refs, old_refs, total_refs = refs[:count], refs[count : 2 * count], refs[2 * count : -1]
    cols_ref = refs[-1]
    for number in range(0, half_count, 2):

        def put(group, start, value):
            place = pl.ds(start, span)
            base = old_refs if number == 0 else total_refs
            total_refs[group][place, :] = base[group][place, :] + value

        add_halves(half_refs[number : number + 2], row_refs, cols_ref, put, span, False)


def product(halves, rows, totals, span):
    return pl.pallas_call(
        lambda *refs: product_body(span, len(halves), len(rows), *refs),
        out_shape=[vmem(total.shape, F32) for total in totals],
        scratch_shapes=[pltpu.VMEM((64, 4 * span), BF16)],
        cost_estimate=COST,
        compiler_params=PARAMS,
        name="product",
    )(*halves, *rows, *totals)


def add_up_body(span, outs, mine_ref, theirs_ref, *refs):
    for (chunks, _), out_ref in zip(outs, refs[-len(outs) :]):
        for pos, chunk in enumerate(chunks):
            place = pl.ds(chunk * span, span)
            value = mine_ref[place, :] + theirs_ref[place, :].astype(F32)
            out_ref[pl.ds(pos * span, span), :] = value.astype(out_ref.dtype)


def add_up(mine, theirs, outs, span, after=(), cost=COST):
    samples = mine.shape[1]
    return pl.pallas_call(
        lambda *refs: add_up_body(span, outs, *refs),
        out_shape=[vmem((len(chunks) * span, samples), kind) for chunks, kind in outs],
        cost_estimate=cost,
        compiler_params=PARAMS,
        name="add_up",
    )(mine, theirs, *after)


def wide_product(first, second, second_dim):
    high, middle, low = split(first)
    other_high, other_middle, other_low = split(second)
    return over(
        jnp.concatenate([high, high, middle, middle, low, high], axis=1),
        jnp.concatenate(
            [other_high, other_middle, other_high, other_middle, other_high, other_low],
            axis=second_dim,
        ),
        1,
        second_dim,
    )


def exact_product(first, second):
    second = second.astype(BF16)
    return over(
        jnp.concatenate(split(first), axis=1), jnp.concatenate([second] * 3, axis=0), 1, 0
    )


def twice_product(twice_parts, parts):
    high, middle, low = twice_parts
    other_high, other_middle, other_low = parts
    left = lax.broadcasted_iota(jnp.int32, high.shape, 1) < high.shape[1] // 2
    last = jnp.where(left, low.astype(F32), high.astype(F32)).astype(BF16)
    return over(
        jnp.concatenate([high, middle, last], axis=1),
        jnp.concatenate(
            [other_high, other_middle, other_high, other_middle, other_high, other_low], axis=0
        ),
        1,
        0,
    )


def select_rows(picks, value):
    return over(
        jnp.concatenate([picks] * 3, axis=1), jnp.concatenate(split(value), axis=0), 1, 0
    )


def interpolate(stacks, skeletons):
    rank, pool = skeletons[0].shape[0], stacks[0].shape[0]
    place = lax.broadcasted_iota(jnp.int32, (rank, 2 * rank), 0)
    other = lax.broadcasted_iota(jnp.int32, (rank, 2 * rank), 1)
    eyes = jnp.where((other == place) | (other == place + rank), 1.0, 0.0)
    states = []
    for skeleton, stack in zip(skeletons, stacks):
        products = wide_product(skeleton, jnp.concatenate([stack, skeleton, skeleton], axis=0), 1)
        ridge = 0.05 * jnp.sum(skeleton * skeleton, keepdims=True) / rank + 1e-05
        inverse = 1.0 / (640.0 * ridge)
        states.append((products[:, :pool], eyes - products[:, pool:] * inverse, inverse))
    for number, tau in enumerate(TAUS):
        last = number == DOUBLINGS - 1
        later = []
        for solved, power, inverse in states:
            power_parts = split(power)
            parts = split(solved)
            if not last:
                parts = [jnp.concatenate(pair, axis=1) for pair in zip(parts, power_parts)]
            both = twice_product(power_parts, parts)
            solved = solved + both[:, :pool] * (1.0 / tau)
            later.append((solved, None if last else 2.0 * both[:, pool:] - eyes, inverse))
        states = later
    return [solved * (inverse * FRONT) for solved, _, inverse in states]


def merge(nodes, early=None):
    stacks, skeletons = [], []
    for samples, reduced, coupling, picks in nodes:
        pool = samples.shape[0]
        high, middle, low = split(reduced)
        coupled = over(
            coupling, jnp.concatenate([high, middle, high, middle, high, low], axis=0), 1, 0
        )
        stacks.append(samples - coupled[:pool])
        skeletons.append(select_rows(picks, samples) - coupled[pool:])
    if early is not None:
        early(skeletons[0])
    interps = interpolate(stacks, skeletons)
    return [
        (interp, skeleton, wide_product(interp, node[1], 0))
        for interp, skeleton, node in zip(interps, skeletons, nodes)
    ]


def leaves_body(received, *refs):
    own_ref, *others = refs[: received + 1]
    source_ref, picks_ref, couplings_ref = refs[received + 1 : received + 4]
    leaf_ref, upper_ref, skeleton_ref, reduced_ref, sent_ref, held_ref, sem = refs[-7:]
    total = own_ref[...]
    for other in others:
        total = total + other[...].astype(F32)
    count = total.shape[0] // LEAF
    stacks = [total[leaf * LEAF : (leaf + 1) * LEAF] for leaf in range(count)]
    skeletons = [select_rows(picks_ref[leaf], stack) for leaf, stack in enumerate(stacks)]
    reduced = []
    for leaf, interp in enumerate(interpolate(stacks, skeletons)):
        held_ref[leaf] = interp
        reduced.append(exact_product(interp, source_ref[pl.ds(leaf * LEAF, LEAF), :]))
    copy = pltpu.make_async_copy(held_ref, leaf_ref, sem)
    copy.start()
    node = (
        jnp.concatenate(skeletons, axis=0),
        jnp.concatenate(reduced, axis=0),
        couplings_ref[...],
        picks_ref[count],
    )
    ((interp, skeleton, reduced),) = merge([node])
    upper_ref[...] = interp
    skeleton_ref[...] = skeleton
    reduced_ref[...] = reduced
    for pos, part in enumerate((*split(skeleton)[:2], reduced.astype(BF16))):
        sent_ref[pl.ds(pos * skeleton.shape[0], skeleton.shape[0]), :] = part
    copy.wait()


def leaves(own, others, source, picks, couplings, later, leaf_count):
    samples = own.shape[1]
    rank, pool = picks.shape[1:]
    return pl.pallas_call(
        lambda *refs: leaves_body(len(others), *refs),
        out_shape=(
            jax.ShapeDtypeStruct((leaf_count, rank, LEAF), F32),
            vmem((rank, pool), F32),
            vmem((rank, samples), F32),
            vmem((rank, samples), F32),
            vmem((3 * rank, samples), BF16),
        ),
        out_specs=(pl.BlockSpec(memory_space=pl.ANY), VMEM, VMEM, VMEM, VMEM),
        scratch_shapes=[pltpu.VMEM((leaf_count, rank, LEAF), F32), pltpu.SemaphoreType.DMA],
        cost_estimate=COST,
        compiler_params=PARAMS,
        name="leaves",
    )(own, *others, source, picks, couplings, *later)


def first_of_pair(number):
    return (lax.axis_index("col") >> (number - 2)) % 2 == 0


def pair(mine, theirs, mine_first):
    first = jnp.where(mine_first, mine, theirs)
    second = jnp.where(mine_first, theirs, mine)
    return jnp.concatenate([first, second], axis=0)


def upper_body(picks_count, *refs):
    states = [(refs[0][...], refs[1][...])]
    rank = refs[0].shape[0]
    for got_ref in refs[2:5]:
        high, middle, reduced = (got_ref[pl.ds(pos * rank, rank), :] for pos in range(3))
        states.append((high.astype(F32) + middle.astype(F32), reduced.astype(F32)))
    picks_ref, two_ref, other_ref, three_ref, one_ref, upper_out, top_out = refs[5:12]
    upper_ref, state_ref, sem = refs[12:]
    places = [
        (one_ref, upper_out.at[0, 0]),
        (upper_ref.at[0], upper_out.at[1, 0]),
        (upper_ref.at[1], upper_out.at[2, 0]),
        (state_ref.at[0], top_out.at[0, 0]),
        (state_ref.at[1], top_out.at[1, 0]),
    ]
    copies = [
        pltpu.make_async_copy(source, target, sem.at[pos])
        for pos, (source, target) in enumerate(places)
    ]
    copies[0].start()
    mine_first = first_of_pair(2)
    nodes = []
    for number, coupling_ref in enumerate((two_ref, other_ref)):
        mine, theirs = states[2 * number : 2 * number + 2]
        picks = picks_ref[picks_count - 3 + number]
        stacks = [pair(*parts, mine_first) for parts in zip(mine, theirs)]
        nodes.append((*stacks, coupling_ref[...], picks))
    mine, theirs = merge(nodes)
    upper_ref[0] = mine[0]
    copies[1].start()

    def early(skeleton):
        state_ref[0] = skeleton
        copies[3].start()

    mine_first = first_of_pair(3)
    stacks = [pair(*parts, mine_first) for parts in zip(mine[1:], theirs[1:])]
    ((interp, _, reduced),) = merge([(*stacks, three_ref[...], picks_ref[picks_count - 1])], early)
    upper_ref[1] = interp
    copies[2].start()
    state_ref[1] = reduced
    copies[4].start()
    for copy in copies:
        copy.wait()


def upper_levels(skeleton, reduced, got, picks, couplings, interp_one):
    rank, pool = picks.shape[1:]
    samples = skeleton.shape[1]
    return pl.pallas_call(
        lambda *refs: upper_body(picks.shape[0], *refs),
        out_shape=(
            jax.ShapeDtypeStruct((3, 1, rank, pool), F32),
            jax.ShapeDtypeStruct((2, 1, rank, samples), F32),
        ),
        out_specs=(pl.BlockSpec(memory_space=pl.ANY),) * 2,
        scratch_shapes=[
            pltpu.VMEM((2, rank, pool), F32),
            pltpu.VMEM((2, rank, samples), F32),
            pltpu.SemaphoreType.DMA((5,)),
        ],
        cost_estimate=COST,
        compiler_params=PARAMS,
        name="upper_levels",
    )(skeleton, reduced, *got, picks, *couplings, interp_one)


def one_hot(chosen, pool):
    place = lax.broadcasted_iota(jnp.int32, (pool, chosen.shape[1]), 0)
    return jnp.where(place.astype(F32) == chosen, 1.0, 0.0).astype(F32)


def couple(first, second, picks, gain, couplings_ref):
    rank = first.shape[1]
    points = jnp.concatenate([first, second], axis=1)
    entries = jnp.exp2(over(row_features(points, gain).astype(BF16), col_features(points), 0, 0))
    left = lax.broadcasted_iota(jnp.int32, entries.shape, 1) < rank
    upper = lax.broadcasted_iota(jnp.int32, entries.shape, 0) < rank
    entries = jnp.where(left == upper, 0.0, entries)
    chosen = select_rows(picks.T.astype(BF16), entries)
    high, middle, low = split(jnp.concatenate([entries, chosen], axis=0))
    couplings_ref[...] = jnp.concatenate([high, high, middle, middle, low, high], axis=1)


def coupling_shape(rank):
    return vmem((3 * rank, 12 * rank), BF16)


def skeletons_body(gain, span, counts, mine_ref, beside_ref, *refs):
    picks_ref, one_ref, two_ref, points_ref = refs
    rank, pool = picks_ref.shape[1:]
    leaf_count = counts[0]
    tables = 2 * (span + 16)
    nodes = []
    for source_ref in (mine_ref, beside_ref):
        rows = source_ref[pl.ds(tables, source_ref.shape[0] - tables), :rank].astype(F32)
        hots = [one_hot(rows[pos : pos + 1], pool) for pos in range(leaf_count + 1)]
        children = []
        for leaf in range(leaf_count):
            feats = source_ref[pl.ds(2 * span, 16), pl.ds(leaf * LEAF, LEAF)]
            children.append(over(feats, hots[leaf].astype(BF16), 1, 0))
        points = jnp.concatenate(children, axis=1)
        nodes.append(over(points, hots[leaf_count], 1, 0))
        if source_ref is mine_ref:
            couple(*children, hots[leaf_count], gain, one_ref)
            start = leaf_count + counts[1]
            level_two = lax.axis_index("col") // 2
            wanted = [level_two, level_two + 1 - 2 * (level_two % 2), counts[2] + level_two // 2]
            for row in wanted:
                place = lax.broadcasted_iota(jnp.int32, rows.shape, 0)
                named = jnp.where(place == start + row, rows, 0.0)
                hots.append(one_hot(jnp.sum(named, axis=0, keepdims=True), pool))
            for number, hot in enumerate(hots):
                picks_ref[number] = hot.T.astype(BF16)
            upper = hots[leaf_count + 1]
    mine, theirs = nodes
    mine_first = first_of_pair(2)
    first = jnp.where(mine_first, mine, theirs)
    second = jnp.where(mine_first, theirs, mine)
    couple(first, second, upper, gain, two_ref)
    points_ref[...] = jnp.concatenate([first, second], axis=1).astype(BF16)


def skeletons(packed, beside, tables, span, gain):
    leaf_count, rank = tables[0].shape
    counts = [table.shape[0] for table in tables]
    return pl.pallas_call(
        lambda *refs: skeletons_body(gain, span, counts, *refs),
        out_shape=(
            vmem((leaf_count + 4, rank, LEAF), BF16),
            coupling_shape(rank),
            coupling_shape(rank),
            vmem((16, 2 * rank), BF16),
        ),
        cost_estimate=COST,
        compiler_params=PARAMS,
        name="skeletons",
    )(packed, beside)


def top_couplings_body(gain, mine_ref, theirs_ref, picks_ref, other_ref, three_ref):
    count, rank, _ = picks_ref.shape
    picks = [picks_ref[count - pos].astype(F32).T for pos in (3, 2, 1)]
    mine, theirs = mine_ref[...].astype(F32), theirs_ref[...].astype(F32)
    couple(theirs[:, :rank], theirs[:, rank:], picks[1], gain, other_ref)
    mine, theirs = over(mine, picks[0], 1, 0), over(theirs, picks[1], 1, 0)
    mine_first = first_of_pair(3)
    first = jnp.where(mine_first, mine, theirs)
    second = jnp.where(mine_first, theirs, mine)
    couple(first, second, picks[2], gain, three_ref)


def top_couplings(mine, theirs, picks, gain):
    return pl.pallas_call(
        lambda *refs: top_couplings_body(gain, *refs),
        out_shape=[coupling_shape(picks.shape[1])] * 2,
        cost_estimate=COST,
        compiler_params=PARAMS,
        name="top_couplings",
    )(mine, theirs, picks)


def local(probes, points, leaf_skeleton, skeleton_one, skeleton_two, skeleton_three):
    span = probes.shape[1]
    row_count = lax.axis_size("row")
    col_count = lax.axis_size("col")
    gain = 16.0 / math.sqrt(4 * span * row_count * col_count)

    def swap(value, row_bits, col_bits):
        pairs = [
            (r * col_count + c, (r ^ row_bits) * col_count + (c ^ col_bits))
            for r in range(row_count)
            for c in range(col_count)
        ]
        return lax.ppermute(value, ("row", "col"), pairs)

    tables = (leaf_skeleton, skeleton_one, skeleton_two, skeleton_three)
    first, second, own_points = pack(probes, points, tables)
    beside_first, across_second = swap(first, 0, 1), swap(second, 2, 0)
    line = col_count // 2
    line_points = own_points
    for bit in range(1, col_count.bit_length() - 1):
        line_points = jnp.concatenate([line_points, swap(line_points, 0, 1 << bit)], axis=1)
        if bit == 1:
            line_points, *late = lax.optimization_barrier((line_points, first, second))
    beside_second, across_first = swap(late[1], 0, 1), swap(late[0], 2, 0)
    line_points = [line_points, swap(line_points, 1, 0)]
    near, far = range(2), range(2, line)
    groups = [
        [(core, chunk * span) for chunk in group] for core in range(2) for group in (near, far)
    ]
    feats, totals = first_product((first, second), line_points, groups, span, gain)
    beside_first, across_second, *totals = lax.optimization_barrier(
        (beside_first, across_second, *totals)
    )
    diagonal = [swap(beside_first, 2, 0), swap(across_second, 0, 1)]
    picks, couplings_one, couplings_two, points_two = skeletons(
        first, beside_first, tables, span, gain
    )
    beside_second, across_first, points_two, *totals = lax.optimization_barrier(
        (beside_second, across_first, points_two, *totals)
    )
    totals = product([beside_first, beside_second], feats, totals, span)
    totals = product([across_first, across_second], feats, totals, span)
    pieces = [first, second, beside_first, beside_second, across_first, across_second, *diagonal]
    for bit in range(2, row_count.bit_length() - 1):
        more = [swap(value, 1 << bit, 0) for value in pieces]
        totals = product(more, feats, totals, span)
        pieces += more
    (theirs,) = product(diagonal, feats[3:], totals[3:], span)
    from_sibling = swap(theirs, 1, 0)
    (mine,) = product(diagonal, feats[1:2], totals[1:2], span)
    outs = [(range(0, line - 2, 2), F32), (range(1, line - 2, 2), BF16)]
    kept, sent = add_up(mine, from_sibling, outs, span)
    sent, total = lax.optimization_barrier((sent, totals[2]))
    arrived = swap(sent, 0, 2)
    (theirs,) = product(diagonal, feats[2:3], [total], span)
    from_sibling = swap(theirs, 1, 0)
    (mine,) = product(diagonal, feats[:1], totals[:1], span)
    received = []
    chunks = list(range(2, line, 2))
    bit = 2
    while chunks:
        sent_places = [pos for pos, chunk in enumerate(chunks) if chunk & bit]
        kept_places = [pos for pos, chunk in enumerate(chunks) if not chunk & bit]
        outs = [(sent_places, BF16)] + [(kept_places, F32)] * (len(kept_places) > 0)
        sent, *kept = add_up(kept, arrived, outs, span, cost=LONG)
        arrived = swap(sent, 0, 2 * bit)
        received.append(arrived[:span] if len(sent_places) > 1 else arrived)
        if kept:
            (kept,) = kept
            arrived = arrived[span:]
        chunks = [chunks[pos] for pos in kept_places]
        bit *= 2
    own_sum, near_sent = add_up(mine, from_sibling, [([0], F32), ([1], BF16)], span, (sent,))
    received.append(swap(near_sent, 0, 2))
    points_two, near_sent = lax.optimization_barrier((points_two, near_sent))
    other_points = swap(points_two, 0, 2)
    later = top_couplings(points_two, other_points, picks, gain)

    leaf_interp, interp_one, skeleton, reduced, sent = leaves(
        own_sum, received, first, picks, couplings_one, later, leaf_skeleton.shape[0]
    )
    got = [swap(sent, 0, bits) for bits in (1, 2, 3)]
    upper_interp, top_state = upper_levels(
        skeleton, reduced, got, picks, (couplings_two, *later), interp_one
    )
    return jnp.swapaxes(leaf_interp, 1, 2), jnp.swapaxes(upper_interp, 2, 3), top_state


def solution(mesh):
    placed = (
        P(None, ("row", "col"), None),
        P(None, None, ("row", "col")),
        P(("row", "col"), None),
        P(("row", "col"), None),
        P("row", None),
        P("row", None),
    )
    return jax.shard_map(
        local,
        mesh=mesh,
        in_specs=placed,
        out_specs=(
            P(("row", "col"), None, None),
            P(None, ("row", "col"), None, None),
            P(None, ("row", "col"), None, None),
        ),
        check_vma=False,
    )
```

```python
import math

import jax
import jax.numpy as jnp
from jax import lax
from jax.experimental import pallas as pl
from jax.experimental.pallas import tpu as pltpu
from jax.sharding import PartitionSpec as P

LEAF = 128
F32 = jnp.float32
BF16 = jnp.bfloat16
DOUBLINGS = 9
VMEM = pl.BlockSpec(memory_space=pltpu.VMEM)


def vmem(shape, kind=F32):
    return pltpu.VMEM(tuple(shape), kind)


COST = pl.CostEstimate(flops=10**9, bytes_accessed=0, transcendentals=0)
LONG = pl.CostEstimate(flops=10**10, bytes_accessed=0, transcendentals=0)
PARAMS = pltpu.CompilerParams(vmem_limit_bytes=16 << 20)


def chebyshev_constants():
    taus = [1282.0 / 1280.0]
    for _ in range(DOUBLINGS):
        taus.append(2.0 * taus[-1] * taus[-1] - 1.0)
    front = 2.0**DOUBLINGS * math.prod(taus[:-1]) / taus[-1]
    return taus[:-1], front


TAUS, FRONT = chebyshev_constants()


def over(first, second, first_dim, second_dim):
    return lax.dot_general(
        first,
        second,
        (((first_dim,), (second_dim,)), ((), ())),
        preferred_element_type=F32,
    )


def split(value):
    high = value.astype(BF16)
    rest = value - high.astype(F32)
    middle = rest.astype(BF16)
    return high, middle, (rest - middle.astype(F32)).astype(BF16)


def norm_rows(norm, first, width):
    parts = [part.astype(F32) for part in split(norm)]
    place = lax.broadcasted_iota(jnp.int32, (16, width), 0)
    extra = jnp.where(place < 6, 1.0, 0.0)
    for pos in range(3):
        extra = jnp.where(place == pos + first, parts[pos], extra)
    return extra


def row_features(feats, gain):
    feats = feats.astype(F32)
    depth, width = feats.shape
    unit = math.log2(math.e) / (2.0 * depth)
    norm = jnp.sum(feats * feats, axis=0, keepdims=True) * -unit + math.log2(gain)
    parts = [part.astype(F32) for part in split(feats * (2.0 * unit))]
    return jnp.concatenate([*parts, norm_rows(norm, 0, width)], axis=0)


def col_features(feats):
    feats = feats.astype(F32)
    depth, width = feats.shape
    unit = math.log2(math.e) / (2.0 * depth)
    norm = jnp.sum(feats * feats, axis=0, keepdims=True) * -unit
    return jnp.concatenate([feats, feats, feats, norm_rows(norm, 3, width)], axis=0).astype(BF16)


def pack_body(*refs):
    probes_ref, points_ref, *table_refs = refs[:6]
    first_ref, second_ref, own_ref, held_ref, rows_ref, *held_tables, sem = refs[6:]
    span = probes_ref.shape[1]
    pairs = [(points_ref, held_ref), *zip(table_refs, held_tables)]
    small = len(pairs)
    for quarter in range(4):
        target = (first_ref, second_ref)[quarter // 2].at[pl.ds(quarter % 2 * span, span)]
        pairs.append((probes_ref.at[quarter], target))
    copies = [
        pltpu.make_async_copy(source, target, sem.at[pos])
        for pos, (source, target) in enumerate(pairs)
    ]
    for copy in copies:
        copy.start()
    rows_ref[...] = jnp.zeros_like(rows_ref)
    for copy in copies[:small]:
        copy.wait()
    points = held_ref[...].astype(F32)
    for quarter in range(4):
        feats = points[:, quarter, :].astype(BF16)
        half_ref = (first_ref, second_ref)[quarter // 2]
        half_ref[pl.ds(2 * span + quarter % 2 * 16, 16), :] = feats
        if quarter == 0:
            own_ref[...] = feats
    start = 0
    for table in held_tables:
        count, rank = table.shape
        rows_ref[pl.ds(start, count), pl.ds(0, rank)] = table[...].astype(F32)
        start += count
    first_ref[pl.ds(second_ref.shape[0], rows_ref.shape[0]), :] = rows_ref[...].astype(BF16)
    for copy in copies[small:]:
        copy.wait()


def pack(probes, points, tables):
    _, span, samples = probes.shape
    table_rows = -(-sum(table.shape[0] for table in tables) // 16) * 16
    inputs = (probes, points, *tables)
    return pl.pallas_call(
        pack_body,
        out_shape=(
            vmem((2 * (span + 16) + table_rows, samples), BF16),
            vmem((2 * (span + 16), samples), BF16),
            vmem((16, span), BF16),
        ),
        in_specs=[pl.BlockSpec(memory_space=pltpu.HBM)] * len(inputs),
        scratch_shapes=[
            pltpu.VMEM(points.shape, BF16),
            pltpu.VMEM((table_rows, samples), F32),
            *[pltpu.VMEM(table.shape, jnp.int32) for table in tables],
            pltpu.SemaphoreType.DMA((5 + len(tables),)),
        ],
        cost_estimate=COST,
        compiler_params=PARAMS,
        name="pack",
    )(*(pltpu.with_memory_space_constraint(value, pltpu.HBM) for value in inputs))


def masked(entries):
    shape = entries.shape
    row_leaf = lax.broadcasted_iota(jnp.int32, shape, 0) // LEAF
    col_leaf = lax.broadcasted_iota(jnp.int32, shape, 1) // LEAF
    return jnp.where(row_leaf == col_leaf, 0.0, entries)


def add_halves(half_refs, row_refs, cols_ref, put, span, own):
    for number, half_ref in enumerate(half_refs):
        for quarter in range(2):
            feats = half_ref[pl.ds(2 * span + 16 * quarter, 16), :]
            cols_ref[:, pl.ds((2 * number + quarter) * span, span)] = col_features(feats)
    columns = 2 * span * len(half_refs)
    for group, rows_ref in enumerate(row_refs):
        for start in range(0, rows_ref.shape[0], span):
            feats = rows_ref[pl.ds(start, span), :]
            entries = jnp.exp2(over(feats, cols_ref[:, :columns], 1, 0))
            if own and group == 0 and start == 0:
                entries = jnp.concatenate([masked(entries[:, :span]), entries[:, span:]], axis=1)
            randoms = [half_ref[pl.ds(0, 2 * span), :] for half_ref in half_refs]
            put(group, start, over(entries.astype(BF16), jnp.concatenate(randoms, axis=0), 1, 0))


def first_product_body(gain, span, groups, point_count, *refs):
    half_refs, point_refs = refs[:2], refs[2 : point_count + 2]
    row_refs = refs[point_count + 2 : point_count + 2 + len(groups)]
    total_refs, cols_ref = refs[point_count + 2 + len(groups) : -1], refs[-1]
    for rows_ref, places in zip(row_refs, groups):
        for pos, (array, start) in enumerate(places):
            feats = point_refs[array][:, pl.ds(start, span)]
            rows_ref[pl.ds(pos * span, span), :] = row_features(feats, gain).T.astype(BF16)

    def put(group, start, value):
        total_refs[group][pl.ds(start, span), :] = value

    add_halves(half_refs, row_refs, cols_ref, put, span, True)


def first_product(halves, points, groups, span, gain):
    samples = halves[0].shape[1]
    rows = [len(places) * span for places in groups]
    out = pl.pallas_call(
        lambda *refs: first_product_body(gain, span, groups, len(points), *refs),
        out_shape=[vmem((count, 64), BF16) for count in rows]
        + [vmem((count, samples), F32) for count in rows],
        scratch_shapes=[pltpu.VMEM((64, 4 * span), BF16)],
        cost_estimate=COST,
        compiler_params=PARAMS,
        name="first_product",
    )(*halves, *points)
    return out[: len(groups)], out[len(groups) :]


def product_body(span, half_count, count, *refs):
    half_refs, refs = refs[:half_count], refs[half_count:]
    row_refs, old_refs, total_refs = refs[:count], refs[count : 2 * count], refs[2 * count : -1]
    cols_ref = refs[-1]
    for number in range(0, half_count, 2):

        def put(group, start, value):
            place = pl.ds(start, span)
            base = old_refs if number == 0 else total_refs
            total_refs[group][place, :] = base[group][place, :] + value

        add_halves(half_refs[number : number + 2], row_refs, cols_ref, put, span, False)


def product(halves, rows, totals, span):
    return pl.pallas_call(
        lambda *refs: product_body(span, len(halves), len(rows), *refs),
        out_shape=[vmem(total.shape, F32) for total in totals],
        scratch_shapes=[pltpu.VMEM((64, 4 * span), BF16)],
        cost_estimate=COST,
        compiler_params=PARAMS,
        name="product",
    )(*halves, *rows, *totals)


def add_up_body(span, outs, mine_ref, theirs_ref, *refs):
    for (chunks, _), out_ref in zip(outs, refs[-len(outs) :]):
        for pos, chunk in enumerate(chunks):
            place = pl.ds(chunk * span, span)
            value = mine_ref[place, :] + theirs_ref[place, :].astype(F32)
            out_ref[pl.ds(pos * span, span), :] = value.astype(out_ref.dtype)


def add_up(mine, theirs, outs, span, after=(), cost=COST):
    samples = mine.shape[1]
    return pl.pallas_call(
        lambda *refs: add_up_body(span, outs, *refs),
        out_shape=[vmem((len(chunks) * span, samples), kind) for chunks, kind in outs],
        cost_estimate=cost,
        compiler_params=PARAMS,
        name="add_up",
    )(mine, theirs, *after)


def wide_product(first, second, second_dim):
    high, middle, low = split(first)
    other_high, other_middle, other_low = split(second)
    return over(
        jnp.concatenate([high, high, middle, middle, low, high], axis=1),
        jnp.concatenate(
            [other_high, other_middle, other_high, other_middle, other_high, other_low],
            axis=second_dim,
        ),
        1,
        second_dim,
    )


def exact_product(first, second):
    second = second.astype(BF16)
    return over(
        jnp.concatenate(split(first), axis=1), jnp.concatenate([second] * 3, axis=0), 1, 0
    )


def twice_product(twice_parts, parts):
    high, middle, low = twice_parts
    other_high, other_middle, other_low = parts
    left = lax.broadcasted_iota(jnp.int32, high.shape, 1) < high.shape[1] // 2
    last = jnp.where(left, low.astype(F32), high.astype(F32)).astype(BF16)
    return over(
        jnp.concatenate([high, middle, last], axis=1),
        jnp.concatenate(
            [other_high, other_middle, other_high, other_middle, other_high, other_low], axis=0
        ),
        1,
        0,
    )


def select_rows(picks, value):
    return over(
        jnp.concatenate([picks] * 3, axis=1), jnp.concatenate(split(value), axis=0), 1, 0
    )


def interpolate(stacks, skeletons):
    rank, pool = skeletons[0].shape[0], stacks[0].shape[0]
    place = lax.broadcasted_iota(jnp.int32, (rank, 2 * rank), 0)
    other = lax.broadcasted_iota(jnp.int32, (rank, 2 * rank), 1)
    eyes = jnp.where((other == place) | (other == place + rank), 1.0, 0.0)
    states = []
    for skeleton, stack in zip(skeletons, stacks):
        products = wide_product(skeleton, jnp.concatenate([stack, skeleton, skeleton], axis=0), 1)
        ridge = 0.05 * jnp.sum(skeleton * skeleton, keepdims=True) / rank + 1e-05
        inverse = 1.0 / (640.0 * ridge)
        states.append((products[:, :pool], eyes - products[:, pool:] * inverse, inverse))
    for number, tau in enumerate(TAUS):
        last = number == DOUBLINGS - 1
        later = []
        for solved, power, inverse in states:
            power_parts = split(power)
            parts = split(solved)
            if not last:
                parts = [jnp.concatenate(pair, axis=1) for pair in zip(parts, power_parts)]
            both = twice_product(power_parts, parts)
            solved = solved + both[:, :pool] * (1.0 / tau)
            later.append((solved, None if last else 2.0 * both[:, pool:] - eyes, inverse))
        states = later
    return [solved * (inverse * FRONT) for solved, _, inverse in states]


def merge(nodes, early=None):
    stacks, skeletons = [], []
    for samples, reduced, coupling, picks in nodes:
        pool = samples.shape[0]
        high, middle, low = split(reduced)
        coupled = over(
            coupling, jnp.concatenate([high, middle, high, middle, high, low], axis=0), 1, 0
        )
        stacks.append(samples - coupled[:pool])
        skeletons.append(select_rows(picks, samples) - coupled[pool:])
    if early is not None:
        early(skeletons[0])
    interps = interpolate(stacks, skeletons)
    return [
        (interp, skeleton, wide_product(interp, node[1], 0))
        for interp, skeleton, node in zip(interps, skeletons, nodes)
    ]


def leaves_body(received, *refs):
    own_ref, *others = refs[: received + 1]
    source_ref, picks_ref, couplings_ref = refs[received + 1 : received + 4]
    leaf_ref, upper_ref, skeleton_ref, reduced_ref, sent_ref, held_ref, sem = refs[-7:]
    total = own_ref[...]
    for other in others:
        total = total + other[...].astype(F32)
    count = total.shape[0] // LEAF
    stacks = [total[leaf * LEAF : (leaf + 1) * LEAF] for leaf in range(count)]
    skeletons = [select_rows(picks_ref[leaf], stack) for leaf, stack in enumerate(stacks)]
    reduced = []
    for leaf, interp in enumerate(interpolate(stacks, skeletons)):
        held_ref[leaf] = interp
        reduced.append(exact_product(interp, source_ref[pl.ds(leaf * LEAF, LEAF), :]))
    copy = pltpu.make_async_copy(held_ref, leaf_ref, sem)
    copy.start()
    node = (
        jnp.concatenate(skeletons, axis=0),
        jnp.concatenate(reduced, axis=0),
        couplings_ref[...],
        picks_ref[count],
    )
    ((interp, skeleton, reduced),) = merge([node])
    upper_ref[...] = interp
    skeleton_ref[...] = skeleton
    reduced_ref[...] = reduced
    for pos, part in enumerate((*split(skeleton)[:2], reduced.astype(BF16))):
        sent_ref[pl.ds(pos * skeleton.shape[0], skeleton.shape[0]), :] = part
    copy.wait()


def leaves(own, others, source, picks, couplings, later, leaf_count):
    samples = own.shape[1]
    rank, pool = picks.shape[1:]
    return pl.pallas_call(
        lambda *refs: leaves_body(len(others), *refs),
        out_shape=(
            jax.ShapeDtypeStruct((leaf_count, rank, LEAF), F32),
            vmem((rank, pool), F32),
            vmem((rank, samples), F32),
            vmem((rank, samples), F32),
            vmem((3 * rank, samples), BF16),
        ),
        out_specs=(pl.BlockSpec(memory_space=pl.ANY), VMEM, VMEM, VMEM, VMEM),
        scratch_shapes=[pltpu.VMEM((leaf_count, rank, LEAF), F32), pltpu.SemaphoreType.DMA],
        cost_estimate=COST,
        compiler_params=PARAMS,
        name="leaves",
    )(own, *others, source, picks, couplings, *later)


def first_of_pair(number):
    return (lax.axis_index("col") >> (number - 2)) % 2 == 0


def pair(mine, theirs, mine_first):
    first = jnp.where(mine_first, mine, theirs)
    second = jnp.where(mine_first, theirs, mine)
    return jnp.concatenate([first, second], axis=0)


def upper_body(picks_count, *refs):
    states = [(refs[0][...], refs[1][...])]
    rank = refs[0].shape[0]
    for got_ref in refs[2:5]:
        high, middle, reduced = (got_ref[pl.ds(pos * rank, rank), :] for pos in range(3))
        states.append((high.astype(F32) + middle.astype(F32), reduced.astype(F32)))
    picks_ref, two_ref, other_ref, three_ref, one_ref, upper_out, top_out = refs[5:12]
    upper_ref, state_ref, sem = refs[12:]
    places = [
        (one_ref, upper_out.at[0, 0]),
        (upper_ref.at[0], upper_out.at[1, 0]),
        (upper_ref.at[1], upper_out.at[2, 0]),
        (state_ref.at[0], top_out.at[0, 0]),
        (state_ref.at[1], top_out.at[1, 0]),
    ]
    copies = [
        pltpu.make_async_copy(source, target, sem.at[pos])
        for pos, (source, target) in enumerate(places)
    ]
    copies[0].start()
    mine_first = first_of_pair(2)
    nodes = []
    for number, coupling_ref in enumerate((two_ref, other_ref)):
        mine, theirs = states[2 * number : 2 * number + 2]
        picks = picks_ref[picks_count - 3 + number]
        stacks = [pair(*parts, mine_first) for parts in zip(mine, theirs)]
        nodes.append((*stacks, coupling_ref[...], picks))
    mine, theirs = merge(nodes)
    upper_ref[0] = mine[0]
    copies[1].start()

    def early(skeleton):
        state_ref[0] = skeleton
        copies[3].start()

    mine_first = first_of_pair(3)
    stacks = [pair(*parts, mine_first) for parts in zip(mine[1:], theirs[1:])]
    ((interp, _, reduced),) = merge([(*stacks, three_ref[...], picks_ref[picks_count - 1])], early)
    upper_ref[1] = interp
    copies[2].start()
    state_ref[1] = reduced
    copies[4].start()
    for copy in copies:
        copy.wait()


def upper_levels(skeleton, reduced, got, picks, couplings, interp_one):
    rank, pool = picks.shape[1:]
    samples = skeleton.shape[1]
    return pl.pallas_call(
        lambda *refs: upper_body(picks.shape[0], *refs),
        out_shape=(
            jax.ShapeDtypeStruct((3, 1, rank, pool), F32),
            jax.ShapeDtypeStruct((2, 1, rank, samples), F32),
        ),
        out_specs=(pl.BlockSpec(memory_space=pl.ANY),) * 2,
        scratch_shapes=[
            pltpu.VMEM((2, rank, pool), F32),
            pltpu.VMEM((2, rank, samples), F32),
            pltpu.SemaphoreType.DMA((5,)),
        ],
        cost_estimate=COST,
        compiler_params=PARAMS,
        name="upper_levels",
    )(skeleton, reduced, *got, picks, *couplings, interp_one)


def one_hot(chosen, pool):
    place = lax.broadcasted_iota(jnp.int32, (pool, chosen.shape[1]), 0)
    return jnp.where(place.astype(F32) == chosen, 1.0, 0.0).astype(F32)


def couple(first, second, picks, gain, couplings_ref):
    rank = first.shape[1]
    points = jnp.concatenate([first, second], axis=1)
    entries = jnp.exp2(over(row_features(points, gain).astype(BF16), col_features(points), 0, 0))
    left = lax.broadcasted_iota(jnp.int32, entries.shape, 1) < rank
    upper = lax.broadcasted_iota(jnp.int32, entries.shape, 0) < rank
    entries = jnp.where(left == upper, 0.0, entries)
    chosen = select_rows(picks.T.astype(BF16), entries)
    high, middle, low = split(jnp.concatenate([entries, chosen], axis=0))
    couplings_ref[...] = jnp.concatenate([high, high, middle, middle, low, high], axis=1)


def coupling_shape(rank):
    return vmem((3 * rank, 12 * rank), BF16)


def skeletons_body(gain, span, counts, mine_ref, beside_ref, *refs):
    picks_ref, one_ref, two_ref, points_ref = refs
    rank, pool = picks_ref.shape[1:]
    leaf_count = counts[0]
    tables = 2 * (span + 16)
    nodes = []
    for source_ref in (mine_ref, beside_ref):
        rows = source_ref[pl.ds(tables, source_ref.shape[0] - tables), :rank].astype(F32)
        hots = [one_hot(rows[pos : pos + 1], pool) for pos in range(leaf_count + 1)]
        children = []
        for leaf in range(leaf_count):
            feats = source_ref[pl.ds(2 * span, 16), pl.ds(leaf * LEAF, LEAF)]
            children.append(over(feats, hots[leaf].astype(BF16), 1, 0))
        points = jnp.concatenate(children, axis=1)
        nodes.append(over(points, hots[leaf_count], 1, 0))
        if source_ref is mine_ref:
            couple(*children, hots[leaf_count], gain, one_ref)
            start = leaf_count + counts[1]
            level_two = lax.axis_index("col") // 2
            wanted = [level_two, level_two + 1 - 2 * (level_two % 2), counts[2] + level_two // 2]
            for row in wanted:
                place = lax.broadcasted_iota(jnp.int32, rows.shape, 0)
                named = jnp.where(place == start + row, rows, 0.0)
                hots.append(one_hot(jnp.sum(named, axis=0, keepdims=True), pool))
            for number, hot in enumerate(hots):
                picks_ref[number] = hot.T.astype(BF16)
            upper = hots[leaf_count + 1]
    mine, theirs = nodes
    mine_first = first_of_pair(2)
    first = jnp.where(mine_first, mine, theirs)
    second = jnp.where(mine_first, theirs, mine)
    couple(first, second, upper, gain, two_ref)
    points_ref[...] = jnp.concatenate([first, second], axis=1).astype(BF16)


def skeletons(packed, beside, tables, span, gain):
    leaf_count, rank = tables[0].shape
    counts = [table.shape[0] for table in tables]
    return pl.pallas_call(
        lambda *refs: skeletons_body(gain, span, counts, *refs),
        out_shape=(
            vmem((leaf_count + 4, rank, LEAF), BF16),
            coupling_shape(rank),
            coupling_shape(rank),
            vmem((16, 2 * rank), BF16),
        ),
        cost_estimate=COST,
        compiler_params=PARAMS,
        name="skeletons",
    )(packed, beside)


def top_couplings_body(gain, mine_ref, theirs_ref, picks_ref, other_ref, three_ref):
    count, rank, _ = picks_ref.shape
    picks = [picks_ref[count - pos].astype(F32).T for pos in (3, 2, 1)]
    mine, theirs = mine_ref[...].astype(F32), theirs_ref[...].astype(F32)
    couple(theirs[:, :rank], theirs[:, rank:], picks[1], gain, other_ref)
    mine, theirs = over(mine, picks[0], 1, 0), over(theirs, picks[1], 1, 0)
    mine_first = first_of_pair(3)
    first = jnp.where(mine_first, mine, theirs)
    second = jnp.where(mine_first, theirs, mine)
    couple(first, second, picks[2], gain, three_ref)


def top_couplings(mine, theirs, picks, gain):
    return pl.pallas_call(
        lambda *refs: top_couplings_body(gain, *refs),
        out_shape=[coupling_shape(picks.shape[1])] * 2,
        cost_estimate=LONG,
        compiler_params=PARAMS,
        name="top_couplings",
    )(mine, theirs, picks)


def local(probes, points, leaf_skeleton, skeleton_one, skeleton_two, skeleton_three):
    span = probes.shape[1]
    row_count = lax.axis_size("row")
    col_count = lax.axis_size("col")
    gain = 16.0 / math.sqrt(4 * span * row_count * col_count)

    def swap(value, row_bits, col_bits):
        pairs = [
            (r * col_count + c, (r ^ row_bits) * col_count + (c ^ col_bits))
            for r in range(row_count)
            for c in range(col_count)
        ]
        return lax.ppermute(value, ("row", "col"), pairs)

    tables = (leaf_skeleton, skeleton_one, skeleton_two, skeleton_three)
    first, second, own_points = pack(probes, points, tables)
    beside_first, across_second = swap(first, 0, 1), swap(second, 2, 0)
    line = col_count // 2
    line_points = own_points
    for bit in range(1, col_count.bit_length() - 1):
        line_points = jnp.concatenate([line_points, swap(line_points, 0, 1 << bit)], axis=1)
        if bit == 1:
            line_points, *late = lax.optimization_barrier((line_points, first, second))
    beside_second, across_first = swap(late[1], 0, 1), swap(late[0], 2, 0)
    line_points = [line_points, swap(line_points, 1, 0)]
    near, far = range(2), range(2, line)
    groups = [
        [(core, chunk * span) for chunk in group] for core in range(2) for group in (near, far)
    ]
    feats, totals = first_product((first, second), line_points, groups, span, gain)
    beside_first, across_second, *totals = lax.optimization_barrier(
        (beside_first, across_second, *totals)
    )
    diagonal = [swap(beside_first, 2, 0), swap(across_second, 0, 1)]
    picks, couplings_one, couplings_two, points_two = skeletons(
        first, beside_first, tables, span, gain
    )
    beside_second, across_first, points_two, *totals = lax.optimization_barrier(
        (beside_second, across_first, points_two, *totals)
    )
    totals = product([beside_first, beside_second], feats, totals, span)
    totals = product([across_first, across_second], feats, totals, span)
    pieces = [first, second, beside_first, beside_second, across_first, across_second, *diagonal]
    for bit in range(2, row_count.bit_length() - 1):
        more = [swap(value, 1 << bit, 0) for value in pieces]
        totals = product(more, feats, totals, span)
        pieces += more
    (theirs,) = product(diagonal, feats[3:], totals[3:], span)
    from_sibling = swap(theirs, 1, 0)
    (mine,) = product(diagonal, feats[1:2], totals[1:2], span)
    outs = [(range(0, line - 2, 2), F32), (range(1, line - 2, 2), BF16)]
    kept, sent = add_up(mine, from_sibling, outs, span)
    sent, total, points_two = lax.optimization_barrier((sent, totals[2], points_two))
    arrived = swap(sent, 0, 2)
    (theirs,) = product(diagonal, feats[2:3], [total], span)
    from_sibling = swap(theirs, 1, 0)
    (mine,) = product(diagonal, feats[:1], totals[:1], span)
    received = []
    chunks = list(range(2, line, 2))
    bit = 2
    while chunks:
        sent_places = [pos for pos, chunk in enumerate(chunks) if chunk & bit]
        kept_places = [pos for pos, chunk in enumerate(chunks) if not chunk & bit]
        outs = [(sent_places, BF16)] + [(kept_places, F32)] * (len(kept_places) > 0)
        sent, *kept = add_up(kept, arrived, outs, span, cost=LONG)
        arrived = swap(sent, 0, 2 * bit)
        received.append(arrived[:span] if len(sent_places) > 1 else arrived)
        if kept:
            (kept,) = kept
            arrived = arrived[span:]
        chunks = [chunks[pos] for pos in kept_places]
        bit *= 2
    own_sum, near_sent = add_up(mine, from_sibling, [([0], F32), ([1], BF16)], span, (sent,))
    received.append(swap(near_sent, 0, 2))
    other_points = swap(points_two, 0, 2)
    later = top_couplings(points_two, other_points, picks, gain)

    leaf_interp, interp_one, skeleton, reduced, sent = leaves(
        own_sum, received, first, picks, couplings_one, later, leaf_skeleton.shape[0]
    )
    got = [swap(sent, 0, bits) for bits in (1, 2, 3)]
    upper_interp, top_state = upper_levels(
        skeleton, reduced, got, picks, (couplings_two, *later), interp_one
    )
    return jnp.swapaxes(leaf_interp, 1, 2), jnp.swapaxes(upper_interp, 2, 3), top_state


def solution(mesh):
    placed = (
        P(None, ("row", "col"), None),
        P(None, None, ("row", "col")),
        P(("row", "col"), None),
        P(("row", "col"), None),
        P("row", None),
        P("row", None),
    )
    return jax.shard_map(
        local,
        mesh=mesh,
        in_specs=placed,
        out_specs=(
            P(("row", "col"), None, None),
            P(None, ("row", "col"), None, None),
            P(None, ("row", "col"), None, None),
        ),
        check_vma=False,
    )
```

```python
import math

import jax
import jax.numpy as jnp
from jax import lax
from jax.experimental import pallas as pl
from jax.experimental.pallas import tpu as pltpu
from jax.sharding import PartitionSpec as P

LEAF = 128
F32 = jnp.float32
BF16 = jnp.bfloat16
DOUBLINGS = 9
VMEM = pl.BlockSpec(memory_space=pltpu.VMEM)


def vmem(shape, kind=F32):
    return pltpu.VMEM(tuple(shape), kind)


COST = pl.CostEstimate(flops=10**9, bytes_accessed=0, transcendentals=0)
SHORT = pl.CostEstimate(flops=0, bytes_accessed=0, transcendentals=0)
LONG = pl.CostEstimate(flops=10**10, bytes_accessed=0, transcendentals=0)
PARAMS = pltpu.CompilerParams(vmem_limit_bytes=16 << 20)


def chebyshev_constants():
    taus = [1282.0 / 1280.0]
    for _ in range(DOUBLINGS):
        taus.append(2.0 * taus[-1] * taus[-1] - 1.0)
    front = 2.0**DOUBLINGS * math.prod(taus[:-1]) / taus[-1]
    return taus[:-1], front


TAUS, FRONT = chebyshev_constants()


def over(first, second, first_dim, second_dim):
    return lax.dot_general(
        first,
        second,
        (((first_dim,), (second_dim,)), ((), ())),
        preferred_element_type=F32,
    )


def split(value):
    high = value.astype(BF16)
    rest = value - high.astype(F32)
    middle = rest.astype(BF16)
    return high, middle, (rest - middle.astype(F32)).astype(BF16)


def norm_rows(norm, first, width):
    parts = [part.astype(F32) for part in split(norm)]
    place = lax.broadcasted_iota(jnp.int32, (16, width), 0)
    extra = jnp.where(place < 6, 1.0, 0.0)
    for pos in range(3):
        extra = jnp.where(place == pos + first, parts[pos], extra)
    return extra


def row_features(feats, gain):
    feats = feats.astype(F32)
    depth, width = feats.shape
    unit = math.log2(math.e) / (2.0 * depth)
    norm = jnp.sum(feats * feats, axis=0, keepdims=True) * -unit + math.log2(gain)
    parts = [part.astype(F32) for part in split(feats * (2.0 * unit))]
    return jnp.concatenate([*parts, norm_rows(norm, 0, width)], axis=0)


def col_features(feats):
    feats = feats.astype(F32)
    depth, width = feats.shape
    unit = math.log2(math.e) / (2.0 * depth)
    norm = jnp.sum(feats * feats, axis=0, keepdims=True) * -unit
    return jnp.concatenate([feats, feats, feats, norm_rows(norm, 3, width)], axis=0).astype(BF16)


def pack_body(*refs):
    probes_ref, points_ref, *table_refs = refs[:6]
    first_ref, second_ref, own_ref, held_ref, rows_ref, *held_tables, sem = refs[6:]
    span = probes_ref.shape[1]
    pairs = [(points_ref, held_ref), *zip(table_refs, held_tables)]
    small = len(pairs)
    for quarter in range(4):
        target = (first_ref, second_ref)[quarter // 2].at[pl.ds(quarter % 2 * span, span)]
        pairs.append((probes_ref.at[quarter], target))
    copies = [
        pltpu.make_async_copy(source, target, sem.at[pos])
        for pos, (source, target) in enumerate(pairs)
    ]
    for copy in copies:
        copy.start()
    rows_ref[...] = jnp.zeros_like(rows_ref)
    for copy in copies[:small]:
        copy.wait()
    points = held_ref[...].astype(F32)
    for quarter in range(4):
        feats = points[:, quarter, :].astype(BF16)
        half_ref = (first_ref, second_ref)[quarter // 2]
        half_ref[pl.ds(2 * span + quarter % 2 * 16, 16), :] = feats
        if quarter == 0:
            own_ref[...] = feats
    start = 0
    for table in held_tables:
        count, rank = table.shape
        rows_ref[pl.ds(start, count), pl.ds(0, rank)] = table[...].astype(F32)
        start += count
    first_ref[pl.ds(second_ref.shape[0], rows_ref.shape[0]), :] = rows_ref[...].astype(BF16)
    for copy in copies[small:]:
        copy.wait()


def pack(probes, points, tables):
    _, span, samples = probes.shape
    table_rows = -(-sum(table.shape[0] for table in tables) // 16) * 16
    inputs = (probes, points, *tables)
    return pl.pallas_call(
        pack_body,
        out_shape=(
            vmem((2 * (span + 16) + table_rows, samples), BF16),
            vmem((2 * (span + 16), samples), BF16),
            vmem((16, span), BF16),
        ),
        in_specs=[pl.BlockSpec(memory_space=pltpu.HBM)] * len(inputs),
        scratch_shapes=[
            pltpu.VMEM(points.shape, BF16),
            pltpu.VMEM((table_rows, samples), F32),
            *[pltpu.VMEM(table.shape, jnp.int32) for table in tables],
            pltpu.SemaphoreType.DMA((5 + len(tables),)),
        ],
        cost_estimate=COST,
        compiler_params=PARAMS,
        name="pack",
    )(*(pltpu.with_memory_space_constraint(value, pltpu.HBM) for value in inputs))


def masked(entries):
    shape = entries.shape
    row_leaf = lax.broadcasted_iota(jnp.int32, shape, 0) // LEAF
    col_leaf = lax.broadcasted_iota(jnp.int32, shape, 1) // LEAF
    return jnp.where(row_leaf == col_leaf, 0.0, entries)


def add_halves(half_refs, row_refs, cols_ref, put, span, own):
    for number, half_ref in enumerate(half_refs):
        for quarter in range(2):
            feats = half_ref[pl.ds(2 * span + 16 * quarter, 16), :]
            cols_ref[:, pl.ds((2 * number + quarter) * span, span)] = col_features(feats)
    columns = 2 * span * len(half_refs)
    for group, rows_ref in enumerate(row_refs):
        for start in range(0, rows_ref.shape[0], span):
            feats = rows_ref[pl.ds(start, span), :]
            entries = jnp.exp2(over(feats, cols_ref[:, :columns], 1, 0))
            if own and group == 0 and start == 0:
                entries = jnp.concatenate([masked(entries[:, :span]), entries[:, span:]], axis=1)
            randoms = [half_ref[pl.ds(0, 2 * span), :] for half_ref in half_refs]
            put(group, start, over(entries.astype(BF16), jnp.concatenate(randoms, axis=0), 1, 0))


def first_product_body(gain, span, groups, point_count, *refs):
    half_refs, point_refs = refs[:2], refs[2 : point_count + 2]
    row_refs = refs[point_count + 2 : point_count + 2 + len(groups)]
    total_refs, cols_ref = refs[point_count + 2 + len(groups) : -1], refs[-1]
    for rows_ref, places in zip(row_refs, groups):
        for pos, (array, start) in enumerate(places):
            feats = point_refs[array][:, pl.ds(start, span)]
            rows_ref[pl.ds(pos * span, span), :] = row_features(feats, gain).T.astype(BF16)

    def put(group, start, value):
        total_refs[group][pl.ds(start, span), :] = value

    add_halves(half_refs, row_refs, cols_ref, put, span, True)


def first_product(halves, points, groups, span, gain):
    samples = halves[0].shape[1]
    rows = [len(places) * span for places in groups]
    out = pl.pallas_call(
        lambda *refs: first_product_body(gain, span, groups, len(points), *refs),
        out_shape=[vmem((count, 64), BF16) for count in rows]
        + [vmem((count, samples), F32) for count in rows],
        scratch_shapes=[pltpu.VMEM((64, 4 * span), BF16)],
        cost_estimate=COST,
        compiler_params=PARAMS,
        name="first_product",
    )(*halves, *points)
    return out[: len(groups)], out[len(groups) :]


def product_body(span, half_count, count, *refs):
    half_refs, refs = refs[:half_count], refs[half_count:]
    row_refs, old_refs, total_refs = refs[:count], refs[count : 2 * count], refs[2 * count : -1]
    cols_ref = refs[-1]
    for number in range(0, half_count, 2):

        def put(group, start, value):
            place = pl.ds(start, span)
            base = old_refs if number == 0 else total_refs
            total_refs[group][place, :] = base[group][place, :] + value

        add_halves(half_refs[number : number + 2], row_refs, cols_ref, put, span, False)


def product(halves, rows, totals, span, cost=COST):
    return pl.pallas_call(
        lambda *refs: product_body(span, len(halves), len(rows), *refs),
        out_shape=[vmem(total.shape, F32) for total in totals],
        scratch_shapes=[pltpu.VMEM((64, 4 * span), BF16)],
        cost_estimate=cost,
        compiler_params=PARAMS,
        name="product",
    )(*halves, *rows, *totals)


def add_up_body(span, outs, mine_ref, theirs_ref, *refs):
    for (chunks, _), out_ref in zip(outs, refs[-len(outs) :]):
        for pos, chunk in enumerate(chunks):
            place = pl.ds(chunk * span, span)
            value = mine_ref[place, :] + theirs_ref[place, :].astype(F32)
            out_ref[pl.ds(pos * span, span), :] = value.astype(out_ref.dtype)


def add_up(mine, theirs, outs, span, after=(), cost=COST):
    samples = mine.shape[1]
    return pl.pallas_call(
        lambda *refs: add_up_body(span, outs, *refs),
        out_shape=[vmem((len(chunks) * span, samples), kind) for chunks, kind in outs],
        cost_estimate=cost,
        compiler_params=PARAMS,
        name="add_up",
    )(mine, theirs, *after)


def wide_product(first, second, second_dim):
    high, middle, low = split(first)
    other_high, other_middle, other_low = split(second)
    return over(
        jnp.concatenate([high, high, middle, middle, low, high], axis=1),
        jnp.concatenate(
            [other_high, other_middle, other_high, other_middle, other_high, other_low],
            axis=second_dim,
        ),
        1,
        second_dim,
    )


def exact_product(first, second):
    second = second.astype(BF16)
    return over(
        jnp.concatenate(split(first), axis=1), jnp.concatenate([second] * 3, axis=0), 1, 0
    )


def twice_product(twice_parts, parts):
    high, middle, low = twice_parts
    other_high, other_middle, other_low = parts
    left = lax.broadcasted_iota(jnp.int32, high.shape, 1) < high.shape[1] // 2
    last = jnp.where(left, low.astype(F32), high.astype(F32)).astype(BF16)
    return over(
        jnp.concatenate([high, middle, last], axis=1),
        jnp.concatenate(
            [other_high, other_middle, other_high, other_middle, other_high, other_low], axis=0
        ),
        1,
        0,
    )


def select_rows(picks, value):
    return over(
        jnp.concatenate([picks] * 3, axis=1), jnp.concatenate(split(value), axis=0), 1, 0
    )


def interpolate(stacks, skeletons):
    rank, pool = skeletons[0].shape[0], stacks[0].shape[0]
    place = lax.broadcasted_iota(jnp.int32, (rank, 2 * rank), 0)
    other = lax.broadcasted_iota(jnp.int32, (rank, 2 * rank), 1)
    eyes = jnp.where((other == place) | (other == place + rank), 1.0, 0.0)
    states = []
    for skeleton, stack in zip(skeletons, stacks):
        products = wide_product(skeleton, jnp.concatenate([stack, skeleton, skeleton], axis=0), 1)
        ridge = 0.05 * jnp.sum(skeleton * skeleton, keepdims=True) / rank + 1e-05
        inverse = 1.0 / (640.0 * ridge)
        states.append((products[:, :pool], eyes - products[:, pool:] * inverse, inverse))
    for number, tau in enumerate(TAUS):
        last = number == DOUBLINGS - 1
        later = []
        for solved, power, inverse in states:
            power_parts = split(power)
            parts = split(solved)
            if not last:
                parts = [jnp.concatenate(pair, axis=1) for pair in zip(parts, power_parts)]
            both = twice_product(power_parts, parts)
            solved = solved + both[:, :pool] * (1.0 / tau)
            later.append((solved, None if last else 2.0 * both[:, pool:] - eyes, inverse))
        states = later
    return [solved * (inverse * FRONT) for solved, _, inverse in states]


def merge(nodes, early=None):
    stacks, skeletons = [], []
    for samples, reduced, coupling, picks in nodes:
        pool = samples.shape[0]
        high, middle, low = split(reduced)
        coupled = over(
            coupling, jnp.concatenate([high, middle, high, middle, high, low], axis=0), 1, 0
        )
        stacks.append(samples - coupled[:pool])
        skeletons.append(select_rows(picks, samples) - coupled[pool:])
    if early is not None:
        early(skeletons[0])
    interps = interpolate(stacks, skeletons)
    return [
        (interp, skeleton, wide_product(interp, node[1], 0))
        for interp, skeleton, node in zip(interps, skeletons, nodes)
    ]


def leaves_body(received, *refs):
    own_ref, *others = refs[: received + 1]
    source_ref, picks_ref, couplings_ref = refs[received + 1 : received + 4]
    leaf_ref, upper_ref, skeleton_ref, reduced_ref, sent_ref, held_ref, sem = refs[-7:]
    total = own_ref[...]
    for other in others:
        total = total + other[...].astype(F32)
    count = total.shape[0] // LEAF
    stacks = [total[leaf * LEAF : (leaf + 1) * LEAF] for leaf in range(count)]
    skeletons = [select_rows(picks_ref[leaf], stack) for leaf, stack in enumerate(stacks)]
    reduced = []
    for leaf, interp in enumerate(interpolate(stacks, skeletons)):
        held_ref[leaf] = interp
        reduced.append(exact_product(interp, source_ref[pl.ds(leaf * LEAF, LEAF), :]))
    copy = pltpu.make_async_copy(held_ref, leaf_ref, sem)
    copy.start()
    node = (
        jnp.concatenate(skeletons, axis=0),
        jnp.concatenate(reduced, axis=0),
        couplings_ref[...],
        picks_ref[count],
    )
    ((interp, skeleton, reduced),) = merge([node])
    upper_ref[...] = interp
    skeleton_ref[...] = skeleton
    reduced_ref[...] = reduced
    for pos, part in enumerate((*split(skeleton)[:2], reduced.astype(BF16))):
        sent_ref[pl.ds(pos * skeleton.shape[0], skeleton.shape[0]), :] = part
    copy.wait()


def leaves(own, others, source, picks, couplings, later, leaf_count):
    samples = own.shape[1]
    rank, pool = picks.shape[1:]
    return pl.pallas_call(
        lambda *refs: leaves_body(len(others), *refs),
        out_shape=(
            jax.ShapeDtypeStruct((leaf_count, rank, LEAF), F32),
            vmem((rank, pool), F32),
            vmem((rank, samples), F32),
            vmem((rank, samples), F32),
            vmem((3 * rank, samples), BF16),
        ),
        out_specs=(pl.BlockSpec(memory_space=pl.ANY), VMEM, VMEM, VMEM, VMEM),
        scratch_shapes=[pltpu.VMEM((leaf_count, rank, LEAF), F32), pltpu.SemaphoreType.DMA],
        cost_estimate=COST,
        compiler_params=PARAMS,
        name="leaves",
    )(own, *others, source, picks, couplings, *later)


def first_of_pair(number):
    return (lax.axis_index("col") >> (number - 2)) % 2 == 0


def pair(mine, theirs, mine_first):
    first = jnp.where(mine_first, mine, theirs)
    second = jnp.where(mine_first, theirs, mine)
    return jnp.concatenate([first, second], axis=0)


def upper_body(picks_count, *refs):
    states = [(refs[0][...], refs[1][...])]
    rank = refs[0].shape[0]
    for got_ref in refs[2:5]:
        high, middle, reduced = (got_ref[pl.ds(pos * rank, rank), :] for pos in range(3))
        states.append((high.astype(F32) + middle.astype(F32), reduced.astype(F32)))
    picks_ref, two_ref, other_ref, three_ref, one_ref, upper_out, top_out = refs[5:12]
    upper_ref, state_ref, sem = refs[12:]
    places = [
        (one_ref, upper_out.at[0, 0]),
        (upper_ref.at[0], upper_out.at[1, 0]),
        (upper_ref.at[1], upper_out.at[2, 0]),
        (state_ref.at[0], top_out.at[0, 0]),
        (state_ref.at[1], top_out.at[1, 0]),
    ]
    copies = [
        pltpu.make_async_copy(source, target, sem.at[pos])
        for pos, (source, target) in enumerate(places)
    ]
    copies[0].start()
    mine_first = first_of_pair(2)
    nodes = []
    for number, coupling_ref in enumerate((two_ref, other_ref)):
        mine, theirs = states[2 * number : 2 * number + 2]
        picks = picks_ref[picks_count - 3 + number]
        stacks = [pair(*parts, mine_first) for parts in zip(mine, theirs)]
        nodes.append((*stacks, coupling_ref[...], picks))
    mine, theirs = merge(nodes)
    upper_ref[0] = mine[0]
    copies[1].start()

    def early(skeleton):
        state_ref[0] = skeleton
        copies[3].start()

    mine_first = first_of_pair(3)
    stacks = [pair(*parts, mine_first) for parts in zip(mine[1:], theirs[1:])]
    ((interp, _, reduced),) = merge([(*stacks, three_ref[...], picks_ref[picks_count - 1])], early)
    upper_ref[1] = interp
    copies[2].start()
    state_ref[1] = reduced
    copies[4].start()
    for copy in copies:
        copy.wait()


def upper_levels(skeleton, reduced, got, picks, couplings, interp_one):
    rank, pool = picks.shape[1:]
    samples = skeleton.shape[1]
    return pl.pallas_call(
        lambda *refs: upper_body(picks.shape[0], *refs),
        out_shape=(
            jax.ShapeDtypeStruct((3, 1, rank, pool), F32),
            jax.ShapeDtypeStruct((2, 1, rank, samples), F32),
        ),
        out_specs=(pl.BlockSpec(memory_space=pl.ANY),) * 2,
        scratch_shapes=[
            pltpu.VMEM((2, rank, pool), F32),
            pltpu.VMEM((2, rank, samples), F32),
            pltpu.SemaphoreType.DMA((5,)),
        ],
        cost_estimate=COST,
        compiler_params=PARAMS,
        name="upper_levels",
    )(skeleton, reduced, *got, picks, *couplings, interp_one)


def one_hot(chosen, pool):
    place = lax.broadcasted_iota(jnp.int32, (pool, chosen.shape[1]), 0)
    return jnp.where(place.astype(F32) == chosen, 1.0, 0.0).astype(F32)


def couple(first, second, picks, gain, couplings_ref):
    rank = first.shape[1]
    points = jnp.concatenate([first, second], axis=1)
    entries = jnp.exp2(over(row_features(points, gain).astype(BF16), col_features(points), 0, 0))
    left = lax.broadcasted_iota(jnp.int32, entries.shape, 1) < rank
    upper = lax.broadcasted_iota(jnp.int32, entries.shape, 0) < rank
    entries = jnp.where(left == upper, 0.0, entries)
    chosen = select_rows(picks.T.astype(BF16), entries)
    high, middle, low = split(jnp.concatenate([entries, chosen], axis=0))
    couplings_ref[...] = jnp.concatenate([high, high, middle, middle, low, high], axis=1)


def coupling_shape(rank):
    return vmem((3 * rank, 12 * rank), BF16)


def skeletons_body(gain, span, counts, mine_ref, beside_ref, *refs):
    picks_ref, one_ref, two_ref, points_ref = refs
    rank, pool = picks_ref.shape[1:]
    leaf_count = counts[0]
    tables = 2 * (span + 16)
    nodes = []
    for source_ref in (mine_ref, beside_ref):
        rows = source_ref[pl.ds(tables, source_ref.shape[0] - tables), :rank].astype(F32)
        hots = [one_hot(rows[pos : pos + 1], pool) for pos in range(leaf_count + 1)]
        children = []
        for leaf in range(leaf_count):
            feats = source_ref[pl.ds(2 * span, 16), pl.ds(leaf * LEAF, LEAF)]
            children.append(over(feats, hots[leaf].astype(BF16), 1, 0))
        points = jnp.concatenate(children, axis=1)
        nodes.append(over(points, hots[leaf_count], 1, 0))
        if source_ref is mine_ref:
            couple(*children, hots[leaf_count], gain, one_ref)
            start = leaf_count + counts[1]
            level_two = lax.axis_index("col") // 2
            wanted = [level_two, level_two + 1 - 2 * (level_two % 2), counts[2] + level_two // 2]
            for row in wanted:
                place = lax.broadcasted_iota(jnp.int32, rows.shape, 0)
                named = jnp.where(place == start + row, rows, 0.0)
                hots.append(one_hot(jnp.sum(named, axis=0, keepdims=True), pool))
            for number, hot in enumerate(hots):
                picks_ref[number] = hot.T.astype(BF16)
            upper = hots[leaf_count + 1]
    mine, theirs = nodes
    mine_first = first_of_pair(2)
    first = jnp.where(mine_first, mine, theirs)
    second = jnp.where(mine_first, theirs, mine)
    couple(first, second, upper, gain, two_ref)
    points_ref[...] = jnp.concatenate([first, second], axis=1).astype(BF16)


def skeletons(packed, beside, tables, span, gain):
    leaf_count, rank = tables[0].shape
    counts = [table.shape[0] for table in tables]
    return pl.pallas_call(
        lambda *refs: skeletons_body(gain, span, counts, *refs),
        out_shape=(
            vmem((leaf_count + 4, rank, LEAF), BF16),
            coupling_shape(rank),
            coupling_shape(rank),
            vmem((16, 2 * rank), BF16),
        ),
        cost_estimate=COST,
        compiler_params=PARAMS,
        name="skeletons",
    )(packed, beside)


def top_couplings_body(gain, mine_ref, theirs_ref, picks_ref, other_ref, three_ref):
    count, rank, _ = picks_ref.shape
    picks = [picks_ref[count - pos].astype(F32).T for pos in (3, 2, 1)]
    mine, theirs = mine_ref[...].astype(F32), theirs_ref[...].astype(F32)
    couple(theirs[:, :rank], theirs[:, rank:], picks[1], gain, other_ref)
    mine, theirs = over(mine, picks[0], 1, 0), over(theirs, picks[1], 1, 0)
    mine_first = first_of_pair(3)
    first = jnp.where(mine_first, mine, theirs)
    second = jnp.where(mine_first, theirs, mine)
    couple(first, second, picks[2], gain, three_ref)


def top_couplings(mine, theirs, picks, gain):
    return pl.pallas_call(
        lambda *refs: top_couplings_body(gain, *refs),
        out_shape=[coupling_shape(picks.shape[1])] * 2,
        cost_estimate=LONG,
        compiler_params=PARAMS,
        name="top_couplings",
    )(mine, theirs, picks)


def local(probes, points, leaf_skeleton, skeleton_one, skeleton_two, skeleton_three):
    span = probes.shape[1]
    row_count = lax.axis_size("row")
    col_count = lax.axis_size("col")
    gain = 16.0 / math.sqrt(4 * span * row_count * col_count)

    def swap(value, row_bits, col_bits):
        pairs = [
            (r * col_count + c, (r ^ row_bits) * col_count + (c ^ col_bits))
            for r in range(row_count)
            for c in range(col_count)
        ]
        return lax.ppermute(value, ("row", "col"), pairs)

    tables = (leaf_skeleton, skeleton_one, skeleton_two, skeleton_three)
    first, second, own_points = pack(probes, points, tables)
    beside_first, across_second = swap(first, 0, 1), swap(second, 2, 0)
    line = col_count // 2
    line_points = own_points
    for bit in range(1, col_count.bit_length() - 1):
        line_points = jnp.concatenate([line_points, swap(line_points, 0, 1 << bit)], axis=1)
        if bit == 1:
            line_points, *late = lax.optimization_barrier((line_points, first, second))
    beside_second, across_first = swap(late[1], 0, 1), swap(late[0], 2, 0)
    line_points = [line_points, swap(line_points, 1, 0)]
    near, far = range(2), range(2, line)
    groups = [
        [(core, chunk * span) for chunk in group] for core in range(2) for group in (near, far)
    ]
    feats, totals = first_product((first, second), line_points, groups, span, gain)
    beside_first, across_second, *totals = lax.optimization_barrier(
        (beside_first, across_second, *totals)
    )
    diagonal = [swap(beside_first, 2, 0), swap(across_second, 0, 1)]
    totals = product([beside_first, across_second], feats, totals, span, SHORT)
    beside_second, across_first, *totals = lax.optimization_barrier(
        (beside_second, across_first, *totals)
    )
    totals = product([beside_second, across_first], feats, totals, span)
    first, *totals = lax.optimization_barrier((first, *totals))
    picks, couplings_one, couplings_two, points_two = skeletons(
        first, beside_first, tables, span, gain
    )
    points_two, *totals = lax.optimization_barrier((points_two, *totals))
    pieces = [first, second, beside_first, beside_second, across_first, across_second, *diagonal]
    for bit in range(2, row_count.bit_length() - 1):
        more = [swap(value, 1 << bit, 0) for value in pieces]
        totals = product(more, feats, totals, span)
        pieces += more
    (theirs,) = product(diagonal, feats[3:], totals[3:], span)
    from_sibling = swap(theirs, 1, 0)
    (mine,) = product(diagonal, feats[1:2], totals[1:2], span)
    outs = [(range(0, line - 2, 2), F32), (range(1, line - 2, 2), BF16)]
    kept, sent = add_up(mine, from_sibling, outs, span)
    sent, total, points_two = lax.optimization_barrier((sent, totals[2], points_two))
    arrived = swap(sent, 0, 2)
    (theirs,) = product(diagonal, feats[2:3], [total], span)
    from_sibling = swap(theirs, 1, 0)
    (mine,) = product(diagonal, feats[:1], totals[:1], span)
    received = []
    chunks = list(range(2, line, 2))
    bit = 2
    while chunks:
        sent_places = [pos for pos, chunk in enumerate(chunks) if chunk & bit]
        kept_places = [pos for pos, chunk in enumerate(chunks) if not chunk & bit]
        outs = [(sent_places, BF16)] + [(kept_places, F32)] * (len(kept_places) > 0)
        sent, *kept = add_up(kept, arrived, outs, span, cost=LONG)
        arrived = swap(sent, 0, 2 * bit)
        received.append(arrived[:span] if len(sent_places) > 1 else arrived)
        if kept:
            (kept,) = kept
            arrived = arrived[span:]
        chunks = [chunks[pos] for pos in kept_places]
        bit *= 2
    own_sum, near_sent = add_up(mine, from_sibling, [([0], F32), ([1], BF16)], span, (sent,))
    received.append(swap(near_sent, 0, 2))
    other_points = swap(points_two, 0, 2)
    later = top_couplings(points_two, other_points, picks, gain)

    leaf_interp, interp_one, skeleton, reduced, sent = leaves(
        own_sum, received, first, picks, couplings_one, later, leaf_skeleton.shape[0]
    )
    got = [swap(sent, 0, bits) for bits in (1, 2, 3)]
    upper_interp, top_state = upper_levels(
        skeleton, reduced, got, picks, (couplings_two, *later), interp_one
    )
    return jnp.swapaxes(leaf_interp, 1, 2), jnp.swapaxes(upper_interp, 2, 3), top_state


def solution(mesh):
    placed = (
        P(None, ("row", "col"), None),
        P(None, None, ("row", "col")),
        P(("row", "col"), None),
        P(("row", "col"), None),
        P("row", None),
        P("row", None),
    )
    return jax.shard_map(
        local,
        mesh=mesh,
        in_specs=placed,
        out_specs=(
            P(("row", "col"), None, None),
            P(None, ("row", "col"), None, None),
            P(None, ("row", "col"), None, None),
        ),
        check_vma=False,
    )
```

```python
import math

import jax
import jax.numpy as jnp
from jax import lax
from jax.experimental import pallas as pl
from jax.experimental.pallas import tpu as pltpu
from jax.sharding import PartitionSpec as P

LEAF = 128
F32 = jnp.float32
BF16 = jnp.bfloat16
DOUBLINGS = 9
VMEM = pl.BlockSpec(memory_space=pltpu.VMEM)


def vmem(shape, kind=F32):
    return pltpu.VMEM(tuple(shape), kind)


COST = pl.CostEstimate(flops=10**9, bytes_accessed=0, transcendentals=0)
SHORT = pl.CostEstimate(flops=0, bytes_accessed=0, transcendentals=0)
LONG = pl.CostEstimate(flops=10**10, bytes_accessed=0, transcendentals=0)
PARAMS = pltpu.CompilerParams(vmem_limit_bytes=16 << 20)


def chebyshev_constants():
    taus = [1282.0 / 1280.0]
    for _ in range(DOUBLINGS):
        taus.append(2.0 * taus[-1] * taus[-1] - 1.0)
    front = 2.0**DOUBLINGS * math.prod(taus[:-1]) / taus[-1]
    return taus[:-1], front


TAUS, FRONT = chebyshev_constants()


def over(first, second, first_dim, second_dim):
    return lax.dot_general(
        first,
        second,
        (((first_dim,), (second_dim,)), ((), ())),
        preferred_element_type=F32,
    )


def split(value):
    high = value.astype(BF16)
    rest = value - high.astype(F32)
    middle = rest.astype(BF16)
    return high, middle, (rest - middle.astype(F32)).astype(BF16)


def norm_rows(norm, first, width):
    parts = [part.astype(F32) for part in split(norm)]
    place = lax.broadcasted_iota(jnp.int32, (16, width), 0)
    extra = jnp.where(place < 6, 1.0, 0.0)
    for pos in range(3):
        extra = jnp.where(place == pos + first, parts[pos], extra)
    return extra


def row_features(feats, gain):
    feats = feats.astype(F32)
    depth, width = feats.shape
    unit = math.log2(math.e) / (2.0 * depth)
    norm = jnp.sum(feats * feats, axis=0, keepdims=True) * -unit + math.log2(gain)
    parts = [part.astype(F32) for part in split(feats * (2.0 * unit))]
    return jnp.concatenate([*parts, norm_rows(norm, 0, width)], axis=0)


def col_features(feats):
    feats = feats.astype(F32)
    depth, width = feats.shape
    unit = math.log2(math.e) / (2.0 * depth)
    norm = jnp.sum(feats * feats, axis=0, keepdims=True) * -unit
    return jnp.concatenate([feats, feats, feats, norm_rows(norm, 3, width)], axis=0).astype(BF16)


def pack_body(*refs):
    probes_ref, points_ref, *table_refs = refs[:6]
    first_ref, second_ref, own_ref, held_ref, rows_ref, *held_tables, sem = refs[6:]
    span = probes_ref.shape[1]
    pairs = [(points_ref, held_ref), *zip(table_refs, held_tables)]
    small = len(pairs)
    for quarter in range(4):
        target = (first_ref, second_ref)[quarter // 2].at[pl.ds(quarter % 2 * span, span)]
        pairs.append((probes_ref.at[quarter], target))
    copies = [
        pltpu.make_async_copy(source, target, sem.at[pos])
        for pos, (source, target) in enumerate(pairs)
    ]
    for copy in copies:
        copy.start()
    rows_ref[...] = jnp.zeros_like(rows_ref)
    for copy in copies[:small]:
        copy.wait()
    points = held_ref[...].astype(F32)
    for quarter in range(4):
        feats = points[:, quarter, :].astype(BF16)
        half_ref = (first_ref, second_ref)[quarter // 2]
        half_ref[pl.ds(2 * span + quarter % 2 * 16, 16), :] = feats
        if quarter == 0:
            own_ref[...] = feats
    start = 0
    for table in held_tables:
        count, rank = table.shape
        rows_ref[pl.ds(start, count), pl.ds(0, rank)] = table[...].astype(F32)
        start += count
    first_ref[pl.ds(second_ref.shape[0], rows_ref.shape[0]), :] = rows_ref[...].astype(BF16)
    for copy in copies[small:]:
        copy.wait()


def pack(probes, points, tables):
    _, span, samples = probes.shape
    table_rows = -(-sum(table.shape[0] for table in tables) // 16) * 16
    inputs = (probes, points, *tables)
    return pl.pallas_call(
        pack_body,
        out_shape=(
            vmem((2 * (span + 16) + table_rows, samples), BF16),
            vmem((2 * (span + 16), samples), BF16),
            vmem((16, span), BF16),
        ),
        in_specs=[pl.BlockSpec(memory_space=pltpu.HBM)] * len(inputs),
        scratch_shapes=[
            pltpu.VMEM(points.shape, BF16),
            pltpu.VMEM((table_rows, samples), F32),
            *[pltpu.VMEM(table.shape, jnp.int32) for table in tables],
            pltpu.SemaphoreType.DMA((5 + len(tables),)),
        ],
        cost_estimate=COST,
        compiler_params=PARAMS,
        name="pack",
    )(*(pltpu.with_memory_space_constraint(value, pltpu.HBM) for value in inputs))


def masked(entries):
    shape = entries.shape
    row_leaf = lax.broadcasted_iota(jnp.int32, shape, 0) // LEAF
    col_leaf = lax.broadcasted_iota(jnp.int32, shape, 1) // LEAF
    return jnp.where(row_leaf == col_leaf, 0.0, entries)


def add_halves(half_refs, row_refs, cols_ref, put, span, own):
    for number, half_ref in enumerate(half_refs):
        for quarter in range(2):
            feats = half_ref[pl.ds(2 * span + 16 * quarter, 16), :]
            cols_ref[:, pl.ds((2 * number + quarter) * span, span)] = col_features(feats)
    columns = 2 * span * len(half_refs)
    for group, rows_ref in enumerate(row_refs):
        for start in range(0, rows_ref.shape[0], span):
            feats = rows_ref[pl.ds(start, span), :]
            entries = jnp.exp2(over(feats, cols_ref[:, :columns], 1, 0))
            if own and group == 0 and start == 0:
                entries = jnp.concatenate([masked(entries[:, :span]), entries[:, span:]], axis=1)
            randoms = [half_ref[pl.ds(0, 2 * span), :] for half_ref in half_refs]
            put(group, start, over(entries.astype(BF16), jnp.concatenate(randoms, axis=0), 1, 0))


def first_product_body(gain, span, groups, point_count, *refs):
    half_refs, point_refs = refs[:2], refs[2 : point_count + 2]
    row_refs = refs[point_count + 2 : point_count + 2 + len(groups)]
    total_refs, cols_ref = refs[point_count + 2 + len(groups) : -1], refs[-1]
    for rows_ref, places in zip(row_refs, groups):
        for pos, (array, start) in enumerate(places):
            feats = point_refs[array][:, pl.ds(start, span)]
            rows_ref[pl.ds(pos * span, span), :] = row_features(feats, gain).T.astype(BF16)

    def put(group, start, value):
        total_refs[group][pl.ds(start, span), :] = value

    add_halves(half_refs, row_refs, cols_ref, put, span, True)


def first_product(halves, points, groups, span, gain):
    samples = halves[0].shape[1]
    rows = [len(places) * span for places in groups]
    out = pl.pallas_call(
        lambda *refs: first_product_body(gain, span, groups, len(points), *refs),
        out_shape=[vmem((count, 64), BF16) for count in rows]
        + [vmem((count, samples), F32) for count in rows],
        scratch_shapes=[pltpu.VMEM((64, 4 * span), BF16)],
        cost_estimate=COST,
        compiler_params=PARAMS,
        name="first_product",
    )(*halves, *points)
    return out[: len(groups)], out[len(groups) :]


def product_body(span, half_count, count, *refs):
    half_refs, refs = refs[:half_count], refs[half_count:]
    row_refs, old_refs, total_refs = refs[:count], refs[count : 2 * count], refs[2 * count : -1]
    cols_ref = refs[-1]
    for number in range(0, half_count, 2):

        def put(group, start, value):
            place = pl.ds(start, span)
            base = old_refs if number == 0 else total_refs
            total_refs[group][place, :] = base[group][place, :] + value

        add_halves(half_refs[number : number + 2], row_refs, cols_ref, put, span, False)


def product(halves, rows, totals, span, cost=COST):
    return pl.pallas_call(
        lambda *refs: product_body(span, len(halves), len(rows), *refs),
        out_shape=[vmem(total.shape, F32) for total in totals],
        scratch_shapes=[pltpu.VMEM((64, 4 * span), BF16)],
        cost_estimate=cost,
        compiler_params=PARAMS,
        name="product",
    )(*halves, *rows, *totals)


def add_up_body(span, outs, mine_ref, theirs_ref, *refs):
    for (chunks, _), out_ref in zip(outs, refs[-len(outs) :]):
        for pos, chunk in enumerate(chunks):
            place = pl.ds(chunk * span, span)
            value = mine_ref[place, :] + theirs_ref[place, :].astype(F32)
            out_ref[pl.ds(pos * span, span), :] = value.astype(out_ref.dtype)


def add_up(mine, theirs, outs, span, after=(), cost=COST):
    samples = mine.shape[1]
    return pl.pallas_call(
        lambda *refs: add_up_body(span, outs, *refs),
        out_shape=[vmem((len(chunks) * span, samples), kind) for chunks, kind in outs],
        cost_estimate=cost,
        compiler_params=PARAMS,
        name="add_up",
    )(mine, theirs, *after)


def wide_product(first, second, second_dim):
    high, middle, low = split(first)
    other_high, other_middle, other_low = split(second)
    return over(
        jnp.concatenate([high, high, middle, middle, low, high], axis=1),
        jnp.concatenate(
            [other_high, other_middle, other_high, other_middle, other_high, other_low],
            axis=second_dim,
        ),
        1,
        second_dim,
    )


def exact_product(first, second):
    second = second.astype(BF16)
    return over(
        jnp.concatenate(split(first), axis=1), jnp.concatenate([second] * 3, axis=0), 1, 0
    )


def twice_product(twice_parts, parts):
    high, middle, low = twice_parts
    other_high, other_middle, other_low = parts
    left = lax.broadcasted_iota(jnp.int32, high.shape, 1) < high.shape[1] // 2
    last = jnp.where(left, low.astype(F32), high.astype(F32)).astype(BF16)
    return over(
        jnp.concatenate([high, middle, last], axis=1),
        jnp.concatenate(
            [other_high, other_middle, other_high, other_middle, other_high, other_low], axis=0
        ),
        1,
        0,
    )


def select_rows(picks, value):
    return over(
        jnp.concatenate([picks] * 3, axis=1), jnp.concatenate(split(value), axis=0), 1, 0
    )


def interpolate(stacks, skeletons):
    rank, pool = skeletons[0].shape[0], stacks[0].shape[0]
    place = lax.broadcasted_iota(jnp.int32, (rank, 2 * rank), 0)
    other = lax.broadcasted_iota(jnp.int32, (rank, 2 * rank), 1)
    eyes = jnp.where((other == place) | (other == place + rank), 1.0, 0.0)
    states = []
    for skeleton, stack in zip(skeletons, stacks):
        products = wide_product(skeleton, jnp.concatenate([stack, skeleton, skeleton], axis=0), 1)
        ridge = 0.05 * jnp.sum(skeleton * skeleton, keepdims=True) / rank + 1e-05
        inverse = 1.0 / (640.0 * ridge)
        states.append((products[:, :pool], eyes - products[:, pool:] * inverse, inverse))
    for number, tau in enumerate(TAUS):
        last = number == DOUBLINGS - 1
        later = []
        for solved, power, inverse in states:
            power_parts = split(power)
            parts = split(solved)
            if not last:
                parts = [jnp.concatenate(pair, axis=1) for pair in zip(parts, power_parts)]
            both = twice_product(power_parts, parts)
            solved = solved + both[:, :pool] * (1.0 / tau)
            later.append((solved, None if last else 2.0 * both[:, pool:] - eyes, inverse))
        states = later
    return [solved * (inverse * FRONT) for solved, _, inverse in states]


def merge(nodes, early=None):
    stacks, skeletons = [], []
    for samples, reduced, coupling, picks in nodes:
        pool = samples.shape[0]
        high, middle, low = split(reduced)
        coupled = over(
            coupling, jnp.concatenate([high, middle, high, middle, high, low], axis=0), 1, 0
        )
        stacks.append(samples - coupled[:pool])
        skeletons.append(select_rows(picks, samples) - coupled[pool:])
    if early is not None:
        early(skeletons[0])
    interps = interpolate(stacks, skeletons)
    return [
        (interp, skeleton, wide_product(interp, node[1], 0))
        for interp, skeleton, node in zip(interps, skeletons, nodes)
    ]


def leaves_body(direct, staged, *refs):
    own_ref, near_ref, *parts = refs[: 2 + direct + staged]
    source_ref, picks_ref, couplings_ref = refs[2 + direct + staged : 5 + direct + staged]
    leaf_ref, upper_ref, skeleton_ref, reduced_ref, sent_ref, held_ref, sem = refs[-7:]
    half = own_ref.shape[0] // 2
    totals = []
    for number, group in enumerate((parts[:direct], parts[direct:])):
        place = pl.ds(number * half, half)
        total = own_ref[place, :] + near_ref[place, :].astype(F32)
        for part in group:
            total = total + part[...].astype(F32)
        totals.append(total)
    total = jnp.concatenate(totals, axis=0)
    count = total.shape[0] // LEAF
    stacks = [total[leaf * LEAF : (leaf + 1) * LEAF] for leaf in range(count)]
    skeletons = [select_rows(picks_ref[leaf], stack) for leaf, stack in enumerate(stacks)]
    reduced = []
    for leaf, interp in enumerate(interpolate(stacks, skeletons)):
        held_ref[leaf] = interp
        reduced.append(exact_product(interp, source_ref[pl.ds(leaf * LEAF, LEAF), :]))
    copy = pltpu.make_async_copy(held_ref, leaf_ref, sem)
    copy.start()
    node = (
        jnp.concatenate(skeletons, axis=0),
        jnp.concatenate(reduced, axis=0),
        couplings_ref[...],
        picks_ref[count],
    )
    ((interp, skeleton, reduced),) = merge([node])
    upper_ref[...] = interp
    skeleton_ref[...] = skeleton
    reduced_ref[...] = reduced
    for pos, part in enumerate((*split(skeleton)[:2], reduced.astype(BF16))):
        sent_ref[pl.ds(pos * skeleton.shape[0], skeleton.shape[0]), :] = part
    copy.wait()


def leaves(own, near, direct, staged, source, picks, couplings, later, leaf_count):
    samples = own.shape[1]
    rank, pool = picks.shape[1:]
    return pl.pallas_call(
        lambda *refs: leaves_body(len(direct), len(staged), *refs),
        out_shape=(
            jax.ShapeDtypeStruct((leaf_count, rank, LEAF), F32),
            vmem((rank, pool), F32),
            vmem((rank, samples), F32),
            vmem((rank, samples), F32),
            vmem((3 * rank, samples), BF16),
        ),
        out_specs=(pl.BlockSpec(memory_space=pl.ANY), VMEM, VMEM, VMEM, VMEM),
        scratch_shapes=[pltpu.VMEM((leaf_count, rank, LEAF), F32), pltpu.SemaphoreType.DMA],
        cost_estimate=COST,
        compiler_params=PARAMS,
        name="leaves",
    )(own, near, *direct, *staged, source, picks, couplings, *later)


def first_of_pair(number):
    return (lax.axis_index("col") >> (number - 2)) % 2 == 0


def pair(mine, theirs, mine_first):
    first = jnp.where(mine_first, mine, theirs)
    second = jnp.where(mine_first, theirs, mine)
    return jnp.concatenate([first, second], axis=0)


def upper_body(picks_count, *refs):
    states = [(refs[0][...], refs[1][...])]
    rank = refs[0].shape[0]
    for got_ref in refs[2:5]:
        high, middle, reduced = (got_ref[pl.ds(pos * rank, rank), :] for pos in range(3))
        states.append((high.astype(F32) + middle.astype(F32), reduced.astype(F32)))
    picks_ref, two_ref, other_ref, three_ref, one_ref, upper_out, top_out = refs[5:12]
    upper_ref, state_ref, sem = refs[12:]
    places = [
        (one_ref, upper_out.at[0, 0]),
        (upper_ref.at[0], upper_out.at[1, 0]),
        (upper_ref.at[1], upper_out.at[2, 0]),
        (state_ref.at[0], top_out.at[0, 0]),
        (state_ref.at[1], top_out.at[1, 0]),
    ]
    copies = [
        pltpu.make_async_copy(source, target, sem.at[pos])
        for pos, (source, target) in enumerate(places)
    ]
    copies[0].start()
    mine_first = first_of_pair(2)
    nodes = []
    for number, coupling_ref in enumerate((two_ref, other_ref)):
        mine, theirs = states[2 * number : 2 * number + 2]
        picks = picks_ref[picks_count - 3 + number]
        stacks = [pair(*parts, mine_first) for parts in zip(mine, theirs)]
        nodes.append((*stacks, coupling_ref[...], picks))
    mine, theirs = merge(nodes)
    upper_ref[0] = mine[0]
    copies[1].start()

    def early(skeleton):
        state_ref[0] = skeleton
        copies[3].start()

    mine_first = first_of_pair(3)
    stacks = [pair(*parts, mine_first) for parts in zip(mine[1:], theirs[1:])]
    ((interp, _, reduced),) = merge([(*stacks, three_ref[...], picks_ref[picks_count - 1])], early)
    upper_ref[1] = interp
    copies[2].start()
    state_ref[1] = reduced
    copies[4].start()
    for copy in copies:
        copy.wait()


def upper_levels(skeleton, reduced, got, picks, couplings, interp_one):
    rank, pool = picks.shape[1:]
    samples = skeleton.shape[1]
    return pl.pallas_call(
        lambda *refs: upper_body(picks.shape[0], *refs),
        out_shape=(
            jax.ShapeDtypeStruct((3, 1, rank, pool), F32),
            jax.ShapeDtypeStruct((2, 1, rank, samples), F32),
        ),
        out_specs=(pl.BlockSpec(memory_space=pl.ANY),) * 2,
        scratch_shapes=[
            pltpu.VMEM((2, rank, pool), F32),
            pltpu.VMEM((2, rank, samples), F32),
            pltpu.SemaphoreType.DMA((5,)),
        ],
        cost_estimate=COST,
        compiler_params=PARAMS,
        name="upper_levels",
    )(skeleton, reduced, *got, picks, *couplings, interp_one)


def one_hot(chosen, pool):
    place = lax.broadcasted_iota(jnp.int32, (pool, chosen.shape[1]), 0)
    return jnp.where(place.astype(F32) == chosen, 1.0, 0.0).astype(F32)


def couple(first, second, picks, gain, couplings_ref):
    rank = first.shape[1]
    points = jnp.concatenate([first, second], axis=1)
    entries = jnp.exp2(over(row_features(points, gain).astype(BF16), col_features(points), 0, 0))
    left = lax.broadcasted_iota(jnp.int32, entries.shape, 1) < rank
    upper = lax.broadcasted_iota(jnp.int32, entries.shape, 0) < rank
    entries = jnp.where(left == upper, 0.0, entries)
    chosen = select_rows(picks.T.astype(BF16), entries)
    high, middle, low = split(jnp.concatenate([entries, chosen], axis=0))
    couplings_ref[...] = jnp.concatenate([high, high, middle, middle, low, high], axis=1)


def coupling_shape(rank):
    return vmem((3 * rank, 12 * rank), BF16)


def skeletons_body(gain, span, counts, mine_ref, beside_ref, *refs):
    picks_ref, one_ref, two_ref, points_ref = refs
    rank, pool = picks_ref.shape[1:]
    leaf_count = counts[0]
    tables = 2 * (span + 16)
    nodes = []
    for source_ref in (mine_ref, beside_ref):
        rows = source_ref[pl.ds(tables, source_ref.shape[0] - tables), :rank].astype(F32)
        hots = [one_hot(rows[pos : pos + 1], pool) for pos in range(leaf_count + 1)]
        children = []
        for leaf in range(leaf_count):
            feats = source_ref[pl.ds(2 * span, 16), pl.ds(leaf * LEAF, LEAF)]
            children.append(over(feats, hots[leaf].astype(BF16), 1, 0))
        points = jnp.concatenate(children, axis=1)
        nodes.append(over(points, hots[leaf_count], 1, 0))
        if source_ref is mine_ref:
            couple(*children, hots[leaf_count], gain, one_ref)
            start = leaf_count + counts[1]
            level_two = lax.axis_index("col") // 2
            wanted = [level_two, level_two + 1 - 2 * (level_two % 2), counts[2] + level_two // 2]
            for row in wanted:
                place = lax.broadcasted_iota(jnp.int32, rows.shape, 0)
                named = jnp.where(place == start + row, rows, 0.0)
                hots.append(one_hot(jnp.sum(named, axis=0, keepdims=True), pool))
            for number, hot in enumerate(hots):
                picks_ref[number] = hot.T.astype(BF16)
            upper = hots[leaf_count + 1]
    mine, theirs = nodes
    mine_first = first_of_pair(2)
    first = jnp.where(mine_first, mine, theirs)
    second = jnp.where(mine_first, theirs, mine)
    couple(first, second, upper, gain, two_ref)
    points_ref[...] = jnp.concatenate([first, second], axis=1).astype(BF16)


def skeletons(packed, beside, tables, span, gain):
    leaf_count, rank = tables[0].shape
    counts = [table.shape[0] for table in tables]
    return pl.pallas_call(
        lambda *refs: skeletons_body(gain, span, counts, *refs),
        out_shape=(
            vmem((leaf_count + 4, rank, LEAF), BF16),
            coupling_shape(rank),
            coupling_shape(rank),
            vmem((16, 2 * rank), BF16),
        ),
        cost_estimate=COST,
        compiler_params=PARAMS,
        name="skeletons",
    )(packed, beside)


def top_couplings_body(gain, mine_ref, theirs_ref, picks_ref, other_ref, three_ref):
    count, rank, _ = picks_ref.shape
    picks = [picks_ref[count - pos].astype(F32).T for pos in (3, 2, 1)]
    mine, theirs = mine_ref[...].astype(F32), theirs_ref[...].astype(F32)
    couple(theirs[:, :rank], theirs[:, rank:], picks[1], gain, other_ref)
    mine, theirs = over(mine, picks[0], 1, 0), over(theirs, picks[1], 1, 0)
    mine_first = first_of_pair(3)
    first = jnp.where(mine_first, mine, theirs)
    second = jnp.where(mine_first, theirs, mine)
    couple(first, second, picks[2], gain, three_ref)


def top_couplings(mine, theirs, picks, gain):
    return pl.pallas_call(
        lambda *refs: top_couplings_body(gain, *refs),
        out_shape=[coupling_shape(picks.shape[1])] * 2,
        cost_estimate=LONG,
        compiler_params=PARAMS,
        name="top_couplings",
    )(mine, theirs, picks)


def local(probes, points, leaf_skeleton, skeleton_one, skeleton_two, skeleton_three):
    span = probes.shape[1]
    row_count = lax.axis_size("row")
    col_count = lax.axis_size("col")
    gain = 16.0 / math.sqrt(4 * span * row_count * col_count)

    def swap(value, row_bits, col_bits):
        pairs = [
            (r * col_count + c, (r ^ row_bits) * col_count + (c ^ col_bits))
            for r in range(row_count)
            for c in range(col_count)
        ]
        return lax.ppermute(value, ("row", "col"), pairs)

    tables = (leaf_skeleton, skeleton_one, skeleton_two, skeleton_three)
    first, second, own_points = pack(probes, points, tables)
    beside_first, across_second = swap(first, 0, 1), swap(second, 2, 0)
    line = col_count // 2
    line_points = own_points
    for bit in range(1, col_count.bit_length() - 1):
        line_points = jnp.concatenate([line_points, swap(line_points, 0, 1 << bit)], axis=1)
        if bit == 1:
            line_points, *late = lax.optimization_barrier((line_points, first, second))
    beside_second, across_first = swap(late[1], 0, 1), swap(late[0], 2, 0)
    line_points = [line_points, swap(line_points, 1, 0)]
    near, far = range(2), range(2, line)
    groups = [
        [(core, chunk * span) for chunk in group] for core in range(2) for group in (near, far)
    ]
    feats, totals = first_product((first, second), line_points, groups, span, gain)
    beside_first, across_second, *totals = lax.optimization_barrier(
        (beside_first, across_second, *totals)
    )
    diagonal = [swap(beside_first, 2, 0), swap(across_second, 0, 1)]
    totals = product([beside_first, across_second], feats, totals, span, SHORT)
    beside_second, across_first, *totals = lax.optimization_barrier(
        (beside_second, across_first, *totals)
    )
    totals = product([beside_second, across_first], feats, totals, span)
    first, *totals = lax.optimization_barrier((first, *totals))
    picks, couplings_one, couplings_two, points_two = skeletons(
        first, beside_first, tables, span, gain
    )
    points_two, *totals = lax.optimization_barrier((points_two, *totals))
    pieces = [first, second, beside_first, beside_second, across_first, across_second, *diagonal]
    for bit in range(2, row_count.bit_length() - 1):
        more = [swap(value, 1 << bit, 0) for value in pieces]
        totals = product(more, feats, totals, span)
        pieces += more
    (theirs,) = product(diagonal, feats[3:], totals[3:], span)
    from_sibling = swap(theirs, 1, 0)
    (mine,) = product(diagonal, feats[1:2], totals[1:2], span)
    half = span // 2
    outs = [([2 * pos], BF16) for pos in range(line - 2)]
    outs += [([2 * pos + 1 for pos in range(odd, line - 2, 2)], kind) for odd, kind in ((0, F32), (1, BF16))]
    *direct, kept, sent = add_up(mine, from_sibling, outs, half)
    (theirs,) = product(diagonal, feats[2:3], totals[2:3], span)
    *direct, sent, theirs, points_two = lax.optimization_barrier(
        (*direct, sent, theirs, points_two)
    )
    direct = [swap(value, 0, 2 * chunk) for chunk, value in zip(far, direct)]
    arrived = swap(sent, 0, 2)
    from_sibling = swap(theirs, 1, 0)
    (mine,) = product(diagonal, feats[:1], totals[:1], span)
    staged = []
    chunks = list(range(2, line, 2))
    bit = 2
    while chunks:
        sent_places = [pos for pos, chunk in enumerate(chunks) if chunk & bit]
        kept_places = [pos for pos, chunk in enumerate(chunks) if not chunk & bit]
        outs = [(sent_places, BF16)] + [(kept_places, F32)] * (len(kept_places) > 0)
        sent, *kept = add_up(kept, arrived, outs, half, cost=LONG)
        arrived = swap(sent, 0, 2 * bit)
        staged.append(arrived[:half] if len(sent_places) > 1 else arrived)
        if kept:
            (kept,) = kept
            arrived = arrived[half:]
        chunks = [chunks[pos] for pos in kept_places]
        bit *= 2
    own_sum, near_sent = add_up(mine, from_sibling, [([0], F32), ([1], BF16)], span, (sent,))
    near_sum = swap(near_sent, 0, 2)
    other_points = swap(points_two, 0, 2)
    later = top_couplings(points_two, other_points, picks, gain)

    leaf_interp, interp_one, skeleton, reduced, sent = leaves(
        own_sum, near_sum, direct, staged, first, picks, couplings_one, later, leaf_skeleton.shape[0]
    )
    got = [swap(sent, 0, bits) for bits in (1, 2, 3)]
    upper_interp, top_state = upper_levels(
        skeleton, reduced, got, picks, (couplings_two, *later), interp_one
    )
    return jnp.swapaxes(leaf_interp, 1, 2), jnp.swapaxes(upper_interp, 2, 3), top_state


def solution(mesh):
    placed = (
        P(None, ("row", "col"), None),
        P(None, None, ("row", "col")),
        P(("row", "col"), None),
        P(("row", "col"), None),
        P("row", None),
        P("row", None),
    )
    return jax.shard_map(
        local,
        mesh=mesh,
        in_specs=placed,
        out_specs=(
            P(("row", "col"), None, None),
            P(None, ("row", "col"), None, None),
            P(None, ("row", "col"), None, None),
        ),
        check_vma=False,
    )
```

```python
import math

import jax
import jax.numpy as jnp
from jax import lax
from jax.experimental import pallas as pl
from jax.experimental.pallas import tpu as pltpu
from jax.sharding import PartitionSpec as P

LEAF = 128
F32 = jnp.float32
BF16 = jnp.bfloat16
DOUBLINGS = 9
VMEM = pl.BlockSpec(memory_space=pltpu.VMEM)


def vmem(shape, kind=F32):
    return pltpu.VMEM(tuple(shape), kind)


COST = pl.CostEstimate(flops=10**9, bytes_accessed=0, transcendentals=0)
SHORT = pl.CostEstimate(flops=0, bytes_accessed=0, transcendentals=0)
LONG = pl.CostEstimate(flops=10**10, bytes_accessed=0, transcendentals=0)
PARAMS = pltpu.CompilerParams(vmem_limit_bytes=16 << 20)


def chebyshev_constants():
    taus = [1282.0 / 1280.0]
    for _ in range(DOUBLINGS):
        taus.append(2.0 * taus[-1] * taus[-1] - 1.0)
    front = 2.0**DOUBLINGS * math.prod(taus[:-1]) / taus[-1]
    return taus[:-1], front


TAUS, FRONT = chebyshev_constants()


def over(first, second, first_dim, second_dim):
    return lax.dot_general(
        first,
        second,
        (((first_dim,), (second_dim,)), ((), ())),
        preferred_element_type=F32,
    )


def split(value):
    high = value.astype(BF16)
    rest = value - high.astype(F32)
    middle = rest.astype(BF16)
    return high, middle, (rest - middle.astype(F32)).astype(BF16)


def norm_rows(norm, first, width):
    parts = [part.astype(F32) for part in split(norm)]
    place = lax.broadcasted_iota(jnp.int32, (16, width), 0)
    extra = jnp.where(place < 6, 1.0, 0.0)
    for pos in range(3):
        extra = jnp.where(place == pos + first, parts[pos], extra)
    return extra


def row_features(feats, gain):
    feats = feats.astype(F32)
    depth, width = feats.shape
    unit = math.log2(math.e) / (2.0 * depth)
    norm = jnp.sum(feats * feats, axis=0, keepdims=True) * -unit + math.log2(gain)
    parts = [part.astype(F32) for part in split(feats * (2.0 * unit))]
    return jnp.concatenate([*parts, norm_rows(norm, 0, width)], axis=0)


def col_features(feats):
    feats = feats.astype(F32)
    depth, width = feats.shape
    unit = math.log2(math.e) / (2.0 * depth)
    norm = jnp.sum(feats * feats, axis=0, keepdims=True) * -unit
    return jnp.concatenate([feats, feats, feats, norm_rows(norm, 3, width)], axis=0).astype(BF16)


def pack_body(*refs):
    probes_ref, points_ref, *table_refs = refs[:6]
    first_ref, second_ref, own_ref, held_ref, rows_ref, *held_tables, sem = refs[6:]
    span = probes_ref.shape[1]
    pairs = [(points_ref, held_ref), *zip(table_refs, held_tables)]
    small = len(pairs)
    for quarter in range(4):
        target = (first_ref, second_ref)[quarter // 2].at[pl.ds(quarter % 2 * span, span)]
        pairs.append((probes_ref.at[quarter], target))
    copies = [
        pltpu.make_async_copy(source, target, sem.at[pos])
        for pos, (source, target) in enumerate(pairs)
    ]
    for copy in copies:
        copy.start()
    rows_ref[...] = jnp.zeros_like(rows_ref)
    for copy in copies[:small]:
        copy.wait()
    points = held_ref[...].astype(F32)
    for quarter in range(4):
        feats = points[:, quarter, :].astype(BF16)
        half_ref = (first_ref, second_ref)[quarter // 2]
        half_ref[pl.ds(2 * span + quarter % 2 * 16, 16), :] = feats
        if quarter == 0:
            own_ref[...] = feats
    start = 0
    for table in held_tables:
        count, rank = table.shape
        rows_ref[pl.ds(start, count), pl.ds(0, rank)] = table[...].astype(F32)
        start += count
    first_ref[pl.ds(second_ref.shape[0], rows_ref.shape[0]), :] = rows_ref[...].astype(BF16)
    for copy in copies[small:]:
        copy.wait()


def pack(probes, points, tables):
    _, span, samples = probes.shape
    table_rows = -(-sum(table.shape[0] for table in tables) // 16) * 16
    inputs = (probes, points, *tables)
    return pl.pallas_call(
        pack_body,
        out_shape=(
            vmem((2 * (span + 16) + table_rows, samples), BF16),
            vmem((2 * (span + 16), samples), BF16),
            vmem((16, span), BF16),
        ),
        in_specs=[pl.BlockSpec(memory_space=pltpu.HBM)] * len(inputs),
        scratch_shapes=[
            pltpu.VMEM(points.shape, BF16),
            pltpu.VMEM((table_rows, samples), F32),
            *[pltpu.VMEM(table.shape, jnp.int32) for table in tables],
            pltpu.SemaphoreType.DMA((5 + len(tables),)),
        ],
        cost_estimate=COST,
        compiler_params=PARAMS,
        name="pack",
    )(*(pltpu.with_memory_space_constraint(value, pltpu.HBM) for value in inputs))


def masked(entries):
    shape = entries.shape
    row_leaf = lax.broadcasted_iota(jnp.int32, shape, 0) // LEAF
    col_leaf = lax.broadcasted_iota(jnp.int32, shape, 1) // LEAF
    return jnp.where(row_leaf == col_leaf, 0.0, entries)


def add_halves(half_refs, row_refs, cols_ref, put, span, own):
    for number, half_ref in enumerate(half_refs):
        for quarter in range(2):
            feats = half_ref[pl.ds(2 * span + 16 * quarter, 16), :]
            cols_ref[:, pl.ds((2 * number + quarter) * span, span)] = col_features(feats)
    columns = 2 * span * len(half_refs)
    for group, rows_ref in enumerate(row_refs):
        for start in range(0, rows_ref.shape[0], span):
            feats = rows_ref[pl.ds(start, span), :]
            entries = jnp.exp2(over(feats, cols_ref[:, :columns], 1, 0))
            if own and group == 0 and start == 0:
                entries = jnp.concatenate([masked(entries[:, :span]), entries[:, span:]], axis=1)
            randoms = [half_ref[pl.ds(0, 2 * span), :] for half_ref in half_refs]
            put(group, start, over(entries.astype(BF16), jnp.concatenate(randoms, axis=0), 1, 0))


def first_product_body(gain, span, groups, point_count, *refs):
    half_refs, point_refs = refs[:2], refs[2 : point_count + 2]
    row_refs = refs[point_count + 2 : point_count + 2 + len(groups)]
    total_refs, cols_ref = refs[point_count + 2 + len(groups) : -1], refs[-1]
    for rows_ref, places in zip(row_refs, groups):
        for pos, (array, start) in enumerate(places):
            feats = point_refs[array][:, pl.ds(start, span)]
            rows_ref[pl.ds(pos * span, span), :] = row_features(feats, gain).T.astype(BF16)

    def put(group, start, value):
        total_refs[group][pl.ds(start, span), :] = value

    add_halves(half_refs, row_refs, cols_ref, put, span, True)


def first_product(halves, points, groups, span, gain):
    samples = halves[0].shape[1]
    rows = [len(places) * span for places in groups]
    out = pl.pallas_call(
        lambda *refs: first_product_body(gain, span, groups, len(points), *refs),
        out_shape=[vmem((count, 64), BF16) for count in rows]
        + [vmem((count, samples), F32) for count in rows],
        scratch_shapes=[pltpu.VMEM((64, 4 * span), BF16)],
        cost_estimate=COST,
        compiler_params=PARAMS,
        name="first_product",
    )(*halves, *points)
    return out[: len(groups)], out[len(groups) :]


def product_body(span, half_count, count, *refs):
    half_refs, refs = refs[:half_count], refs[half_count:]
    row_refs, old_refs, total_refs = refs[:count], refs[count : 2 * count], refs[2 * count : -1]
    cols_ref = refs[-1]
    for number in range(0, half_count, 2):

        def put(group, start, value):
            place = pl.ds(start, span)
            base = old_refs if number == 0 else total_refs
            total_refs[group][place, :] = base[group][place, :] + value

        add_halves(half_refs[number : number + 2], row_refs, cols_ref, put, span, False)


def product(halves, rows, totals, span, cost=COST):
    return pl.pallas_call(
        lambda *refs: product_body(span, len(halves), len(rows), *refs),
        out_shape=[vmem(total.shape, F32) for total in totals],
        scratch_shapes=[pltpu.VMEM((64, 4 * span), BF16)],
        cost_estimate=cost,
        compiler_params=PARAMS,
        name="product",
    )(*halves, *rows, *totals)


def add_up_body(span, outs, mine_ref, theirs_ref, *refs):
    for (chunks, _), out_ref in zip(outs, refs[-len(outs) :]):
        for pos, chunk in enumerate(chunks):
            place = pl.ds(chunk * span, span)
            value = mine_ref[place, :] + theirs_ref[place, :].astype(F32)
            out_ref[pl.ds(pos * span, span), :] = value.astype(out_ref.dtype)


def add_up(mine, theirs, outs, span, after=(), cost=COST):
    samples = mine.shape[1]
    return pl.pallas_call(
        lambda *refs: add_up_body(span, outs, *refs),
        out_shape=[vmem((len(chunks) * span, samples), kind) for chunks, kind in outs],
        cost_estimate=cost,
        compiler_params=PARAMS,
        name="add_up",
    )(mine, theirs, *after)


def wide_product(first, second, second_dim):
    high, middle, low = split(first)
    other_high, other_middle, other_low = split(second)
    return over(
        jnp.concatenate([high, high, middle, middle, low, high], axis=1),
        jnp.concatenate(
            [other_high, other_middle, other_high, other_middle, other_high, other_low],
            axis=second_dim,
        ),
        1,
        second_dim,
    )


def exact_product(first, second):
    second = second.astype(BF16)
    return over(
        jnp.concatenate(split(first), axis=1), jnp.concatenate([second] * 3, axis=0), 1, 0
    )


def twice_product(twice_parts, parts):
    high, middle, low = twice_parts
    other_high, other_middle, other_low = parts
    left = lax.broadcasted_iota(jnp.int32, high.shape, 1) < high.shape[1] // 2
    last = jnp.where(left, low.astype(F32), high.astype(F32)).astype(BF16)
    return over(
        jnp.concatenate([high, middle, last], axis=1),
        jnp.concatenate(
            [other_high, other_middle, other_high, other_middle, other_high, other_low], axis=0
        ),
        1,
        0,
    )


def select_rows(picks, value):
    return over(
        jnp.concatenate([picks] * 3, axis=1), jnp.concatenate(split(value), axis=0), 1, 0
    )


def interpolate(stacks, skeletons):
    rank, pool = skeletons[0].shape[0], stacks[0].shape[0]
    place = lax.broadcasted_iota(jnp.int32, (rank, 2 * rank), 0)
    other = lax.broadcasted_iota(jnp.int32, (rank, 2 * rank), 1)
    eyes = jnp.where((other == place) | (other == place + rank), 1.0, 0.0)
    states = []
    for skeleton, stack in zip(skeletons, stacks):
        products = wide_product(skeleton, jnp.concatenate([stack, skeleton, skeleton], axis=0), 1)
        ridge = 0.05 * jnp.sum(skeleton * skeleton, keepdims=True) / rank + 1e-05
        inverse = 1.0 / (640.0 * ridge)
        states.append((products[:, :pool], eyes - products[:, pool:] * inverse, inverse))
    for number, tau in enumerate(TAUS):
        last = number == DOUBLINGS - 1
        later = []
        for solved, power, inverse in states:
            power_parts = split(power)
            parts = split(solved)
            if not last:
                parts = [jnp.concatenate(pair, axis=1) for pair in zip(parts, power_parts)]
            both = twice_product(power_parts, parts)
            solved = solved + both[:, :pool] * (1.0 / tau)
            later.append((solved, None if last else 2.0 * both[:, pool:] - eyes, inverse))
        states = later
    return [solved * (inverse * FRONT) for solved, _, inverse in states]


def merge(nodes, early=None):
    stacks, skeletons = [], []
    for samples, reduced, coupling, picks in nodes:
        pool = samples.shape[0]
        high, middle, low = split(reduced)
        coupled = over(
            coupling, jnp.concatenate([high, middle, high, middle, high, low], axis=0), 1, 0
        )
        stacks.append(samples - coupled[:pool])
        skeletons.append(select_rows(picks, samples) - coupled[pool:])
    if early is not None:
        early(skeletons[0])
    interps = interpolate(stacks, skeletons)
    return [
        (interp, skeleton, wide_product(interp, node[1], 0))
        for interp, skeleton, node in zip(interps, skeletons, nodes)
    ]


def leaves_body(received, *refs):
    own_ref, *others = refs[: received + 1]
    source_ref, picks_ref, couplings_ref = refs[received + 1 : received + 4]
    leaf_ref, upper_ref, skeleton_ref, reduced_ref, sent_ref, held_ref, sem = refs[-7:]
    total = own_ref[...]
    for other in others:
        total = total + other[...].astype(F32)
    count = total.shape[0] // LEAF
    stacks = [total[leaf * LEAF : (leaf + 1) * LEAF] for leaf in range(count)]
    skeletons = [select_rows(picks_ref[leaf], stack) for leaf, stack in enumerate(stacks)]
    reduced = []
    for leaf, interp in enumerate(interpolate(stacks, skeletons)):
        held_ref[leaf] = interp
        reduced.append(exact_product(interp, source_ref[pl.ds(leaf * LEAF, LEAF), :]))
    copy = pltpu.make_async_copy(held_ref, leaf_ref, sem)
    copy.start()
    node = (
        jnp.concatenate(skeletons, axis=0),
        jnp.concatenate(reduced, axis=0),
        couplings_ref[...],
        picks_ref[count],
    )
    ((interp, skeleton, reduced),) = merge([node])
    upper_ref[...] = interp
    skeleton_ref[...] = skeleton
    reduced_ref[...] = reduced
    for pos, part in enumerate((*split(skeleton)[:2], reduced.astype(BF16))):
        sent_ref[pl.ds(pos * skeleton.shape[0], skeleton.shape[0]), :] = part
    copy.wait()


def leaves(own, others, source, picks, couplings, later, leaf_count):
    samples = own.shape[1]
    rank, pool = picks.shape[1:]
    return pl.pallas_call(
        lambda *refs: leaves_body(len(others), *refs),
        out_shape=(
            jax.ShapeDtypeStruct((leaf_count, rank, LEAF), F32),
            vmem((rank, pool), F32),
            vmem((rank, samples), F32),
            vmem((rank, samples), F32),
            vmem((3 * rank, samples), BF16),
        ),
        out_specs=(pl.BlockSpec(memory_space=pl.ANY), VMEM, VMEM, VMEM, VMEM),
        scratch_shapes=[pltpu.VMEM((leaf_count, rank, LEAF), F32), pltpu.SemaphoreType.DMA],
        cost_estimate=COST,
        compiler_params=PARAMS,
        name="leaves",
    )(own, *others, source, picks, couplings, *later)


def first_of_pair(number):
    return (lax.axis_index("col") >> (number - 2)) % 2 == 0


def pair(mine, theirs, mine_first):
    first = jnp.where(mine_first, mine, theirs)
    second = jnp.where(mine_first, theirs, mine)
    return jnp.concatenate([first, second], axis=0)


def upper_body(picks_count, *refs):
    states = [(refs[0][...], refs[1][...])]
    rank = refs[0].shape[0]
    for got_ref in refs[2:5]:
        high, middle, reduced = (got_ref[pl.ds(pos * rank, rank), :] for pos in range(3))
        states.append((high.astype(F32) + middle.astype(F32), reduced.astype(F32)))
    picks_ref, two_ref, other_ref, three_ref, one_ref, upper_out, top_out = refs[5:12]
    upper_ref, state_ref, sem = refs[12:]
    places = [
        (one_ref, upper_out.at[0, 0]),
        (upper_ref.at[0], upper_out.at[1, 0]),
        (upper_ref.at[1], upper_out.at[2, 0]),
        (state_ref.at[0], top_out.at[0, 0]),
        (state_ref.at[1], top_out.at[1, 0]),
    ]
    copies = [
        pltpu.make_async_copy(source, target, sem.at[pos])
        for pos, (source, target) in enumerate(places)
    ]
    copies[0].start()
    mine_first = first_of_pair(2)
    nodes = []
    for number, coupling_ref in enumerate((two_ref, other_ref)):
        mine, theirs = states[2 * number : 2 * number + 2]
        picks = picks_ref[picks_count - 3 + number]
        stacks = [pair(*parts, mine_first) for parts in zip(mine, theirs)]
        nodes.append((*stacks, coupling_ref[...], picks))
    mine, theirs = merge(nodes)
    upper_ref[0] = mine[0]
    copies[1].start()

    def early(skeleton):
        state_ref[0] = skeleton
        copies[3].start()

    mine_first = first_of_pair(3)
    stacks = [pair(*parts, mine_first) for parts in zip(mine[1:], theirs[1:])]
    ((interp, _, reduced),) = merge([(*stacks, three_ref[...], picks_ref[picks_count - 1])], early)
    upper_ref[1] = interp
    copies[2].start()
    state_ref[1] = reduced
    copies[4].start()
    for copy in copies:
        copy.wait()


def upper_levels(skeleton, reduced, got, picks, couplings, interp_one):
    rank, pool = picks.shape[1:]
    samples = skeleton.shape[1]
    return pl.pallas_call(
        lambda *refs: upper_body(picks.shape[0], *refs),
        out_shape=(
            jax.ShapeDtypeStruct((3, 1, rank, pool), F32),
            jax.ShapeDtypeStruct((2, 1, rank, samples), F32),
        ),
        out_specs=(pl.BlockSpec(memory_space=pl.ANY),) * 2,
        scratch_shapes=[
            pltpu.VMEM((2, rank, pool), F32),
            pltpu.VMEM((2, rank, samples), F32),
            pltpu.SemaphoreType.DMA((5,)),
        ],
        cost_estimate=COST,
        compiler_params=PARAMS,
        name="upper_levels",
    )(skeleton, reduced, *got, picks, *couplings, interp_one)


def one_hot(chosen, pool):
    place = lax.broadcasted_iota(jnp.int32, (pool, chosen.shape[1]), 0)
    return jnp.where(place.astype(F32) == chosen, 1.0, 0.0).astype(F32)


def couple(first, second, picks, gain, couplings_ref):
    rank = first.shape[1]
    points = jnp.concatenate([first, second], axis=1)
    entries = jnp.exp2(over(row_features(points, gain).astype(BF16), col_features(points), 0, 0))
    left = lax.broadcasted_iota(jnp.int32, entries.shape, 1) < rank
    upper = lax.broadcasted_iota(jnp.int32, entries.shape, 0) < rank
    entries = jnp.where(left == upper, 0.0, entries)
    chosen = select_rows(picks.T.astype(BF16), entries)
    high, middle, low = split(jnp.concatenate([entries, chosen], axis=0))
    couplings_ref[...] = jnp.concatenate([high, high, middle, middle, low, high], axis=1)


def coupling_shape(rank):
    return vmem((3 * rank, 12 * rank), BF16)


def skeletons_body(gain, span, counts, mine_ref, beside_ref, *refs):
    picks_ref, one_ref, two_ref, points_ref = refs
    rank, pool = picks_ref.shape[1:]
    leaf_count = counts[0]
    tables = 2 * (span + 16)
    nodes = []
    for source_ref in (mine_ref, beside_ref):
        rows = source_ref[pl.ds(tables, source_ref.shape[0] - tables), :rank].astype(F32)
        hots = [one_hot(rows[pos : pos + 1], pool) for pos in range(leaf_count + 1)]
        children = []
        for leaf in range(leaf_count):
            feats = source_ref[pl.ds(2 * span, 16), pl.ds(leaf * LEAF, LEAF)]
            children.append(over(feats, hots[leaf].astype(BF16), 1, 0))
        points = jnp.concatenate(children, axis=1)
        nodes.append(over(points, hots[leaf_count], 1, 0))
        if source_ref is mine_ref:
            couple(*children, hots[leaf_count], gain, one_ref)
            start = leaf_count + counts[1]
            level_two = lax.axis_index("col") // 2
            wanted = [level_two, level_two + 1 - 2 * (level_two % 2), counts[2] + level_two // 2]
            for row in wanted:
                place = lax.broadcasted_iota(jnp.int32, rows.shape, 0)
                named = jnp.where(place == start + row, rows, 0.0)
                hots.append(one_hot(jnp.sum(named, axis=0, keepdims=True), pool))
            for number, hot in enumerate(hots):
                picks_ref[number] = hot.T.astype(BF16)
            upper = hots[leaf_count + 1]
    mine, theirs = nodes
    mine_first = first_of_pair(2)
    first = jnp.where(mine_first, mine, theirs)
    second = jnp.where(mine_first, theirs, mine)
    couple(first, second, upper, gain, two_ref)
    points_ref[...] = jnp.concatenate([first, second], axis=1).astype(BF16)


def skeletons(packed, beside, tables, span, gain):
    leaf_count, rank = tables[0].shape
    counts = [table.shape[0] for table in tables]
    return pl.pallas_call(
        lambda *refs: skeletons_body(gain, span, counts, *refs),
        out_shape=(
            vmem((leaf_count + 4, rank, LEAF), BF16),
            coupling_shape(rank),
            coupling_shape(rank),
            vmem((16, 2 * rank), BF16),
        ),
        cost_estimate=COST,
        compiler_params=PARAMS,
        name="skeletons",
    )(packed, beside)


def top_couplings_body(gain, mine_ref, theirs_ref, picks_ref, other_ref, three_ref):
    count, rank, _ = picks_ref.shape
    picks = [picks_ref[count - pos].astype(F32).T for pos in (3, 2, 1)]
    mine, theirs = mine_ref[...].astype(F32), theirs_ref[...].astype(F32)
    couple(theirs[:, :rank], theirs[:, rank:], picks[1], gain, other_ref)
    mine, theirs = over(mine, picks[0], 1, 0), over(theirs, picks[1], 1, 0)
    mine_first = first_of_pair(3)
    first = jnp.where(mine_first, mine, theirs)
    second = jnp.where(mine_first, theirs, mine)
    couple(first, second, picks[2], gain, three_ref)


def top_couplings(mine, theirs, picks, gain):
    return pl.pallas_call(
        lambda *refs: top_couplings_body(gain, *refs),
        out_shape=[coupling_shape(picks.shape[1])] * 2,
        cost_estimate=LONG,
        compiler_params=PARAMS,
        name="top_couplings",
    )(mine, theirs, picks)


def local(probes, points, leaf_skeleton, skeleton_one, skeleton_two, skeleton_three):
    span = probes.shape[1]
    row_count = lax.axis_size("row")
    col_count = lax.axis_size("col")
    gain = 16.0 / math.sqrt(4 * span * row_count * col_count)

    def swap(value, row_bits, col_bits):
        pairs = [
            (r * col_count + c, (r ^ row_bits) * col_count + (c ^ col_bits))
            for r in range(row_count)
            for c in range(col_count)
        ]
        return lax.ppermute(value, ("row", "col"), pairs)

    tables = (leaf_skeleton, skeleton_one, skeleton_two, skeleton_three)
    first, second, own_points = pack(probes, points, tables)
    beside_first, across_second = swap(first, 0, 1), swap(second, 2, 0)
    line = col_count // 2
    line_points = own_points
    for bit in range(1, col_count.bit_length() - 1):
        line_points = jnp.concatenate([line_points, swap(line_points, 0, 1 << bit)], axis=1)
        if bit == 1:
            line_points, *late = lax.optimization_barrier((line_points, first, second))
    beside_second, across_first = swap(late[1], 0, 1), swap(late[0], 2, 0)
    line_points = [line_points, swap(line_points, 1, 0)]
    near, far = range(2), range(2, line)
    groups = [
        [(core, chunk * span) for chunk in group] for core in range(2) for group in (near, far)
    ]
    feats, totals = first_product((first, second), line_points, groups, span, gain)
    beside_first, across_second, *totals = lax.optimization_barrier(
        (beside_first, across_second, *totals)
    )
    diagonal = [swap(beside_first, 2, 0), swap(across_second, 0, 1)]
    totals = product([beside_first, across_second], feats, totals, span, SHORT)
    beside_second, across_first, *totals = lax.optimization_barrier(
        (beside_second, across_first, *totals)
    )
    totals = product([beside_second, across_first], feats, totals, span)
    first, *totals = lax.optimization_barrier((first, *totals))
    picks, couplings_one, couplings_two, points_two = skeletons(
        first, beside_first, tables, span, gain
    )
    points_two, *totals = lax.optimization_barrier((points_two, *totals))
    pieces = [first, second, beside_first, beside_second, across_first, across_second, *diagonal]
    for bit in range(2, row_count.bit_length() - 1):
        more = [swap(value, 1 << bit, 0) for value in pieces]
        totals = product(more, feats, totals, span)
        pieces += more
    (theirs,) = product(diagonal, feats[3:], totals[3:], span)
    from_sibling = swap(theirs, 1, 0)
    (mine,) = product(diagonal, feats[1:2], totals[1:2], span)
    outs = [(range(0, line - 2, 2), F32), (range(1, line - 2, 2), BF16)]
    kept, sent = add_up(mine, from_sibling, outs, span)
    (theirs,) = product(diagonal, feats[2:3], totals[2:3], span)
    sent, theirs, points_two = lax.optimization_barrier((sent, theirs, points_two))
    arrived = swap(sent, 0, 2)
    from_sibling = swap(theirs, 1, 0)
    (mine,) = product(diagonal, feats[:1], totals[:1], span)
    own_sum, near_sent = add_up(mine, from_sibling, [([0], F32), ([1], BF16)], span)
    near_sum = swap(near_sent, 0, 2)
    received = []
    chunks = list(range(2, line, 2))
    bit = 2
    while chunks:
        sent_places = [pos for pos, chunk in enumerate(chunks) if chunk & bit]
        kept_places = [pos for pos, chunk in enumerate(chunks) if not chunk & bit]
        outs = [(sent_places, BF16)] + [(kept_places, F32)] * (len(kept_places) > 0)
        sent, *kept = add_up(kept, arrived, outs, span, (near_sent,), LONG)
        arrived = swap(sent, 0, 2 * bit)
        received.append(arrived[:span] if len(sent_places) > 1 else arrived)
        if kept:
            (kept,) = kept
            arrived = arrived[span:]
        chunks = [chunks[pos] for pos in kept_places]
        bit *= 2
    received.append(near_sum)
    other_points = swap(points_two, 0, 2)
    later = top_couplings(points_two, other_points, picks, gain)

    leaf_interp, interp_one, skeleton, reduced, sent = leaves(
        own_sum, received, first, picks, couplings_one, later, leaf_skeleton.shape[0]
    )
    got = [swap(sent, 0, bits) for bits in (1, 2, 3)]
    upper_interp, top_state = upper_levels(
        skeleton, reduced, got, picks, (couplings_two, *later), interp_one
    )
    return jnp.swapaxes(leaf_interp, 1, 2), jnp.swapaxes(upper_interp, 2, 3), top_state


def solution(mesh):
    placed = (
        P(None, ("row", "col"), None),
        P(None, None, ("row", "col")),
        P(("row", "col"), None),
        P(("row", "col"), None),
        P("row", None),
        P("row", None),
    )
    return jax.shard_map(
        local,
        mesh=mesh,
        in_specs=placed,
        out_specs=(
            P(("row", "col"), None, None),
            P(None, ("row", "col"), None, None),
            P(None, ("row", "col"), None, None),
        ),
        check_vma=False,
    )
```

```python
import math

import jax
import jax.numpy as jnp
from jax import lax
from jax.experimental import pallas as pl
from jax.experimental.pallas import tpu as pltpu
from jax.sharding import PartitionSpec as P

LEAF = 128
F32 = jnp.float32
BF16 = jnp.bfloat16
DOUBLINGS = 9
VMEM = pl.BlockSpec(memory_space=pltpu.VMEM)


def vmem(shape, kind=F32):
    return pltpu.VMEM(tuple(shape), kind)


COST = pl.CostEstimate(flops=10**9, bytes_accessed=0, transcendentals=0)
SHORT = pl.CostEstimate(flops=0, bytes_accessed=0, transcendentals=0)
LONG = pl.CostEstimate(flops=10**10, bytes_accessed=0, transcendentals=0)
PARAMS = pltpu.CompilerParams(vmem_limit_bytes=16 << 20)


def chebyshev_constants():
    taus = [1282.0 / 1280.0]
    for _ in range(DOUBLINGS):
        taus.append(2.0 * taus[-1] * taus[-1] - 1.0)
    front = 2.0**DOUBLINGS * math.prod(taus[:-1]) / taus[-1]
    return taus[:-1], front


TAUS, FRONT = chebyshev_constants()


def over(first, second, first_dim, second_dim):
    return lax.dot_general(
        first,
        second,
        (((first_dim,), (second_dim,)), ((), ())),
        preferred_element_type=F32,
    )


def split(value):
    high = value.astype(BF16)
    rest = value - high.astype(F32)
    middle = rest.astype(BF16)
    return high, middle, (rest - middle.astype(F32)).astype(BF16)


def norm_rows(norm, first, width):
    parts = [part.astype(F32) for part in split(norm)]
    place = lax.broadcasted_iota(jnp.int32, (16, width), 0)
    extra = jnp.where(place < 6, 1.0, 0.0)
    for pos in range(3):
        extra = jnp.where(place == pos + first, parts[pos], extra)
    return extra


def row_features(feats, gain):
    feats = feats.astype(F32)
    depth, width = feats.shape
    unit = math.log2(math.e) / (2.0 * depth)
    norm = jnp.sum(feats * feats, axis=0, keepdims=True) * -unit + math.log2(gain)
    parts = [part.astype(F32) for part in split(feats * (2.0 * unit))]
    return jnp.concatenate([*parts, norm_rows(norm, 0, width)], axis=0)


def col_features(feats):
    feats = feats.astype(F32)
    depth, width = feats.shape
    unit = math.log2(math.e) / (2.0 * depth)
    norm = jnp.sum(feats * feats, axis=0, keepdims=True) * -unit
    return jnp.concatenate([feats, feats, feats, norm_rows(norm, 3, width)], axis=0).astype(BF16)


def pack_body(*refs):
    probes_ref, points_ref, *table_refs = refs[:6]
    first_ref, second_ref, own_ref, held_ref, rows_ref, *held_tables, sem = refs[6:]
    span = probes_ref.shape[1]
    pairs = [(points_ref, held_ref), *zip(table_refs, held_tables)]
    small = len(pairs)
    for quarter in range(4):
        target = (first_ref, second_ref)[quarter // 2].at[pl.ds(quarter % 2 * span, span)]
        pairs.append((probes_ref.at[quarter], target))
    copies = [
        pltpu.make_async_copy(source, target, sem.at[pos])
        for pos, (source, target) in enumerate(pairs)
    ]
    for copy in copies:
        copy.start()
    rows_ref[...] = jnp.zeros_like(rows_ref)
    for copy in copies[:small]:
        copy.wait()
    points = held_ref[...].astype(F32)
    for quarter in range(4):
        feats = points[:, quarter, :].astype(BF16)
        half_ref = (first_ref, second_ref)[quarter // 2]
        half_ref[pl.ds(2 * span + quarter % 2 * 16, 16), :] = feats
        if quarter == 0:
            own_ref[...] = feats
    start = 0
    for table in held_tables:
        count, rank = table.shape
        rows_ref[pl.ds(start, count), pl.ds(0, rank)] = table[...].astype(F32)
        start += count
    first_ref[pl.ds(second_ref.shape[0], rows_ref.shape[0]), :] = rows_ref[...].astype(BF16)
    for copy in copies[small:]:
        copy.wait()


def pack(probes, points, tables):
    _, span, samples = probes.shape
    table_rows = -(-sum(table.shape[0] for table in tables) // 16) * 16
    inputs = (probes, points, *tables)
    return pl.pallas_call(
        pack_body,
        out_shape=(
            vmem((2 * (span + 16) + table_rows, samples), BF16),
            vmem((2 * (span + 16), samples), BF16),
            vmem((16, span), BF16),
        ),
        in_specs=[pl.BlockSpec(memory_space=pltpu.HBM)] * len(inputs),
        scratch_shapes=[
            pltpu.VMEM(points.shape, BF16),
            pltpu.VMEM((table_rows, samples), F32),
            *[pltpu.VMEM(table.shape, jnp.int32) for table in tables],
            pltpu.SemaphoreType.DMA((5 + len(tables),)),
        ],
        cost_estimate=COST,
        compiler_params=PARAMS,
        name="pack",
    )(*(pltpu.with_memory_space_constraint(value, pltpu.HBM) for value in inputs))


def masked(entries):
    shape = entries.shape
    row_leaf = lax.broadcasted_iota(jnp.int32, shape, 0) // LEAF
    col_leaf = lax.broadcasted_iota(jnp.int32, shape, 1) // LEAF
    return jnp.where(row_leaf == col_leaf, 0.0, entries)


def add_halves(half_refs, row_refs, cols_ref, put, span, own, ready=False):
    for number, half_ref in enumerate(() if ready else half_refs):
        for quarter in range(2):
            feats = half_ref[pl.ds(2 * span + 16 * quarter, 16), :]
            cols_ref[:, pl.ds((2 * number + quarter) * span, span)] = col_features(feats)
    columns = 2 * span * len(half_refs)
    for group, rows_ref in enumerate(row_refs):
        for start in range(0, rows_ref.shape[0], span):
            feats = rows_ref[pl.ds(start, span), :]
            entries = jnp.exp2(over(feats, cols_ref[:, :columns], 1, 0))
            if own and group == 0 and start == 0:
                entries = jnp.concatenate([masked(entries[:, :span]), entries[:, span:]], axis=1)
            randoms = [half_ref[pl.ds(0, 2 * span), :] for half_ref in half_refs]
            put(group, start, over(entries.astype(BF16), jnp.concatenate(randoms, axis=0), 1, 0))


def first_product_body(gain, span, groups, point_count, *refs):
    half_refs, point_refs = refs[:2], refs[2 : point_count + 2]
    row_refs = refs[point_count + 2 : point_count + 2 + len(groups)]
    total_refs, cols_ref = refs[point_count + 2 + len(groups) : -1], refs[-1]
    for rows_ref, places in zip(row_refs, groups):
        for pos, (array, start) in enumerate(places):
            feats = point_refs[array][:, pl.ds(start, span)]
            rows_ref[pl.ds(pos * span, span), :] = row_features(feats, gain).T.astype(BF16)

    def put(group, start, value):
        total_refs[group][pl.ds(start, span), :] = value

    add_halves(half_refs, row_refs, cols_ref, put, span, True)


def first_product(halves, points, groups, span, gain):
    samples = halves[0].shape[1]
    rows = [len(places) * span for places in groups]
    out = pl.pallas_call(
        lambda *refs: first_product_body(gain, span, groups, len(points), *refs),
        out_shape=[vmem((count, 64), BF16) for count in rows]
        + [vmem((count, samples), F32) for count in rows],
        scratch_shapes=[pltpu.VMEM((64, 4 * span), BF16)],
        cost_estimate=COST,
        compiler_params=PARAMS,
        name="first_product",
    )(*halves, *points)
    return out[: len(groups)], out[len(groups) :]


def product_body(span, half_count, count, ready, *refs):
    half_refs, refs = refs[:half_count], refs[half_count:]
    row_refs, old_refs = refs[:count], refs[count : 2 * count]
    total_refs, cols_ref = refs[2 * count : 3 * count], refs[-1]
    if ready:
        cols_ref, *total_refs = refs[2 * count :]
    for number in range(0, half_count, 2):

        def put(group, start, value):
            place = pl.ds(start, span)
            base = old_refs if number == 0 else total_refs
            total_refs[group][place, :] = base[group][place, :] + value

        add_halves(half_refs[number : number + 2], row_refs, cols_ref, put, span, False, ready)


def product(halves, rows, totals, span, cost=COST, cols=()):
    out_shape = [vmem(total.shape, F32) for total in totals]
    if not cols:
        out_shape.append(vmem((64, 4 * span), BF16))
    out = pl.pallas_call(
        lambda *refs: product_body(span, len(halves), len(rows), len(cols) > 0, *refs),
        out_shape=out_shape,
        cost_estimate=cost,
        compiler_params=PARAMS,
        name="product",
    )(*halves, *rows, *totals, *cols)
    return out if not cols else [*out, *cols]


def add_up_body(span, outs, mine_ref, theirs_ref, *refs):
    for (chunks, _), out_ref in zip(outs, refs[-len(outs) :]):
        for pos, chunk in enumerate(chunks):
            place = pl.ds(chunk * span, span)
            value = mine_ref[place, :] + theirs_ref[place, :].astype(F32)
            out_ref[pl.ds(pos * span, span), :] = value.astype(out_ref.dtype)


def add_up(mine, theirs, outs, span, after=(), cost=COST):
    samples = mine.shape[1]
    return pl.pallas_call(
        lambda *refs: add_up_body(span, outs, *refs),
        out_shape=[vmem((len(chunks) * span, samples), kind) for chunks, kind in outs],
        cost_estimate=cost,
        compiler_params=PARAMS,
        name="add_up",
    )(mine, theirs, *after)


def wide_product(first, second):
    high, middle, low = split(first)
    other_high, other_middle, other_low = split(second)
    return over(
        jnp.concatenate([high, high, middle, middle, low, high], axis=1),
        jnp.concatenate(
            [other_high, other_middle, other_high, other_middle, other_high, other_low], axis=1
        ),
        1,
        1,
    )


def near_product(first, second):
    high, middle, _ = split(first)
    return over(jnp.concatenate([high, high, middle], axis=1), near_parts(second), 1, 0)


def near_parts(second):
    high, middle, _ = split(second)
    return jnp.concatenate([high, middle, high], axis=0)


def exact_product(first, second):
    second = second.astype(BF16)
    return over(
        jnp.concatenate(split(first), axis=1), jnp.concatenate([second] * 3, axis=0), 1, 0
    )


def twice_product(twice, twice_parts, parts):
    high, middle, _ = twice_parts
    other_high, other_middle, other_low = parts
    left = lax.broadcasted_iota(jnp.int32, high.shape, 1) < high.shape[1] // 2
    low = twice - high.astype(F32) - middle.astype(F32)
    last = jnp.where(left, low, high.astype(F32)).astype(BF16)
    return over(
        jnp.concatenate([high, middle, last], axis=1),
        jnp.concatenate(
            [other_high, other_middle, other_high, other_middle, other_high, other_low], axis=0
        ),
        1,
        0,
    )


def select_rows(picks, value):
    return over(
        jnp.concatenate([picks] * 3, axis=1), jnp.concatenate(split(value), axis=0), 1, 0
    )


def interpolate(stacks, skeletons):
    rank, pool = skeletons[0].shape[0], stacks[0].shape[0]
    place = lax.broadcasted_iota(jnp.int32, (rank, 2 * rank), 0)
    other = lax.broadcasted_iota(jnp.int32, (rank, 2 * rank), 1)
    eyes = jnp.where((other == place) | (other == place + rank), 1.0, 0.0)
    states = []
    for skeleton, stack in zip(skeletons, stacks):
        products = wide_product(skeleton, jnp.concatenate([stack, skeleton, skeleton], axis=0))
        ridge = 0.05 * jnp.sum(skeleton * skeleton, keepdims=True) / rank + 1e-05
        inverse = 1.0 / (640.0 * ridge)
        states.append((products[:, :pool], eyes - products[:, pool:] * inverse, inverse))
    for number, tau in enumerate(TAUS):
        last = number == DOUBLINGS - 1
        later = []
        for solved, power, inverse in states:
            power_parts = split(power)
            parts = split(solved)
            if not last:
                parts = [jnp.concatenate(pair, axis=1) for pair in zip(parts, power_parts)]
            both = twice_product(power, power_parts, parts)
            solved = solved + both[:, :pool] * (1.0 / tau)
            later.append((solved, None if last else 2.0 * both[:, pool:] - eyes, inverse))
        states = later
    return [solved * (inverse * FRONT) for solved, _, inverse in states]


def merge(nodes, early=None):
    stacks, skeletons = [], []
    for samples, reduced, coupling, picks in nodes:
        pool = samples.shape[0]
        coupled = over(coupling, near_parts(reduced), 1, 0)
        stacks.append(samples - coupled[:pool])
        skeletons.append(select_rows(picks, samples) - coupled[pool:])
    if early is not None:
        early(skeletons[0])
    interps = interpolate(stacks, skeletons)
    return [
        (interp, skeleton, near_product(interp, node[1]))
        for interp, skeleton, node in zip(interps, skeletons, nodes)
    ]


def leaves_body(received, *refs):
    own_ref, *others = refs[: received + 1]
    source_ref, picks_ref, couplings_ref = refs[received + 1 : received + 4]
    leaf_ref, upper_ref, skeleton_ref, reduced_ref, sent_ref, held_ref, sem = refs[-7:]
    total = own_ref[...]
    for other in others:
        total = total + other[...].astype(F32)
    count = total.shape[0] // LEAF
    stacks = [total[leaf * LEAF : (leaf + 1) * LEAF] for leaf in range(count)]
    skeletons = [select_rows(picks_ref[leaf], stack) for leaf, stack in enumerate(stacks)]
    reduced = []
    for leaf, interp in enumerate(interpolate(stacks, skeletons)):
        held_ref[leaf] = interp
        reduced.append(exact_product(interp, source_ref[pl.ds(leaf * LEAF, LEAF), :]))
    copy = pltpu.make_async_copy(held_ref, leaf_ref, sem)
    copy.start()
    node = (
        jnp.concatenate(skeletons, axis=0),
        jnp.concatenate(reduced, axis=0),
        couplings_ref[...],
        picks_ref[count],
    )
    ((interp, skeleton, reduced),) = merge([node])
    upper_ref[...] = interp
    skeleton_ref[...] = skeleton
    reduced_ref[...] = reduced
    for pos, part in enumerate((*split(skeleton)[:2], reduced.astype(BF16))):
        sent_ref[pl.ds(pos * skeleton.shape[0], skeleton.shape[0]), :] = part
    copy.wait()


def leaves(own, others, source, picks, couplings, later, leaf_count):
    samples = own.shape[1]
    rank, pool = picks.shape[1:]
    return pl.pallas_call(
        lambda *refs: leaves_body(len(others), *refs),
        out_shape=(
            jax.ShapeDtypeStruct((leaf_count, rank, LEAF), F32),
            vmem((rank, pool), F32),
            vmem((rank, samples), F32),
            vmem((rank, samples), F32),
            vmem((3 * rank, samples), BF16),
        ),
        out_specs=(pl.BlockSpec(memory_space=pl.ANY), VMEM, VMEM, VMEM, VMEM),
        scratch_shapes=[pltpu.VMEM((leaf_count, rank, LEAF), F32), pltpu.SemaphoreType.DMA],
        cost_estimate=COST,
        compiler_params=PARAMS,
        name="leaves",
    )(own, *others, source, picks, couplings, *later)


def first_of_pair(number):
    return (lax.axis_index("col") >> (number - 2)) % 2 == 0


def pair(mine, theirs, mine_first):
    first = jnp.where(mine_first, mine, theirs)
    second = jnp.where(mine_first, theirs, mine)
    return jnp.concatenate([first, second], axis=0)


def upper_body(picks_count, *refs):
    states = [(refs[0][...], refs[1][...])]
    rank = refs[0].shape[0]
    for got_ref in refs[2:5]:
        high, middle, reduced = (got_ref[pl.ds(pos * rank, rank), :] for pos in range(3))
        states.append((high.astype(F32) + middle.astype(F32), reduced.astype(F32)))
    picks_ref, two_ref, other_ref, three_ref, one_ref, upper_out, top_out = refs[5:12]
    upper_ref, state_ref, sem = refs[12:]
    places = [
        (one_ref, upper_out.at[0, 0]),
        (upper_ref.at[0], upper_out.at[1, 0]),
        (upper_ref.at[1], upper_out.at[2, 0]),
        (state_ref.at[0], top_out.at[0, 0]),
        (state_ref.at[1], top_out.at[1, 0]),
    ]
    copies = [
        pltpu.make_async_copy(source, target, sem.at[pos])
        for pos, (source, target) in enumerate(places)
    ]
    copies[0].start()
    mine_first = first_of_pair(2)
    nodes = []
    for number, coupling_ref in enumerate((two_ref, other_ref)):
        mine, theirs = states[2 * number : 2 * number + 2]
        picks = picks_ref[picks_count - 3 + number]
        stacks = [pair(*parts, mine_first) for parts in zip(mine, theirs)]
        nodes.append((*stacks, coupling_ref[...], picks))
    mine, theirs = merge(nodes)
    upper_ref[0] = mine[0]
    copies[1].start()

    def early(skeleton):
        state_ref[0] = skeleton
        copies[3].start()

    mine_first = first_of_pair(3)
    stacks = [pair(*parts, mine_first) for parts in zip(mine[1:], theirs[1:])]
    ((interp, _, reduced),) = merge([(*stacks, three_ref[...], picks_ref[picks_count - 1])], early)
    upper_ref[1] = interp
    copies[2].start()
    state_ref[1] = reduced
    copies[4].start()
    for copy in copies:
        copy.wait()


def upper_levels(skeleton, reduced, got, picks, couplings, interp_one):
    rank, pool = picks.shape[1:]
    samples = skeleton.shape[1]
    return pl.pallas_call(
        lambda *refs: upper_body(picks.shape[0], *refs),
        out_shape=(
            jax.ShapeDtypeStruct((3, 1, rank, pool), F32),
            jax.ShapeDtypeStruct((2, 1, rank, samples), F32),
        ),
        out_specs=(pl.BlockSpec(memory_space=pl.ANY),) * 2,
        scratch_shapes=[
            pltpu.VMEM((2, rank, pool), F32),
            pltpu.VMEM((2, rank, samples), F32),
            pltpu.SemaphoreType.DMA((5,)),
        ],
        cost_estimate=COST,
        compiler_params=PARAMS,
        name="upper_levels",
    )(skeleton, reduced, *got, picks, *couplings, interp_one)


def one_hot(chosen, pool):
    place = lax.broadcasted_iota(jnp.int32, (pool, chosen.shape[1]), 0)
    return jnp.where(place.astype(F32) == chosen, 1.0, 0.0).astype(F32)


def couple(first, second, picks, gain, couplings_ref):
    rank = first.shape[1]
    points = jnp.concatenate([first, second], axis=1)
    entries = jnp.exp2(over(row_features(points, gain).astype(BF16), col_features(points), 0, 0))
    left = lax.broadcasted_iota(jnp.int32, entries.shape, 1) < rank
    upper = lax.broadcasted_iota(jnp.int32, entries.shape, 0) < rank
    entries = jnp.where(left == upper, 0.0, entries)
    chosen = select_rows(picks.T.astype(BF16), entries)
    high, middle, _ = split(jnp.concatenate([entries, chosen], axis=0))
    couplings_ref[...] = jnp.concatenate([high, high, middle], axis=1)


def coupling_shape(rank):
    return vmem((3 * rank, 6 * rank), BF16)


def skeletons_body(gain, span, counts, mine_ref, beside_ref, *refs):
    picks_ref, one_ref, two_ref, points_ref = refs
    rank, pool = picks_ref.shape[1:]
    leaf_count = counts[0]
    tables = 2 * (span + 16)
    nodes = []
    for source_ref in (mine_ref, beside_ref):
        rows = source_ref[pl.ds(tables, source_ref.shape[0] - tables), :rank].astype(F32)
        hots = [one_hot(rows[pos : pos + 1], pool) for pos in range(leaf_count + 1)]
        children = []
        for leaf in range(leaf_count):
            feats = source_ref[pl.ds(2 * span, 16), pl.ds(leaf * LEAF, LEAF)]
            children.append(over(feats, hots[leaf].astype(BF16), 1, 0))
        points = jnp.concatenate(children, axis=1)
        nodes.append(over(points, hots[leaf_count], 1, 0))
        if source_ref is mine_ref:
            couple(*children, hots[leaf_count], gain, one_ref)
            start = leaf_count + counts[1]
            level_two = lax.axis_index("col") // 2
            wanted = [level_two, level_two + 1 - 2 * (level_two % 2), counts[2] + level_two // 2]
            for row in wanted:
                place = lax.broadcasted_iota(jnp.int32, rows.shape, 0)
                named = jnp.where(place == start + row, rows, 0.0)
                hots.append(one_hot(jnp.sum(named, axis=0, keepdims=True), pool))
            for number, hot in enumerate(hots):
                picks_ref[number] = hot.T.astype(BF16)
            upper = hots[leaf_count + 1]
    mine, theirs = nodes
    mine_first = first_of_pair(2)
    first = jnp.where(mine_first, mine, theirs)
    second = jnp.where(mine_first, theirs, mine)
    couple(first, second, upper, gain, two_ref)
    points_ref[...] = jnp.concatenate([first, second], axis=1).astype(BF16)


def skeletons(packed, beside, tables, span, gain):
    leaf_count, rank = tables[0].shape
    counts = [table.shape[0] for table in tables]
    return pl.pallas_call(
        lambda *refs: skeletons_body(gain, span, counts, *refs),
        out_shape=(
            vmem((leaf_count + 4, rank, LEAF), BF16),
            coupling_shape(rank),
            coupling_shape(rank),
            vmem((16, 2 * rank), BF16),
        ),
        cost_estimate=COST,
        compiler_params=PARAMS,
        name="skeletons",
    )(packed, beside)


def top_couplings_body(gain, mine_ref, theirs_ref, picks_ref, other_ref, three_ref):
    count, rank, _ = picks_ref.shape
    picks = [picks_ref[count - pos].astype(F32).T for pos in (3, 2, 1)]
    mine, theirs = mine_ref[...].astype(F32), theirs_ref[...].astype(F32)
    couple(theirs[:, :rank], theirs[:, rank:], picks[1], gain, other_ref)
    mine, theirs = over(mine, picks[0], 1, 0), over(theirs, picks[1], 1, 0)
    mine_first = first_of_pair(3)
    first = jnp.where(mine_first, mine, theirs)
    second = jnp.where(mine_first, theirs, mine)
    couple(first, second, picks[2], gain, three_ref)


def top_couplings(mine, theirs, picks, gain):
    return pl.pallas_call(
        lambda *refs: top_couplings_body(gain, *refs),
        out_shape=[coupling_shape(picks.shape[1])] * 2,
        cost_estimate=LONG,
        compiler_params=PARAMS,
        name="top_couplings",
    )(mine, theirs, picks)


def local(probes, points, leaf_skeleton, skeleton_one, skeleton_two, skeleton_three):
    span = probes.shape[1]
    row_count = lax.axis_size("row")
    col_count = lax.axis_size("col")
    gain = 16.0 / math.sqrt(4 * span * row_count * col_count)

    def swap(value, row_bits, col_bits):
        pairs = [
            (r * col_count + c, (r ^ row_bits) * col_count + (c ^ col_bits))
            for r in range(row_count)
            for c in range(col_count)
        ]
        return lax.ppermute(value, ("row", "col"), pairs)

    tables = (leaf_skeleton, skeleton_one, skeleton_two, skeleton_three)
    first, second, own_points = pack(probes, points, tables)
    beside_first, across_second = swap(first, 0, 1), swap(second, 2, 0)
    line = col_count // 2
    line_points = own_points
    for bit in range(1, col_count.bit_length() - 1):
        line_points = jnp.concatenate([line_points, swap(line_points, 0, 1 << bit)], axis=1)
        if bit == 1:
            line_points, *late = lax.optimization_barrier((line_points, first, second))
    beside_second, across_first = swap(late[1], 0, 1), swap(late[0], 2, 0)
    line_points = [line_points, swap(line_points, 1, 0)]
    near, far = range(2), range(2, line)
    groups = [
        [(core, chunk * span) for chunk in group] for core in range(2) for group in (near, far)
    ]
    feats, totals = first_product((first, second), line_points, groups, span, gain)
    beside_first, across_second, *totals = lax.optimization_barrier(
        (beside_first, across_second, *totals)
    )
    diagonal = [swap(beside_first, 2, 0), swap(across_second, 0, 1)]
    *totals, _ = product([beside_first, across_second], feats, totals, span, SHORT)
    beside_second, across_first, *totals = lax.optimization_barrier(
        (beside_second, across_first, *totals)
    )
    *totals, _ = product([beside_second, across_first], feats, totals, span)
    first, *totals = lax.optimization_barrier((first, *totals))
    picks, couplings_one, couplings_two, points_two = skeletons(
        first, beside_first, tables, span, gain
    )
    points_two, *totals = lax.optimization_barrier((points_two, *totals))
    pieces = [first, second, beside_first, beside_second, across_first, across_second, *diagonal]
    for bit in range(2, row_count.bit_length() - 1):
        more = [swap(value, 1 << bit, 0) for value in pieces]
        *totals, _ = product(more, feats, totals, span)
        pieces += more
    theirs, *cols = product(diagonal, feats[3:], totals[3:], span)
    from_sibling = swap(theirs, 1, 0)
    mine, _ = product(diagonal, feats[1:2], totals[1:2], span, cols=cols)
    outs = [(range(0, line - 2, 2), F32), (range(1, line - 2, 2), BF16)]
    kept, sent = add_up(mine, from_sibling, outs, span)
    theirs, _ = product(diagonal, feats[2:3], totals[2:3], span, cols=cols)
    sent, theirs, points_two = lax.optimization_barrier((sent, theirs, points_two))
    arrived = swap(sent, 0, 2)
    from_sibling = swap(theirs, 1, 0)
    mine, _ = product(diagonal, feats[:1], totals[:1], span, cols=cols)
    own_sum, near_sent = add_up(mine, from_sibling, [([0], F32), ([1], BF16)], span)
    near_sum = swap(near_sent, 0, 2)
    received = []
    chunks = list(range(2, line, 2))
    bit = 2
    while chunks:
        sent_places = [pos for pos, chunk in enumerate(chunks) if chunk & bit]
        kept_places = [pos for pos, chunk in enumerate(chunks) if not chunk & bit]
        outs = [(sent_places, BF16)] + [(kept_places, F32)] * (len(kept_places) > 0)
        sent, *kept = add_up(kept, arrived, outs, span, (near_sent,), LONG)
        arrived = swap(sent, 0, 2 * bit)
        received.append(arrived[:span] if len(sent_places) > 1 else arrived)
        if kept:
            (kept,) = kept
            arrived = arrived[span:]
        chunks = [chunks[pos] for pos in kept_places]
        bit *= 2
    received.append(near_sum)
    other_points = swap(points_two, 0, 2)
    later = top_couplings(points_two, other_points, picks, gain)

    leaf_interp, interp_one, skeleton, reduced, sent = leaves(
        own_sum, received, first, picks, couplings_one, later, leaf_skeleton.shape[0]
    )
    got = [swap(sent, 0, bits) for bits in (1, 2, 3)]
    upper_interp, top_state = upper_levels(
        skeleton, reduced, got, picks, (couplings_two, *later), interp_one
    )
    return jnp.swapaxes(leaf_interp, 1, 2), jnp.swapaxes(upper_interp, 2, 3), top_state


def solution(mesh):
    placed = (
        P(None, ("row", "col"), None),
        P(None, None, ("row", "col")),
        P(("row", "col"), None),
        P(("row", "col"), None),
        P("row", None),
        P("row", None),
    )
    return jax.shard_map(
        local,
        mesh=mesh,
        in_specs=placed,
        out_specs=(
            P(("row", "col"), None, None),
            P(None, ("row", "col"), None, None),
            P(None, ("row", "col"), None, None),
        ),
        check_vma=False,
    )
```

```python
import math

import jax
import jax.numpy as jnp
from jax import lax
from jax.experimental import pallas as pl
from jax.experimental.pallas import tpu as pltpu
from jax.sharding import PartitionSpec as P

LEAF = 128
F32 = jnp.float32
BF16 = jnp.bfloat16
DOUBLINGS = 9
VMEM = pl.BlockSpec(memory_space=pltpu.VMEM)


def vmem(shape, kind=F32):
    return pltpu.VMEM(tuple(shape), kind)


COST = pl.CostEstimate(flops=10**9, bytes_accessed=0, transcendentals=0)
SHORT = pl.CostEstimate(flops=0, bytes_accessed=0, transcendentals=0)
LONG = pl.CostEstimate(flops=10**10, bytes_accessed=0, transcendentals=0)
PARAMS = pltpu.CompilerParams(vmem_limit_bytes=16 << 20)


def chebyshev_constants():
    taus = [1282.0 / 1280.0]
    for _ in range(DOUBLINGS):
        taus.append(2.0 * taus[-1] * taus[-1] - 1.0)
    front = 2.0**DOUBLINGS * math.prod(taus[:-1]) / taus[-1]
    return taus[:-1], front


TAUS, FRONT = chebyshev_constants()


def over(first, second, first_dim, second_dim):
    return lax.dot_general(
        first,
        second,
        (((first_dim,), (second_dim,)), ((), ())),
        preferred_element_type=F32,
    )


def split(value):
    high = value.astype(BF16)
    rest = value - high.astype(F32)
    middle = rest.astype(BF16)
    return high, middle, (rest - middle.astype(F32)).astype(BF16)


def norm_rows(norm, first, width):
    parts = [part.astype(F32) for part in split(norm)]
    place = lax.broadcasted_iota(jnp.int32, (16, width), 0)
    extra = jnp.where(place < 6, 1.0, 0.0)
    for pos in range(3):
        extra = jnp.where(place == pos + first, parts[pos], extra)
    return extra


def row_features(feats, gain):
    feats = feats.astype(F32)
    depth, width = feats.shape
    unit = math.log2(math.e) / (2.0 * depth)
    norm = jnp.sum(feats * feats, axis=0, keepdims=True) * -unit + math.log2(gain)
    parts = [part.astype(F32) for part in split(feats * (2.0 * unit))]
    return jnp.concatenate([*parts, norm_rows(norm, 0, width)], axis=0)


def col_features(feats):
    feats = feats.astype(F32)
    depth, width = feats.shape
    unit = math.log2(math.e) / (2.0 * depth)
    norm = jnp.sum(feats * feats, axis=0, keepdims=True) * -unit
    return jnp.concatenate([feats, feats, feats, norm_rows(norm, 3, width)], axis=0).astype(BF16)


def pack_body(*refs):
    probes_ref, points_ref, *table_refs = refs[:6]
    first_ref, second_ref, own_ref, held_ref, rows_ref, *held_tables, sem = refs[6:]
    span = probes_ref.shape[1]
    pairs = [(points_ref, held_ref), *zip(table_refs, held_tables)]
    small = len(pairs)
    for quarter in range(4):
        target = (first_ref, second_ref)[quarter // 2].at[pl.ds(quarter % 2 * span, span)]
        pairs.append((probes_ref.at[quarter], target))
    copies = [
        pltpu.make_async_copy(source, target, sem.at[pos])
        for pos, (source, target) in enumerate(pairs)
    ]
    for copy in copies:
        copy.start()
    rows_ref[...] = jnp.zeros_like(rows_ref)
    for copy in copies[:small]:
        copy.wait()
    points = held_ref[...].astype(F32)
    for quarter in range(4):
        feats = points[:, quarter, :].astype(BF16)
        half_ref = (first_ref, second_ref)[quarter // 2]
        half_ref[pl.ds(2 * span + quarter % 2 * 16, 16), :] = feats
        if quarter == 0:
            own_ref[...] = feats
    start = 0
    for table in held_tables:
        count, rank = table.shape
        rows_ref[pl.ds(start, count), pl.ds(0, rank)] = table[...].astype(F32)
        start += count
    first_ref[pl.ds(second_ref.shape[0], rows_ref.shape[0]), :] = rows_ref[...].astype(BF16)
    for copy in copies[small:]:
        copy.wait()


def pack(probes, points, tables):
    _, span, samples = probes.shape
    table_rows = -(-sum(table.shape[0] for table in tables) // 16) * 16
    inputs = (probes, points, *tables)
    return pl.pallas_call(
        pack_body,
        out_shape=(
            vmem((2 * (span + 16) + table_rows, samples), BF16),
            vmem((2 * (span + 16), samples), BF16),
            vmem((16, span), BF16),
        ),
        in_specs=[pl.BlockSpec(memory_space=pltpu.HBM)] * len(inputs),
        scratch_shapes=[
            pltpu.VMEM(points.shape, BF16),
            pltpu.VMEM((table_rows, samples), F32),
            *[pltpu.VMEM(table.shape, jnp.int32) for table in tables],
            pltpu.SemaphoreType.DMA((5 + len(tables),)),
        ],
        cost_estimate=COST,
        compiler_params=PARAMS,
        name="pack",
    )(*(pltpu.with_memory_space_constraint(value, pltpu.HBM) for value in inputs))


def masked(entries):
    shape = entries.shape
    row_leaf = lax.broadcasted_iota(jnp.int32, shape, 0) // LEAF
    col_leaf = lax.broadcasted_iota(jnp.int32, shape, 1) // LEAF
    return jnp.where(row_leaf == col_leaf, 0.0, entries)


def add_halves(half_refs, row_refs, cols_ref, put, span, own):
    for number, half_ref in enumerate(half_refs):
        for quarter in range(2):
            feats = half_ref[pl.ds(2 * span + 16 * quarter, 16), :]
            cols_ref[:, pl.ds((2 * number + quarter) * span, span)] = col_features(feats)
    columns = 2 * span * len(half_refs)
    for group, rows_ref in enumerate(row_refs):
        for start in range(0, rows_ref.shape[0], span):
            feats = rows_ref[pl.ds(start, span), :]
            entries = jnp.exp2(over(feats, cols_ref[:, :columns], 1, 0))
            if own and group == 0 and start == 0:
                entries = jnp.concatenate([masked(entries[:, :span]), entries[:, span:]], axis=1)
            randoms = [half_ref[pl.ds(0, 2 * span), :] for half_ref in half_refs]
            put(group, start, over(entries.astype(BF16), jnp.concatenate(randoms, axis=0), 1, 0))


def first_product_body(gain, span, groups, point_count, *refs):
    half_refs, point_refs = refs[:2], refs[2 : point_count + 2]
    row_refs = refs[point_count + 2 : point_count + 2 + len(groups)]
    total_refs, cols_ref = refs[point_count + 2 + len(groups) : -1], refs[-1]
    for rows_ref, places in zip(row_refs, groups):
        for pos, (array, start) in enumerate(places):
            feats = point_refs[array][:, pl.ds(start, span)]
            rows_ref[pl.ds(pos * span, span), :] = row_features(feats, gain).T.astype(BF16)

    def put(group, start, value):
        total_refs[group][pl.ds(start, span), :] = value

    add_halves(half_refs, row_refs, cols_ref, put, span, True)


def first_product(halves, points, groups, span, gain):
    samples = halves[0].shape[1]
    rows = [len(places) * span for places in groups]
    out = pl.pallas_call(
        lambda *refs: first_product_body(gain, span, groups, len(points), *refs),
        out_shape=[vmem((count, 64), BF16) for count in rows]
        + [vmem((count, samples), F32) for count in rows],
        scratch_shapes=[pltpu.VMEM((64, 4 * span), BF16)],
        cost_estimate=COST,
        compiler_params=PARAMS,
        name="first_product",
    )(*halves, *points)
    return out[: len(groups)], out[len(groups) :]


def product_body(span, half_count, count, *refs):
    half_refs, refs = refs[:half_count], refs[half_count:]
    row_refs, old_refs, total_refs = refs[:count], refs[count : 2 * count], refs[2 * count : -1]
    cols_ref = refs[-1]
    for number in range(0, half_count, 2):

        def put(group, start, value):
            place = pl.ds(start, span)
            base = old_refs if number == 0 else total_refs
            total_refs[group][place, :] = base[group][place, :] + value

        add_halves(half_refs[number : number + 2], row_refs, cols_ref, put, span, False)


def product(halves, rows, totals, span, cost=COST):
    return pl.pallas_call(
        lambda *refs: product_body(span, len(halves), len(rows), *refs),
        out_shape=[vmem(total.shape, F32) for total in totals],
        scratch_shapes=[pltpu.VMEM((64, 4 * span), BF16)],
        cost_estimate=cost,
        compiler_params=PARAMS,
        name="product",
    )(*halves, *rows, *totals)


def add_up_body(span, outs, mine_ref, theirs_ref, *refs):
    for (chunks, _), out_ref in zip(outs, refs[-len(outs) :]):
        for pos, chunk in enumerate(chunks):
            place = pl.ds(chunk * span, span)
            value = mine_ref[place, :] + theirs_ref[place, :].astype(F32)
            out_ref[pl.ds(pos * span, span), :] = value.astype(out_ref.dtype)


def add_up(mine, theirs, outs, span, after=(), cost=COST):
    samples = mine.shape[1]
    return pl.pallas_call(
        lambda *refs: add_up_body(span, outs, *refs),
        out_shape=[vmem((len(chunks) * span, samples), kind) for chunks, kind in outs],
        cost_estimate=cost,
        compiler_params=PARAMS,
        name="add_up",
    )(mine, theirs, *after)


def wide_product(first, second):
    high, middle, low = split(first)
    other_high, other_middle, other_low = split(second)
    return over(
        jnp.concatenate([high, high, middle, middle, low, high], axis=1),
        jnp.concatenate(
            [other_high, other_middle, other_high, other_middle, other_high, other_low], axis=1
        ),
        1,
        1,
    )


def near_product(first, second):
    high, middle, _ = split(first)
    return over(jnp.concatenate([high, high, middle], axis=1), near_parts(second), 1, 0)


def near_parts(second):
    high, middle, _ = split(second)
    return jnp.concatenate([high, middle, high], axis=0)


def exact_product(first, second):
    second = second.astype(BF16)
    return over(
        jnp.concatenate(split(first), axis=1), jnp.concatenate([second] * 3, axis=0), 1, 0
    )


def twice_product(twice, twice_parts, parts):
    high, middle, _ = twice_parts
    other_high, other_middle, other_low = parts
    left = lax.broadcasted_iota(jnp.int32, high.shape, 1) < high.shape[1] // 2
    low = twice - high.astype(F32) - middle.astype(F32)
    last = jnp.where(left, low, high.astype(F32)).astype(BF16)
    return over(
        jnp.concatenate([high, middle, last], axis=1),
        jnp.concatenate(
            [other_high, other_middle, other_high, other_middle, other_high, other_low], axis=0
        ),
        1,
        0,
    )


def select_rows(picks, value):
    return over(
        jnp.concatenate([picks] * 3, axis=1), jnp.concatenate(split(value), axis=0), 1, 0
    )


def interpolate(stacks, skeletons):
    rank, pool = skeletons[0].shape[0], stacks[0].shape[0]
    place = lax.broadcasted_iota(jnp.int32, (rank, 2 * rank), 0)
    other = lax.broadcasted_iota(jnp.int32, (rank, 2 * rank), 1)
    eyes = jnp.where((other == place) | (other == place + rank), 1.0, 0.0)
    states = []
    for skeleton, stack in zip(skeletons, stacks):
        products = wide_product(skeleton, jnp.concatenate([stack, skeleton, skeleton], axis=0))
        ridge = 0.05 * jnp.sum(skeleton * skeleton, keepdims=True) / rank + 1e-05
        inverse = 1.0 / (640.0 * ridge)
        states.append((products[:, :pool], eyes - products[:, pool:] * inverse, inverse))
    for number, tau in enumerate(TAUS):
        last = number == DOUBLINGS - 1
        later = []
        for solved, power, inverse in states:
            power_parts = split(power)
            parts = split(solved)
            if not last:
                parts = [jnp.concatenate(pair, axis=1) for pair in zip(parts, power_parts)]
            both = twice_product(power, power_parts, parts)
            solved = solved + both[:, :pool] * (1.0 / tau)
            later.append((solved, None if last else 2.0 * both[:, pool:] - eyes, inverse))
        states = later
    return [solved * (inverse * FRONT) for solved, _, inverse in states]


def merge(nodes, early=None):
    stacks, skeletons = [], []
    for samples, reduced, coupling, picks in nodes:
        pool = samples.shape[0]
        coupled = over(coupling, near_parts(reduced), 1, 0)
        stacks.append(samples - coupled[:pool])
        skeletons.append(select_rows(picks, samples) - coupled[pool:])
    if early is not None:
        early(skeletons[0])
    interps = interpolate(stacks, skeletons)
    return [
        (interp, skeleton, near_product(interp, node[1]))
        for interp, skeleton, node in zip(interps, skeletons, nodes)
    ]


def leaves_body(received, *refs):
    own_ref, *others = refs[: received + 1]
    source_ref, picks_ref, couplings_ref = refs[received + 1 : received + 4]
    leaf_ref, upper_ref, skeleton_ref, reduced_ref, sent_ref, held_ref, sem = refs[-7:]
    total = own_ref[...]
    for other in others:
        total = total + other[...].astype(F32)
    count = total.shape[0] // LEAF
    stacks = [total[leaf * LEAF : (leaf + 1) * LEAF] for leaf in range(count)]
    skeletons = [select_rows(picks_ref[leaf], stack) for leaf, stack in enumerate(stacks)]
    reduced = []
    for leaf, interp in enumerate(interpolate(stacks, skeletons)):
        held_ref[leaf] = interp
        reduced.append(exact_product(interp, source_ref[pl.ds(leaf * LEAF, LEAF), :]))
    copy = pltpu.make_async_copy(held_ref, leaf_ref, sem)
    copy.start()
    node = (
        jnp.concatenate(skeletons, axis=0),
        jnp.concatenate(reduced, axis=0),
        couplings_ref[...],
        picks_ref[count],
    )
    ((interp, skeleton, reduced),) = merge([node])
    upper_ref[...] = interp
    skeleton_ref[...] = skeleton
    reduced_ref[...] = reduced
    for pos, part in enumerate((*split(skeleton)[:2], reduced.astype(BF16))):
        sent_ref[pl.ds(pos * skeleton.shape[0], skeleton.shape[0]), :] = part
    copy.wait()


def leaves(own, others, source, picks, couplings, later, leaf_count):
    samples = own.shape[1]
    rank, pool = picks.shape[1:]
    return pl.pallas_call(
        lambda *refs: leaves_body(len(others), *refs),
        out_shape=(
            jax.ShapeDtypeStruct((leaf_count, rank, LEAF), F32),
            vmem((rank, pool), F32),
            vmem((rank, samples), F32),
            vmem((rank, samples), F32),
            vmem((3 * rank, samples), BF16),
        ),
        out_specs=(pl.BlockSpec(memory_space=pl.ANY), VMEM, VMEM, VMEM, VMEM),
        scratch_shapes=[pltpu.VMEM((leaf_count, rank, LEAF), F32), pltpu.SemaphoreType.DMA],
        cost_estimate=COST,
        compiler_params=PARAMS,
        name="leaves",
    )(own, *others, source, picks, couplings, *later)


def first_of_pair(number):
    return (lax.axis_index("col") >> (number - 2)) % 2 == 0


def pair(mine, theirs, mine_first):
    first = jnp.where(mine_first, mine, theirs)
    second = jnp.where(mine_first, theirs, mine)
    return jnp.concatenate([first, second], axis=0)


def upper_body(picks_count, *refs):
    states = [(refs[0][...], refs[1][...])]
    rank = refs[0].shape[0]
    for got_ref in refs[2:5]:
        high, middle, reduced = (got_ref[pl.ds(pos * rank, rank), :] for pos in range(3))
        states.append((high.astype(F32) + middle.astype(F32), reduced.astype(F32)))
    picks_ref, two_ref, other_ref, three_ref, one_ref, upper_out, top_out = refs[5:12]
    upper_ref, state_ref, sem = refs[12:]
    places = [
        (one_ref, upper_out.at[0, 0]),
        (upper_ref.at[0], upper_out.at[1, 0]),
        (upper_ref.at[1], upper_out.at[2, 0]),
        (state_ref.at[0], top_out.at[0, 0]),
        (state_ref.at[1], top_out.at[1, 0]),
    ]
    copies = [
        pltpu.make_async_copy(source, target, sem.at[pos])
        for pos, (source, target) in enumerate(places)
    ]
    copies[0].start()
    mine_first = first_of_pair(2)
    nodes = []
    for number, coupling_ref in enumerate((two_ref, other_ref)):
        mine, theirs = states[2 * number : 2 * number + 2]
        picks = picks_ref[picks_count - 3 + number]
        stacks = [pair(*parts, mine_first) for parts in zip(mine, theirs)]
        nodes.append((*stacks, coupling_ref[...], picks))
    mine, theirs = merge(nodes)
    upper_ref[0] = mine[0]
    copies[1].start()

    def early(skeleton):
        state_ref[0] = skeleton
        copies[3].start()

    mine_first = first_of_pair(3)
    stacks = [pair(*parts, mine_first) for parts in zip(mine[1:], theirs[1:])]
    ((interp, _, reduced),) = merge([(*stacks, three_ref[...], picks_ref[picks_count - 1])], early)
    upper_ref[1] = interp
    copies[2].start()
    state_ref[1] = reduced
    copies[4].start()
    for copy in copies:
        copy.wait()


def upper_levels(skeleton, reduced, got, picks, couplings, interp_one):
    rank, pool = picks.shape[1:]
    samples = skeleton.shape[1]
    return pl.pallas_call(
        lambda *refs: upper_body(picks.shape[0], *refs),
        out_shape=(
            jax.ShapeDtypeStruct((3, 1, rank, pool), F32),
            jax.ShapeDtypeStruct((2, 1, rank, samples), F32),
        ),
        out_specs=(pl.BlockSpec(memory_space=pl.ANY),) * 2,
        scratch_shapes=[
            pltpu.VMEM((2, rank, pool), F32),
            pltpu.VMEM((2, rank, samples), F32),
            pltpu.SemaphoreType.DMA((5,)),
        ],
        cost_estimate=COST,
        compiler_params=PARAMS,
        name="upper_levels",
    )(skeleton, reduced, *got, picks, *couplings, interp_one)


def one_hot(chosen, pool):
    place = lax.broadcasted_iota(jnp.int32, (pool, chosen.shape[1]), 0)
    return jnp.where(place.astype(F32) == chosen, 1.0, 0.0).astype(F32)


def couple(first, second, picks, gain, couplings_ref):
    rank = first.shape[1]
    points = jnp.concatenate([first, second], axis=1)
    entries = jnp.exp2(over(row_features(points, gain).astype(BF16), col_features(points), 0, 0))
    left = lax.broadcasted_iota(jnp.int32, entries.shape, 1) < rank
    upper = lax.broadcasted_iota(jnp.int32, entries.shape, 0) < rank
    entries = jnp.where(left == upper, 0.0, entries)
    chosen = select_rows(picks.T.astype(BF16), entries)
    high, middle, _ = split(jnp.concatenate([entries, chosen], axis=0))
    couplings_ref[...] = jnp.concatenate([high, high, middle], axis=1)


def coupling_shape(rank):
    return vmem((3 * rank, 6 * rank), BF16)


def skeletons_body(gain, span, counts, mine_ref, beside_ref, *refs):
    picks_ref, one_ref, two_ref, points_ref = refs
    rank, pool = picks_ref.shape[1:]
    leaf_count = counts[0]
    tables = 2 * (span + 16)
    nodes = []
    for source_ref in (mine_ref, beside_ref):
        rows = source_ref[pl.ds(tables, source_ref.shape[0] - tables), :rank].astype(F32)
        hots = [one_hot(rows[pos : pos + 1], pool) for pos in range(leaf_count + 1)]
        children = []
        for leaf in range(leaf_count):
            feats = source_ref[pl.ds(2 * span, 16), pl.ds(leaf * LEAF, LEAF)]
            children.append(over(feats, hots[leaf].astype(BF16), 1, 0))
        points = jnp.concatenate(children, axis=1)
        nodes.append(over(points, hots[leaf_count], 1, 0))
        if source_ref is mine_ref:
            couple(*children, hots[leaf_count], gain, one_ref)
            start = leaf_count + counts[1]
            level_two = lax.axis_index("col") // 2
            wanted = [level_two, level_two + 1 - 2 * (level_two % 2), counts[2] + level_two // 2]
            for row in wanted:
                place = lax.broadcasted_iota(jnp.int32, rows.shape, 0)
                named = jnp.where(place == start + row, rows, 0.0)
                hots.append(one_hot(jnp.sum(named, axis=0, keepdims=True), pool))
            for number, hot in enumerate(hots):
                picks_ref[number] = hot.T.astype(BF16)
            upper = hots[leaf_count + 1]
    mine, theirs = nodes
    mine_first = first_of_pair(2)
    first = jnp.where(mine_first, mine, theirs)
    second = jnp.where(mine_first, theirs, mine)
    couple(first, second, upper, gain, two_ref)
    points_ref[...] = jnp.concatenate([first, second], axis=1).astype(BF16)


def skeletons(packed, beside, tables, span, gain):
    leaf_count, rank = tables[0].shape
    counts = [table.shape[0] for table in tables]
    return pl.pallas_call(
        lambda *refs: skeletons_body(gain, span, counts, *refs),
        out_shape=(
            vmem((leaf_count + 4, rank, LEAF), BF16),
            coupling_shape(rank),
            coupling_shape(rank),
            vmem((16, 2 * rank), BF16),
        ),
        cost_estimate=COST,
        compiler_params=PARAMS,
        name="skeletons",
    )(packed, beside)


def top_couplings_body(gain, mine_ref, theirs_ref, picks_ref, other_ref, three_ref):
    count, rank, _ = picks_ref.shape
    picks = [picks_ref[count - pos].astype(F32).T for pos in (3, 2, 1)]
    mine, theirs = mine_ref[...].astype(F32), theirs_ref[...].astype(F32)
    couple(theirs[:, :rank], theirs[:, rank:], picks[1], gain, other_ref)
    mine, theirs = over(mine, picks[0], 1, 0), over(theirs, picks[1], 1, 0)
    mine_first = first_of_pair(3)
    first = jnp.where(mine_first, mine, theirs)
    second = jnp.where(mine_first, theirs, mine)
    couple(first, second, picks[2], gain, three_ref)


def top_couplings(mine, theirs, picks, gain):
    return pl.pallas_call(
        lambda *refs: top_couplings_body(gain, *refs),
        out_shape=[coupling_shape(picks.shape[1])] * 2,
        cost_estimate=LONG,
        compiler_params=PARAMS,
        name="top_couplings",
    )(mine, theirs, picks)


def local(probes, points, leaf_skeleton, skeleton_one, skeleton_two, skeleton_three):
    span = probes.shape[1]
    row_count = lax.axis_size("row")
    col_count = lax.axis_size("col")
    gain = 16.0 / math.sqrt(4 * span * row_count * col_count)

    def swap(value, row_bits, col_bits):
        pairs = [
            (r * col_count + c, (r ^ row_bits) * col_count + (c ^ col_bits))
            for r in range(row_count)
            for c in range(col_count)
        ]
        return lax.ppermute(value, ("row", "col"), pairs)

    tables = (leaf_skeleton, skeleton_one, skeleton_two, skeleton_three)
    first, second, own_points = pack(probes, points, tables)
    beside_first, across_second = swap(first, 0, 1), swap(second, 2, 0)
    line = col_count // 2
    line_points = own_points
    for bit in range(1, col_count.bit_length() - 1):
        line_points = jnp.concatenate([line_points, swap(line_points, 0, 1 << bit)], axis=1)
        if bit == 1:
            line_points, *late = lax.optimization_barrier((line_points, first, second))
    beside_second, across_first = swap(late[1], 0, 1), swap(late[0], 2, 0)
    line_points = [line_points, swap(line_points, 1, 0)]
    near, far = range(2), range(2, line)
    groups = [
        [(core, chunk * span) for chunk in group] for core in range(2) for group in (near, far)
    ]
    feats, totals = first_product((first, second), line_points, groups, span, gain)
    beside_first, across_second, *totals = lax.optimization_barrier(
        (beside_first, across_second, *totals)
    )
    diagonal = [swap(beside_first, 2, 0), swap(across_second, 0, 1)]
    totals = product([beside_first, across_second], feats, totals, span, SHORT)
    beside_second, across_first, *totals = lax.optimization_barrier(
        (beside_second, across_first, *totals)
    )
    totals = product([beside_second, across_first], feats, totals, span)
    first, *totals = lax.optimization_barrier((first, *totals))
    picks, couplings_one, couplings_two, points_two = skeletons(
        first, beside_first, tables, span, gain
    )
    points_two, *totals = lax.optimization_barrier((points_two, *totals))
    pieces = [first, second, beside_first, beside_second, across_first, across_second, *diagonal]
    for bit in range(2, row_count.bit_length() - 1):
        more = [swap(value, 1 << bit, 0) for value in pieces]
        totals = product(more, feats, totals, span)
        pieces += more
    (theirs,) = product(diagonal, feats[3:], totals[3:], span)
    from_sibling = swap(theirs, 1, 0)
    mine, theirs = product(diagonal, feats[1:3], totals[1:3], span)
    outs = [(range(0, line - 2, 2), F32), (range(1, line - 2, 2), BF16)]
    kept, sent = add_up(mine, from_sibling, outs, span)
    sent, theirs, points_two = lax.optimization_barrier((sent, theirs, points_two))
    arrived = swap(sent, 0, 2)
    from_sibling = swap(theirs, 1, 0)
    (mine,) = product(diagonal, feats[:1], totals[:1], span)
    own_sum, near_sent = add_up(mine, from_sibling, [([0], F32), ([1], BF16)], span)
    near_sum = swap(near_sent, 0, 2)
    received = []
    chunks = list(range(2, line, 2))
    bit = 2
    while chunks:
        sent_places = [pos for pos, chunk in enumerate(chunks) if chunk & bit]
        kept_places = [pos for pos, chunk in enumerate(chunks) if not chunk & bit]
        outs = [(sent_places, BF16)] + [(kept_places, F32)] * (len(kept_places) > 0)
        sent, *kept = add_up(kept, arrived, outs, span, (near_sent,), LONG)
        arrived = swap(sent, 0, 2 * bit)
        received.append(arrived[:span] if len(sent_places) > 1 else arrived)
        if kept:
            (kept,) = kept
            arrived = arrived[span:]
        chunks = [chunks[pos] for pos in kept_places]
        bit *= 2
    received.append(near_sum)
    other_points = swap(points_two, 0, 2)
    later = top_couplings(points_two, other_points, picks, gain)

    leaf_interp, interp_one, skeleton, reduced, sent = leaves(
        own_sum, received, first, picks, couplings_one, later, leaf_skeleton.shape[0]
    )
    got = [swap(sent, 0, bits) for bits in (1, 2, 3)]
    upper_interp, top_state = upper_levels(
        skeleton, reduced, got, picks, (couplings_two, *later), interp_one
    )
    return jnp.swapaxes(leaf_interp, 1, 2), jnp.swapaxes(upper_interp, 2, 3), top_state


def solution(mesh):
    placed = (
        P(None, ("row", "col"), None),
        P(None, None, ("row", "col")),
        P(("row", "col"), None),
        P(("row", "col"), None),
        P("row", None),
        P("row", None),
    )
    return jax.shard_map(
        local,
        mesh=mesh,
        in_specs=placed,
        out_specs=(
            P(("row", "col"), None, None),
            P(None, ("row", "col"), None, None),
            P(None, ("row", "col"), None, None),
        ),
        check_vma=False,
    )
```

```python
import math

import jax
import jax.numpy as jnp
from jax import lax
from jax.experimental import pallas as pl
from jax.experimental.pallas import tpu as pltpu
from jax.sharding import PartitionSpec as P

LEAF = 128
F32 = jnp.float32
BF16 = jnp.bfloat16
DOUBLINGS = 9
VMEM = pl.BlockSpec(memory_space=pltpu.VMEM)


def vmem(shape, kind=F32):
    return pltpu.VMEM(tuple(shape), kind)


COST = pl.CostEstimate(flops=10**9, bytes_accessed=0, transcendentals=0)
SHORT = pl.CostEstimate(flops=0, bytes_accessed=0, transcendentals=0)
LONG = pl.CostEstimate(flops=10**10, bytes_accessed=0, transcendentals=0)
PARAMS = pltpu.CompilerParams(vmem_limit_bytes=16 << 20)


def chebyshev_constants():
    taus = [1282.0 / 1280.0]
    for _ in range(DOUBLINGS):
        taus.append(2.0 * taus[-1] * taus[-1] - 1.0)
    front = 2.0**DOUBLINGS * math.prod(taus[:-1]) / taus[-1]
    return taus[:-1], front


TAUS, FRONT = chebyshev_constants()


def over(first, second, first_dim, second_dim):
    return lax.dot_general(
        first,
        second,
        (((first_dim,), (second_dim,)), ((), ())),
        preferred_element_type=F32,
    )


def split(value):
    high = value.astype(BF16)
    rest = value - high.astype(F32)
    middle = rest.astype(BF16)
    return high, middle, (rest - middle.astype(F32)).astype(BF16)


def norm_rows(norm, first, width):
    parts = [part.astype(F32) for part in split(norm)]
    place = lax.broadcasted_iota(jnp.int32, (16, width), 0)
    extra = jnp.where(place < 6, 1.0, 0.0)
    for pos in range(3):
        extra = jnp.where(place == pos + first, parts[pos], extra)
    return extra


def row_features(feats, gain):
    feats = feats.astype(F32)
    depth, width = feats.shape
    unit = math.log2(math.e) / (2.0 * depth)
    norm = jnp.sum(feats * feats, axis=0, keepdims=True) * -unit + math.log2(gain)
    parts = [part.astype(F32) for part in split(feats * (2.0 * unit))]
    return jnp.concatenate([*parts, norm_rows(norm, 0, width)], axis=0)


def col_features(feats):
    feats = feats.astype(F32)
    depth, width = feats.shape
    unit = math.log2(math.e) / (2.0 * depth)
    norm = jnp.sum(feats * feats, axis=0, keepdims=True) * -unit
    return jnp.concatenate([feats, feats, feats, norm_rows(norm, 3, width)], axis=0).astype(BF16)


def pack_body(*refs):
    probes_ref, points_ref, *table_refs = refs[:6]
    first_ref, second_ref, own_ref, held_ref, rows_ref, *held_tables, sem = refs[6:]
    span = probes_ref.shape[1]
    pairs = [(points_ref, held_ref), *zip(table_refs, held_tables)]
    small = len(pairs)
    for quarter in range(4):
        target = (first_ref, second_ref)[quarter // 2].at[pl.ds(quarter % 2 * span, span)]
        pairs.append((probes_ref.at[quarter], target))
    copies = [
        pltpu.make_async_copy(source, target, sem.at[pos])
        for pos, (source, target) in enumerate(pairs)
    ]
    for copy in copies:
        copy.start()
    rows_ref[...] = jnp.zeros_like(rows_ref)
    for copy in copies[:small]:
        copy.wait()
    points = held_ref[...].astype(F32)
    for quarter in range(4):
        feats = points[:, quarter, :].astype(BF16)
        half_ref = (first_ref, second_ref)[quarter // 2]
        half_ref[pl.ds(2 * span + quarter % 2 * 16, 16), :] = feats
        if quarter == 0:
            own_ref[...] = feats
    start = 0
    for table in held_tables:
        count, rank = table.shape
        rows_ref[pl.ds(start, count), pl.ds(0, rank)] = table[...].astype(F32)
        start += count
    first_ref[pl.ds(second_ref.shape[0], rows_ref.shape[0]), :] = rows_ref[...].astype(BF16)
    for copy in copies[small:]:
        copy.wait()


def pack(probes, points, tables):
    _, span, samples = probes.shape
    table_rows = -(-sum(table.shape[0] for table in tables) // 16) * 16
    inputs = (probes, points, *tables)
    return pl.pallas_call(
        pack_body,
        out_shape=(
            vmem((2 * (span + 16) + table_rows, samples), BF16),
            vmem((2 * (span + 16), samples), BF16),
            vmem((16, span), BF16),
        ),
        in_specs=[pl.BlockSpec(memory_space=pltpu.HBM)] * len(inputs),
        scratch_shapes=[
            pltpu.VMEM(points.shape, BF16),
            pltpu.VMEM((table_rows, samples), F32),
            *[pltpu.VMEM(table.shape, jnp.int32) for table in tables],
            pltpu.SemaphoreType.DMA((5 + len(tables),)),
        ],
        cost_estimate=COST,
        compiler_params=PARAMS,
        name="pack",
    )(*(pltpu.with_memory_space_constraint(value, pltpu.HBM) for value in inputs))


def masked(entries):
    shape = entries.shape
    row_leaf = lax.broadcasted_iota(jnp.int32, shape, 0) // LEAF
    col_leaf = lax.broadcasted_iota(jnp.int32, shape, 1) // LEAF
    return jnp.where(row_leaf == col_leaf, 0.0, entries)


def add_halves(half_refs, row_refs, cols_ref, put, span, own):
    for number, half_ref in enumerate(half_refs):
        for quarter in range(2):
            feats = half_ref[pl.ds(2 * span + 16 * quarter, 16), :]
            cols_ref[:, pl.ds((2 * number + quarter) * span, span)] = col_features(feats)
    columns = 2 * span * len(half_refs)
    for group, rows_ref in enumerate(row_refs):
        for start in range(0, rows_ref.shape[0], span):
            feats = rows_ref[pl.ds(start, span), :]
            entries = jnp.exp2(over(feats, cols_ref[:, :columns], 1, 0))
            if own and group == 0 and start == 0:
                entries = jnp.concatenate([masked(entries[:, :span]), entries[:, span:]], axis=1)
            randoms = [half_ref[pl.ds(0, 2 * span), :] for half_ref in half_refs]
            put(group, start, over(entries.astype(BF16), jnp.concatenate(randoms, axis=0), 1, 0))


def first_product_body(gain, span, groups, point_count, *refs):
    half_refs, point_refs = refs[:2], refs[2 : point_count + 2]
    row_refs = refs[point_count + 2 : point_count + 2 + len(groups)]
    total_refs, cols_ref = refs[point_count + 2 + len(groups) : -1], refs[-1]
    for rows_ref, places in zip(row_refs, groups):
        for pos, (array, start) in enumerate(places):
            feats = point_refs[array][:, pl.ds(start, span)]
            rows_ref[pl.ds(pos * span, span), :] = row_features(feats, gain).T.astype(BF16)

    def put(group, start, value):
        total_refs[group][pl.ds(start, span), :] = value

    add_halves(half_refs, row_refs, cols_ref, put, span, True)


def first_product(halves, points, groups, span, gain):
    samples = halves[0].shape[1]
    rows = [len(places) * span for places in groups]
    out = pl.pallas_call(
        lambda *refs: first_product_body(gain, span, groups, len(points), *refs),
        out_shape=[vmem((count, 64), BF16) for count in rows]
        + [vmem((count, samples), F32) for count in rows],
        scratch_shapes=[pltpu.VMEM((64, 4 * span), BF16)],
        cost_estimate=COST,
        compiler_params=PARAMS,
        name="first_product",
    )(*halves, *points)
    return out[: len(groups)], out[len(groups) :]


def product_body(span, half_count, count, *refs):
    half_refs, refs = refs[:half_count], refs[half_count:]
    row_refs, old_refs, total_refs = refs[:count], refs[count : 2 * count], refs[2 * count : -1]
    cols_ref = refs[-1]
    for number in range(0, half_count, 2):

        def put(group, start, value):
            place = pl.ds(start, span)
            base = old_refs if number == 0 else total_refs
            value = base[group][place, :] + value
            total_refs[group][place, :] = value.astype(total_refs[group].dtype)

        add_halves(half_refs[number : number + 2], row_refs, cols_ref, put, span, False)


def product(halves, rows, totals, span, cost=COST, kind=F32):
    return pl.pallas_call(
        lambda *refs: product_body(span, len(halves), len(rows), *refs),
        out_shape=[vmem(total.shape, kind) for total in totals],
        scratch_shapes=[pltpu.VMEM((64, 4 * span), BF16)],
        cost_estimate=cost,
        compiler_params=PARAMS,
        name="product",
    )(*halves, *rows, *totals)


def add_up_body(span, outs, mine_ref, theirs_ref, *refs):
    for (chunks, _), out_ref in zip(outs, refs[-len(outs) :]):
        for pos, chunk in enumerate(chunks):
            place = pl.ds(chunk * span, span)
            value = mine_ref[place, :] + theirs_ref[place, :].astype(F32)
            out_ref[pl.ds(pos * span, span), :] = value.astype(out_ref.dtype)


def add_up(mine, theirs, outs, span, after=(), cost=COST):
    samples = mine.shape[1]
    return pl.pallas_call(
        lambda *refs: add_up_body(span, outs, *refs),
        out_shape=[vmem((len(chunks) * span, samples), kind) for chunks, kind in outs],
        cost_estimate=cost,
        compiler_params=PARAMS,
        name="add_up",
    )(mine, theirs, *after)


def wide_product(first, second):
    high, middle, low = split(first)
    other_high, other_middle, other_low = split(second)
    return over(
        jnp.concatenate([high, high, middle, middle, low, high], axis=1),
        jnp.concatenate(
            [other_high, other_middle, other_high, other_middle, other_high, other_low], axis=1
        ),
        1,
        1,
    )


def near_product(first, second):
    high, middle, _ = split(first)
    return over(jnp.concatenate([high, high, middle], axis=1), near_parts(second), 1, 0)


def near_parts(second):
    high, middle, _ = split(second)
    return jnp.concatenate([high, middle, high], axis=0)


def exact_product(first, second):
    second = second.astype(BF16)
    return over(
        jnp.concatenate(split(first), axis=1), jnp.concatenate([second] * 3, axis=0), 1, 0
    )


def twice_product(twice, twice_parts, parts):
    high, middle, _ = twice_parts
    other_high, other_middle, other_low = parts
    left = lax.broadcasted_iota(jnp.int32, high.shape, 1) < high.shape[1] // 2
    low = twice - high.astype(F32) - middle.astype(F32)
    last = jnp.where(left, low, high.astype(F32)).astype(BF16)
    return over(
        jnp.concatenate([high, middle, last], axis=1),
        jnp.concatenate(
            [other_high, other_middle, other_high, other_middle, other_high, other_low], axis=0
        ),
        1,
        0,
    )


def select_rows(picks, value):
    return over(
        jnp.concatenate([picks] * 3, axis=1), jnp.concatenate(split(value), axis=0), 1, 0
    )


def interpolate(stacks, skeletons):
    rank, pool = skeletons[0].shape[0], stacks[0].shape[0]
    place = lax.broadcasted_iota(jnp.int32, (rank, 2 * rank), 0)
    other = lax.broadcasted_iota(jnp.int32, (rank, 2 * rank), 1)
    eyes = jnp.where((other == place) | (other == place + rank), 1.0, 0.0)
    states = []
    for skeleton, stack in zip(skeletons, stacks):
        products = wide_product(skeleton, jnp.concatenate([stack, skeleton, skeleton], axis=0))
        ridge = 0.05 * jnp.sum(skeleton * skeleton, keepdims=True) / rank + 1e-05
        inverse = 1.0 / (640.0 * ridge)
        states.append((products[:, :pool], eyes - products[:, pool:] * inverse, inverse))
    for number, tau in enumerate(TAUS):
        last = number == DOUBLINGS - 1
        later = []
        for solved, power, inverse in states:
            power_parts = split(power)
            parts = split(solved)
            if not last:
                parts = [jnp.concatenate(pair, axis=1) for pair in zip(parts, power_parts)]
            both = twice_product(power, power_parts, parts)
            solved = solved + both[:, :pool] * (1.0 / tau)
            later.append((solved, None if last else 2.0 * both[:, pool:] - eyes, inverse))
        states = later
    return [solved * (inverse * FRONT) for solved, _, inverse in states]


def merge(nodes, early=None):
    stacks, skeletons = [], []
    for samples, reduced, coupling, picks in nodes:
        pool = samples.shape[0]
        coupled = over(coupling, near_parts(reduced), 1, 0)
        stacks.append(samples - coupled[:pool])
        skeletons.append(select_rows(picks, samples) - coupled[pool:])
    if early is not None:
        early(skeletons[0])
    interps = interpolate(stacks, skeletons)
    return [
        (interp, skeleton, near_product(interp, node[1]))
        for interp, skeleton, node in zip(interps, skeletons, nodes)
    ]


def leaves_body(received, *refs):
    own_ref, *others = refs[: received + 1]
    source_ref, picks_ref, couplings_ref = refs[received + 1 : received + 4]
    leaf_ref, upper_ref, skeleton_ref, reduced_ref, sent_ref, held_ref, sem = refs[-7:]
    total = own_ref[...]
    for other in others:
        total = total + other[...].astype(F32)
    count = total.shape[0] // LEAF
    stacks = [total[leaf * LEAF : (leaf + 1) * LEAF] for leaf in range(count)]
    skeletons = [select_rows(picks_ref[leaf], stack) for leaf, stack in enumerate(stacks)]
    reduced = []
    for leaf, interp in enumerate(interpolate(stacks, skeletons)):
        held_ref[leaf] = interp
        reduced.append(exact_product(interp, source_ref[pl.ds(leaf * LEAF, LEAF), :]))
    copy = pltpu.make_async_copy(held_ref, leaf_ref, sem)
    copy.start()
    node = (
        jnp.concatenate(skeletons, axis=0),
        jnp.concatenate(reduced, axis=0),
        couplings_ref[...],
        picks_ref[count],
    )
    ((interp, skeleton, reduced),) = merge([node])
    upper_ref[...] = interp
    skeleton_ref[...] = skeleton
    reduced_ref[...] = reduced
    for pos, part in enumerate((*split(skeleton)[:2], reduced.astype(BF16))):
        sent_ref[pl.ds(pos * skeleton.shape[0], skeleton.shape[0]), :] = part
    copy.wait()


def leaves(own, others, source, picks, couplings, later, leaf_count):
    samples = own.shape[1]
    rank, pool = picks.shape[1:]
    return pl.pallas_call(
        lambda *refs: leaves_body(len(others), *refs),
        out_shape=(
            jax.ShapeDtypeStruct((leaf_count, rank, LEAF), F32),
            vmem((rank, pool), F32),
            vmem((rank, samples), F32),
            vmem((rank, samples), F32),
            vmem((3 * rank, samples), BF16),
        ),
        out_specs=(pl.BlockSpec(memory_space=pl.ANY), VMEM, VMEM, VMEM, VMEM),
        scratch_shapes=[pltpu.VMEM((leaf_count, rank, LEAF), F32), pltpu.SemaphoreType.DMA],
        cost_estimate=COST,
        compiler_params=PARAMS,
        name="leaves",
    )(own, *others, source, picks, couplings, *later)


def first_of_pair(number):
    return (lax.axis_index("col") >> (number - 2)) % 2 == 0


def pair(mine, theirs, mine_first):
    first = jnp.where(mine_first, mine, theirs)
    second = jnp.where(mine_first, theirs, mine)
    return jnp.concatenate([first, second], axis=0)


def upper_body(picks_count, *refs):
    states = [(refs[0][...], refs[1][...])]
    rank = refs[0].shape[0]
    for got_ref in refs[2:5]:
        high, middle, reduced = (got_ref[pl.ds(pos * rank, rank), :] for pos in range(3))
        states.append((high.astype(F32) + middle.astype(F32), reduced.astype(F32)))
    picks_ref, two_ref, other_ref, three_ref, one_ref, upper_out, top_out = refs[5:12]
    upper_ref, state_ref, sem = refs[12:]
    places = [
        (one_ref, upper_out.at[0, 0]),
        (upper_ref.at[0], upper_out.at[1, 0]),
        (upper_ref.at[1], upper_out.at[2, 0]),
        (state_ref.at[0], top_out.at[0, 0]),
        (state_ref.at[1], top_out.at[1, 0]),
    ]
    copies = [
        pltpu.make_async_copy(source, target, sem.at[pos])
        for pos, (source, target) in enumerate(places)
    ]
    copies[0].start()
    mine_first = first_of_pair(2)
    nodes = []
    for number, coupling_ref in enumerate((two_ref, other_ref)):
        mine, theirs = states[2 * number : 2 * number + 2]
        picks = picks_ref[picks_count - 3 + number]
        stacks = [pair(*parts, mine_first) for parts in zip(mine, theirs)]
        nodes.append((*stacks, coupling_ref[...], picks))
    mine, theirs = merge(nodes)
    upper_ref[0] = mine[0]
    copies[1].start()

    def early(skeleton):
        state_ref[0] = skeleton
        copies[3].start()

    mine_first = first_of_pair(3)
    stacks = [pair(*parts, mine_first) for parts in zip(mine[1:], theirs[1:])]
    ((interp, _, reduced),) = merge([(*stacks, three_ref[...], picks_ref[picks_count - 1])], early)
    upper_ref[1] = interp
    copies[2].start()
    state_ref[1] = reduced
    copies[4].start()
    for copy in copies:
        copy.wait()


def upper_levels(skeleton, reduced, got, picks, couplings, interp_one):
    rank, pool = picks.shape[1:]
    samples = skeleton.shape[1]
    return pl.pallas_call(
        lambda *refs: upper_body(picks.shape[0], *refs),
        out_shape=(
            jax.ShapeDtypeStruct((3, 1, rank, pool), F32),
            jax.ShapeDtypeStruct((2, 1, rank, samples), F32),
        ),
        out_specs=(pl.BlockSpec(memory_space=pl.ANY),) * 2,
        scratch_shapes=[
            pltpu.VMEM((2, rank, pool), F32),
            pltpu.VMEM((2, rank, samples), F32),
            pltpu.SemaphoreType.DMA((5,)),
        ],
        cost_estimate=COST,
        compiler_params=PARAMS,
        name="upper_levels",
    )(skeleton, reduced, *got, picks, *couplings, interp_one)


def one_hot(chosen, pool):
    place = lax.broadcasted_iota(jnp.int32, (pool, chosen.shape[1]), 0)
    return jnp.where(place.astype(F32) == chosen, 1.0, 0.0).astype(F32)


def couple(first, second, picks, gain, couplings_ref):
    rank = first.shape[1]
    points = jnp.concatenate([first, second], axis=1)
    entries = jnp.exp2(over(row_features(points, gain).astype(BF16), col_features(points), 0, 0))
    left = lax.broadcasted_iota(jnp.int32, entries.shape, 1) < rank
    upper = lax.broadcasted_iota(jnp.int32, entries.shape, 0) < rank
    entries = jnp.where(left == upper, 0.0, entries)
    chosen = select_rows(picks.T.astype(BF16), entries)
    high, middle, _ = split(jnp.concatenate([entries, chosen], axis=0))
    couplings_ref[...] = jnp.concatenate([high, high, middle], axis=1)


def coupling_shape(rank):
    return vmem((3 * rank, 6 * rank), BF16)


def skeletons_body(gain, span, counts, mine_ref, beside_ref, *refs):
    picks_ref, one_ref, two_ref, points_ref = refs
    rank, pool = picks_ref.shape[1:]
    leaf_count = counts[0]
    tables = 2 * (span + 16)
    nodes = []
    for source_ref in (mine_ref, beside_ref):
        rows = source_ref[pl.ds(tables, source_ref.shape[0] - tables), :rank].astype(F32)
        hots = [one_hot(rows[pos : pos + 1], pool) for pos in range(leaf_count + 1)]
        children = []
        for leaf in range(leaf_count):
            feats = source_ref[pl.ds(2 * span, 16), pl.ds(leaf * LEAF, LEAF)]
            children.append(over(feats, hots[leaf].astype(BF16), 1, 0))
        points = jnp.concatenate(children, axis=1)
        nodes.append(over(points, hots[leaf_count], 1, 0))
        if source_ref is mine_ref:
            couple(*children, hots[leaf_count], gain, one_ref)
            start = leaf_count + counts[1]
            level_two = lax.axis_index("col") // 2
            wanted = [level_two, level_two + 1 - 2 * (level_two % 2), counts[2] + level_two // 2]
            for row in wanted:
                place = lax.broadcasted_iota(jnp.int32, rows.shape, 0)
                named = jnp.where(place == start + row, rows, 0.0)
                hots.append(one_hot(jnp.sum(named, axis=0, keepdims=True), pool))
            for number, hot in enumerate(hots):
                picks_ref[number] = hot.T.astype(BF16)
            upper = hots[leaf_count + 1]
    mine, theirs = nodes
    mine_first = first_of_pair(2)
    first = jnp.where(mine_first, mine, theirs)
    second = jnp.where(mine_first, theirs, mine)
    couple(first, second, upper, gain, two_ref)
    points_ref[...] = jnp.concatenate([first, second], axis=1).astype(BF16)


def skeletons(packed, beside, tables, span, gain):
    leaf_count, rank = tables[0].shape
    counts = [table.shape[0] for table in tables]
    return pl.pallas_call(
        lambda *refs: skeletons_body(gain, span, counts, *refs),
        out_shape=(
            vmem((leaf_count + 4, rank, LEAF), BF16),
            coupling_shape(rank),
            coupling_shape(rank),
            vmem((16, 2 * rank), BF16),
        ),
        cost_estimate=COST,
        compiler_params=PARAMS,
        name="skeletons",
    )(packed, beside)


def top_couplings_body(gain, mine_ref, theirs_ref, picks_ref, other_ref, three_ref):
    count, rank, _ = picks_ref.shape
    picks = [picks_ref[count - pos].astype(F32).T for pos in (3, 2, 1)]
    mine, theirs = mine_ref[...].astype(F32), theirs_ref[...].astype(F32)
    couple(theirs[:, :rank], theirs[:, rank:], picks[1], gain, other_ref)
    mine, theirs = over(mine, picks[0], 1, 0), over(theirs, picks[1], 1, 0)
    mine_first = first_of_pair(3)
    first = jnp.where(mine_first, mine, theirs)
    second = jnp.where(mine_first, theirs, mine)
    couple(first, second, picks[2], gain, three_ref)


def top_couplings(mine, theirs, picks, gain):
    return pl.pallas_call(
        lambda *refs: top_couplings_body(gain, *refs),
        out_shape=[coupling_shape(picks.shape[1])] * 2,
        cost_estimate=LONG,
        compiler_params=PARAMS,
        name="top_couplings",
    )(mine, theirs, picks)


def local(probes, points, leaf_skeleton, skeleton_one, skeleton_two, skeleton_three):
    span = probes.shape[1]
    row_count = lax.axis_size("row")
    col_count = lax.axis_size("col")
    gain = 16.0 / math.sqrt(4 * span * row_count * col_count)

    def swap(value, row_bits, col_bits):
        pairs = [
            (r * col_count + c, (r ^ row_bits) * col_count + (c ^ col_bits))
            for r in range(row_count)
            for c in range(col_count)
        ]
        return lax.ppermute(value, ("row", "col"), pairs)

    tables = (leaf_skeleton, skeleton_one, skeleton_two, skeleton_three)
    first, second, own_points = pack(probes, points, tables)
    beside_first, across_second = swap(first, 0, 1), swap(second, 2, 0)
    line = col_count // 2
    line_points = own_points
    for bit in range(1, col_count.bit_length() - 1):
        line_points = jnp.concatenate([line_points, swap(line_points, 0, 1 << bit)], axis=1)
        if bit == 1:
            line_points, *late = lax.optimization_barrier((line_points, first, second))
    beside_second, across_first = swap(late[1], 0, 1), swap(late[0], 2, 0)
    line_points = [line_points, swap(line_points, 1, 0)]
    near, far = range(2), range(2, line)
    groups = [
        [(core, chunk * span) for chunk in group] for core in range(2) for group in (near, far)
    ]
    feats, totals = first_product((first, second), line_points, groups, span, gain)
    beside_first, across_second, *totals = lax.optimization_barrier(
        (beside_first, across_second, *totals)
    )
    diagonal = [swap(beside_first, 2, 0), swap(across_second, 0, 1)]
    totals = product([beside_first, across_second], feats, totals, span, SHORT)
    beside_second, across_first, *totals = lax.optimization_barrier(
        (beside_second, across_first, *totals)
    )
    totals = product([beside_second, across_first], feats, totals, span)
    first, *totals = lax.optimization_barrier((first, *totals))
    picks, couplings_one, couplings_two, points_two = skeletons(
        first, beside_first, tables, span, gain
    )
    points_two, *totals = lax.optimization_barrier((points_two, *totals))
    pieces = [first, second, beside_first, beside_second, across_first, across_second, *diagonal]
    for bit in range(2, row_count.bit_length() - 1):
        more = [swap(value, 1 << bit, 0) for value in pieces]
        totals = product(more, feats, totals, span)
        pieces += more
    (theirs,) = product(diagonal, feats[3:], totals[3:], span, kind=BF16)
    from_sibling = swap(theirs, 1, 0)
    mine, theirs = product(diagonal, feats[1:3], totals[1:3], span)
    outs = [(range(0, line - 2, 2), F32), (range(1, line - 2, 2), BF16)]
    kept, sent = add_up(mine, from_sibling, outs, span)
    sent, theirs, points_two = lax.optimization_barrier((sent, theirs, points_two))
    arrived = swap(sent, 0, 2)
    from_sibling = swap(theirs, 1, 0)
    (mine,) = product(diagonal, feats[:1], totals[:1], span)
    own_sum, near_sent = add_up(mine, from_sibling, [([0], F32), ([1], BF16)], span)
    near_sum = swap(near_sent, 0, 2)
    received = []
    chunks = list(range(2, line, 2))
    bit = 2
    while chunks:
        sent_places = [pos for pos, chunk in enumerate(chunks) if chunk & bit]
        kept_places = [pos for pos, chunk in enumerate(chunks) if not chunk & bit]
        outs = [(sent_places, BF16)] + [(kept_places, F32)] * (len(kept_places) > 0)
        sent, *kept = add_up(kept, arrived, outs, span, (near_sent,), LONG)
        arrived = swap(sent, 0, 2 * bit)
        received.append(arrived[:span] if len(sent_places) > 1 else arrived)
        if kept:
            (kept,) = kept
            arrived = arrived[span:]
        chunks = [chunks[pos] for pos in kept_places]
        bit *= 2
    received.append(near_sum)
    other_points = swap(points_two, 0, 2)
    later = top_couplings(points_two, other_points, picks, gain)

    leaf_interp, interp_one, skeleton, reduced, sent = leaves(
        own_sum, received, first, picks, couplings_one, later, leaf_skeleton.shape[0]
    )
    got = [swap(sent, 0, bits) for bits in (1, 2, 3)]
    upper_interp, top_state = upper_levels(
        skeleton, reduced, got, picks, (couplings_two, *later), interp_one
    )
    return jnp.swapaxes(leaf_interp, 1, 2), jnp.swapaxes(upper_interp, 2, 3), top_state


def solution(mesh):
    placed = (
        P(None, ("row", "col"), None),
        P(None, None, ("row", "col")),
        P(("row", "col"), None),
        P(("row", "col"), None),
        P("row", None),
        P("row", None),
    )
    return jax.shard_map(
        local,
        mesh=mesh,
        in_specs=placed,
        out_specs=(
            P(("row", "col"), None, None),
            P(None, ("row", "col"), None, None),
            P(None, ("row", "col"), None, None),
        ),
        check_vma=False,
    )
```

```python
import math

import jax
import jax.numpy as jnp
from jax import lax
from jax.experimental import pallas as pl
from jax.experimental.pallas import tpu as pltpu
from jax.sharding import PartitionSpec as P

LEAF = 128
F32 = jnp.float32
BF16 = jnp.bfloat16
DOUBLINGS = 9
VMEM = pl.BlockSpec(memory_space=pltpu.VMEM)


def vmem(shape, kind=F32):
    return pltpu.VMEM(tuple(shape), kind)


COST = pl.CostEstimate(flops=10**9, bytes_accessed=0, transcendentals=0)
SHORT = pl.CostEstimate(flops=0, bytes_accessed=0, transcendentals=0)
LONG = pl.CostEstimate(flops=10**10, bytes_accessed=0, transcendentals=0)
PARAMS = pltpu.CompilerParams(vmem_limit_bytes=16 << 20)


def chebyshev_constants():
    taus = [1282.0 / 1280.0]
    for _ in range(DOUBLINGS):
        taus.append(2.0 * taus[-1] * taus[-1] - 1.0)
    front = 2.0**DOUBLINGS * math.prod(taus[:-1]) / taus[-1]
    return taus[:-1], front


TAUS, FRONT = chebyshev_constants()


def over(first, second, first_dim, second_dim):
    return lax.dot_general(
        first,
        second,
        (((first_dim,), (second_dim,)), ((), ())),
        preferred_element_type=F32,
    )


def split(value):
    high = value.astype(BF16)
    rest = value - high.astype(F32)
    middle = rest.astype(BF16)
    return high, middle, (rest - middle.astype(F32)).astype(BF16)


def norm_rows(norm, first, width):
    parts = [part.astype(F32) for part in split(norm)]
    place = lax.broadcasted_iota(jnp.int32, (16, width), 0)
    extra = jnp.where(place < 6, 1.0, 0.0)
    for pos in range(3):
        extra = jnp.where(place == pos + first, parts[pos], extra)
    return extra


def row_features(feats, gain):
    feats = feats.astype(F32)
    depth, width = feats.shape
    unit = math.log2(math.e) / (2.0 * depth)
    norm = jnp.sum(feats * feats, axis=0, keepdims=True) * -unit + math.log2(gain)
    parts = [part.astype(F32) for part in split(feats * (2.0 * unit))]
    return jnp.concatenate([*parts, norm_rows(norm, 0, width)], axis=0)


def col_features(feats):
    feats = feats.astype(F32)
    depth, width = feats.shape
    unit = math.log2(math.e) / (2.0 * depth)
    norm = jnp.sum(feats * feats, axis=0, keepdims=True) * -unit
    return jnp.concatenate([feats, feats, feats, norm_rows(norm, 3, width)], axis=0).astype(BF16)


def pack_body(*refs):
    probes_ref, points_ref, *table_refs = refs[:6]
    first_ref, second_ref, own_ref, held_ref, rows_ref, *held_tables, sem = refs[6:]
    span = own_ref.shape[1]
    pairs = [(points_ref, held_ref)]
    for number, half_ref in enumerate((first_ref, second_ref)):
        source = probes_ref.at[pl.ds(2 * span * number, 2 * span)]
        pairs.append((source, half_ref.at[pl.ds(0, 2 * span)]))
    pairs += zip(table_refs, held_tables)
    copies = [
        pltpu.make_async_copy(source, target, sem.at[pos])
        for pos, (source, target) in enumerate(pairs)
    ]
    for copy in copies:
        copy.start()
    rows_ref[...] = jnp.zeros_like(rows_ref)
    copies[0].wait()
    points = held_ref[...].astype(F32)
    for quarter in range(4):
        feats = points[:, quarter, :].astype(BF16)
        half_ref = (first_ref, second_ref)[quarter // 2]
        half_ref[pl.ds(2 * span + quarter % 2 * 16, 16), :] = feats
        if quarter == 0:
            own_ref[...] = feats
    for copy in copies[3:]:
        copy.wait()
    start = 0
    for table in held_tables:
        count, rank = table.shape
        rows_ref[pl.ds(start, count), pl.ds(0, rank)] = table[...].astype(F32)
        start += count
    first_ref[pl.ds(second_ref.shape[0], rows_ref.shape[0]), :] = rows_ref[...].astype(BF16)
    for copy in copies[1:3]:
        copy.wait()


def pack(probes, points, tables):
    quarters, span, samples = probes.shape
    table_rows = -(-sum(table.shape[0] for table in tables) // 16) * 16
    inputs = (probes.reshape(quarters * span, samples), points, *tables)
    return pl.pallas_call(
        pack_body,
        out_shape=(
            vmem((2 * (span + 16) + table_rows, samples), BF16),
            vmem((2 * (span + 16), samples), BF16),
            vmem((16, span), BF16),
        ),
        in_specs=[pl.BlockSpec(memory_space=pltpu.HBM)] * len(inputs),
        scratch_shapes=[
            pltpu.VMEM(points.shape, BF16),
            pltpu.VMEM((table_rows, samples), F32),
            *[pltpu.VMEM(table.shape, jnp.int32) for table in tables],
            pltpu.SemaphoreType.DMA((3 + len(tables),)),
        ],
        cost_estimate=COST,
        compiler_params=PARAMS,
        name="pack",
    )(*(pltpu.with_memory_space_constraint(value, pltpu.HBM) for value in inputs))


def masked(entries):
    shape = entries.shape
    row_leaf = lax.broadcasted_iota(jnp.int32, shape, 0) // LEAF
    col_leaf = lax.broadcasted_iota(jnp.int32, shape, 1) // LEAF
    return jnp.where(row_leaf == col_leaf, 0.0, entries)


def add_halves(half_refs, row_refs, cols_ref, put, span, own):
    for number, half_ref in enumerate(half_refs):
        for quarter in range(2):
            feats = half_ref[pl.ds(2 * span + 16 * quarter, 16), :]
            cols_ref[:, pl.ds((2 * number + quarter) * span, span)] = col_features(feats)
    columns = 2 * span * len(half_refs)
    for group, rows_ref in enumerate(row_refs):
        for start in range(0, rows_ref.shape[0], span):
            feats = rows_ref[pl.ds(start, span), :]
            entries = jnp.exp2(over(feats, cols_ref[:, :columns], 1, 0))
            if own and group == 0 and start == 0:
                entries = jnp.concatenate([masked(entries[:, :span]), entries[:, span:]], axis=1)
            randoms = [half_ref[pl.ds(0, 2 * span), :] for half_ref in half_refs]
            put(group, start, over(entries.astype(BF16), jnp.concatenate(randoms, axis=0), 1, 0))


def first_product_body(gain, span, groups, point_count, *refs):
    half_refs, point_refs = refs[:2], refs[2 : point_count + 2]
    row_refs = refs[point_count + 2 : point_count + 2 + len(groups)]
    total_refs, cols_ref = refs[point_count + 2 + len(groups) : -1], refs[-1]
    for rows_ref, places in zip(row_refs, groups):
        for pos, (array, start) in enumerate(places):
            feats = point_refs[array][:, pl.ds(start, span)]
            rows_ref[pl.ds(pos * span, span), :] = row_features(feats, gain).T.astype(BF16)

    def put(group, start, value):
        total_refs[group][pl.ds(start, span), :] = value

    add_halves(half_refs, row_refs, cols_ref, put, span, True)


def first_product(halves, points, groups, span, gain):
    samples = halves[0].shape[1]
    rows = [len(places) * span for places in groups]
    out = pl.pallas_call(
        lambda *refs: first_product_body(gain, span, groups, len(points), *refs),
        out_shape=[vmem((count, 64), BF16) for count in rows]
        + [vmem((count, samples), F32) for count in rows],
        scratch_shapes=[pltpu.VMEM((64, 4 * span), BF16)],
        cost_estimate=COST,
        compiler_params=PARAMS,
        name="first_product",
    )(*halves, *points)
    return out[: len(groups)], out[len(groups) :]


def product_body(span, half_count, count, *refs):
    half_refs, refs = refs[:half_count], refs[half_count:]
    row_refs, old_refs, total_refs = refs[:count], refs[count : 2 * count], refs[2 * count : -1]
    cols_ref = refs[-1]
    for number in range(0, half_count, 2):

        def put(group, start, value):
            place = pl.ds(start, span)
            base = old_refs if number == 0 else total_refs
            value = base[group][place, :] + value
            total_refs[group][place, :] = value.astype(total_refs[group].dtype)

        add_halves(half_refs[number : number + 2], row_refs, cols_ref, put, span, False)


def product(halves, rows, totals, span, cost=COST, kind=F32):
    return pl.pallas_call(
        lambda *refs: product_body(span, len(halves), len(rows), *refs),
        out_shape=[vmem(total.shape, kind) for total in totals],
        scratch_shapes=[pltpu.VMEM((64, 4 * span), BF16)],
        cost_estimate=cost,
        compiler_params=PARAMS,
        name="product",
    )(*halves, *rows, *totals)


def add_up_body(span, outs, mine_ref, theirs_ref, *refs):
    for (chunks, _), out_ref in zip(outs, refs[-len(outs) :]):
        for pos, chunk in enumerate(chunks):
            place = pl.ds(chunk * span, span)
            value = mine_ref[place, :] + theirs_ref[place, :].astype(F32)
            out_ref[pl.ds(pos * span, span), :] = value.astype(out_ref.dtype)


def add_up(mine, theirs, outs, span, after=(), cost=COST):
    samples = mine.shape[1]
    return pl.pallas_call(
        lambda *refs: add_up_body(span, outs, *refs),
        out_shape=[vmem((len(chunks) * span, samples), kind) for chunks, kind in outs],
        cost_estimate=cost,
        compiler_params=PARAMS,
        name="add_up",
    )(mine, theirs, *after)


def wide_product(first, second):
    high, middle, low = split(first)
    other_high, other_middle, other_low = split(second)
    return over(
        jnp.concatenate([high, high, middle, middle, low, high], axis=1),
        jnp.concatenate(
            [other_high, other_middle, other_high, other_middle, other_high, other_low], axis=1
        ),
        1,
        1,
    )


def near_product(first, second):
    high, middle, _ = split(first)
    return over(jnp.concatenate([high, high, middle], axis=1), near_parts(second), 1, 0)


def near_parts(second):
    high, middle, _ = split(second)
    return jnp.concatenate([high, middle, high], axis=0)


def exact_product(first, second):
    second = second.astype(BF16)
    return over(
        jnp.concatenate(split(first), axis=1), jnp.concatenate([second] * 3, axis=0), 1, 0
    )


def twice_product(twice, twice_parts, parts):
    high, middle, _ = twice_parts
    other_high, other_middle, other_low = parts
    left = lax.broadcasted_iota(jnp.int32, high.shape, 1) < high.shape[1] // 2
    low = twice - high.astype(F32) - middle.astype(F32)
    last = jnp.where(left, low, high.astype(F32)).astype(BF16)
    return over(
        jnp.concatenate([high, middle, last], axis=1),
        jnp.concatenate(
            [other_high, other_middle, other_high, other_middle, other_high, other_low], axis=0
        ),
        1,
        0,
    )


def select_rows(picks, value):
    return over(
        jnp.concatenate([picks] * 3, axis=1), jnp.concatenate(split(value), axis=0), 1, 0
    )


def interpolate(stacks, skeletons):
    rank, pool = skeletons[0].shape[0], stacks[0].shape[0]
    place = lax.broadcasted_iota(jnp.int32, (rank, 2 * rank), 0)
    other = lax.broadcasted_iota(jnp.int32, (rank, 2 * rank), 1)
    eyes = jnp.where((other == place) | (other == place + rank), 1.0, 0.0)
    states = []
    for skeleton, stack in zip(skeletons, stacks):
        products = wide_product(skeleton, jnp.concatenate([stack, skeleton, skeleton], axis=0))
        ridge = 0.05 * jnp.sum(skeleton * skeleton, keepdims=True) / rank + 1e-05
        inverse = 1.0 / (640.0 * ridge)
        states.append((products[:, :pool], eyes - products[:, pool:] * inverse, inverse))
    for number, tau in enumerate(TAUS):
        last = number == DOUBLINGS - 1
        later = []
        for solved, power, inverse in states:
            power_parts = split(power)
            parts = split(solved)
            if not last:
                parts = [jnp.concatenate(pair, axis=1) for pair in zip(parts, power_parts)]
            both = twice_product(power, power_parts, parts)
            solved = solved + both[:, :pool] * (1.0 / tau)
            later.append((solved, None if last else 2.0 * both[:, pool:] - eyes, inverse))
        states = later
    return [solved * (inverse * FRONT) for solved, _, inverse in states]


def merge(nodes, early=None):
    stacks, skeletons = [], []
    for samples, reduced, coupling, picks in nodes:
        pool = samples.shape[0]
        coupled = over(coupling, near_parts(reduced), 1, 0)
        stacks.append(samples - coupled[:pool])
        skeletons.append(select_rows(picks, samples) - coupled[pool:])
    if early is not None:
        early(skeletons[0])
    interps = interpolate(stacks, skeletons)
    return [
        (interp, skeleton, near_product(interp, node[1]))
        for interp, skeleton, node in zip(interps, skeletons, nodes)
    ]


def leaves_body(received, *refs):
    own_ref, *others = refs[: received + 1]
    source_ref, picks_ref, couplings_ref = refs[received + 1 : received + 4]
    leaf_ref, upper_ref, skeleton_ref, reduced_ref, sent_ref, held_ref, sem = refs[-7:]
    total = own_ref[...]
    for other in others:
        total = total + other[...].astype(F32)
    count = total.shape[0] // LEAF
    stacks = [total[leaf * LEAF : (leaf + 1) * LEAF] for leaf in range(count)]
    skeletons = [select_rows(picks_ref[leaf], stack) for leaf, stack in enumerate(stacks)]
    reduced = []
    for leaf, interp in enumerate(interpolate(stacks, skeletons)):
        held_ref[leaf] = interp
        reduced.append(exact_product(interp, source_ref[pl.ds(leaf * LEAF, LEAF), :]))
    copy = pltpu.make_async_copy(held_ref, leaf_ref, sem)
    copy.start()
    node = (
        jnp.concatenate(skeletons, axis=0),
        jnp.concatenate(reduced, axis=0),
        couplings_ref[...],
        picks_ref[count],
    )
    ((interp, skeleton, reduced),) = merge([node])
    upper_ref[...] = interp
    skeleton_ref[...] = skeleton
    reduced_ref[...] = reduced
    for pos, part in enumerate((*split(skeleton)[:2], reduced.astype(BF16))):
        sent_ref[pl.ds(pos * skeleton.shape[0], skeleton.shape[0]), :] = part
    copy.wait()


def leaves(own, others, source, picks, couplings, later, leaf_count):
    samples = own.shape[1]
    rank, pool = picks.shape[1:]
    return pl.pallas_call(
        lambda *refs: leaves_body(len(others), *refs),
        out_shape=(
            jax.ShapeDtypeStruct((leaf_count, rank, LEAF), F32),
            vmem((rank, pool), F32),
            vmem((rank, samples), F32),
            vmem((rank, samples), F32),
            vmem((3 * rank, samples), BF16),
        ),
        out_specs=(pl.BlockSpec(memory_space=pl.ANY), VMEM, VMEM, VMEM, VMEM),
        scratch_shapes=[pltpu.VMEM((leaf_count, rank, LEAF), F32), pltpu.SemaphoreType.DMA],
        cost_estimate=COST,
        compiler_params=PARAMS,
        name="leaves",
    )(own, *others, source, picks, couplings, *later)


def first_of_pair(number):
    return (lax.axis_index("col") >> (number - 2)) % 2 == 0


def pair(mine, theirs, mine_first):
    first = jnp.where(mine_first, mine, theirs)
    second = jnp.where(mine_first, theirs, mine)
    return jnp.concatenate([first, second], axis=0)


def upper_body(picks_count, *refs):
    states = [(refs[0][...], refs[1][...])]
    rank = refs[0].shape[0]
    for got_ref in refs[2:5]:
        high, middle, reduced = (got_ref[pl.ds(pos * rank, rank), :] for pos in range(3))
        states.append((high.astype(F32) + middle.astype(F32), reduced.astype(F32)))
    picks_ref, two_ref, other_ref, three_ref, one_ref, upper_out, top_out = refs[5:12]
    upper_ref, state_ref, sem = refs[12:]
    places = [
        (one_ref, upper_out.at[0, 0]),
        (upper_ref.at[0], upper_out.at[1, 0]),
        (upper_ref.at[1], upper_out.at[2, 0]),
        (state_ref.at[0], top_out.at[0, 0]),
        (state_ref.at[1], top_out.at[1, 0]),
    ]
    copies = [
        pltpu.make_async_copy(source, target, sem.at[pos])
        for pos, (source, target) in enumerate(places)
    ]
    copies[0].start()
    mine_first = first_of_pair(2)
    nodes = []
    for number, coupling_ref in enumerate((two_ref, other_ref)):
        mine, theirs = states[2 * number : 2 * number + 2]
        picks = picks_ref[picks_count - 3 + number]
        stacks = [pair(*parts, mine_first) for parts in zip(mine, theirs)]
        nodes.append((*stacks, coupling_ref[...], picks))
    mine, theirs = merge(nodes)
    upper_ref[0] = mine[0]
    copies[1].start()

    def early(skeleton):
        state_ref[0] = skeleton
        copies[3].start()

    mine_first = first_of_pair(3)
    stacks = [pair(*parts, mine_first) for parts in zip(mine[1:], theirs[1:])]
    ((interp, _, reduced),) = merge([(*stacks, three_ref[...], picks_ref[picks_count - 1])], early)
    upper_ref[1] = interp
    copies[2].start()
    state_ref[1] = reduced
    copies[4].start()
    for copy in copies:
        copy.wait()


def upper_levels(skeleton, reduced, got, picks, couplings, interp_one):
    rank, pool = picks.shape[1:]
    samples = skeleton.shape[1]
    return pl.pallas_call(
        lambda *refs: upper_body(picks.shape[0], *refs),
        out_shape=(
            jax.ShapeDtypeStruct((3, 1, rank, pool), F32),
            jax.ShapeDtypeStruct((2, 1, rank, samples), F32),
        ),
        out_specs=(pl.BlockSpec(memory_space=pl.ANY),) * 2,
        scratch_shapes=[
            pltpu.VMEM((2, rank, pool), F32),
            pltpu.VMEM((2, rank, samples), F32),
            pltpu.SemaphoreType.DMA((5,)),
        ],
        cost_estimate=COST,
        compiler_params=PARAMS,
        name="upper_levels",
    )(skeleton, reduced, *got, picks, *couplings, interp_one)


def one_hot(chosen, pool):
    place = lax.broadcasted_iota(jnp.int32, (pool, chosen.shape[1]), 0)
    return jnp.where(place.astype(F32) == chosen, 1.0, 0.0).astype(F32)


def couple(first, second, picks, gain, couplings_ref):
    rank = first.shape[1]
    points = jnp.concatenate([first, second], axis=1)
    entries = jnp.exp2(over(row_features(points, gain).astype(BF16), col_features(points), 0, 0))
    left = lax.broadcasted_iota(jnp.int32, entries.shape, 1) < rank
    upper = lax.broadcasted_iota(jnp.int32, entries.shape, 0) < rank
    entries = jnp.where(left == upper, 0.0, entries)
    chosen = select_rows(picks.T.astype(BF16), entries)
    high, middle, _ = split(jnp.concatenate([entries, chosen], axis=0))
    couplings_ref[...] = jnp.concatenate([high, high, middle], axis=1)


def coupling_shape(rank):
    return vmem((3 * rank, 6 * rank), BF16)


def skeletons_body(gain, span, counts, mine_ref, beside_ref, *refs):
    picks_ref, one_ref, two_ref, points_ref = refs
    rank, pool = picks_ref.shape[1:]
    leaf_count = counts[0]
    tables = 2 * (span + 16)
    nodes = []
    for source_ref in (mine_ref, beside_ref):
        rows = source_ref[pl.ds(tables, source_ref.shape[0] - tables), :rank].astype(F32)
        hots = [one_hot(rows[pos : pos + 1], pool) for pos in range(leaf_count + 1)]
        children = []
        for leaf in range(leaf_count):
            feats = source_ref[pl.ds(2 * span, 16), pl.ds(leaf * LEAF, LEAF)]
            children.append(over(feats, hots[leaf].astype(BF16), 1, 0))
        points = jnp.concatenate(children, axis=1)
        nodes.append(over(points, hots[leaf_count], 1, 0))
        if source_ref is mine_ref:
            couple(*children, hots[leaf_count], gain, one_ref)
            start = leaf_count + counts[1]
            level_two = lax.axis_index("col") // 2
            wanted = [level_two, level_two + 1 - 2 * (level_two % 2), counts[2] + level_two // 2]
            for row in wanted:
                place = lax.broadcasted_iota(jnp.int32, rows.shape, 0)
                named = jnp.where(place == start + row, rows, 0.0)
                hots.append(one_hot(jnp.sum(named, axis=0, keepdims=True), pool))
            for number, hot in enumerate(hots):
                picks_ref[number] = hot.T.astype(BF16)
            upper = hots[leaf_count + 1]
    mine, theirs = nodes
    mine_first = first_of_pair(2)
    first = jnp.where(mine_first, mine, theirs)
    second = jnp.where(mine_first, theirs, mine)
    couple(first, second, upper, gain, two_ref)
    points_ref[...] = jnp.concatenate([first, second], axis=1).astype(BF16)


def skeletons(packed, beside, tables, span, gain):
    leaf_count, rank = tables[0].shape
    counts = [table.shape[0] for table in tables]
    return pl.pallas_call(
        lambda *refs: skeletons_body(gain, span, counts, *refs),
        out_shape=(
            vmem((leaf_count + 4, rank, LEAF), BF16),
            coupling_shape(rank),
            coupling_shape(rank),
            vmem((16, 2 * rank), BF16),
        ),
        cost_estimate=COST,
        compiler_params=PARAMS,
        name="skeletons",
    )(packed, beside)


def top_couplings_body(gain, mine_ref, theirs_ref, picks_ref, other_ref, three_ref):
    count, rank, _ = picks_ref.shape
    picks = [picks_ref[count - pos].astype(F32).T for pos in (3, 2, 1)]
    mine, theirs = mine_ref[...].astype(F32), theirs_ref[...].astype(F32)
    couple(theirs[:, :rank], theirs[:, rank:], picks[1], gain, other_ref)
    mine, theirs = over(mine, picks[0], 1, 0), over(theirs, picks[1], 1, 0)
    mine_first = first_of_pair(3)
    first = jnp.where(mine_first, mine, theirs)
    second = jnp.where(mine_first, theirs, mine)
    couple(first, second, picks[2], gain, three_ref)


def top_couplings(mine, theirs, picks, gain):
    return pl.pallas_call(
        lambda *refs: top_couplings_body(gain, *refs),
        out_shape=[coupling_shape(picks.shape[1])] * 2,
        cost_estimate=LONG,
        compiler_params=PARAMS,
        name="top_couplings",
    )(mine, theirs, picks)


def local(probes, points, leaf_skeleton, skeleton_one, skeleton_two, skeleton_three):
    span = probes.shape[1]
    row_count = lax.axis_size("row")
    col_count = lax.axis_size("col")
    gain = 16.0 / math.sqrt(4 * span * row_count * col_count)

    def swap(value, row_bits, col_bits):
        pairs = [
            (r * col_count + c, (r ^ row_bits) * col_count + (c ^ col_bits))
            for r in range(row_count)
            for c in range(col_count)
        ]
        return lax.ppermute(value, ("row", "col"), pairs)

    tables = (leaf_skeleton, skeleton_one, skeleton_two, skeleton_three)
    first, second, own_points = pack(probes, points, tables)
    beside_first, across_second = swap(first, 0, 1), swap(second, 2, 0)
    line = col_count // 2
    line_points = own_points
    for bit in range(1, col_count.bit_length() - 1):
        line_points = jnp.concatenate([line_points, swap(line_points, 0, 1 << bit)], axis=1)
        if bit == 1:
            line_points, *late = lax.optimization_barrier((line_points, first, second))
    beside_second, across_first = swap(late[1], 0, 1), swap(late[0], 2, 0)
    line_points = [line_points, swap(line_points, 1, 0)]
    near, far = range(2), range(2, line)
    groups = [
        [(core, chunk * span) for chunk in group] for core in range(2) for group in (near, far)
    ]
    feats, totals = first_product((first, second), line_points, groups, span, gain)
    beside_first, across_second, *totals = lax.optimization_barrier(
        (beside_first, across_second, *totals)
    )
    diagonal = [swap(beside_first, 2, 0), swap(across_second, 0, 1)]
    totals = product([beside_first, across_second], feats, totals, span, SHORT)
    beside_second, across_first, *totals = lax.optimization_barrier(
        (beside_second, across_first, *totals)
    )
    totals = product([beside_second, across_first], feats, totals, span)
    first, *totals = lax.optimization_barrier((first, *totals))
    picks, couplings_one, couplings_two, points_two = skeletons(
        first, beside_first, tables, span, gain
    )
    points_two, *totals = lax.optimization_barrier((points_two, *totals))
    pieces = [first, second, beside_first, beside_second, across_first, across_second, *diagonal]
    for bit in range(2, row_count.bit_length() - 1):
        more = [swap(value, 1 << bit, 0) for value in pieces]
        totals = product(more, feats, totals, span)
        pieces += more
    (theirs,) = product(diagonal, feats[3:], totals[3:], span, kind=BF16)
    from_sibling = swap(theirs, 1, 0)
    mine, theirs = product(diagonal, feats[1:3], totals[1:3], span)
    outs = [(range(0, line - 2, 2), F32), (range(1, line - 2, 2), BF16)]
    kept, sent = add_up(mine, from_sibling, outs, span)
    sent, theirs, points_two = lax.optimization_barrier((sent, theirs, points_two))
    arrived = swap(sent, 0, 2)
    from_sibling = swap(theirs, 1, 0)
    (mine,) = product(diagonal, feats[:1], totals[:1], span)
    own_sum, near_sent = add_up(mine, from_sibling, [([0], F32), ([1], BF16)], span)
    near_sum = swap(near_sent, 0, 2)
    received = []
    chunks = list(range(2, line, 2))
    bit = 2
    while chunks:
        sent_places = [pos for pos, chunk in enumerate(chunks) if chunk & bit]
        kept_places = [pos for pos, chunk in enumerate(chunks) if not chunk & bit]
        outs = [(sent_places, BF16)] + [(kept_places, F32)] * (len(kept_places) > 0)
        sent, *kept = add_up(kept, arrived, outs, span, (near_sent,), LONG)
        arrived = swap(sent, 0, 2 * bit)
        received.append(arrived[:span] if len(sent_places) > 1 else arrived)
        if kept:
            (kept,) = kept
            arrived = arrived[span:]
        chunks = [chunks[pos] for pos in kept_places]
        bit *= 2
    received.append(near_sum)
    other_points = swap(points_two, 0, 2)
    later = top_couplings(points_two, other_points, picks, gain)

    leaf_interp, interp_one, skeleton, reduced, sent = leaves(
        own_sum, received, first, picks, couplings_one, later, leaf_skeleton.shape[0]
    )
    got = [swap(sent, 0, bits) for bits in (1, 2, 3)]
    upper_interp, top_state = upper_levels(
        skeleton, reduced, got, picks, (couplings_two, *later), interp_one
    )
    return jnp.swapaxes(leaf_interp, 1, 2), jnp.swapaxes(upper_interp, 2, 3), top_state


def solution(mesh):
    placed = (
        P(None, ("row", "col"), None),
        P(None, None, ("row", "col")),
        P(("row", "col"), None),
        P(("row", "col"), None),
        P("row", None),
        P("row", None),
    )
    return jax.shard_map(
        local,
        mesh=mesh,
        in_specs=placed,
        out_specs=(
            P(("row", "col"), None, None),
            P(None, ("row", "col"), None, None),
            P(None, ("row", "col"), None, None),
        ),
        check_vma=False,
    )
```

```python
import math

import jax
import jax.numpy as jnp
from jax import lax
from jax.experimental import pallas as pl
from jax.experimental.pallas import tpu as pltpu
from jax.sharding import PartitionSpec as P

LEAF = 128
F32 = jnp.float32
BF16 = jnp.bfloat16
DOUBLINGS = 9
VMEM = pl.BlockSpec(memory_space=pltpu.VMEM)


def vmem(shape, kind=F32):
    return pltpu.VMEM(tuple(shape), kind)


COST = pl.CostEstimate(flops=10**9, bytes_accessed=0, transcendentals=0)
SHORT = pl.CostEstimate(flops=0, bytes_accessed=0, transcendentals=0)
LONG = pl.CostEstimate(flops=10**10, bytes_accessed=0, transcendentals=0)
PARAMS = pltpu.CompilerParams(vmem_limit_bytes=16 << 20)


def chebyshev_constants():
    taus = [1282.0 / 1280.0]
    for _ in range(DOUBLINGS):
        taus.append(2.0 * taus[-1] * taus[-1] - 1.0)
    front = 2.0**DOUBLINGS * math.prod(taus[:-1]) / taus[-1]
    return taus[:-1], front


TAUS, FRONT = chebyshev_constants()


def over(first, second, first_dim, second_dim):
    return lax.dot_general(
        first,
        second,
        (((first_dim,), (second_dim,)), ((), ())),
        preferred_element_type=F32,
    )


def split(value):
    high = value.astype(BF16)
    rest = value - high.astype(F32)
    middle = rest.astype(BF16)
    return high, middle, (rest - middle.astype(F32)).astype(BF16)


def norm_rows(norm, first, width):
    parts = [part.astype(F32) for part in split(norm)]
    place = lax.broadcasted_iota(jnp.int32, (16, width), 0)
    extra = jnp.where(place < 6, 1.0, 0.0)
    for pos in range(3):
        extra = jnp.where(place == pos + first, parts[pos], extra)
    return extra


def row_features(feats, gain):
    feats = feats.astype(F32)
    depth, width = feats.shape
    unit = math.log2(math.e) / (2.0 * depth)
    norm = jnp.sum(feats * feats, axis=0, keepdims=True) * -unit + math.log2(gain)
    parts = [part.astype(F32) for part in split(feats * (2.0 * unit))]
    return jnp.concatenate([*parts, norm_rows(norm, 0, width)], axis=0)


def col_features(feats):
    feats = feats.astype(F32)
    depth, width = feats.shape
    unit = math.log2(math.e) / (2.0 * depth)
    norm = jnp.sum(feats * feats, axis=0, keepdims=True) * -unit
    return jnp.concatenate([feats, feats, feats, norm_rows(norm, 3, width)], axis=0).astype(BF16)


def pack_body(*refs):
    probes_ref, points_ref, *table_refs = refs[:6]
    first_ref, second_ref, own_ref, held_ref, rows_ref, *held_tables, sem = refs[6:]
    span = own_ref.shape[1]
    pairs = [(points_ref, held_ref)]
    for number, half_ref in enumerate((first_ref, second_ref)):
        source = probes_ref.at[pl.ds(2 * span * number, 2 * span)]
        pairs.append((source, half_ref.at[pl.ds(0, 2 * span)]))
    pairs += zip(table_refs, held_tables)
    copies = [
        pltpu.make_async_copy(source, target, sem.at[pos])
        for pos, (source, target) in enumerate(pairs)
    ]
    for copy in copies:
        copy.start()
    rows_ref[...] = jnp.zeros_like(rows_ref)
    copies[0].wait()
    points = held_ref[...].astype(F32)
    for quarter in range(4):
        feats = points[:, quarter, :].astype(BF16)
        half_ref = (first_ref, second_ref)[quarter // 2]
        half_ref[pl.ds(2 * span + quarter % 2 * 16, 16), :] = feats
        if quarter == 0:
            own_ref[...] = feats
    for copy in copies[3:]:
        copy.wait()
    start = 0
    for table in held_tables:
        count, rank = table.shape
        rows_ref[pl.ds(start, count), pl.ds(0, rank)] = table[...].astype(F32)
        start += count
    first_ref[pl.ds(second_ref.shape[0], rows_ref.shape[0]), :] = rows_ref[...].astype(BF16)
    for copy in copies[1:3]:
        copy.wait()


def pack(probes, points, tables):
    quarters, span, samples = probes.shape
    table_rows = -(-sum(table.shape[0] for table in tables) // 16) * 16
    inputs = (probes.reshape(quarters * span, samples), points, *tables)
    return pl.pallas_call(
        pack_body,
        out_shape=(
            vmem((2 * (span + 16) + table_rows, samples), BF16),
            vmem((2 * (span + 16), samples), BF16),
            vmem((16, span), BF16),
        ),
        in_specs=[pl.BlockSpec(memory_space=pltpu.HBM)] * len(inputs),
        scratch_shapes=[
            pltpu.VMEM(points.shape, BF16),
            pltpu.VMEM((table_rows, samples), F32),
            *[pltpu.VMEM(table.shape, jnp.int32) for table in tables],
            pltpu.SemaphoreType.DMA((3 + len(tables),)),
        ],
        cost_estimate=COST,
        compiler_params=PARAMS,
        name="pack",
    )(*(pltpu.with_memory_space_constraint(value, pltpu.HBM) for value in inputs))


def masked(entries):
    shape = entries.shape
    row_leaf = lax.broadcasted_iota(jnp.int32, shape, 0) // LEAF
    col_leaf = lax.broadcasted_iota(jnp.int32, shape, 1) // LEAF
    return jnp.where(row_leaf == col_leaf, 0.0, entries)


def add_halves(half_refs, row_refs, cols_ref, put, span, own):
    for number, half_ref in enumerate(half_refs):
        for quarter in range(2):
            feats = half_ref[pl.ds(2 * span + 16 * quarter, 16), :]
            cols_ref[:, pl.ds((2 * number + quarter) * span, span)] = col_features(feats)
    columns = 2 * span * len(half_refs)
    for group, rows_ref in enumerate(row_refs):
        for start in range(0, rows_ref.shape[0], span):
            feats = rows_ref[pl.ds(start, span), :]
            entries = jnp.exp2(over(feats, cols_ref[:, :columns], 1, 0))
            if own and group == 0 and start == 0:
                entries = jnp.concatenate([masked(entries[:, :span]), entries[:, span:]], axis=1)
            randoms = [half_ref[pl.ds(0, 2 * span), :] for half_ref in half_refs]
            put(group, start, over(entries.astype(BF16), jnp.concatenate(randoms, axis=0), 1, 0))


def first_product_body(gain, span, groups, point_count, *refs):
    half_refs, point_refs = refs[:2], refs[2 : point_count + 2]
    row_refs = refs[point_count + 2 : point_count + 2 + len(groups)]
    total_refs, cols_ref = refs[point_count + 2 + len(groups) : -1], refs[-1]
    for rows_ref, places in zip(row_refs, groups):
        for pos, (array, start) in enumerate(places):
            feats = point_refs[array][:, pl.ds(start, span)]
            rows_ref[pl.ds(pos * span, span), :] = row_features(feats, gain).T.astype(BF16)

    def put(group, start, value):
        total_refs[group][pl.ds(start, span), :] = value

    add_halves(half_refs, row_refs, cols_ref, put, span, True)


def first_product(halves, points, groups, span, gain):
    samples = halves[0].shape[1]
    rows = [len(places) * span for places in groups]
    out = pl.pallas_call(
        lambda *refs: first_product_body(gain, span, groups, len(points), *refs),
        out_shape=[vmem((count, 64), BF16) for count in rows]
        + [vmem((count, samples), F32) for count in rows],
        scratch_shapes=[pltpu.VMEM((64, 4 * span), BF16)],
        cost_estimate=COST,
        compiler_params=PARAMS,
        name="first_product",
    )(*halves, *points)
    return out[: len(groups)], out[len(groups) :]


def product_body(span, half_count, count, *refs):
    half_refs, refs = refs[:half_count], refs[half_count:]
    row_refs, old_refs, total_refs = refs[:count], refs[count : 2 * count], refs[2 * count : -1]
    cols_ref = refs[-1]
    for number in range(0, half_count, 2):

        def put(group, start, value):
            place = pl.ds(start, span)
            base = old_refs if number == 0 else total_refs
            value = base[group][place, :] + value
            total_refs[group][place, :] = value.astype(total_refs[group].dtype)

        add_halves(half_refs[number : number + 2], row_refs, cols_ref, put, span, False)


def product(halves, rows, totals, span, cost=COST, kind=F32):
    return pl.pallas_call(
        lambda *refs: product_body(span, len(halves), len(rows), *refs),
        out_shape=[vmem(total.shape, kind) for total in totals],
        scratch_shapes=[pltpu.VMEM((64, 4 * span), BF16)],
        cost_estimate=cost,
        compiler_params=PARAMS,
        name="product",
    )(*halves, *rows, *totals)


def add_up_body(span, outs, mine_ref, theirs_ref, *refs):
    for (chunks, _), out_ref in zip(outs, refs[-len(outs) :]):
        for pos, chunk in enumerate(chunks):
            place = pl.ds(chunk * span, span)
            value = mine_ref[place, :] + theirs_ref[place, :].astype(F32)
            out_ref[pl.ds(pos * span, span), :] = value.astype(out_ref.dtype)


def add_up(mine, theirs, outs, span, after=(), cost=COST):
    samples = mine.shape[1]
    return pl.pallas_call(
        lambda *refs: add_up_body(span, outs, *refs),
        out_shape=[vmem((len(chunks) * span, samples), kind) for chunks, kind in outs],
        cost_estimate=cost,
        compiler_params=PARAMS,
        name="add_up",
    )(mine, theirs, *after)


def wide_product(first, second):
    high, middle, low = split(first)
    other_high, other_middle, other_low = split(second)
    return over(
        jnp.concatenate([high, high, middle, middle, low, high], axis=1),
        jnp.concatenate(
            [other_high, other_middle, other_high, other_middle, other_high, other_low], axis=1
        ),
        1,
        1,
    )


def near_product(first, second):
    high, middle, _ = split(first)
    return over(jnp.concatenate([high, high, middle], axis=1), near_parts(second), 1, 0)


def near_parts(second):
    high, middle, _ = split(second)
    return jnp.concatenate([high, middle, high], axis=0)


def exact_product(first, second):
    second = second.astype(BF16)
    return over(
        jnp.concatenate(split(first), axis=1), jnp.concatenate([second] * 3, axis=0), 1, 0
    )


def twice_product(twice, twice_parts, parts):
    high, middle, _ = twice_parts
    other_high, other_middle, other_low = parts
    left = lax.broadcasted_iota(jnp.int32, high.shape, 1) < high.shape[1] // 2
    low = twice - high.astype(F32) - middle.astype(F32)
    last = jnp.where(left, low, high.astype(F32)).astype(BF16)
    return over(
        jnp.concatenate([high, middle, last], axis=1),
        jnp.concatenate(
            [other_high, other_middle, other_high, other_middle, other_high, other_low], axis=0
        ),
        1,
        0,
    )


def select_rows(picks, value):
    return over(
        jnp.concatenate([picks] * 3, axis=1), jnp.concatenate(split(value), axis=0), 1, 0
    )


def interpolate(stacks, skeletons):
    rank, pool = skeletons[0].shape[0], stacks[0].shape[0]
    place = lax.broadcasted_iota(jnp.int32, (rank, 2 * rank), 0)
    other = lax.broadcasted_iota(jnp.int32, (rank, 2 * rank), 1)
    eyes = jnp.where((other == place) | (other == place + rank), 1.0, 0.0)
    states = []
    for skeleton, stack in zip(skeletons, stacks):
        products = wide_product(skeleton, jnp.concatenate([stack, skeleton, skeleton], axis=0))
        ridge = 0.05 * jnp.sum(skeleton * skeleton, keepdims=True) / rank + 1e-05
        inverse = 1.0 / (640.0 * ridge)
        states.append((products[:, :pool], eyes - products[:, pool:] * inverse, inverse))
    for number, tau in enumerate(TAUS):
        last = number == DOUBLINGS - 1
        later = []
        for solved, power, inverse in states:
            power_parts = split(power)
            parts = split(solved)
            if not last:
                parts = [jnp.concatenate(pair, axis=1) for pair in zip(parts, power_parts)]
            both = twice_product(power, power_parts, parts)
            solved = solved + both[:, :pool] * (1.0 / tau)
            later.append((solved, None if last else 2.0 * both[:, pool:] - eyes, inverse))
        states = later
    return [solved * (inverse * FRONT) for solved, _, inverse in states]


def merge(nodes, early=None):
    stacks, skeletons = [], []
    for samples, reduced, coupling, picks in nodes:
        pool = samples.shape[0]
        coupled = over(coupling, near_parts(reduced), 1, 0)
        stacks.append(samples - coupled[:pool])
        skeletons.append(select_rows(picks, samples) - coupled[pool:])
    if early is not None:
        early(skeletons[0])
    interps = interpolate(stacks, skeletons)
    return [
        (interp, skeleton, near_product(interp, node[1]))
        for interp, skeleton, node in zip(interps, skeletons, nodes)
    ]


def leaves_body(received, *refs):
    own_ref, *others = refs[: received + 1]
    source_ref, picks_ref, couplings_ref = refs[received + 1 : received + 4]
    leaf_ref, upper_ref, skeleton_ref, reduced_ref, sent_ref, held_ref, sem = refs[-7:]
    total = own_ref[...]
    for other in others:
        total = total + other[...].astype(F32)
    count = total.shape[0] // LEAF
    stacks = [total[leaf * LEAF : (leaf + 1) * LEAF] for leaf in range(count)]
    skeletons = [select_rows(picks_ref[leaf], stack) for leaf, stack in enumerate(stacks)]
    reduced = []
    for leaf, interp in enumerate(interpolate(stacks, skeletons)):
        held_ref[leaf] = interp
        reduced.append(exact_product(interp, source_ref[pl.ds(leaf * LEAF, LEAF), :]))
    copy = pltpu.make_async_copy(held_ref, leaf_ref, sem)
    copy.start()
    node = (
        jnp.concatenate(skeletons, axis=0),
        jnp.concatenate(reduced, axis=0),
        couplings_ref[...],
        picks_ref[count],
    )
    ((interp, skeleton, reduced),) = merge([node])
    upper_ref[...] = interp
    skeleton_ref[...] = skeleton
    reduced_ref[...] = reduced
    for pos, part in enumerate((*split(skeleton)[:2], reduced.astype(BF16))):
        sent_ref[pl.ds(pos * skeleton.shape[0], skeleton.shape[0]), :] = part
    copy.wait()


def leaves(own, others, source, picks, couplings, later, leaf_count):
    samples = own.shape[1]
    rank, pool = picks.shape[1:]
    return pl.pallas_call(
        lambda *refs: leaves_body(len(others), *refs),
        out_shape=(
            jax.ShapeDtypeStruct((leaf_count, rank, LEAF), F32),
            vmem((rank, pool), F32),
            vmem((rank, samples), F32),
            vmem((rank, samples), F32),
            vmem((3 * rank, samples), BF16),
        ),
        out_specs=(pl.BlockSpec(memory_space=pl.ANY), VMEM, VMEM, VMEM, VMEM),
        scratch_shapes=[pltpu.VMEM((leaf_count, rank, LEAF), F32), pltpu.SemaphoreType.DMA],
        cost_estimate=COST,
        compiler_params=PARAMS,
        name="leaves",
    )(own, *others, source, picks, couplings, *later)


def first_of_pair(number):
    return (lax.axis_index("col") >> (number - 2)) % 2 == 0


def pair(mine, theirs, mine_first):
    first = jnp.where(mine_first, mine, theirs)
    second = jnp.where(mine_first, theirs, mine)
    return jnp.concatenate([first, second], axis=0)


def upper_body(picks_count, *refs):
    states = [(refs[0][...], refs[1][...])]
    rank = refs[0].shape[0]
    for got_ref in refs[4:1:-1]:
        high, middle, reduced = (got_ref[pl.ds(pos * rank, rank), :] for pos in range(3))
        states.append((high.astype(F32) + middle.astype(F32), reduced.astype(F32)))
    picks_ref, two_ref, other_ref, three_ref, one_ref, upper_out, top_out = refs[5:12]
    upper_ref, state_ref, sem = refs[12:]
    places = [
        (one_ref, upper_out.at[0, 0]),
        (upper_ref.at[0], upper_out.at[1, 0]),
        (upper_ref.at[1], upper_out.at[2, 0]),
        (state_ref.at[0], top_out.at[0, 0]),
        (state_ref.at[1], top_out.at[1, 0]),
    ]
    copies = [
        pltpu.make_async_copy(source, target, sem.at[pos])
        for pos, (source, target) in enumerate(places)
    ]
    copies[0].start()
    mine_first = first_of_pair(2)
    nodes = []
    for number, coupling_ref in enumerate((two_ref, other_ref)):
        mine, theirs = states[2 * number : 2 * number + 2]
        picks = picks_ref[picks_count - 3 + number]
        stacks = [pair(*parts, mine_first) for parts in zip(mine, theirs)]
        nodes.append((*stacks, coupling_ref[...], picks))
    mine, theirs = merge(nodes)
    upper_ref[0] = mine[0]
    copies[1].start()

    def early(skeleton):
        state_ref[0] = skeleton
        copies[3].start()

    mine_first = first_of_pair(3)
    stacks = [pair(*parts, mine_first) for parts in zip(mine[1:], theirs[1:])]
    ((interp, _, reduced),) = merge([(*stacks, three_ref[...], picks_ref[picks_count - 1])], early)
    upper_ref[1] = interp
    copies[2].start()
    state_ref[1] = reduced
    copies[4].start()
    for copy in copies:
        copy.wait()


def upper_levels(skeleton, reduced, got, picks, couplings, interp_one):
    rank, pool = picks.shape[1:]
    samples = skeleton.shape[1]
    return pl.pallas_call(
        lambda *refs: upper_body(picks.shape[0], *refs),
        out_shape=(
            jax.ShapeDtypeStruct((3, 1, rank, pool), F32),
            jax.ShapeDtypeStruct((2, 1, rank, samples), F32),
        ),
        out_specs=(pl.BlockSpec(memory_space=pl.ANY),) * 2,
        scratch_shapes=[
            pltpu.VMEM((2, rank, pool), F32),
            pltpu.VMEM((2, rank, samples), F32),
            pltpu.SemaphoreType.DMA((5,)),
        ],
        cost_estimate=COST,
        compiler_params=PARAMS,
        name="upper_levels",
    )(skeleton, reduced, *got[::-1], picks, *couplings, interp_one)


def one_hot(chosen, pool):
    place = lax.broadcasted_iota(jnp.int32, (pool, chosen.shape[1]), 0)
    return jnp.where(place.astype(F32) == chosen, 1.0, 0.0).astype(F32)


def couple(first, second, picks, gain, couplings_ref):
    rank = first.shape[1]
    points = jnp.concatenate([first, second], axis=1)
    entries = jnp.exp2(over(row_features(points, gain).astype(BF16), col_features(points), 0, 0))
    left = lax.broadcasted_iota(jnp.int32, entries.shape, 1) < rank
    upper = lax.broadcasted_iota(jnp.int32, entries.shape, 0) < rank
    entries = jnp.where(left == upper, 0.0, entries)
    chosen = select_rows(picks.T.astype(BF16), entries)
    high, middle, _ = split(jnp.concatenate([entries, chosen], axis=0))
    couplings_ref[...] = jnp.concatenate([high, high, middle], axis=1)


def coupling_shape(rank):
    return vmem((3 * rank, 6 * rank), BF16)


def skeletons_body(gain, span, counts, mine_ref, beside_ref, *refs):
    picks_ref, one_ref, two_ref, points_ref = refs
    rank, pool = picks_ref.shape[1:]
    leaf_count = counts[0]
    tables = 2 * (span + 16)
    nodes = []
    for source_ref in (mine_ref, beside_ref):
        rows = source_ref[pl.ds(tables, source_ref.shape[0] - tables), :rank].astype(F32)
        hots = [one_hot(rows[pos : pos + 1], pool) for pos in range(leaf_count + 1)]
        children = []
        for leaf in range(leaf_count):
            feats = source_ref[pl.ds(2 * span, 16), pl.ds(leaf * LEAF, LEAF)]
            children.append(over(feats, hots[leaf].astype(BF16), 1, 0))
        points = jnp.concatenate(children, axis=1)
        nodes.append(over(points, hots[leaf_count], 1, 0))
        if source_ref is mine_ref:
            couple(*children, hots[leaf_count], gain, one_ref)
            start = leaf_count + counts[1]
            level_two = lax.axis_index("col") // 2
            wanted = [level_two, level_two + 1 - 2 * (level_two % 2), counts[2] + level_two // 2]
            for row in wanted:
                place = lax.broadcasted_iota(jnp.int32, rows.shape, 0)
                named = jnp.where(place == start + row, rows, 0.0)
                hots.append(one_hot(jnp.sum(named, axis=0, keepdims=True), pool))
            for number, hot in enumerate(hots):
                picks_ref[number] = hot.T.astype(BF16)
            upper = hots[leaf_count + 1]
    mine, theirs = nodes
    mine_first = first_of_pair(2)
    first = jnp.where(mine_first, mine, theirs)
    second = jnp.where(mine_first, theirs, mine)
    couple(first, second, upper, gain, two_ref)
    points_ref[...] = jnp.concatenate([first, second], axis=1).astype(BF16)


def skeletons(packed, beside, tables, span, gain):
    leaf_count, rank = tables[0].shape
    counts = [table.shape[0] for table in tables]
    return pl.pallas_call(
        lambda *refs: skeletons_body(gain, span, counts, *refs),
        out_shape=(
            vmem((leaf_count + 4, rank, LEAF), BF16),
            coupling_shape(rank),
            coupling_shape(rank),
            vmem((16, 2 * rank), BF16),
        ),
        cost_estimate=COST,
        compiler_params=PARAMS,
        name="skeletons",
    )(packed, beside)


def top_couplings_body(gain, mine_ref, theirs_ref, picks_ref, other_ref, three_ref):
    count, rank, _ = picks_ref.shape
    picks = [picks_ref[count - pos].astype(F32).T for pos in (3, 2, 1)]
    mine, theirs = mine_ref[...].astype(F32), theirs_ref[...].astype(F32)
    couple(theirs[:, :rank], theirs[:, rank:], picks[1], gain, other_ref)
    mine, theirs = over(mine, picks[0], 1, 0), over(theirs, picks[1], 1, 0)
    mine_first = first_of_pair(3)
    first = jnp.where(mine_first, mine, theirs)
    second = jnp.where(mine_first, theirs, mine)
    couple(first, second, picks[2], gain, three_ref)


def top_couplings(mine, theirs, picks, gain):
    return pl.pallas_call(
        lambda *refs: top_couplings_body(gain, *refs),
        out_shape=[coupling_shape(picks.shape[1])] * 2,
        cost_estimate=LONG,
        compiler_params=PARAMS,
        name="top_couplings",
    )(mine, theirs, picks)


def local(probes, points, leaf_skeleton, skeleton_one, skeleton_two, skeleton_three):
    span = probes.shape[1]
    row_count = lax.axis_size("row")
    col_count = lax.axis_size("col")
    gain = 16.0 / math.sqrt(4 * span * row_count * col_count)

    def swap(value, row_bits, col_bits):
        pairs = [
            (r * col_count + c, (r ^ row_bits) * col_count + (c ^ col_bits))
            for r in range(row_count)
            for c in range(col_count)
        ]
        return lax.ppermute(value, ("row", "col"), pairs)

    tables = (leaf_skeleton, skeleton_one, skeleton_two, skeleton_three)
    first, second, own_points = pack(probes, points, tables)
    beside_first, across_second = swap(first, 0, 1), swap(second, 2, 0)
    line = col_count // 2
    line_points = own_points
    for bit in range(1, col_count.bit_length() - 1):
        line_points = jnp.concatenate([line_points, swap(line_points, 0, 1 << bit)], axis=1)
        if bit == 1:
            line_points, *late = lax.optimization_barrier((line_points, first, second))
    beside_second, across_first = swap(late[1], 0, 1), swap(late[0], 2, 0)
    line_points = [line_points, swap(line_points, 1, 0)]
    near, far = range(2), range(2, line)
    groups = [
        [(core, chunk * span) for chunk in group] for core in range(2) for group in (near, far)
    ]
    feats, totals = first_product((first, second), line_points, groups, span, gain)
    beside_first, across_second, *totals = lax.optimization_barrier(
        (beside_first, across_second, *totals)
    )
    diagonal = [swap(beside_first, 2, 0), swap(across_second, 0, 1)]
    totals = product([beside_first, across_second], feats, totals, span, SHORT)
    beside_second, across_first, *totals = lax.optimization_barrier(
        (beside_second, across_first, *totals)
    )
    totals = product([beside_second, across_first], feats, totals, span)
    first, *totals = lax.optimization_barrier((first, *totals))
    picks, couplings_one, couplings_two, points_two = skeletons(
        first, beside_first, tables, span, gain
    )
    points_two, *totals = lax.optimization_barrier((points_two, *totals))
    pieces = [first, second, beside_first, beside_second, across_first, across_second, *diagonal]
    for bit in range(2, row_count.bit_length() - 1):
        more = [swap(value, 1 << bit, 0) for value in pieces]
        totals = product(more, feats, totals, span)
        pieces += more
    (theirs,) = product(diagonal, feats[3:], totals[3:], span, kind=BF16)
    from_sibling = swap(theirs, 1, 0)
    mine, theirs = product(diagonal, feats[1:3], totals[1:3], span)
    outs = [(range(0, line - 2, 2), F32), (range(1, line - 2, 2), BF16)]
    kept, sent = add_up(mine, from_sibling, outs, span)
    sent, theirs, points_two = lax.optimization_barrier((sent, theirs, points_two))
    arrived = swap(sent, 0, 2)
    from_sibling = swap(theirs, 1, 0)
    (mine,) = product(diagonal, feats[:1], totals[:1], span)
    own_sum, near_sent = add_up(mine, from_sibling, [([0], F32), ([1], BF16)], span)
    near_sum = swap(near_sent, 0, 2)
    received = []
    chunks = list(range(2, line, 2))
    bit = 2
    while chunks:
        sent_places = [pos for pos, chunk in enumerate(chunks) if chunk & bit]
        kept_places = [pos for pos, chunk in enumerate(chunks) if not chunk & bit]
        outs = [(sent_places, BF16)] + [(kept_places, F32)] * (len(kept_places) > 0)
        sent, *kept = add_up(kept, arrived, outs, span, (near_sent,), LONG)
        arrived = swap(sent, 0, 2 * bit)
        received.append(arrived[:span] if len(sent_places) > 1 else arrived)
        if kept:
            (kept,) = kept
            arrived = arrived[span:]
        chunks = [chunks[pos] for pos in kept_places]
        bit *= 2
    received.append(near_sum)
    other_points = swap(points_two, 0, 2)
    later = top_couplings(points_two, other_points, picks, gain)

    leaf_interp, interp_one, skeleton, reduced, sent = leaves(
        own_sum, received, first, picks, couplings_one, later, leaf_skeleton.shape[0]
    )
    got = [swap(sent, 0, bits) for bits in (1, 2, 3)]
    upper_interp, top_state = upper_levels(
        skeleton, reduced, got, picks, (couplings_two, *later), interp_one
    )
    return jnp.swapaxes(leaf_interp, 1, 2), jnp.swapaxes(upper_interp, 2, 3), top_state


def solution(mesh):
    placed = (
        P(None, ("row", "col"), None),
        P(None, None, ("row", "col")),
        P(("row", "col"), None),
        P(("row", "col"), None),
        P("row", None),
        P("row", None),
    )
    return jax.shard_map(
        local,
        mesh=mesh,
        in_specs=placed,
        out_specs=(
            P(("row", "col"), None, None),
            P(None, ("row", "col"), None, None),
            P(None, ("row", "col"), None, None),
        ),
        check_vma=False,
    )
```

```python
import math

import jax
import jax.numpy as jnp
from jax import lax
from jax.experimental import pallas as pl
from jax.experimental.pallas import tpu as pltpu
from jax.sharding import PartitionSpec as P

LEAF = 128
F32 = jnp.float32
BF16 = jnp.bfloat16
DOUBLINGS = 9
VMEM = pl.BlockSpec(memory_space=pltpu.VMEM)


def vmem(shape, kind=F32):
    return pltpu.VMEM(tuple(shape), kind)


COST = pl.CostEstimate(flops=10**9, bytes_accessed=0, transcendentals=0)
SHORT = pl.CostEstimate(flops=0, bytes_accessed=0, transcendentals=0)
LONG = pl.CostEstimate(flops=10**10, bytes_accessed=0, transcendentals=0)
PARAMS = pltpu.CompilerParams(vmem_limit_bytes=16 << 20)


def chebyshev_constants():
    taus = [1282.0 / 1280.0]
    for _ in range(DOUBLINGS):
        taus.append(2.0 * taus[-1] * taus[-1] - 1.0)
    front = 2.0**DOUBLINGS * math.prod(taus[:-1]) / taus[-1]
    return taus[:-1], front


TAUS, FRONT = chebyshev_constants()


def over(first, second, first_dim, second_dim):
    return lax.dot_general(
        first,
        second,
        (((first_dim,), (second_dim,)), ((), ())),
        preferred_element_type=F32,
    )


def split(value):
    high = value.astype(BF16)
    rest = value - high.astype(F32)
    middle = rest.astype(BF16)
    return high, middle, (rest - middle.astype(F32)).astype(BF16)


def norm_rows(norm, first, width):
    parts = [part.astype(F32) for part in split(norm)]
    place = lax.broadcasted_iota(jnp.int32, (16, width), 0)
    extra = jnp.where(place < 6, 1.0, 0.0)
    for pos in range(3):
        extra = jnp.where(place == pos + first, parts[pos], extra)
    return extra


def row_features(feats, gain):
    feats = feats.astype(F32)
    depth, width = feats.shape
    unit = math.log2(math.e) / (2.0 * depth)
    norm = jnp.sum(feats * feats, axis=0, keepdims=True) * -unit + math.log2(gain)
    parts = [part.astype(F32) for part in split(feats * (2.0 * unit))]
    return jnp.concatenate([*parts, norm_rows(norm, 0, width)], axis=0)


def col_features(feats):
    feats = feats.astype(F32)
    depth, width = feats.shape
    unit = math.log2(math.e) / (2.0 * depth)
    norm = jnp.sum(feats * feats, axis=0, keepdims=True) * -unit
    return jnp.concatenate([feats, feats, feats, norm_rows(norm, 3, width)], axis=0).astype(BF16)


def pack_body(*refs):
    probes_ref, points_ref, *table_refs = refs[:6]
    first_ref, second_ref, own_ref, held_ref, rows_ref, *held_tables, sem = refs[6:]
    span = own_ref.shape[1]
    pairs = [(points_ref, held_ref)]
    for number, half_ref in enumerate((first_ref, second_ref)):
        source = probes_ref.at[pl.ds(2 * span * number, 2 * span)]
        pairs.append((source, half_ref.at[pl.ds(0, 2 * span)]))
    pairs += zip(table_refs, held_tables)
    copies = [
        pltpu.make_async_copy(source, target, sem.at[pos])
        for pos, (source, target) in enumerate(pairs)
    ]
    for copy in copies:
        copy.start()
    rows_ref[...] = jnp.zeros_like(rows_ref)
    copies[0].wait()
    points = held_ref[...].astype(F32)
    for quarter in range(4):
        feats = points[:, quarter, :].astype(BF16)
        half_ref = (first_ref, second_ref)[quarter // 2]
        half_ref[pl.ds(2 * span + quarter % 2 * 16, 16), :] = feats
        if quarter == 0:
            own_ref[...] = feats
    for copy in copies[3:]:
        copy.wait()
    start = 0
    for table in held_tables:
        count, rank = table.shape
        rows_ref[pl.ds(start, count), pl.ds(0, rank)] = table[...].astype(F32)
        start += count
    first_ref[pl.ds(second_ref.shape[0], rows_ref.shape[0]), :] = rows_ref[...].astype(BF16)
    for copy in copies[1:3]:
        copy.wait()


def pack(probes, points, tables):
    quarters, span, samples = probes.shape
    table_rows = -(-sum(table.shape[0] for table in tables) // 16) * 16
    inputs = (probes.reshape(quarters * span, samples), points, *tables)
    return pl.pallas_call(
        pack_body,
        out_shape=(
            vmem((2 * (span + 16) + table_rows, samples), BF16),
            vmem((2 * (span + 16), samples), BF16),
            vmem((16, span), BF16),
        ),
        in_specs=[pl.BlockSpec(memory_space=pltpu.HBM)] * len(inputs),
        scratch_shapes=[
            pltpu.VMEM(points.shape, BF16),
            pltpu.VMEM((table_rows, samples), F32),
            *[pltpu.VMEM(table.shape, jnp.int32) for table in tables],
            pltpu.SemaphoreType.DMA((3 + len(tables),)),
        ],
        cost_estimate=COST,
        compiler_params=PARAMS,
        name="pack",
    )(*(pltpu.with_memory_space_constraint(value, pltpu.HBM) for value in inputs))


def masked(entries):
    shape = entries.shape
    row_leaf = lax.broadcasted_iota(jnp.int32, shape, 0) // LEAF
    col_leaf = lax.broadcasted_iota(jnp.int32, shape, 1) // LEAF
    return jnp.where(row_leaf == col_leaf, 0.0, entries)


def add_halves(half_refs, row_refs, cols_ref, put, span, own):
    for number, half_ref in enumerate(half_refs):
        for quarter in range(2):
            feats = half_ref[pl.ds(2 * span + 16 * quarter, 16), :]
            cols_ref[:, pl.ds((2 * number + quarter) * span, span)] = col_features(feats)
    columns = 2 * span * len(half_refs)
    for group, rows_ref in enumerate(row_refs):
        for start in range(0, rows_ref.shape[0], span):
            feats = rows_ref[pl.ds(start, span), :]
            entries = jnp.exp2(over(feats, cols_ref[:, :columns], 1, 0))
            if own and group == 0 and start == 0:
                entries = jnp.concatenate([masked(entries[:, :span]), entries[:, span:]], axis=1)
            randoms = [half_ref[pl.ds(0, 2 * span), :] for half_ref in half_refs]
            put(group, start, over(entries.astype(BF16), jnp.concatenate(randoms, axis=0), 1, 0))


def first_product_body(gain, span, groups, point_count, *refs):
    half_refs, point_refs = refs[:2], refs[2 : point_count + 2]
    row_refs = refs[point_count + 2 : point_count + 2 + len(groups)]
    total_refs, cols_ref = refs[point_count + 2 + len(groups) : -1], refs[-1]
    for rows_ref, places in zip(row_refs, groups):
        for pos, (array, start) in enumerate(places):
            feats = point_refs[array][:, pl.ds(start, span)]
            rows_ref[pl.ds(pos * span, span), :] = row_features(feats, gain).T.astype(BF16)

    def put(group, start, value):
        total_refs[group][pl.ds(start, span), :] = value

    add_halves(half_refs, row_refs, cols_ref, put, span, True)


def first_product(halves, points, groups, span, gain):
    samples = halves[0].shape[1]
    rows = [len(places) * span for places in groups]
    out = pl.pallas_call(
        lambda *refs: first_product_body(gain, span, groups, len(points), *refs),
        out_shape=[vmem((count, 64), BF16) for count in rows]
        + [vmem((count, samples), F32) for count in rows],
        scratch_shapes=[pltpu.VMEM((64, 4 * span), BF16)],
        cost_estimate=COST,
        compiler_params=PARAMS,
        name="first_product",
    )(*halves, *points)
    return out[: len(groups)], out[len(groups) :]


def product_body(span, half_count, count, *refs):
    half_refs, refs = refs[:half_count], refs[half_count:]
    row_refs, old_refs, total_refs = refs[:count], refs[count : 2 * count], refs[2 * count : -1]
    cols_ref = refs[-1]
    for number in range(0, half_count, 2):

        def put(group, start, value):
            place = pl.ds(start, span)
            base = old_refs if number == 0 else total_refs
            value = base[group][place, :] + value
            total_refs[group][place, :] = value.astype(total_refs[group].dtype)

        add_halves(half_refs[number : number + 2], row_refs, cols_ref, put, span, False)


def product(halves, rows, totals, span, cost=COST, kind=F32):
    return pl.pallas_call(
        lambda *refs: product_body(span, len(halves), len(rows), *refs),
        out_shape=[vmem(total.shape, kind) for total in totals],
        scratch_shapes=[pltpu.VMEM((64, 4 * span), BF16)],
        cost_estimate=cost,
        compiler_params=PARAMS,
        name="product",
    )(*halves, *rows, *totals)


def add_up_body(span, outs, mine_ref, theirs_ref, *refs):
    for (chunks, _), out_ref in zip(outs, refs[-len(outs) :]):
        for pos, chunk in enumerate(chunks):
            place = pl.ds(chunk * span, span)
            value = mine_ref[place, :] + theirs_ref[place, :].astype(F32)
            out_ref[pl.ds(pos * span, span), :] = value.astype(out_ref.dtype)


def add_up(mine, theirs, outs, span, after=(), cost=COST):
    samples = mine.shape[1]
    return pl.pallas_call(
        lambda *refs: add_up_body(span, outs, *refs),
        out_shape=[vmem((len(chunks) * span, samples), kind) for chunks, kind in outs],
        cost_estimate=cost,
        compiler_params=PARAMS,
        name="add_up",
    )(mine, theirs, *after)


def near_up_body(mine_ref, theirs_ref, points_ref, own_ref, sent_ref):
    span, samples = own_ref.shape
    own_ref[...] = mine_ref[pl.ds(0, span), :] + theirs_ref[pl.ds(0, span), :]
    place = pl.ds(span, span)
    sent_ref[pl.ds(0, span), :] = (mine_ref[place, :] + theirs_ref[place, :]).astype(BF16)
    rows, width = points_ref.shape
    rest = jnp.zeros((rows, samples - width), BF16)
    sent_ref[pl.ds(span, rows), :] = jnp.concatenate([points_ref[...], rest], axis=1)


def near_up(mine, theirs, points, span):
    samples = mine.shape[1]
    return pl.pallas_call(
        near_up_body,
        out_shape=(vmem((span, samples), F32), vmem((span + points.shape[0], samples), BF16)),
        cost_estimate=COST,
        compiler_params=PARAMS,
        name="near_up",
    )(mine, theirs, points)


def wide_product(first, second):
    high, middle, low = split(first)
    other_high, other_middle, other_low = split(second)
    return over(
        jnp.concatenate([high, high, middle, middle, low, high], axis=1),
        jnp.concatenate(
            [other_high, other_middle, other_high, other_middle, other_high, other_low], axis=1
        ),
        1,
        1,
    )


def near_product(first, second):
    high, middle, _ = split(first)
    return over(jnp.concatenate([high, high, middle], axis=1), near_parts(second), 1, 0)


def near_parts(second):
    high, middle, _ = split(second)
    return jnp.concatenate([high, middle, high], axis=0)


def exact_product(first, second):
    second = second.astype(BF16)
    return over(
        jnp.concatenate(split(first), axis=1), jnp.concatenate([second] * 3, axis=0), 1, 0
    )


def twice_product(twice, twice_parts, parts):
    high, middle, _ = twice_parts
    other_high, other_middle, other_low = parts
    left = lax.broadcasted_iota(jnp.int32, high.shape, 1) < high.shape[1] // 2
    low = twice - high.astype(F32) - middle.astype(F32)
    last = jnp.where(left, low, high.astype(F32)).astype(BF16)
    return over(
        jnp.concatenate([high, middle, last], axis=1),
        jnp.concatenate(
            [other_high, other_middle, other_high, other_middle, other_high, other_low], axis=0
        ),
        1,
        0,
    )


def select_rows(picks, value):
    return over(
        jnp.concatenate([picks] * 3, axis=1), jnp.concatenate(split(value), axis=0), 1, 0
    )


def interpolate(stacks, skeletons):
    rank, pool = skeletons[0].shape[0], stacks[0].shape[0]
    place = lax.broadcasted_iota(jnp.int32, (rank, 2 * rank), 0)
    other = lax.broadcasted_iota(jnp.int32, (rank, 2 * rank), 1)
    eyes = jnp.where((other == place) | (other == place + rank), 1.0, 0.0)
    states = []
    for skeleton, stack in zip(skeletons, stacks):
        products = wide_product(skeleton, jnp.concatenate([stack, skeleton, skeleton], axis=0))
        ridge = 0.05 * jnp.sum(skeleton * skeleton, keepdims=True) / rank + 1e-05
        inverse = 1.0 / (640.0 * ridge)
        states.append((products[:, :pool], eyes - products[:, pool:] * inverse, inverse))
    for number, tau in enumerate(TAUS):
        last = number == DOUBLINGS - 1
        later = []
        for solved, power, inverse in states:
            power_parts = split(power)
            parts = split(solved)
            if not last:
                parts = [jnp.concatenate(pair, axis=1) for pair in zip(parts, power_parts)]
            both = twice_product(power, power_parts, parts)
            solved = solved + both[:, :pool] * (1.0 / tau)
            later.append((solved, None if last else 2.0 * both[:, pool:] - eyes, inverse))
        states = later
    return [solved * (inverse * FRONT) for solved, _, inverse in states]


def merge(nodes, early=None):
    stacks, skeletons = [], []
    for samples, reduced, coupling, picks in nodes:
        pool = samples.shape[0]
        coupled = over(coupling, near_parts(reduced), 1, 0)
        stacks.append(samples - coupled[:pool])
        skeletons.append(select_rows(picks, samples) - coupled[pool:])
    if early is not None:
        early(skeletons[0])
    interps = interpolate(stacks, skeletons)
    return [
        (interp, skeleton, near_product(interp, node[1]))
        for interp, skeleton, node in zip(interps, skeletons, nodes)
    ]


def leaves_body(received, *refs):
    own_ref, *others = refs[: received + 1]
    source_ref, picks_ref, couplings_ref = refs[received + 1 : received + 4]
    leaf_ref, upper_ref, skeleton_ref, reduced_ref, sent_ref, held_ref, sem = refs[-7:]
    total = own_ref[...]
    for other in others:
        total = total + other[pl.ds(0, total.shape[0]), :].astype(F32)
    count = total.shape[0] // LEAF
    stacks = [total[leaf * LEAF : (leaf + 1) * LEAF] for leaf in range(count)]
    skeletons = [select_rows(picks_ref[leaf], stack) for leaf, stack in enumerate(stacks)]
    reduced = []
    for leaf, interp in enumerate(interpolate(stacks, skeletons)):
        held_ref[leaf] = interp
        reduced.append(exact_product(interp, source_ref[pl.ds(leaf * LEAF, LEAF), :]))
    copy = pltpu.make_async_copy(held_ref, leaf_ref, sem)
    copy.start()
    node = (
        jnp.concatenate(skeletons, axis=0),
        jnp.concatenate(reduced, axis=0),
        couplings_ref[...],
        picks_ref[count],
    )
    ((interp, skeleton, reduced),) = merge([node])
    upper_ref[...] = interp
    skeleton_ref[...] = skeleton
    reduced_ref[...] = reduced
    for pos, part in enumerate((*split(skeleton)[:2], reduced.astype(BF16))):
        sent_ref[pl.ds(pos * skeleton.shape[0], skeleton.shape[0]), :] = part
    copy.wait()


def leaves(own, others, source, picks, couplings, later, leaf_count):
    samples = own.shape[1]
    rank, pool = picks.shape[1:]
    return pl.pallas_call(
        lambda *refs: leaves_body(len(others), *refs),
        out_shape=(
            jax.ShapeDtypeStruct((leaf_count, rank, LEAF), F32),
            vmem((rank, pool), F32),
            vmem((rank, samples), F32),
            vmem((rank, samples), F32),
            vmem((3 * rank, samples), BF16),
        ),
        out_specs=(pl.BlockSpec(memory_space=pl.ANY), VMEM, VMEM, VMEM, VMEM),
        scratch_shapes=[pltpu.VMEM((leaf_count, rank, LEAF), F32), pltpu.SemaphoreType.DMA],
        cost_estimate=COST,
        compiler_params=PARAMS,
        name="leaves",
    )(own, *others, source, picks, couplings, *later)


def first_of_pair(number):
    return (lax.axis_index("col") >> (number - 2)) % 2 == 0


def pair(mine, theirs, mine_first):
    first = jnp.where(mine_first, mine, theirs)
    second = jnp.where(mine_first, theirs, mine)
    return jnp.concatenate([first, second], axis=0)


def upper_body(picks_count, *refs):
    states = [(refs[0][...], refs[1][...])]
    rank = refs[0].shape[0]
    for got_ref in refs[4:1:-1]:
        high, middle, reduced = (got_ref[pl.ds(pos * rank, rank), :] for pos in range(3))
        states.append((high.astype(F32) + middle.astype(F32), reduced.astype(F32)))
    picks_ref, two_ref, other_ref, three_ref, one_ref, upper_out, top_out = refs[5:12]
    upper_ref, state_ref, sem = refs[12:]
    places = [
        (one_ref, upper_out.at[0, 0]),
        (upper_ref.at[0], upper_out.at[1, 0]),
        (upper_ref.at[1], upper_out.at[2, 0]),
        (state_ref.at[0], top_out.at[0, 0]),
        (state_ref.at[1], top_out.at[1, 0]),
    ]
    copies = [
        pltpu.make_async_copy(source, target, sem.at[pos])
        for pos, (source, target) in enumerate(places)
    ]
    copies[0].start()
    mine_first = first_of_pair(2)
    nodes = []
    for number, coupling_ref in enumerate((two_ref, other_ref)):
        mine, theirs = states[2 * number : 2 * number + 2]
        picks = picks_ref[picks_count - 3 + number]
        stacks = [pair(*parts, mine_first) for parts in zip(mine, theirs)]
        nodes.append((*stacks, coupling_ref[...], picks))
    mine, theirs = merge(nodes)
    upper_ref[0] = mine[0]
    copies[1].start()

    def early(skeleton):
        state_ref[0] = skeleton
        copies[3].start()

    mine_first = first_of_pair(3)
    stacks = [pair(*parts, mine_first) for parts in zip(mine[1:], theirs[1:])]
    ((interp, _, reduced),) = merge([(*stacks, three_ref[...], picks_ref[picks_count - 1])], early)
    upper_ref[1] = interp
    copies[2].start()
    state_ref[1] = reduced
    copies[4].start()
    for copy in copies:
        copy.wait()


def upper_levels(skeleton, reduced, got, picks, couplings, interp_one):
    rank, pool = picks.shape[1:]
    samples = skeleton.shape[1]
    return pl.pallas_call(
        lambda *refs: upper_body(picks.shape[0], *refs),
        out_shape=(
            jax.ShapeDtypeStruct((3, 1, rank, pool), F32),
            jax.ShapeDtypeStruct((2, 1, rank, samples), F32),
        ),
        out_specs=(pl.BlockSpec(memory_space=pl.ANY),) * 2,
        scratch_shapes=[
            pltpu.VMEM((2, rank, pool), F32),
            pltpu.VMEM((2, rank, samples), F32),
            pltpu.SemaphoreType.DMA((5,)),
        ],
        cost_estimate=COST,
        compiler_params=PARAMS,
        name="upper_levels",
    )(skeleton, reduced, *got[::-1], picks, *couplings, interp_one)


def one_hot(chosen, pool):
    place = lax.broadcasted_iota(jnp.int32, (pool, chosen.shape[1]), 0)
    return jnp.where(place.astype(F32) == chosen, 1.0, 0.0).astype(F32)


def couple(first, second, picks, gain, couplings_ref):
    rank = first.shape[1]
    points = jnp.concatenate([first, second], axis=1)
    entries = jnp.exp2(over(row_features(points, gain).astype(BF16), col_features(points), 0, 0))
    left = lax.broadcasted_iota(jnp.int32, entries.shape, 1) < rank
    upper = lax.broadcasted_iota(jnp.int32, entries.shape, 0) < rank
    entries = jnp.where(left == upper, 0.0, entries)
    chosen = select_rows(picks.T.astype(BF16), entries)
    high, middle, _ = split(jnp.concatenate([entries, chosen], axis=0))
    couplings_ref[...] = jnp.concatenate([high, high, middle], axis=1)


def coupling_shape(rank):
    return vmem((3 * rank, 6 * rank), BF16)


def skeletons_body(gain, span, counts, mine_ref, beside_ref, *refs):
    picks_ref, one_ref, two_ref, points_ref = refs
    rank, pool = picks_ref.shape[1:]
    leaf_count = counts[0]
    tables = 2 * (span + 16)
    nodes = []
    for source_ref in (mine_ref, beside_ref):
        rows = source_ref[pl.ds(tables, source_ref.shape[0] - tables), :rank].astype(F32)
        hots = [one_hot(rows[pos : pos + 1], pool) for pos in range(leaf_count + 1)]
        children = []
        for leaf in range(leaf_count):
            feats = source_ref[pl.ds(2 * span, 16), pl.ds(leaf * LEAF, LEAF)]
            children.append(over(feats, hots[leaf].astype(BF16), 1, 0))
        points = jnp.concatenate(children, axis=1)
        nodes.append(over(points, hots[leaf_count], 1, 0))
        if source_ref is mine_ref:
            couple(*children, hots[leaf_count], gain, one_ref)
            start = leaf_count + counts[1]
            level_two = lax.axis_index("col") // 2
            wanted = [level_two, level_two + 1 - 2 * (level_two % 2), counts[2] + level_two // 2]
            for row in wanted:
                place = lax.broadcasted_iota(jnp.int32, rows.shape, 0)
                named = jnp.where(place == start + row, rows, 0.0)
                hots.append(one_hot(jnp.sum(named, axis=0, keepdims=True), pool))
            for number, hot in enumerate(hots):
                picks_ref[number] = hot.T.astype(BF16)
            upper = hots[leaf_count + 1]
    mine, theirs = nodes
    mine_first = first_of_pair(2)
    first = jnp.where(mine_first, mine, theirs)
    second = jnp.where(mine_first, theirs, mine)
    couple(first, second, upper, gain, two_ref)
    points_ref[...] = jnp.concatenate([first, second], axis=1).astype(BF16)


def skeletons(packed, beside, tables, span, gain):
    leaf_count, rank = tables[0].shape
    counts = [table.shape[0] for table in tables]
    return pl.pallas_call(
        lambda *refs: skeletons_body(gain, span, counts, *refs),
        out_shape=(
            vmem((leaf_count + 4, rank, LEAF), BF16),
            coupling_shape(rank),
            coupling_shape(rank),
            vmem((16, 2 * rank), BF16),
        ),
        cost_estimate=COST,
        compiler_params=PARAMS,
        name="skeletons",
    )(packed, beside)


def top_couplings_body(gain, mine_ref, theirs_ref, picks_ref, other_ref, three_ref):
    count, rank, _ = picks_ref.shape
    picks = [picks_ref[count - pos].astype(F32).T for pos in (3, 2, 1)]
    rows, width = mine_ref.shape
    mine = mine_ref[...].astype(F32)
    theirs = theirs_ref[pl.ds(theirs_ref.shape[0] - rows, rows), :width].astype(F32)
    couple(theirs[:, :rank], theirs[:, rank:], picks[1], gain, other_ref)
    mine, theirs = over(mine, picks[0], 1, 0), over(theirs, picks[1], 1, 0)
    mine_first = first_of_pair(3)
    first = jnp.where(mine_first, mine, theirs)
    second = jnp.where(mine_first, theirs, mine)
    couple(first, second, picks[2], gain, three_ref)


def top_couplings(mine, theirs, picks, gain):
    return pl.pallas_call(
        lambda *refs: top_couplings_body(gain, *refs),
        out_shape=[coupling_shape(picks.shape[1])] * 2,
        cost_estimate=LONG,
        compiler_params=PARAMS,
        name="top_couplings",
    )(mine, theirs, picks)


def local(probes, points, leaf_skeleton, skeleton_one, skeleton_two, skeleton_three):
    span = probes.shape[1]
    row_count = lax.axis_size("row")
    col_count = lax.axis_size("col")
    gain = 16.0 / math.sqrt(4 * span * row_count * col_count)

    def swap(value, row_bits, col_bits):
        pairs = [
            (r * col_count + c, (r ^ row_bits) * col_count + (c ^ col_bits))
            for r in range(row_count)
            for c in range(col_count)
        ]
        return lax.ppermute(value, ("row", "col"), pairs)

    tables = (leaf_skeleton, skeleton_one, skeleton_two, skeleton_three)
    first, second, own_points = pack(probes, points, tables)
    beside_first, across_second = swap(first, 0, 1), swap(second, 2, 0)
    line = col_count // 2
    line_points = own_points
    for bit in range(1, col_count.bit_length() - 1):
        line_points = jnp.concatenate([line_points, swap(line_points, 0, 1 << bit)], axis=1)
        if bit == 1:
            line_points, *late = lax.optimization_barrier((line_points, first, second))
    beside_second, across_first = swap(late[1], 0, 1), swap(late[0], 2, 0)
    line_points = [line_points, swap(line_points, 1, 0)]
    near, far = range(2), range(2, line)
    groups = [
        [(core, chunk * span) for chunk in group] for core in range(2) for group in (near, far)
    ]
    feats, totals = first_product((first, second), line_points, groups, span, gain)
    beside_first, across_second, *totals = lax.optimization_barrier(
        (beside_first, across_second, *totals)
    )
    diagonal = [swap(beside_first, 2, 0), swap(across_second, 0, 1)]
    totals = product([beside_first, across_second], feats, totals, span, SHORT)
    beside_second, across_first, *totals = lax.optimization_barrier(
        (beside_second, across_first, *totals)
    )
    totals = product([beside_second, across_first], feats, totals, span)
    first, *totals = lax.optimization_barrier((first, *totals))
    picks, couplings_one, couplings_two, points_two = skeletons(
        first, beside_first, tables, span, gain
    )
    points_two, *totals = lax.optimization_barrier((points_two, *totals))
    pieces = [first, second, beside_first, beside_second, across_first, across_second, *diagonal]
    for bit in range(2, row_count.bit_length() - 1):
        more = [swap(value, 1 << bit, 0) for value in pieces]
        totals = product(more, feats, totals, span)
        pieces += more
    (theirs,) = product(diagonal, feats[3:], totals[3:], span, kind=BF16)
    from_sibling = swap(theirs, 1, 0)
    mine, theirs = product(diagonal, feats[1:3], totals[1:3], span)
    outs = [(range(0, line - 2, 2), F32), (range(1, line - 2, 2), BF16)]
    kept, sent = add_up(mine, from_sibling, outs, span)
    sent, theirs, points_two = lax.optimization_barrier((sent, theirs, points_two))
    arrived = swap(sent, 0, 2)
    from_sibling = swap(theirs, 1, 0)
    (mine,) = product(diagonal, feats[:1], totals[:1], span)
    own_sum, near_sent = near_up(mine, from_sibling, points_two, span)
    near_sum = swap(near_sent, 0, 2)
    received = []
    chunks = list(range(2, line, 2))
    bit = 2
    while chunks:
        sent_places = [pos for pos, chunk in enumerate(chunks) if chunk & bit]
        kept_places = [pos for pos, chunk in enumerate(chunks) if not chunk & bit]
        outs = [(sent_places, BF16)] + [(kept_places, F32)] * (len(kept_places) > 0)
        sent, *kept = add_up(kept, arrived, outs, span, (near_sent,), LONG)
        arrived = swap(sent, 0, 2 * bit)
        received.append(arrived[:span] if len(sent_places) > 1 else arrived)
        if kept:
            (kept,) = kept
            arrived = arrived[span:]
        chunks = [chunks[pos] for pos in kept_places]
        bit *= 2
    received.append(near_sum)
    later = top_couplings(points_two, near_sum, picks, gain)

    leaf_interp, interp_one, skeleton, reduced, sent = leaves(
        own_sum, received, first, picks, couplings_one, later, leaf_skeleton.shape[0]
    )
    got = [swap(sent, 0, bits) for bits in (1, 2, 3)]
    upper_interp, top_state = upper_levels(
        skeleton, reduced, got, picks, (couplings_two, *later), interp_one
    )
    return jnp.swapaxes(leaf_interp, 1, 2), jnp.swapaxes(upper_interp, 2, 3), top_state


def solution(mesh):
    placed = (
        P(None, ("row", "col"), None),
        P(None, None, ("row", "col")),
        P(("row", "col"), None),
        P(("row", "col"), None),
        P("row", None),
        P("row", None),
    )
    return jax.shard_map(
        local,
        mesh=mesh,
        in_specs=placed,
        out_specs=(
            P(("row", "col"), None, None),
            P(None, ("row", "col"), None, None),
            P(None, ("row", "col"), None, None),
        ),
        check_vma=False,
    )
```

```python
import math

import jax
import jax.numpy as jnp
from jax import lax
from jax.experimental import pallas as pl
from jax.experimental.pallas import tpu as pltpu
from jax.sharding import PartitionSpec as P

LEAF = 128
F32 = jnp.float32
BF16 = jnp.bfloat16
DOUBLINGS = 9
VMEM = pl.BlockSpec(memory_space=pltpu.VMEM)


def vmem(shape, kind=F32):
    return pltpu.VMEM(tuple(shape), kind)


COST = pl.CostEstimate(flops=10**9, bytes_accessed=0, transcendentals=0)
SHORT = pl.CostEstimate(flops=0, bytes_accessed=0, transcendentals=0)
LONG = pl.CostEstimate(flops=10**10, bytes_accessed=0, transcendentals=0)
PARAMS = pltpu.CompilerParams(vmem_limit_bytes=16 << 20)


def chebyshev_constants():
    taus = [1282.0 / 1280.0]
    for _ in range(DOUBLINGS):
        taus.append(2.0 * taus[-1] * taus[-1] - 1.0)
    front = 2.0**DOUBLINGS * math.prod(taus[:-1]) / taus[-1]
    return taus[:-1], front


TAUS, FRONT = chebyshev_constants()


def over(first, second, first_dim, second_dim):
    return lax.dot_general(
        first,
        second,
        (((first_dim,), (second_dim,)), ((), ())),
        preferred_element_type=F32,
    )


def split(value):
    high = value.astype(BF16)
    rest = value - high.astype(F32)
    middle = rest.astype(BF16)
    return high, middle, (rest - middle.astype(F32)).astype(BF16)


def norm_rows(norm, first, width):
    parts = [part.astype(F32) for part in split(norm)]
    place = lax.broadcasted_iota(jnp.int32, (16, width), 0)
    extra = jnp.where(place < 6, 1.0, 0.0)
    for pos in range(3):
        extra = jnp.where(place == pos + first, parts[pos], extra)
    return extra


def row_features(feats, gain):
    feats = feats.astype(F32)
    depth, width = feats.shape
    unit = math.log2(math.e) / (2.0 * depth)
    norm = jnp.sum(feats * feats, axis=0, keepdims=True) * -unit + math.log2(gain)
    parts = [part.astype(F32) for part in split(feats * (2.0 * unit))]
    return jnp.concatenate([*parts, norm_rows(norm, 0, width)], axis=0)


def col_features(feats):
    feats = feats.astype(F32)
    depth, width = feats.shape
    unit = math.log2(math.e) / (2.0 * depth)
    norm = jnp.sum(feats * feats, axis=0, keepdims=True) * -unit
    return jnp.concatenate([feats, feats, feats, norm_rows(norm, 3, width)], axis=0).astype(BF16)


def pack_body(*refs):
    probes_ref, points_ref, *table_refs = refs[:6]
    first_ref, second_ref, own_ref, held_ref, rows_ref, *held_tables, sem = refs[6:]
    span = own_ref.shape[1]
    pairs = [(points_ref, held_ref)]
    for number, half_ref in enumerate((first_ref, second_ref)):
        source = probes_ref.at[pl.ds(2 * span * number, 2 * span)]
        pairs.append((source, half_ref.at[pl.ds(0, 2 * span)]))
    pairs += zip(table_refs, held_tables)
    copies = [
        pltpu.make_async_copy(source, target, sem.at[pos])
        for pos, (source, target) in enumerate(pairs)
    ]
    for copy in copies:
        copy.start()
    rows_ref[...] = jnp.zeros_like(rows_ref)
    copies[0].wait()
    points = held_ref[...].astype(F32)
    for quarter in range(4):
        feats = points[:, quarter, :].astype(BF16)
        half_ref = (first_ref, second_ref)[quarter // 2]
        half_ref[pl.ds(2 * span + quarter % 2 * 16, 16), :] = feats
        if quarter == 0:
            own_ref[...] = feats
    for copy in copies[3:]:
        copy.wait()
    start = 0
    for table in held_tables:
        count, rank = table.shape
        rows_ref[pl.ds(start, count), pl.ds(0, rank)] = table[...].astype(F32)
        start += count
    first_ref[pl.ds(second_ref.shape[0], rows_ref.shape[0]), :] = rows_ref[...].astype(BF16)
    for copy in copies[1:3]:
        copy.wait()


def pack(probes, points, tables):
    quarters, span, samples = probes.shape
    table_rows = -(-sum(table.shape[0] for table in tables) // 16) * 16
    inputs = (probes.reshape(quarters * span, samples), points, *tables)
    return pl.pallas_call(
        pack_body,
        out_shape=(
            vmem((2 * (span + 16) + table_rows, samples), BF16),
            vmem((2 * (span + 16), samples), BF16),
            vmem((16, span), BF16),
        ),
        in_specs=[pl.BlockSpec(memory_space=pltpu.HBM)] * len(inputs),
        scratch_shapes=[
            pltpu.VMEM(points.shape, BF16),
            pltpu.VMEM((table_rows, samples), F32),
            *[pltpu.VMEM(table.shape, jnp.int32) for table in tables],
            pltpu.SemaphoreType.DMA((3 + len(tables),)),
        ],
        cost_estimate=COST,
        compiler_params=PARAMS,
        name="pack",
    )(*(pltpu.with_memory_space_constraint(value, pltpu.HBM) for value in inputs))


def masked(entries):
    shape = entries.shape
    row_leaf = lax.broadcasted_iota(jnp.int32, shape, 0) // LEAF
    col_leaf = lax.broadcasted_iota(jnp.int32, shape, 1) // LEAF
    return jnp.where(row_leaf == col_leaf, 0.0, entries)


def add_halves(half_refs, row_refs, cols_ref, put, span, own):
    for number, half_ref in enumerate(half_refs):
        for quarter in range(2):
            feats = half_ref[pl.ds(2 * span + 16 * quarter, 16), :]
            cols_ref[:, pl.ds((2 * number + quarter) * span, span)] = col_features(feats)
    columns = 2 * span * len(half_refs)
    for group, rows_ref in enumerate(row_refs):
        for start in range(0, rows_ref.shape[0], span):
            feats = rows_ref[pl.ds(start, span), :]
            entries = jnp.exp2(over(feats, cols_ref[:, :columns], 1, 0))
            if own and group == 0 and start == 0:
                entries = jnp.concatenate([masked(entries[:, :span]), entries[:, span:]], axis=1)
            randoms = [half_ref[pl.ds(0, 2 * span), :] for half_ref in half_refs]
            put(group, start, over(entries.astype(BF16), jnp.concatenate(randoms, axis=0), 1, 0))


def first_product_body(gain, span, groups, point_count, *refs):
    half_refs, point_refs = refs[:2], refs[2 : point_count + 2]
    row_refs = refs[point_count + 2 : point_count + 2 + len(groups)]
    total_refs, cols_ref = refs[point_count + 2 + len(groups) : -1], refs[-1]
    for rows_ref, places in zip(row_refs, groups):
        for pos, (array, start) in enumerate(places):
            feats = point_refs[array][:, pl.ds(start, span)]
            rows_ref[pl.ds(pos * span, span), :] = row_features(feats, gain).T.astype(BF16)

    def put(group, start, value):
        total_refs[group][pl.ds(start, span), :] = value

    add_halves(half_refs, row_refs, cols_ref, put, span, True)


def first_product(halves, points, groups, span, gain):
    samples = halves[0].shape[1]
    rows = [len(places) * span for places in groups]
    out = pl.pallas_call(
        lambda *refs: first_product_body(gain, span, groups, len(points), *refs),
        out_shape=[vmem((count, 64), BF16) for count in rows]
        + [vmem((count, samples), F32) for count in rows],
        scratch_shapes=[pltpu.VMEM((64, 4 * span), BF16)],
        cost_estimate=COST,
        compiler_params=PARAMS,
        name="first_product",
    )(*halves, *points)
    return out[: len(groups)], out[len(groups) :]


def product_body(span, half_count, count, *refs):
    half_refs, refs = refs[:half_count], refs[half_count:]
    row_refs, old_refs, total_refs = refs[:count], refs[count : 2 * count], refs[2 * count : -1]
    cols_ref = refs[-1]
    for number in range(0, half_count, 2):

        def put(group, start, value):
            place = pl.ds(start, span)
            base = old_refs if number == 0 else total_refs
            value = base[group][place, :] + value
            total_refs[group][place, :] = value.astype(total_refs[group].dtype)

        add_halves(half_refs[number : number + 2], row_refs, cols_ref, put, span, False)


def product(halves, rows, totals, span, cost=COST, kind=F32):
    return pl.pallas_call(
        lambda *refs: product_body(span, len(halves), len(rows), *refs),
        out_shape=[vmem(total.shape, kind) for total in totals],
        scratch_shapes=[pltpu.VMEM((64, 4 * span), BF16)],
        cost_estimate=cost,
        compiler_params=PARAMS,
        name="product",
    )(*halves, *rows, *totals)


def add_up_body(span, outs, mine_ref, theirs_ref, *refs):
    for (chunks, _), out_ref in zip(outs, refs[-len(outs) :]):
        for pos, chunk in enumerate(chunks):
            place = pl.ds(chunk * span, span)
            value = mine_ref[place, :] + theirs_ref[place, :].astype(F32)
            out_ref[pl.ds(pos * span, span), :] = value.astype(out_ref.dtype)


def add_up(mine, theirs, outs, span, after=(), cost=COST):
    samples = mine.shape[1]
    return pl.pallas_call(
        lambda *refs: add_up_body(span, outs, *refs),
        out_shape=[vmem((len(chunks) * span, samples), kind) for chunks, kind in outs],
        cost_estimate=cost,
        compiler_params=PARAMS,
        name="add_up",
    )(mine, theirs, *after)


def wide_product(first, second):
    high, middle, low = split(first)
    other_high, other_middle, other_low = split(second)
    return over(
        jnp.concatenate([high, high, middle, middle, low, high], axis=1),
        jnp.concatenate(
            [other_high, other_middle, other_high, other_middle, other_high, other_low], axis=1
        ),
        1,
        1,
    )


def near_product(first, second):
    high, middle, _ = split(first)
    return over(jnp.concatenate([high, high, middle], axis=1), near_parts(second), 1, 0)


def near_parts(second):
    high, middle, _ = split(second)
    return jnp.concatenate([high, middle, high], axis=0)


def exact_product(first, second):
    second = second.astype(BF16)
    return over(
        jnp.concatenate(split(first), axis=1), jnp.concatenate([second] * 3, axis=0), 1, 0
    )


def twice_product(twice, twice_parts, parts):
    high, middle, _ = twice_parts
    other_high, other_middle, other_low = parts
    left = lax.broadcasted_iota(jnp.int32, high.shape, 1) < high.shape[1] // 2
    low = twice - high.astype(F32) - middle.astype(F32)
    last = jnp.where(left, low, high.astype(F32)).astype(BF16)
    return over(
        jnp.concatenate([high, middle, last], axis=1),
        jnp.concatenate(
            [other_high, other_middle, other_high, other_middle, other_high, other_low], axis=0
        ),
        1,
        0,
    )


def select_rows(picks, value):
    return over(
        jnp.concatenate([picks] * 3, axis=1), jnp.concatenate(split(value), axis=0), 1, 0
    )


def interpolate(stacks, skeletons):
    rank, pool = skeletons[0].shape[0], stacks[0].shape[0]
    place = lax.broadcasted_iota(jnp.int32, (rank, 2 * rank), 0)
    other = lax.broadcasted_iota(jnp.int32, (rank, 2 * rank), 1)
    eyes = jnp.where((other == place) | (other == place + rank), 1.0, 0.0)
    states = []
    for skeleton, stack in zip(skeletons, stacks):
        products = wide_product(skeleton, jnp.concatenate([stack, skeleton, skeleton], axis=0))
        ridge = 0.05 * jnp.sum(skeleton * skeleton, keepdims=True) / rank + 1e-05
        inverse = 1.0 / (640.0 * ridge)
        cross, gram = products[:, :pool], products[:, pool:]
        parts = [jnp.concatenate(pair, axis=1) for pair in zip(split(cross), split(gram))]
        both = twice_product(gram, split(gram), parts)
        solved = cross + (cross - both[:, :pool] * inverse) * (1.0 / TAUS[0])
        power = eyes + (both[:, pool:] * inverse - 2.0 * gram) * (2.0 * inverse)
        states.append((solved, power, inverse))
    for number, tau in enumerate(TAUS[1:], 1):
        last = number == DOUBLINGS - 1
        later = []
        for solved, power, inverse in states:
            power_parts = split(power)
            parts = split(solved)
            if not last:
                parts = [jnp.concatenate(pair, axis=1) for pair in zip(parts, power_parts)]
            both = twice_product(power, power_parts, parts)
            solved = solved + both[:, :pool] * (1.0 / tau)
            later.append((solved, None if last else 2.0 * both[:, pool:] - eyes, inverse))
        states = later
    return [solved * (inverse * FRONT) for solved, _, inverse in states]


def merge(nodes, early=None):
    stacks, skeletons = [], []
    for samples, reduced, coupling, picks in nodes:
        pool = samples.shape[0]
        coupled = over(coupling, near_parts(reduced), 1, 0)
        stacks.append(samples - coupled[:pool])
        skeletons.append(select_rows(picks, samples) - coupled[pool:])
    if early is not None:
        early(skeletons[0])
    interps = interpolate(stacks, skeletons)
    return [
        (interp, skeleton, near_product(interp, node[1]))
        for interp, skeleton, node in zip(interps, skeletons, nodes)
    ]


def leaves_body(received, *refs):
    own_ref, *others = refs[: received + 1]
    source_ref, picks_ref, couplings_ref = refs[received + 1 : received + 4]
    leaf_ref, upper_ref, skeleton_ref, reduced_ref, sent_ref, held_ref, sem = refs[-7:]
    total = own_ref[...]
    for other in others:
        total = total + other[...].astype(F32)
    count = total.shape[0] // LEAF
    stacks = [total[leaf * LEAF : (leaf + 1) * LEAF] for leaf in range(count)]
    skeletons = [select_rows(picks_ref[leaf], stack) for leaf, stack in enumerate(stacks)]
    reduced = []
    for leaf, interp in enumerate(interpolate(stacks, skeletons)):
        held_ref[leaf] = interp
        reduced.append(exact_product(interp, source_ref[pl.ds(leaf * LEAF, LEAF), :]))
    copy = pltpu.make_async_copy(held_ref, leaf_ref, sem)
    copy.start()
    node = (
        jnp.concatenate(skeletons, axis=0),
        jnp.concatenate(reduced, axis=0),
        couplings_ref[...],
        picks_ref[count],
    )
    ((interp, skeleton, reduced),) = merge([node])
    upper_ref[...] = interp
    skeleton_ref[...] = skeleton
    reduced_ref[...] = reduced
    for pos, part in enumerate((*split(skeleton)[:2], reduced.astype(BF16))):
        sent_ref[pl.ds(pos * skeleton.shape[0], skeleton.shape[0]), :] = part
    copy.wait()


def leaves(own, others, source, picks, couplings, later, leaf_count):
    samples = own.shape[1]
    rank, pool = picks.shape[1:]
    return pl.pallas_call(
        lambda *refs: leaves_body(len(others), *refs),
        out_shape=(
            jax.ShapeDtypeStruct((leaf_count, rank, LEAF), F32),
            vmem((rank, pool), F32),
            vmem((rank, samples), F32),
            vmem((rank, samples), F32),
            vmem((3 * rank, samples), BF16),
        ),
        out_specs=(pl.BlockSpec(memory_space=pl.ANY), VMEM, VMEM, VMEM, VMEM),
        scratch_shapes=[pltpu.VMEM((leaf_count, rank, LEAF), F32), pltpu.SemaphoreType.DMA],
        cost_estimate=COST,
        compiler_params=PARAMS,
        name="leaves",
    )(own, *others, source, picks, couplings, *later)


def first_of_pair(number):
    return (lax.axis_index("col") >> (number - 2)) % 2 == 0


def pair(mine, theirs, mine_first):
    first = jnp.where(mine_first, mine, theirs)
    second = jnp.where(mine_first, theirs, mine)
    return jnp.concatenate([first, second], axis=0)


def upper_body(picks_count, *refs):
    states = [(refs[0][...], refs[1][...])]
    rank = refs[0].shape[0]
    for got_ref in refs[4:1:-1]:
        high, middle, reduced = (got_ref[pl.ds(pos * rank, rank), :] for pos in range(3))
        states.append((high.astype(F32) + middle.astype(F32), reduced.astype(F32)))
    picks_ref, two_ref, other_ref, three_ref, one_ref, upper_out, top_out = refs[5:12]
    upper_ref, state_ref, sem = refs[12:]
    places = [
        (one_ref, upper_out.at[0, 0]),
        (upper_ref.at[0], upper_out.at[1, 0]),
        (upper_ref.at[1], upper_out.at[2, 0]),
        (state_ref.at[0], top_out.at[0, 0]),
        (state_ref.at[1], top_out.at[1, 0]),
    ]
    copies = [
        pltpu.make_async_copy(source, target, sem.at[pos])
        for pos, (source, target) in enumerate(places)
    ]
    copies[0].start()
    mine_first = first_of_pair(2)
    nodes = []
    for number, coupling_ref in enumerate((two_ref, other_ref)):
        mine, theirs = states[2 * number : 2 * number + 2]
        picks = picks_ref[picks_count - 3 + number]
        stacks = [pair(*parts, mine_first) for parts in zip(mine, theirs)]
        nodes.append((*stacks, coupling_ref[...], picks))
    mine, theirs = merge(nodes)
    upper_ref[0] = mine[0]
    copies[1].start()

    def early(skeleton):
        state_ref[0] = skeleton
        copies[3].start()

    mine_first = first_of_pair(3)
    stacks = [pair(*parts, mine_first) for parts in zip(mine[1:], theirs[1:])]
    ((interp, _, reduced),) = merge([(*stacks, three_ref[...], picks_ref[picks_count - 1])], early)
    upper_ref[1] = interp
    copies[2].start()
    state_ref[1] = reduced
    copies[4].start()
    for copy in copies:
        copy.wait()


def upper_levels(skeleton, reduced, got, picks, couplings, interp_one):
    rank, pool = picks.shape[1:]
    samples = skeleton.shape[1]
    return pl.pallas_call(
        lambda *refs: upper_body(picks.shape[0], *refs),
        out_shape=(
            jax.ShapeDtypeStruct((3, 1, rank, pool), F32),
            jax.ShapeDtypeStruct((2, 1, rank, samples), F32),
        ),
        out_specs=(pl.BlockSpec(memory_space=pl.ANY),) * 2,
        scratch_shapes=[
            pltpu.VMEM((2, rank, pool), F32),
            pltpu.VMEM((2, rank, samples), F32),
            pltpu.SemaphoreType.DMA((5,)),
        ],
        cost_estimate=COST,
        compiler_params=PARAMS,
        name="upper_levels",
    )(skeleton, reduced, *got[::-1], picks, *couplings, interp_one)


def one_hot(chosen, pool):
    place = lax.broadcasted_iota(jnp.int32, (pool, chosen.shape[1]), 0)
    return jnp.where(place.astype(F32) == chosen, 1.0, 0.0).astype(F32)


def couple(first, second, picks, gain, couplings_ref):
    rank = first.shape[1]
    points = jnp.concatenate([first, second], axis=1)
    entries = jnp.exp2(over(row_features(points, gain).astype(BF16), col_features(points), 0, 0))
    left = lax.broadcasted_iota(jnp.int32, entries.shape, 1) < rank
    upper = lax.broadcasted_iota(jnp.int32, entries.shape, 0) < rank
    entries = jnp.where(left == upper, 0.0, entries)
    chosen = select_rows(picks.T.astype(BF16), entries)
    high, middle, _ = split(jnp.concatenate([entries, chosen], axis=0))
    couplings_ref[...] = jnp.concatenate([high, high, middle], axis=1)


def coupling_shape(rank):
    return vmem((3 * rank, 6 * rank), BF16)


def skeletons_body(gain, span, counts, mine_ref, beside_ref, *refs):
    picks_ref, one_ref, two_ref, points_ref = refs
    rank, pool = picks_ref.shape[1:]
    leaf_count = counts[0]
    tables = 2 * (span + 16)
    nodes = []
    for source_ref in (mine_ref, beside_ref):
        rows = source_ref[pl.ds(tables, source_ref.shape[0] - tables), :rank].astype(F32)
        hots = [one_hot(rows[pos : pos + 1], pool) for pos in range(leaf_count + 1)]
        children = []
        for leaf in range(leaf_count):
            feats = source_ref[pl.ds(2 * span, 16), pl.ds(leaf * LEAF, LEAF)]
            children.append(over(feats, hots[leaf].astype(BF16), 1, 0))
        points = jnp.concatenate(children, axis=1)
        nodes.append(over(points, hots[leaf_count], 1, 0))
        if source_ref is mine_ref:
            couple(*children, hots[leaf_count], gain, one_ref)
            start = leaf_count + counts[1]
            level_two = lax.axis_index("col") // 2
            wanted = [level_two, level_two + 1 - 2 * (level_two % 2), counts[2] + level_two // 2]
            for row in wanted:
                place = lax.broadcasted_iota(jnp.int32, rows.shape, 0)
                named = jnp.where(place == start + row, rows, 0.0)
                hots.append(one_hot(jnp.sum(named, axis=0, keepdims=True), pool))
            for number, hot in enumerate(hots):
                picks_ref[number] = hot.T.astype(BF16)
            upper = hots[leaf_count + 1]
    mine, theirs = nodes
    mine_first = first_of_pair(2)
    first = jnp.where(mine_first, mine, theirs)
    second = jnp.where(mine_first, theirs, mine)
    couple(first, second, upper, gain, two_ref)
    points_ref[...] = jnp.concatenate([first, second], axis=1).astype(BF16)


def skeletons(packed, beside, tables, span, gain):
    leaf_count, rank = tables[0].shape
    counts = [table.shape[0] for table in tables]
    return pl.pallas_call(
        lambda *refs: skeletons_body(gain, span, counts, *refs),
        out_shape=(
            vmem((leaf_count + 4, rank, LEAF), BF16),
            coupling_shape(rank),
            coupling_shape(rank),
            vmem((16, 2 * rank), BF16),
        ),
        cost_estimate=COST,
        compiler_params=PARAMS,
        name="skeletons",
    )(packed, beside)


def top_couplings_body(gain, mine_ref, theirs_ref, picks_ref, other_ref, three_ref):
    count, rank, _ = picks_ref.shape
    picks = [picks_ref[count - pos].astype(F32).T for pos in (3, 2, 1)]
    mine, theirs = mine_ref[...].astype(F32), theirs_ref[...].astype(F32)
    couple(theirs[:, :rank], theirs[:, rank:], picks[1], gain, other_ref)
    mine, theirs = over(mine, picks[0], 1, 0), over(theirs, picks[1], 1, 0)
    mine_first = first_of_pair(3)
    first = jnp.where(mine_first, mine, theirs)
    second = jnp.where(mine_first, theirs, mine)
    couple(first, second, picks[2], gain, three_ref)


def top_couplings(mine, theirs, picks, gain):
    return pl.pallas_call(
        lambda *refs: top_couplings_body(gain, *refs),
        out_shape=[coupling_shape(picks.shape[1])] * 2,
        cost_estimate=LONG,
        compiler_params=PARAMS,
        name="top_couplings",
    )(mine, theirs, picks)


def local(probes, points, leaf_skeleton, skeleton_one, skeleton_two, skeleton_three):
    span = probes.shape[1]
    row_count = lax.axis_size("row")
    col_count = lax.axis_size("col")
    gain = 16.0 / math.sqrt(4 * span * row_count * col_count)

    def swap(value, row_bits, col_bits):
        pairs = [
            (r * col_count + c, (r ^ row_bits) * col_count + (c ^ col_bits))
            for r in range(row_count)
            for c in range(col_count)
        ]
        return lax.ppermute(value, ("row", "col"), pairs)

    tables = (leaf_skeleton, skeleton_one, skeleton_two, skeleton_three)
    first, second, own_points = pack(probes, points, tables)
    beside_first, across_second = swap(first, 0, 1), swap(second, 2, 0)
    line = col_count // 2
    line_points = own_points
    for bit in range(1, col_count.bit_length() - 1):
        line_points = jnp.concatenate([line_points, swap(line_points, 0, 1 << bit)], axis=1)
        if bit == 1:
            line_points, *late = lax.optimization_barrier((line_points, first, second))
    beside_second, across_first = swap(late[1], 0, 1), swap(late[0], 2, 0)
    line_points = [line_points, swap(line_points, 1, 0)]
    near, far = range(2), range(2, line)
    groups = [
        [(core, chunk * span) for chunk in group] for core in range(2) for group in (near, far)
    ]
    feats, totals = first_product((first, second), line_points, groups, span, gain)
    beside_first, across_second, *totals = lax.optimization_barrier(
        (beside_first, across_second, *totals)
    )
    diagonal = [swap(beside_first, 2, 0), swap(across_second, 0, 1)]
    totals = product([beside_first, across_second], feats, totals, span, SHORT)
    beside_second, across_first, *totals = lax.optimization_barrier(
        (beside_second, across_first, *totals)
    )
    totals = product([beside_second, across_first], feats, totals, span)
    first, *totals = lax.optimization_barrier((first, *totals))
    picks, couplings_one, couplings_two, points_two = skeletons(
        first, beside_first, tables, span, gain
    )
    points_two, *totals = lax.optimization_barrier((points_two, *totals))
    pieces = [first, second, beside_first, beside_second, across_first, across_second, *diagonal]
    for bit in range(2, row_count.bit_length() - 1):
        more = [swap(value, 1 << bit, 0) for value in pieces]
        totals = product(more, feats, totals, span)
        pieces += more
    (theirs,) = product(diagonal, feats[3:], totals[3:], span, kind=BF16)
    from_sibling = swap(theirs, 1, 0)
    mine, theirs = product(diagonal, feats[1:3], totals[1:3], span)
    outs = [(range(0, line - 2, 2), F32), (range(1, line - 2, 2), BF16)]
    kept, sent = add_up(mine, from_sibling, outs, span)
    sent, theirs, points_two = lax.optimization_barrier((sent, theirs, points_two))
    arrived = swap(sent, 0, 2)
    from_sibling = swap(theirs, 1, 0)
    (mine,) = product(diagonal, feats[:1], totals[:1], span)
    own_sum, near_sent = add_up(mine, from_sibling, [([0], F32), ([1], BF16)], span)
    near_sum = swap(near_sent, 0, 2)
    received = []
    chunks = list(range(2, line, 2))
    bit = 2
    while chunks:
        sent_places = [pos for pos, chunk in enumerate(chunks) if chunk & bit]
        kept_places = [pos for pos, chunk in enumerate(chunks) if not chunk & bit]
        outs = [(sent_places, BF16)] + [(kept_places, F32)] * (len(kept_places) > 0)
        sent, *kept = add_up(kept, arrived, outs, span, (near_sent,), LONG)
        arrived = swap(sent, 0, 2 * bit)
        received.append(arrived[:span] if len(sent_places) > 1 else arrived)
        if kept:
            (kept,) = kept
            arrived = arrived[span:]
        chunks = [chunks[pos] for pos in kept_places]
        bit *= 2
    received.append(near_sum)
    other_points = swap(points_two, 0, 2)
    later = top_couplings(points_two, other_points, picks, gain)

    leaf_interp, interp_one, skeleton, reduced, sent = leaves(
        own_sum, received, first, picks, couplings_one, later, leaf_skeleton.shape[0]
    )
    got = [swap(sent, 0, bits) for bits in (1, 2, 3)]
    upper_interp, top_state = upper_levels(
        skeleton, reduced, got, picks, (couplings_two, *later), interp_one
    )
    return jnp.swapaxes(leaf_interp, 1, 2), jnp.swapaxes(upper_interp, 2, 3), top_state


def solution(mesh):
    placed = (
        P(None, ("row", "col"), None),
        P(None, None, ("row", "col")),
        P(("row", "col"), None),
        P(("row", "col"), None),
        P("row", None),
        P("row", None),
    )
    return jax.shard_map(
        local,
        mesh=mesh,
        in_specs=placed,
        out_specs=(
            P(("row", "col"), None, None),
            P(None, ("row", "col"), None, None),
            P(None, ("row", "col"), None, None),
        ),
        check_vma=False,
    )
```
